32 devices in a mesh: tm: 2 (over core), tile: 4 (over y, x), head: 4 (over z).
Axes of the slice: x: 2, y: 2, z: 4, core: 2. Of those that a mesh axis runs over, the one named last changes fastest.
Arguments:
- query: bfloat16 [2, 4, 2, 16, 16, 1536], P('tm', 'tile', None, None, None, 'head'), may hold values from -80 to 80
- keys: bfloat16 [2, 4, 2, 16, 16, 1536], P('tm', 'tile', None, None, None, 'head'), may hold values from -80 to 80
- values: bfloat16 [2, 4, 2, 16, 16, 1536], P('tm', 'tile', None, None, None, 'head'), may hold values from -6 to 6
- out_weight: bfloat16 [1536, 1536], P('head'), may hold values from -0.15625 to 0.15625
- radius: int32 [12], P('head'), may hold values from 1 to 4
- block_mask: int32 [12, 2, 2], P('head'), may hold values from 0 to 1, as said below
Outputs:
- mixed: bfloat16 [2, 4, 512, 1536], P('tm', 'tile', 'head')
The draws below stay inside these ranges and needn't reach their ends.
Inputs may be any that keep to these rules, and one draw needn't show every extreme that they name: For every head, block_mask is 1 on the diagonal of its table and 0 above it.
All inputs are finite; a program needn't handle non-finite values.
Results may differ from the reference program's by a relative error of at most 0.015.
Values may be sent and summed in bfloat16 or wider, within the bound.
No kernel may reach another device: no remote copies, remote signals or barrier semaphores. Data moves between devices by JAX's collectives and lax.ppermute only.
A program may use at most 128 MiB of HBM per device.

```python
import math
import jax
import jax.numpy as jnp
import numpy as np
from jax import lax

D = 1536
HEADS = 12
HD = 128
FRAMES = 2
TH = 16
TW = 16
RMAX = 4
NC = 2
TILES = 4
TOK = 512
N_TM = 2
N_TILE = 4


def paired_fields(key):
    shape = (N_TM, N_TILE, FRAMES, TH, TW, HEADS * HD)
    query = jax.random.normal(jax.random.fold_in(key, 101), shape, jnp.float32)
    keys = jax.random.normal(jax.random.fold_in(key, 202), shape, jnp.float32)
    return (jnp.clip(query, -80.0, 80.0), jnp.clip(keys, -80.0, 80.0))


def draw_query(key, part):
    return paired_fields(key)[0].astype(jnp.bfloat16)


def draw_keys(key, part):
    return paired_fields(key)[1].astype(jnp.bfloat16)


def draw_block_mask(key, part):
    shape = (HEADS, N_TM, N_TM)
    coins = jax.random.randint(jax.random.fold_in(key, 404), shape, 0, 2)
    rows_at = lax.broadcasted_iota(jnp.int32, shape, 1)
    cols_at = lax.broadcasted_iota(jnp.int32, shape, 2)
    below = jnp.where(rows_at > cols_at, coins, 0)
    return jnp.where(rows_at == cols_at, 1, below).astype(jnp.int32)


def touch_ends(drawn, rng, low, largest):
    longest = drawn.shape.index(max(drawn.shape))
    spots = []
    for shift in (0, 1):
        where = [jax.random.randint(jax.random.fold_in(rng, axis), (), 0, length) for axis, length in enumerate(drawn.shape)]
        where[longest] = (where[longest] + shift) % drawn.shape[longest]
        spots.append(tuple(where))
    return drawn.at[spots[0]].set(low).at[spots[1]].set(largest)


def shard_levels(key, shape, pieces, least, largest):
    def one(dim, blocks):
        draws = jax.random.uniform(jax.random.fold_in(jax.random.fold_in(key, 6), dim), (blocks,), jnp.float32, least / len(pieces), largest / len(pieces))
        return jnp.repeat(jnp.exp(draws), shape[dim] // blocks).reshape((-1,) + (1,) * (len(shape) - dim - 1))

    loudness = one(*pieces[0])
    for cut in pieces[1:]:
        loudness = loudness * one(*cut)
    return loudness


def normal_values(rng, extent, scale, bound, shards=(), kind=jnp.bfloat16):
    loudness = shard_levels(rng, extent, shards, -0.22, 0.18) if shards else 1.0
    entries = jax.random.normal(rng, extent, jnp.float32) * scale * loudness
    return jnp.minimum(jnp.maximum(entries, -bound), bound).astype(kind)


def setup_inputs(seed: int = 0) -> dict:
    streams_of = jax.random.split(jax.random.key(seed), 7)
    query = draw_query(jax.random.fold_in(streams_of[6], 71), 0)
    keys = draw_keys(jax.random.fold_in(streams_of[6], 71), 0)
    values = normal_values(streams_of[2], (NC, TILES, FRAMES, TH, TW, HEADS * HD), 1.0, 6.0, ((0, 2), (1, 4), (5, 4)))
    out_weight = normal_values(streams_of[3], (HEADS * HD, D), (HEADS * HD) ** -0.5, 0.15625, ((0, 4),))
    radius = touch_ends(jax.random.randint(streams_of[4], (HEADS,), 1, RMAX + 1), jax.random.fold_in(streams_of[4], 1), 1, RMAX).astype(jnp.int32)
    block_mask = draw_block_mask(jax.random.fold_in(streams_of[6], 71), 0)
    return {"query": query, "keys": keys, "values": values, "out_weight": out_weight, "radius": radius, "block_mask": block_mask}


def to_image(array, grid):
    width = array.shape[-1]
    array = array.reshape(NC, grid, grid, FRAMES, TH, TW, width)
    array = array.transpose(0, 3, 1, 4, 2, 5, 6)
    return array.reshape(NC, FRAMES, grid * TH, grid * TW, width)

def reference(query, keys, values, out_weight, radius, block_mask):
    grid = math.isqrt(N_TILE)
    high = grid * TH
    wide = grid * TW
    span = RMAX
    side = 2 * span + 1
    q_image = to_image(query, grid)
    pad_cfg = ((0, 0), (0, 0), (span, span), (span, span), (0, 0))
    k_image = jnp.pad(to_image(keys, grid), pad_cfg)
    v_image = jnp.pad(to_image(values, grid), pad_cfg)
    inside = jnp.pad(jnp.ones((high, wide), jnp.float32), span)
    shift_y = jnp.array(np.repeat(np.arange(-span, span + 1), side), dtype=jnp.int32)
    shift_x = jnp.array(np.tile(np.arange(-span, span + 1), side), dtype=jnp.int32)
    scale = 1.0 / math.sqrt(HD)

    def head_fn(head):
        q_head = lax.dynamic_slice_in_dim(q_image, head * HD, HD, 4).astype(jnp.float32)
        k_head = lax.dynamic_slice_in_dim(k_image, head * HD, HD, 4)
        v_head = lax.dynamic_slice_in_dim(v_image, head * HD, HD, 4)
        reach = radius[head]
        stretch_ok = (block_mask[head] > 0)[:, None, None, None, :, None]

        def score_at(index):
            step_y = shift_y[index]
            step_x = shift_x[index]
            zero = jnp.int32(0)
            starts = (zero, zero, (span + step_y).astype(jnp.int32), (span + step_x).astype(jnp.int32), zero)
            k_part = lax.dynamic_slice(k_head, starts, (NC, FRAMES, high, wide, HD)).astype(jnp.float32)
            v_part = lax.dynamic_slice(v_head, starts, (NC, FRAMES, high, wide, HD)).astype(jnp.float32)
            in_part = lax.dynamic_slice(inside, starts[2:4], (high, wide))
            scores = jnp.einsum('afyxd,bgyxd->afyxbg', q_head, k_part) * scale
            near = jnp.maximum(jnp.abs(step_y), jnp.abs(step_x)) <= reach
            usable = stretch_ok & (in_part[None, None, :, :, None, None] > 0) & near
            return (scores, usable, v_part)

        def top_step(index, best):
            scores, usable, v_part = score_at(index)
            masked = jnp.where(usable, scores, jnp.float32(-1e+30))
            return jnp.maximum(best, lax.optimization_barrier(jnp.max(masked, axis=(4, 5))))
        best = lax.fori_loop(0, side * side, top_step, jnp.full((NC, FRAMES, high, wide), -1e+30, jnp.float32))

        def add_step(index, carry):
            numer, denom = carry
            scores, usable, v_part = score_at(index)
            probs = jnp.where(usable, jnp.exp(scores - best[..., None, None]), jnp.float32(0.0))
            rounded = lax.optimization_barrier(probs.astype(jnp.bfloat16)).astype(jnp.float32)
            numer = numer + jnp.einsum('afyxbg,bgyxd->afyxd', rounded, v_part)
            denom = denom + lax.optimization_barrier(jnp.sum(probs, axis=(4, 5)))
            return (numer, denom)
        start = (jnp.zeros((NC, FRAMES, high, wide, HD), jnp.float32), jnp.zeros((NC, FRAMES, high, wide), jnp.float32))
        numer, denom = lax.fori_loop(0, side * side, add_step, start)
        return (numer / denom[..., None]).astype(jnp.bfloat16)
    attn = lax.map(head_fn, jnp.arange(HEADS, dtype=jnp.int32))
    attn = attn.transpose(1, 2, 3, 4, 0, 5).reshape(NC, FRAMES, grid, TH, grid, TW, HEADS * HD)
    attn = attn.transpose(0, 2, 4, 1, 3, 5, 6).reshape(NC * TILES * TOK, HEADS * HD)
    mixed = jnp.dot(attn, out_weight, preferred_element_type=jnp.float32).astype(jnp.bfloat16)
    return mixed.reshape(NC, TILES, TOK, D)
```

```python
import functools
import math

import jax
import jax.numpy as jnp
from jax import lax
from jax.experimental import pallas as pl
from jax.experimental.pallas import tpu as pltpu
from jax.sharding import PartitionSpec as P

RMAX = 4
FAR = -1e30
LOG2E = 1.4426950408889634
VMEM_LIMIT = 40 * 1024 * 1024


def passed_along(value, axis, by):
    peers = lax.axis_size(axis)
    pairs = [(i, i + by) for i in range(peers) if 0 <= i + by < peers]
    return lax.ppermute(value, axis, pairs)


def widen(key_part, value_part, span, row_move, col_move):
    grid = math.isqrt(lax.axis_size("tile"))
    above = None
    below = None
    for offset in (grid, -grid):
        if offset > 0:
            face_key = key_part[:, :, key_part.shape[2] - span :]
            face_value = value_part[:, :, value_part.shape[2] - span :]
        else:
            face_key = key_part[:, :, :span]
            face_value = value_part[:, :, :span]
        got = row_move(face_key, face_value, offset)
        if offset > 0:
            above = got
        else:
            below = got
    key_rows = jnp.concatenate([above[0], key_part, below[0]], axis=2)
    value_rows = jnp.concatenate([above[1], value_part, below[1]], axis=2)
    left = None
    right = None
    for offset in (1, -1):
        if offset > 0:
            face_key = key_rows[:, :, :, key_rows.shape[3] - span :]
            face_value = value_rows[:, :, :, value_rows.shape[3] - span :]
        else:
            face_key = key_rows[:, :, :, :span]
            face_value = value_rows[:, :, :, :span]
        got = col_move(face_key, face_value, offset)
        if offset > 0:
            left = got
        else:
            right = got
    key_full = jnp.concatenate([left[0], key_rows, right[0]], axis=3)
    value_full = jnp.concatenate([left[1], value_rows, right[1]], axis=3)
    return (key_full, value_full)


def windows_of(block, half_high, half_wide, win_high, win_wide, heads_here, head_dim):
    parts = []
    for band in (0, 1):
        for strip in (0, 1):
            parts.append(
                block[
                    :,
                    band * half_high : band * half_high + win_high,
                    strip * half_wide : strip * half_wide + win_wide,
                ]
            )
    stacked = jnp.stack(parts)
    return stacked.reshape(4, -1, heads_here, head_dim)


def any_grid(query, keys, values, out_weight, radius, block_mask):
    span = RMAX
    grid = math.isqrt(lax.axis_size("tile"))
    tile_at = lax.axis_index("tile")
    row_at = tile_at // grid
    col_at = tile_at % grid
    stretch_at = lax.axis_index("tm")
    frames, high, wide, channels = query.shape[2:]
    heads_here = radius.shape[0]
    head_dim = channels // heads_here
    tokens_here = frames * high * wide
    half_high = high // 2
    half_wide = wide // 2
    win_high = half_high + 2 * span
    win_wide = half_wide + 2 * span
    quarter = frames * half_high * half_wide
    queries = query[0, 0].reshape(frames, 2, half_high, 2, half_wide, channels)
    queries = queries.transpose(1, 3, 0, 2, 4, 5).reshape(4, quarter, heads_here, head_dim)
    query_y = jnp.broadcast_to(
        jnp.arange(half_high, dtype=jnp.int32)[None, :, None], (frames, half_high, half_wide)
    ).reshape(-1)
    query_x = jnp.broadcast_to(
        jnp.arange(half_wide, dtype=jnp.int32)[None, None, :], (frames, half_high, half_wide)
    ).reshape(-1)
    key_y = jnp.broadcast_to(
        jnp.arange(win_high, dtype=jnp.int32)[None, :, None] - span, (frames, win_high, win_wide)
    ).reshape(-1)
    key_x = jnp.broadcast_to(
        jnp.arange(win_wide, dtype=jnp.int32)[None, None, :] - span, (frames, win_high, win_wide)
    ).reshape(-1)
    band_at = jnp.array([0, 0, 1, 1], dtype=jnp.int32)
    strip_at = jnp.array([0, 1, 0, 1], dtype=jnp.int32)
    global_y = row_at * high + band_at[:, None] * half_high + key_y[None, :]
    global_x = col_at * wide + strip_at[:, None] * half_wide + key_x[None, :]
    inside = (global_y >= 0) & (global_y < grid * high) & (global_x >= 0) & (global_x < grid * wide)
    distance = jnp.maximum(
        jnp.abs(query_y[:, None] - key_y[None, :]), jnp.abs(query_x[:, None] - key_x[None, :])
    )
    near = distance[None, :, :] <= radius[:, None, None]
    allowed = near[None, :, :, :] & inside[:, None, None, :]
    scale = 1.0 / math.sqrt(head_dim)
    initial = (
        jnp.full((4, heads_here, quarter), -1e30, jnp.float32),
        jnp.zeros((4, heads_here, quarter), jnp.float32),
        jnp.zeros((4, heads_here, quarter, head_dim), jnp.float32),
    )

    def tile_move(face_key, face_value, offset):
        return passed_along((face_key, face_value), "tile", offset)

    key_all, value_all = (
        lax.all_gather(keys[0], "tm", axis=0, tiled=True),
        lax.all_gather(values[0], "tm", axis=0, tiled=True),
    )
    key_full, value_full = widen(key_all, value_all, span, tile_move, tile_move)
    stretch_ids = jnp.arange(key_full.shape[0], dtype=jnp.int32)

    def one_stretch(state, item):
        key_block, value_block, stretch_id = item
        visible = (
            lax.dynamic_slice_in_dim(
                lax.dynamic_index_in_dim(block_mask, stretch_at, 1, False), stretch_id, 1, 1
            )[:, 0]
            > 0
        )
        best, total, acc = state
        key_win = windows_of(
            key_block, half_high, half_wide, win_high, win_wide, heads_here, head_dim
        )
        value_win = windows_of(
            value_block, half_high, half_wide, win_high, win_wide, heads_here, head_dim
        )
        usable = allowed & visible[None, :, None, None]
        scores = (
            jnp.einsum("nqhd,nkhd->nhqk", queries, key_win, preferred_element_type=jnp.float32)
            * scale
        )
        masked = jnp.where(usable, scores, jnp.float32(-1e30))
        fresh = jnp.maximum(best, jnp.max(masked, axis=3))
        probs = jnp.where(usable, jnp.exp(scores - fresh[..., None]), jnp.float32(0.0))
        shrink = jnp.exp(best - fresh)
        total = total * shrink + jnp.sum(probs, axis=3)
        acc = acc * shrink[..., None] + jnp.einsum(
            "nhqk,nkhd->nhqd",
            probs.astype(jnp.bfloat16),
            value_win,
            preferred_element_type=jnp.float32,
        )
        return ((fresh, total, acc), None)

    final, unused = lax.scan(one_stretch, initial, (key_full, value_full, stretch_ids))
    best, total, acc = final
    attn = (acc / total[..., None]).astype(jnp.bfloat16)
    attn = attn.transpose(0, 2, 1, 3).reshape(
        2, 2, frames, half_high, half_wide, heads_here * head_dim
    )
    attn = attn.transpose(2, 0, 3, 1, 4, 5).reshape(tokens_here, heads_here * head_dim)
    mixed = lax.psum_scatter(
        jnp.dot(attn, out_weight, preferred_element_type=jnp.float32).astype(jnp.bfloat16),
        "head",
        scatter_dimension=0,
        tiled=True,
    )
    return mixed.reshape(1, 1, -1, out_weight.shape[1])


def face_kernel(at_ref, k_ref, v_ref, row_ref, col_ref, corner_ref, *, high, wide, span):
    frames = k_ref.shape[0]
    cells = high * wide
    y0 = jnp.where(at_ref[0] == 0, high - span, 0)
    x0 = jnp.where(at_ref[1] == 0, wide - span, 0)

    def picker(count, cell_of):
        row = lax.broadcasted_iota(jnp.int32, (count, cells), 0)
        col = lax.broadcasted_iota(jnp.int32, (count, cells), 1)
        return (col == cell_of(row)).astype(jnp.bfloat16)

    beside = picker(high * span, lambda i: (i // span) * wide + x0 + i % span)
    across = picker(span * span, lambda i: (y0 + i // span) * wide + x0 + i % span)
    for which, ref in enumerate((k_ref, v_ref)):
        for f in range(frames):
            row_ref[which, f] = ref[f, pl.ds(y0, span)].reshape(span * wide, -1)
            whole = ref[f].reshape(cells, -1)
            col_ref[which, f] = jnp.dot(
                beside, whole, preferred_element_type=jnp.float32
            ).astype(jnp.bfloat16)
            corner_ref[which, f] = jnp.dot(
                across, whole, preferred_element_type=jnp.float32
            ).astype(jnp.bfloat16)


def join_kernel(k_ref, v_ref, row_ref, col_ref, corner_ref, out_ref, *, cells):
    frames = k_ref.shape[0]
    for which, ref in enumerate((k_ref, v_ref)):
        at = 0
        for f in range(frames):
            out_ref[which, at : at + cells] = ref[f].reshape(cells, -1)
            at += cells
        for part in (row_ref, col_ref, corner_ref):
            for f in range(frames):
                size = part.shape[2]
                out_ref[which, at : at + size] = part[which, f]
                at += size


def distances(at_ref, count, high, wide, span, frames):
    cells = high * wide
    j = lax.broadcasted_iota(jnp.int32, (1, count), 1)
    y_off = jnp.where(at_ref[0] == 0, high, -span)
    x_off = jnp.where(at_ref[1] == 0, wide, -span)
    own = j % cells
    ky, kx = own // wide, own % wide
    base = frames * cells
    c = (j - base) % (span * wide)
    ky = jnp.where(j >= base, y_off + c // wide, ky)
    kx = jnp.where(j >= base, c % wide, kx)
    base += frames * span * wide
    c = (j - base) % (span * high)
    ky = jnp.where(j >= base, c // span, ky)
    kx = jnp.where(j >= base, x_off + c % span, kx)
    base += frames * span * high
    c = (j - base) % (span * span)
    ky = jnp.where(j >= base, y_off + c // span, ky)
    kx = jnp.where(j >= base, x_off + c % span, kx)
    i = lax.broadcasted_iota(jnp.int32, (cells, 1), 0)
    return jnp.maximum(jnp.abs(i // wide - ky), jnp.abs(i % wide - kx))


def attend(at_ref, q_ref, kv_ref, dist_ref, head, start, step, head_dim, factor, before):
    cells = dist_ref.shape[0]
    cols = slice(head * head_dim, (head + 1) * head_dim)
    s = lax.dot_general(
        q_ref[start : start + step, cols],
        kv_ref[0, :, cols],
        (((1,), (1,)), ((), ())),
        preferred_element_type=jnp.float32,
    )
    d = dist_ref[start % cells : start % cells + step]
    s = jnp.where(d <= at_ref[2 + head], s * factor, FAR)
    m = jnp.max(s, axis=1, keepdims=True)
    if before is not None:
        m = jnp.maximum(m, before)
    p = jnp.exp2(s - m).astype(jnp.bfloat16)
    v = kv_ref[1, :, cols]
    both = jnp.concatenate([v, jnp.ones_like(v)], axis=1)
    return m, jnp.dot(p, both, preferred_element_type=jnp.float32)


def own_kernel(at_ref, q_ref, kv_ref, acc_ref, sum_ref, max_ref, dist_ref, *, geometry, heads, step):
    high, wide, span, frames, head_dim, factor = geometry
    dist_ref[...] = distances(at_ref, kv_ref.shape[1], high, wide, span, frames)
    for head in range(heads):
        cols = slice(head * head_dim, (head + 1) * head_dim)
        for start in range(0, q_ref.shape[0], step):
            m, got = attend(
                at_ref, q_ref, kv_ref, dist_ref, head, start, step, head_dim, factor, None
            )
            rows = slice(start, start + step)
            acc_ref[rows, cols] = got[:, :head_dim]
            sum_ref[rows, cols] = got[:, head_dim:]
            max_ref[rows, cols] = jnp.broadcast_to(m, (step, head_dim))


def other_kernel(
    at_ref, q_ref, kv_ref, acc_ref, sum_ref, max_ref, out_ref, dist_ref, *, geometry, heads, step
):
    high, wide, span, frames, head_dim, factor = geometry
    dist_ref[...] = distances(at_ref, kv_ref.shape[1], high, wide, span, frames)
    for head in range(heads):
        cols = slice(head * head_dim, (head + 1) * head_dim)
        seen = at_ref[2 + heads + head] > 0

        @pl.when(seen)
        def _():
            for start in range(0, q_ref.shape[0], step):
                rows = slice(start, start + step)
                old = max_ref[rows, cols]
                m, got = attend(
                    at_ref, q_ref, kv_ref, dist_ref, head, start, step, head_dim, factor, old[:, :1]
                )
                shrink = jnp.exp2(old - m)
                acc = acc_ref[rows, cols] * shrink + got[:, :head_dim]
                total = sum_ref[rows, cols] * shrink + got[:, head_dim:]
                out_ref[rows, cols] = (acc / total).astype(jnp.bfloat16)

        @pl.when(jnp.logical_not(seen))
        def _():
            out_ref[:, cols] = (acc_ref[:, cols] / sum_ref[:, cols]).astype(jnp.bfloat16)


def project_kernel(attn_ref, w_ref, out_ref):
    groups, tokens, width = attn_ref.shape
    total = jnp.zeros(out_ref.shape, jnp.float32)
    for g in range(groups):
        total += jnp.dot(
            attn_ref[g],
            w_ref[g * width : (g + 1) * width],
            preferred_element_type=jnp.float32,
        )
    out_ref[...] = total.astype(jnp.bfloat16)


def two_by_two(query, keys, values, out_weight, radius, block_mask):
    span = RMAX
    frames, high, wide, channels = query.shape[2:]
    heads = radius.shape[0]
    head_dim = channels // heads
    cells = high * wide
    tokens = frames * cells
    groups = lax.axis_size("head")
    width = out_weight.shape[1]
    tile_at = lax.axis_index("tile")
    stretch_at = lax.axis_index("tm")
    smem = pl.BlockSpec(memory_space=pltpu.SMEM)
    vmem = pl.BlockSpec(memory_space=pltpu.VMEM)
    params = pltpu.CompilerParams(vmem_limit_bytes=VMEM_LIMIT)

    peers = lax.axis_size("tm") * lax.axis_size("tile")
    part = out_weight.shape[0] // peers
    place = stretch_at * lax.axis_size("tile") + tile_at
    mine = lax.dynamic_slice_in_dim(out_weight, place * part, part, 0)
    weight = lax.all_gather(mine, ("head", "tm", "tile"), axis=0, tiled=True)

    seen = lax.dynamic_index_in_dim(block_mask, stretch_at, 1, False)[:, 0]
    seen = jnp.where(stretch_at > 0, seen, 0)
    at = jnp.concatenate([jnp.stack([tile_at // 2, tile_at % 2]), radius, seen]).astype(jnp.int32)

    q = query[0, 0].reshape(tokens, channels)
    k = keys[0, 0]
    v = values[0, 0]
    bf16 = jnp.bfloat16
    faces = pl.pallas_call(
        functools.partial(face_kernel, high=high, wide=wide, span=span),
        out_shape=[
            jax.ShapeDtypeStruct((2, frames, span * wide, channels), bf16),
            jax.ShapeDtypeStruct((2, frames, span * high, channels), bf16),
            jax.ShapeDtypeStruct((2, frames, span * span, channels), bf16),
        ],
        in_specs=[smem, vmem, vmem],
        out_specs=[vmem] * 3,
        compiler_params=params,
        name="faces",
    )(at, k, v)
    got = [
        lax.ppermute(face, "tile", [(t, t ^ flip) for t in range(4)])
        for face, flip in zip(faces, (2, 1, 3))
    ]
    count = frames * (cells + span * (wide + high + span))
    kv = pl.pallas_call(
        functools.partial(join_kernel, cells=cells),
        out_shape=jax.ShapeDtypeStruct((2, count, channels), bf16),
        in_specs=[vmem] * 5,
        out_specs=vmem,
        compiler_params=params,
        name="join",
    )(k, v, *got)
    kv_first = lax.ppermute(kv, "tm", [(0, 1)])

    geometry = (high, wide, span, frames, head_dim, LOG2E / math.sqrt(head_dim))
    step = 128
    f32 = jnp.float32
    scratch = [pltpu.VMEM((cells, count), jnp.int32)]
    flops = 4 * tokens * count * channels
    state = pl.pallas_call(
        functools.partial(own_kernel, geometry=geometry, heads=heads, step=step),
        out_shape=[jax.ShapeDtypeStruct((tokens, channels), f32)] * 3,
        in_specs=[smem, vmem, vmem],
        out_specs=[vmem] * 3,
        scratch_shapes=scratch,
        compiler_params=params,
        cost_estimate=pl.CostEstimate(
            flops=flops, bytes_accessed=4 * tokens * channels * 4, transcendentals=0
        ),
        name="own",
    )(at, q, kv)
    attn = pl.pallas_call(
        functools.partial(other_kernel, geometry=geometry, heads=heads, step=step),
        out_shape=jax.ShapeDtypeStruct((tokens, channels), bf16),
        in_specs=[smem] + [vmem] * 5,
        out_specs=vmem,
        scratch_shapes=scratch,
        compiler_params=params,
        cost_estimate=pl.CostEstimate(
            flops=flops, bytes_accessed=4 * tokens * channels * 4, transcendentals=0
        ),
        name="other",
    )(at, q, kv_first, *state)

    spread = lax.all_to_all(
        attn.reshape(groups, tokens // groups, channels), "head", 0, 0, tiled=False
    )
    mixed = pl.pallas_call(
        project_kernel,
        out_shape=jax.ShapeDtypeStruct((tokens // groups, width), bf16),
        in_specs=[vmem] * 2,
        out_specs=vmem,
        compiler_params=params,
        name="project",
    )(spread, weight)
    return mixed.reshape(1, 1, -1, width)


def solution(mesh):
    in_specs = (
        P("tm", "tile", None, None, None, "head"),
        P("tm", "tile", None, None, None, "head"),
        P("tm", "tile", None, None, None, "head"),
        P("head", None),
        P("head"),
        P("head", None, None),
    )
    out_specs = P("tm", "tile", "head", None)
    small = mesh.shape["tile"] == 4 and mesh.shape["tm"] == 2
    return jax.shard_map(
        two_by_two if small else any_grid,
        mesh=mesh,
        in_specs=in_specs,
        out_specs=out_specs,
        check_vma=False,
    )
```

```python
import functools
import math

import jax
import jax.numpy as jnp
from jax import lax
from jax.experimental import pallas as pl
from jax.experimental.pallas import tpu as pltpu
from jax.sharding import PartitionSpec as P

RMAX = 4
FAR = -1e30
LOG2E = 1.4426950408889634
VMEM_LIMIT = 24 * 1024 * 1024


def passed_along(value, axis, by):
    peers = lax.axis_size(axis)
    pairs = [(i, i + by) for i in range(peers) if 0 <= i + by < peers]
    return lax.ppermute(value, axis, pairs)


def widen(key_part, value_part, span, row_move, col_move):
    grid = math.isqrt(lax.axis_size("tile"))
    above = None
    below = None
    for offset in (grid, -grid):
        if offset > 0:
            face_key = key_part[:, :, key_part.shape[2] - span :]
            face_value = value_part[:, :, value_part.shape[2] - span :]
        else:
            face_key = key_part[:, :, :span]
            face_value = value_part[:, :, :span]
        got = row_move(face_key, face_value, offset)
        if offset > 0:
            above = got
        else:
            below = got
    key_rows = jnp.concatenate([above[0], key_part, below[0]], axis=2)
    value_rows = jnp.concatenate([above[1], value_part, below[1]], axis=2)
    left = None
    right = None
    for offset in (1, -1):
        if offset > 0:
            face_key = key_rows[:, :, :, key_rows.shape[3] - span :]
            face_value = value_rows[:, :, :, value_rows.shape[3] - span :]
        else:
            face_key = key_rows[:, :, :, :span]
            face_value = value_rows[:, :, :, :span]
        got = col_move(face_key, face_value, offset)
        if offset > 0:
            left = got
        else:
            right = got
    key_full = jnp.concatenate([left[0], key_rows, right[0]], axis=3)
    value_full = jnp.concatenate([left[1], value_rows, right[1]], axis=3)
    return (key_full, value_full)


def windows_of(block, half_high, half_wide, win_high, win_wide, heads_here, head_dim):
    parts = []
    for band in (0, 1):
        for strip in (0, 1):
            parts.append(
                block[
                    :,
                    band * half_high : band * half_high + win_high,
                    strip * half_wide : strip * half_wide + win_wide,
                ]
            )
    stacked = jnp.stack(parts)
    return stacked.reshape(4, -1, heads_here, head_dim)


def any_grid(query, keys, values, out_weight, radius, block_mask):
    span = RMAX
    grid = math.isqrt(lax.axis_size("tile"))
    tile_at = lax.axis_index("tile")
    row_at = tile_at // grid
    col_at = tile_at % grid
    stretch_at = lax.axis_index("tm")
    frames, high, wide, channels = query.shape[2:]
    heads_here = radius.shape[0]
    head_dim = channels // heads_here
    tokens_here = frames * high * wide
    half_high = high // 2
    half_wide = wide // 2
    win_high = half_high + 2 * span
    win_wide = half_wide + 2 * span
    quarter = frames * half_high * half_wide
    queries = query[0, 0].reshape(frames, 2, half_high, 2, half_wide, channels)
    queries = queries.transpose(1, 3, 0, 2, 4, 5).reshape(4, quarter, heads_here, head_dim)
    query_y = jnp.broadcast_to(
        jnp.arange(half_high, dtype=jnp.int32)[None, :, None], (frames, half_high, half_wide)
    ).reshape(-1)
    query_x = jnp.broadcast_to(
        jnp.arange(half_wide, dtype=jnp.int32)[None, None, :], (frames, half_high, half_wide)
    ).reshape(-1)
    key_y = jnp.broadcast_to(
        jnp.arange(win_high, dtype=jnp.int32)[None, :, None] - span, (frames, win_high, win_wide)
    ).reshape(-1)
    key_x = jnp.broadcast_to(
        jnp.arange(win_wide, dtype=jnp.int32)[None, None, :] - span, (frames, win_high, win_wide)
    ).reshape(-1)
    band_at = jnp.array([0, 0, 1, 1], dtype=jnp.int32)
    strip_at = jnp.array([0, 1, 0, 1], dtype=jnp.int32)
    global_y = row_at * high + band_at[:, None] * half_high + key_y[None, :]
    global_x = col_at * wide + strip_at[:, None] * half_wide + key_x[None, :]
    inside = (global_y >= 0) & (global_y < grid * high) & (global_x >= 0) & (global_x < grid * wide)
    distance = jnp.maximum(
        jnp.abs(query_y[:, None] - key_y[None, :]), jnp.abs(query_x[:, None] - key_x[None, :])
    )
    near = distance[None, :, :] <= radius[:, None, None]
    allowed = near[None, :, :, :] & inside[:, None, None, :]
    scale = 1.0 / math.sqrt(head_dim)
    initial = (
        jnp.full((4, heads_here, quarter), -1e30, jnp.float32),
        jnp.zeros((4, heads_here, quarter), jnp.float32),
        jnp.zeros((4, heads_here, quarter, head_dim), jnp.float32),
    )

    def tile_move(face_key, face_value, offset):
        return passed_along((face_key, face_value), "tile", offset)

    key_all, value_all = (
        lax.all_gather(keys[0], "tm", axis=0, tiled=True),
        lax.all_gather(values[0], "tm", axis=0, tiled=True),
    )
    key_full, value_full = widen(key_all, value_all, span, tile_move, tile_move)
    stretch_ids = jnp.arange(key_full.shape[0], dtype=jnp.int32)

    def one_stretch(state, item):
        key_block, value_block, stretch_id = item
        visible = (
            lax.dynamic_slice_in_dim(
                lax.dynamic_index_in_dim(block_mask, stretch_at, 1, False), stretch_id, 1, 1
            )[:, 0]
            > 0
        )
        best, total, acc = state
        key_win = windows_of(
            key_block, half_high, half_wide, win_high, win_wide, heads_here, head_dim
        )
        value_win = windows_of(
            value_block, half_high, half_wide, win_high, win_wide, heads_here, head_dim
        )
        usable = allowed & visible[None, :, None, None]
        scores = (
            jnp.einsum("nqhd,nkhd->nhqk", queries, key_win, preferred_element_type=jnp.float32)
            * scale
        )
        masked = jnp.where(usable, scores, jnp.float32(-1e30))
        fresh = jnp.maximum(best, jnp.max(masked, axis=3))
        probs = jnp.where(usable, jnp.exp(scores - fresh[..., None]), jnp.float32(0.0))
        shrink = jnp.exp(best - fresh)
        total = total * shrink + jnp.sum(probs, axis=3)
        acc = acc * shrink[..., None] + jnp.einsum(
            "nhqk,nkhd->nhqd",
            probs.astype(jnp.bfloat16),
            value_win,
            preferred_element_type=jnp.float32,
        )
        return ((fresh, total, acc), None)

    final, unused = lax.scan(one_stretch, initial, (key_full, value_full, stretch_ids))
    best, total, acc = final
    attn = (acc / total[..., None]).astype(jnp.bfloat16)
    attn = attn.transpose(0, 2, 1, 3).reshape(
        2, 2, frames, half_high, half_wide, heads_here * head_dim
    )
    attn = attn.transpose(2, 0, 3, 1, 4, 5).reshape(tokens_here, heads_here * head_dim)
    mixed = lax.psum_scatter(
        jnp.dot(attn, out_weight, preferred_element_type=jnp.float32).astype(jnp.bfloat16),
        "head",
        scatter_dimension=0,
        tiled=True,
    )
    return mixed.reshape(1, 1, -1, out_weight.shape[1])


def tile_place():
    tile_at = lax.axis_index("tile")
    return tile_at // 2, tile_at % 2


def face_kernel(
    k_ref, v_ref, w_ref, row_ref, col_ref, corner_ref, tile_ref, part_ref, sems, *, geometry
):
    high, wide, span, frames = geometry[:4]
    cells = high * wide
    row_at, col_at = tile_place()
    y0 = jnp.where(row_at == 0, high - span, 0)
    x0 = jnp.where(col_at == 0, wide - span, 0)
    tall, broad = part_ref.shape
    top = pl.multiple_of(lax.axis_index("tile") * tall, 16)
    edge = pl.multiple_of(lax.axis_index("tm") * broad, 128)
    copies = [
        pltpu.make_async_copy(ref, tile_ref.at[which], sems.at[which])
        for which, ref in enumerate((k_ref, v_ref))
    ]
    copies.append(
        pltpu.make_async_copy(
            w_ref.at[pl.ds(top, tall), pl.ds(edge, broad)], part_ref, sems.at[2]
        )
    )
    for copy in copies:
        copy.start()

    def picker(count, cell_of):
        row = lax.broadcasted_iota(jnp.int32, (count, cells), 0)
        col = lax.broadcasted_iota(jnp.int32, (count, cells), 1)
        return (col == cell_of(row)).astype(jnp.bfloat16)

    beside = picker(high * span, lambda i: (i // span) * wide + x0 + i % span)
    across = picker(span * span, lambda i: (y0 + i // span) * wide + x0 + i % span)
    for which in range(2):
        copies[which].wait()
        for f in range(frames):
            start = pl.multiple_of(f * cells + y0 * wide, 16)
            row_ref[which, f] = tile_ref[which, pl.ds(start, span * wide)]
            whole = tile_ref[which, f * cells : (f + 1) * cells]
            col_ref[which, f] = jnp.dot(
                beside, whole, preferred_element_type=jnp.float32
            ).astype(jnp.bfloat16)
            corner_ref[which, f] = jnp.dot(
                across, whole, preferred_element_type=jnp.float32
            ).astype(jnp.bfloat16)
    copies[2].wait()


def edge_kernel(row_ref, col_ref, corner_ref, out_ref):
    for which in range(2):
        at = 0
        for part in (row_ref, col_ref, corner_ref):
            for f in range(part.shape[1]):
                size = part.shape[2]
                out_ref[which, at : at + size] = part[which, f]
                at += size


def join(tile_ref, edge_ref, kv_ref):
    base = tile_ref.shape[1]
    kv_ref[:, :base] = tile_ref[...]
    kv_ref[:, base:] = edge_ref[...]


def distances(count, high, wide, span, frames):
    row_at, col_at = tile_place()
    cells = high * wide
    j = lax.broadcasted_iota(jnp.int32, (1, count), 1)
    y_off = jnp.where(row_at == 0, high, -span)
    x_off = jnp.where(col_at == 0, wide, -span)
    own = j % cells
    ky, kx = own // wide, own % wide
    base = frames * cells
    c = (j - base) % (span * wide)
    ky = jnp.where(j >= base, y_off + c // wide, ky)
    kx = jnp.where(j >= base, c % wide, kx)
    base += frames * span * wide
    c = (j - base) % (span * high)
    ky = jnp.where(j >= base, c // span, ky)
    kx = jnp.where(j >= base, x_off + c % span, kx)
    base += frames * span * high
    c = (j - base) % (span * span)
    ky = jnp.where(j >= base, y_off + c // span, ky)
    kx = jnp.where(j >= base, x_off + c % span, kx)
    i = lax.broadcasted_iota(jnp.int32, (cells, 1), 0)
    return jnp.maximum(jnp.abs(i // wide - ky), jnp.abs(i % wide - kx))


def attend(reach, q, kv_ref, dist, cols, factor, before):
    s = lax.dot_general(
        q, kv_ref[0, :, cols], (((1,), (1,)), ((), ())), preferred_element_type=jnp.float32
    )
    s = jnp.where(dist <= reach, s * factor, FAR)
    m = jnp.max(s, axis=1, keepdims=True)
    if before is not None:
        m = jnp.maximum(m, before)
    p = jnp.exp2(s - m).astype(jnp.bfloat16)
    v = kv_ref[1, :, cols]
    both = jnp.concatenate([v, jnp.ones_like(v)], axis=1)
    return m, jnp.dot(p, both, preferred_element_type=jnp.float32)


def own_kernel(
    reach_ref,
    q_ref,
    tile_ref,
    edge_ref,
    acc_ref,
    sum_ref,
    max_ref,
    kv_ref,
    dist_ref,
    *,
    geometry,
    heads,
):
    high, wide, span, frames, head_dim, factor, step = geometry
    cells = high * wide
    join(tile_ref, edge_ref, kv_ref)
    dist_ref[...] = distances(kv_ref.shape[1], high, wide, span, frames)
    for head in range(heads):
        cols = slice(head * head_dim, (head + 1) * head_dim)
        for start in range(0, q_ref.shape[0], step):
            rows = slice(start, start + step)
            near = slice(start % cells, start % cells + step)
            m, got = attend(
                reach_ref[head], q_ref[rows, cols], kv_ref, dist_ref[near], cols, factor, None
            )
            acc_ref[rows, cols] = got[:, :head_dim]
            sum_ref[rows, cols] = got[:, head_dim:]
            max_ref[rows, cols] = jnp.broadcast_to(m, (step, head_dim))


def other_kernel(
    reach_ref,
    mask_ref,
    q_ref,
    acc_ref,
    sum_ref,
    max_ref,
    tile_ref,
    edge_ref,
    *rest,
    geometry,
    heads,
):
    *outs, kv_ref, dist_ref = rest
    high, wide, span, frames, head_dim, factor, step = geometry
    cells = high * wide
    groups = len(outs)
    head_at = lax.axis_index("head")
    stretch_at = lax.axis_index("tm")

    @pl.when(stretch_at > 0)
    def _():
        join(tile_ref, edge_ref, kv_ref)
        dist_ref[...] = distances(kv_ref.shape[1], high, wide, span, frames)

    for head in range(heads):
        cols = slice(head * head_dim, (head + 1) * head_dim)
        seen = (stretch_at > 0) & (mask_ref[stretch_at, 0, head] > 0)
        for ahead, out_ref in enumerate(outs):
            start = pl.multiple_of(lax.rem(head_at + ahead, groups) * step, step)
            rows = pl.ds(start, step)

            @pl.when(seen)
            def _(start=start, rows=rows, out_ref=out_ref):
                old = max_ref[rows, cols]
                near = pl.ds(pl.multiple_of(lax.rem(start, cells), step), step)
                m, got = attend(
                    reach_ref[head],
                    q_ref[rows, cols],
                    kv_ref,
                    dist_ref[near],
                    cols,
                    factor,
                    old[:, :1],
                )
                shrink = jnp.exp2(old - m)
                acc = acc_ref[rows, cols] * shrink + got[:, :head_dim]
                total = sum_ref[rows, cols] * shrink + got[:, head_dim:]
                out_ref[:, cols] = (acc / total).astype(jnp.bfloat16)

            @pl.when(jnp.logical_not(seen))
            def _(rows=rows, out_ref=out_ref):
                out_ref[:, cols] = (acc_ref[rows, cols] / sum_ref[rows, cols]).astype(jnp.bfloat16)


def others_kernel(all_ref, out_ref):
    groups = all_ref.shape[0]
    head_at = lax.axis_index("head")
    for back in range(1, groups):
        out_ref[back - 1] = all_ref[lax.rem(head_at + groups - back, groups)]


def collect_kernel(*refs):
    *parts, out_ref = refs
    for i, part in enumerate(parts):
        out_ref[i] = part[...]


def halves_kernel(beside_ref, below_ref, upper_ref, lower_ref):
    half = upper_ref.shape[1]
    upper_ref[...] = beside_ref[:, :half]
    lower_ref[...] = below_ref[:, half:]


def stack_kernel(lone_ref, beside_ref, below_ref, upper_ref, lower_ref, out_ref):
    tile_at = lax.axis_index("tile")
    tall = lone_ref.shape[1]
    half = tall // 2
    for flip, shift, ref in (
        (0, 0, lone_ref),
        (1, 0, beside_ref),
        (2, 0, below_ref),
        (3, 0, upper_ref),
        (3, half, lower_ref),
    ):
        top = pl.multiple_of(jnp.bitwise_xor(tile_at, flip) * tall + shift, 16)
        out_ref[:, pl.ds(top, ref.shape[1])] = ref[...]


def project_kernel(w_ref, here_ref, there_ref, attn_ref, out_ref):
    broad = here_ref.shape[2]
    core = lax.axis_index("tm")
    for mine, ref in ((core, here_ref), (1 - core, there_ref)):
        cols = pl.ds(pl.multiple_of(mine * broad, 128), broad)
        total = jnp.dot(attn_ref[0], w_ref[:, cols], preferred_element_type=jnp.float32)
        for s in range(1, attn_ref.shape[0]):
            total += jnp.dot(attn_ref[s], ref[s - 1], preferred_element_type=jnp.float32)
        out_ref[:, cols] = total.astype(jnp.bfloat16)


def two_by_two(query, keys, values, out_weight, radius, block_mask):
    span = RMAX
    frames, high, wide, channels = query.shape[2:]
    heads = radius.shape[0]
    head_dim = channels // heads
    cells = high * wide
    tokens = frames * cells
    groups = lax.axis_size("head")
    tiles = lax.axis_size("tile")
    depth, width = out_weight.shape
    step = tokens // groups
    geometry = (high, wide, span, frames, head_dim, LOG2E / math.sqrt(head_dim), step)
    smem = pl.BlockSpec(memory_space=pltpu.SMEM)
    vmem = pl.BlockSpec(memory_space=pltpu.VMEM)
    hbm = pl.BlockSpec(memory_space=pltpu.HBM)
    params = pltpu.CompilerParams(vmem_limit_bytes=VMEM_LIMIT)
    bf16, f32 = jnp.bfloat16, jnp.float32
    shape = jax.ShapeDtypeStruct

    def across(value, flip):
        return lax.ppermute(value, "tile", [(t, t ^ flip) for t in range(tiles)])

    def along(value, ahead):
        return lax.ppermute(value, "head", [(i, (i + ahead) % groups) for i in range(groups)])

    q = query.reshape(tokens, channels)
    k = keys.reshape(tokens, channels)
    v = values.reshape(tokens, channels)
    count = frames * (cells + span * (wide + high + span))
    row, col, corner, tile, part = pl.pallas_call(
        functools.partial(face_kernel, geometry=geometry),
        out_shape=[
            shape((2, frames, span * wide, channels), bf16),
            shape((2, frames, span * high, channels), bf16),
            shape((2, frames, span * span, channels), bf16),
            shape((2, tokens, channels), bf16),
            shape((depth // tiles, width // 2), bf16),
        ],
        in_specs=[hbm] * 3,
        out_specs=[vmem] * 4 + [hbm],
        scratch_shapes=[pltpu.SemaphoreType.DMA((3,))],
        name="faces",
    )(k, v, out_weight)
    faces = [across(row, 2), across(col, 1), across(corner, 3)]
    lone = lax.all_gather(part, "head", axis=0)
    edge = pl.pallas_call(
        edge_kernel,
        out_shape=shape((2, count - tokens, channels), bf16),
        in_specs=[vmem] * 3,
        out_specs=vmem,
        compiler_params=params,
        name="edges",
    )(*faces)
    own = [tile, edge]
    first = [lax.ppermute(piece, "tm", [(0, 1)]) for piece in own]

    scratch = [pltpu.VMEM((2, count, channels), bf16), pltpu.VMEM((cells, count), jnp.int32)]
    cost = pl.CostEstimate(
        flops=4 * tokens * count * channels,
        bytes_accessed=4 * tokens * channels * 4,
        transcendentals=0,
    )
    state = pl.pallas_call(
        functools.partial(own_kernel, geometry=geometry, heads=heads),
        out_shape=[shape((tokens, channels), f32)] * 3,
        in_specs=[smem] + [vmem] * 3,
        out_specs=[vmem] * 3,
        scratch_shapes=scratch,
        compiler_params=params,
        cost_estimate=cost,
        name="own",
    )(radius, q, *own)

    lone, state, first = lax.optimization_barrier((lone, state, first))
    lone = pl.pallas_call(
        others_kernel,
        out_shape=shape((groups - 1,) + part.shape, bf16),
        in_specs=[vmem],
        out_specs=vmem,
        compiler_params=params,
        name="others",
    )(lone)
    beside, below = across(lone, 1), across(lone, 2)
    attn = pl.pallas_call(
        functools.partial(other_kernel, geometry=geometry, heads=heads),
        out_shape=[shape((step, channels), bf16)] * groups,
        in_specs=[smem, smem] + [vmem] * 6,
        out_specs=[vmem] * groups,
        scratch_shapes=scratch,
        compiler_params=params,
        cost_estimate=cost,
        name="other",
    )(radius, block_mask.transpose(1, 2, 0), q, *state, *first)
    spread = pl.pallas_call(
        collect_kernel,
        out_shape=shape((groups, step, channels), bf16),
        in_specs=[vmem] * groups,
        out_specs=vmem,
        compiler_params=params,
        cost_estimate=pl.CostEstimate(
            flops=40 * 10**9, bytes_accessed=4 * tokens * channels, transcendentals=0
        ),
        name="collect",
    )(attn[0], *[along(attn[ahead], ahead) for ahead in range(1, groups)])

    beside, below, attn = lax.optimization_barrier((beside, below, attn))
    halves = pl.pallas_call(
        halves_kernel,
        out_shape=[shape((groups - 1, depth // tiles // 2, width // 2), bf16)] * 2,
        in_specs=[vmem] * 2,
        out_specs=[vmem] * 2,
        compiler_params=params,
        name="halves",
    )(beside, below)
    here = pl.pallas_call(
        stack_kernel,
        out_shape=shape((groups - 1, depth, width // 2), bf16),
        in_specs=[vmem] * 5,
        out_specs=vmem,
        compiler_params=params,
        name="stack",
    )(lone, beside, below, across(halves[0], 2), across(halves[1], 1))
    there = lax.ppermute(here, "tm", [(0, 1), (1, 0)])
    mixed = pl.pallas_call(
        project_kernel,
        out_shape=shape((step, width), bf16),
        in_specs=[vmem] * 4,
        out_specs=vmem,
        compiler_params=params,
        name="project",
    )(out_weight, here, there, spread)
    return mixed.reshape(1, 1, step, width)


def solution(mesh):
    in_specs = (
        P("tm", "tile", None, None, None, "head"),
        P("tm", "tile", None, None, None, "head"),
        P("tm", "tile", None, None, None, "head"),
        P("head", None),
        P("head"),
        P("head", None, None),
    )
    out_specs = P("tm", "tile", "head", None)
    small = mesh.shape["tile"] == 4 and mesh.shape["tm"] == 2
    return jax.shard_map(
        two_by_two if small else any_grid,
        mesh=mesh,
        in_specs=in_specs,
        out_specs=out_specs,
        check_vma=False,
    )
```

```python
import functools
import math

import jax
import jax.numpy as jnp
from jax import lax
from jax.experimental import pallas as pl
from jax.experimental.pallas import tpu as pltpu
from jax.sharding import PartitionSpec as P

RMAX = 4
FAR = -1e30
LOG2E = 1.4426950408889634
VMEM_LIMIT = 24 * 1024 * 1024


def passed_along(value, axis, by):
    peers = lax.axis_size(axis)
    pairs = [(i, i + by) for i in range(peers) if 0 <= i + by < peers]
    return lax.ppermute(value, axis, pairs)


def widen(key_part, value_part, span, row_move, col_move):
    grid = math.isqrt(lax.axis_size("tile"))
    above = None
    below = None
    for offset in (grid, -grid):
        if offset > 0:
            face_key = key_part[:, :, key_part.shape[2] - span :]
            face_value = value_part[:, :, value_part.shape[2] - span :]
        else:
            face_key = key_part[:, :, :span]
            face_value = value_part[:, :, :span]
        got = row_move(face_key, face_value, offset)
        if offset > 0:
            above = got
        else:
            below = got
    key_rows = jnp.concatenate([above[0], key_part, below[0]], axis=2)
    value_rows = jnp.concatenate([above[1], value_part, below[1]], axis=2)
    left = None
    right = None
    for offset in (1, -1):
        if offset > 0:
            face_key = key_rows[:, :, :, key_rows.shape[3] - span :]
            face_value = value_rows[:, :, :, value_rows.shape[3] - span :]
        else:
            face_key = key_rows[:, :, :, :span]
            face_value = value_rows[:, :, :, :span]
        got = col_move(face_key, face_value, offset)
        if offset > 0:
            left = got
        else:
            right = got
    key_full = jnp.concatenate([left[0], key_rows, right[0]], axis=3)
    value_full = jnp.concatenate([left[1], value_rows, right[1]], axis=3)
    return (key_full, value_full)


def windows_of(block, half_high, half_wide, win_high, win_wide, heads_here, head_dim):
    parts = []
    for band in (0, 1):
        for strip in (0, 1):
            parts.append(
                block[
                    :,
                    band * half_high : band * half_high + win_high,
                    strip * half_wide : strip * half_wide + win_wide,
                ]
            )
    stacked = jnp.stack(parts)
    return stacked.reshape(4, -1, heads_here, head_dim)


def any_grid(query, keys, values, out_weight, radius, block_mask):
    span = RMAX
    grid = math.isqrt(lax.axis_size("tile"))
    tile_at = lax.axis_index("tile")
    row_at = tile_at // grid
    col_at = tile_at % grid
    stretch_at = lax.axis_index("tm")
    frames, high, wide, channels = query.shape[2:]
    heads_here = radius.shape[0]
    head_dim = channels // heads_here
    tokens_here = frames * high * wide
    half_high = high // 2
    half_wide = wide // 2
    win_high = half_high + 2 * span
    win_wide = half_wide + 2 * span
    quarter = frames * half_high * half_wide
    queries = query[0, 0].reshape(frames, 2, half_high, 2, half_wide, channels)
    queries = queries.transpose(1, 3, 0, 2, 4, 5).reshape(4, quarter, heads_here, head_dim)
    query_y = jnp.broadcast_to(
        jnp.arange(half_high, dtype=jnp.int32)[None, :, None], (frames, half_high, half_wide)
    ).reshape(-1)
    query_x = jnp.broadcast_to(
        jnp.arange(half_wide, dtype=jnp.int32)[None, None, :], (frames, half_high, half_wide)
    ).reshape(-1)
    key_y = jnp.broadcast_to(
        jnp.arange(win_high, dtype=jnp.int32)[None, :, None] - span, (frames, win_high, win_wide)
    ).reshape(-1)
    key_x = jnp.broadcast_to(
        jnp.arange(win_wide, dtype=jnp.int32)[None, None, :] - span, (frames, win_high, win_wide)
    ).reshape(-1)
    band_at = jnp.array([0, 0, 1, 1], dtype=jnp.int32)
    strip_at = jnp.array([0, 1, 0, 1], dtype=jnp.int32)
    global_y = row_at * high + band_at[:, None] * half_high + key_y[None, :]
    global_x = col_at * wide + strip_at[:, None] * half_wide + key_x[None, :]
    inside = (global_y >= 0) & (global_y < grid * high) & (global_x >= 0) & (global_x < grid * wide)
    distance = jnp.maximum(
        jnp.abs(query_y[:, None] - key_y[None, :]), jnp.abs(query_x[:, None] - key_x[None, :])
    )
    near = distance[None, :, :] <= radius[:, None, None]
    allowed = near[None, :, :, :] & inside[:, None, None, :]
    scale = 1.0 / math.sqrt(head_dim)
    initial = (
        jnp.full((4, heads_here, quarter), -1e30, jnp.float32),
        jnp.zeros((4, heads_here, quarter), jnp.float32),
        jnp.zeros((4, heads_here, quarter, head_dim), jnp.float32),
    )

    def tile_move(face_key, face_value, offset):
        return passed_along((face_key, face_value), "tile", offset)

    key_all, value_all = (
        lax.all_gather(keys[0], "tm", axis=0, tiled=True),
        lax.all_gather(values[0], "tm", axis=0, tiled=True),
    )
    key_full, value_full = widen(key_all, value_all, span, tile_move, tile_move)
    stretch_ids = jnp.arange(key_full.shape[0], dtype=jnp.int32)

    def one_stretch(state, item):
        key_block, value_block, stretch_id = item
        visible = (
            lax.dynamic_slice_in_dim(
                lax.dynamic_index_in_dim(block_mask, stretch_at, 1, False), stretch_id, 1, 1
            )[:, 0]
            > 0
        )
        best, total, acc = state
        key_win = windows_of(
            key_block, half_high, half_wide, win_high, win_wide, heads_here, head_dim
        )
        value_win = windows_of(
            value_block, half_high, half_wide, win_high, win_wide, heads_here, head_dim
        )
        usable = allowed & visible[None, :, None, None]
        scores = (
            jnp.einsum("nqhd,nkhd->nhqk", queries, key_win, preferred_element_type=jnp.float32)
            * scale
        )
        masked = jnp.where(usable, scores, jnp.float32(-1e30))
        fresh = jnp.maximum(best, jnp.max(masked, axis=3))
        probs = jnp.where(usable, jnp.exp(scores - fresh[..., None]), jnp.float32(0.0))
        shrink = jnp.exp(best - fresh)
        total = total * shrink + jnp.sum(probs, axis=3)
        acc = acc * shrink[..., None] + jnp.einsum(
            "nhqk,nkhd->nhqd",
            probs.astype(jnp.bfloat16),
            value_win,
            preferred_element_type=jnp.float32,
        )
        return ((fresh, total, acc), None)

    final, unused = lax.scan(one_stretch, initial, (key_full, value_full, stretch_ids))
    best, total, acc = final
    attn = (acc / total[..., None]).astype(jnp.bfloat16)
    attn = attn.transpose(0, 2, 1, 3).reshape(
        2, 2, frames, half_high, half_wide, heads_here * head_dim
    )
    attn = attn.transpose(2, 0, 3, 1, 4, 5).reshape(tokens_here, heads_here * head_dim)
    mixed = lax.psum_scatter(
        jnp.dot(attn, out_weight, preferred_element_type=jnp.float32).astype(jnp.bfloat16),
        "head",
        scatter_dimension=0,
        tiled=True,
    )
    return mixed.reshape(1, 1, -1, out_weight.shape[1])


def tile_place():
    tile_at = lax.axis_index("tile")
    return tile_at // 2, tile_at % 2


def face_kernel(k_ref, v_ref, row_ref, col_ref, corner_ref, *, geometry):
    high, wide, span, frames = geometry[:4]
    cells = high * wide
    row_at, col_at = tile_place()
    y0 = jnp.where(row_at == 0, high - span, 0)
    x0 = jnp.where(col_at == 0, wide - span, 0)

    def picker(count, cell_of):
        row = lax.broadcasted_iota(jnp.int32, (count, cells), 0)
        col = lax.broadcasted_iota(jnp.int32, (count, cells), 1)
        return (col == cell_of(row)).astype(jnp.bfloat16)

    beside = picker(high * span, lambda i: (i // span) * wide + x0 + i % span)
    across = picker(span * span, lambda i: (y0 + i // span) * wide + x0 + i % span)
    for which, ref in enumerate((k_ref, v_ref)):
        for f in range(frames):
            start = pl.multiple_of(f * cells + y0 * wide, 16)
            row_ref[which, f] = ref[pl.ds(start, span * wide)]
            whole = ref[f * cells : (f + 1) * cells]
            col_ref[which, f] = jnp.dot(
                beside, whole, preferred_element_type=jnp.float32
            ).astype(jnp.bfloat16)
            corner_ref[which, f] = jnp.dot(
                across, whole, preferred_element_type=jnp.float32
            ).astype(jnp.bfloat16)


def join_kernel(k_ref, v_ref, row_ref, col_ref, corner_ref, kv_ref):
    for which, ref in enumerate((k_ref, v_ref)):
        at = ref.shape[0]
        kv_ref[which, :at] = ref[...]
        for part in (row_ref, col_ref, corner_ref):
            for f in range(part.shape[1]):
                size = part.shape[2]
                kv_ref[which, at : at + size] = part[which, f]
                at += size


def distances(count, high, wide, span, frames):
    row_at, col_at = tile_place()
    cells = high * wide
    j = lax.broadcasted_iota(jnp.int32, (1, count), 1)
    y_off = jnp.where(row_at == 0, high, -span)
    x_off = jnp.where(col_at == 0, wide, -span)
    own = j % cells
    ky, kx = own // wide, own % wide
    base = frames * cells
    c = (j - base) % (span * wide)
    ky = jnp.where(j >= base, y_off + c // wide, ky)
    kx = jnp.where(j >= base, c % wide, kx)
    base += frames * span * wide
    c = (j - base) % (span * high)
    ky = jnp.where(j >= base, c // span, ky)
    kx = jnp.where(j >= base, x_off + c % span, kx)
    base += frames * span * high
    c = (j - base) % (span * span)
    ky = jnp.where(j >= base, y_off + c // span, ky)
    kx = jnp.where(j >= base, x_off + c % span, kx)
    i = lax.broadcasted_iota(jnp.int32, (cells, 1), 0)
    return jnp.maximum(jnp.abs(i // wide - ky), jnp.abs(i % wide - kx))


def attend(reach, q, k, v, dist, factor, before):
    s = lax.dot_general(
        q, k, (((1,), (1,)), ((), ())), preferred_element_type=jnp.float32
    )
    s = jnp.where(dist <= reach, s * factor, FAR)
    m = jnp.max(s, axis=1, keepdims=True)
    if before is not None:
        m = jnp.maximum(m, before)
    p = jnp.exp2(s - m).astype(jnp.bfloat16)
    both = jnp.concatenate([v, jnp.ones_like(v)], axis=1)
    return m, jnp.dot(p, both, preferred_element_type=jnp.float32)


def tile_kernel(
    reach_ref, q_ref, k_ref, v_ref, acc_ref, sum_ref, max_ref, dist_ref, *, geometry, heads
):
    high, wide, span, frames, head_dim, factor, step = geometry
    cells = high * wide
    dist_ref[...] = distances(dist_ref.shape[1], high, wide, span, frames)
    for head in range(heads):
        cols = slice(head * head_dim, (head + 1) * head_dim)
        for start in range(0, q_ref.shape[0], step):
            rows = slice(start, start + step)
            near = dist_ref[start % cells : start % cells + step, : k_ref.shape[0]]
            m, got = attend(
                reach_ref[head], q_ref[rows, cols], k_ref[:, cols], v_ref[:, cols], near, factor, None
            )
            acc_ref[rows, cols] = got[:, :head_dim]
            sum_ref[rows, cols] = got[:, head_dim:]
            max_ref[rows, cols] = jnp.broadcast_to(m, (step, head_dim))


def merge(reach, rows, near, cols, q_ref, k, v, state, factor, head_dim):
    acc_ref, sum_ref, max_ref = state
    old = max_ref[rows, cols]
    m, got = attend(reach, q_ref[rows, cols], k, v, near, factor, old[:, :1])
    shrink = jnp.exp2(old - m)
    acc = acc_ref[rows, cols] * shrink + got[:, :head_dim]
    total = sum_ref[rows, cols] * shrink + got[:, head_dim:]
    return acc, total, jnp.broadcast_to(m, old.shape)


def edge_kernel(
    reach_ref, q_ref, kv_ref, dist_ref, acc_ref, sum_ref, max_ref, *outs, geometry, heads
):
    high, wide, span, frames, head_dim, factor, step = geometry
    cells = high * wide
    base = frames * cells
    for head in range(heads):
        cols = slice(head * head_dim, (head + 1) * head_dim)
        for start in range(0, q_ref.shape[0], step):
            rows = slice(start, start + step)
            near = dist_ref[start % cells : start % cells + step, base:]
            new = merge(
                reach_ref[head],
                rows,
                near,
                cols,
                q_ref,
                kv_ref[0, base:, cols],
                kv_ref[1, base:, cols],
                (acc_ref, sum_ref, max_ref),
                factor,
                head_dim,
            )
            for ref, value in zip(outs, new):
                ref[rows, cols] = value


def first_kernel(
    reach_ref,
    mask_ref,
    q_ref,
    kv_ref,
    dist_ref,
    acc_ref,
    sum_ref,
    max_ref,
    *outs,
    geometry,
    heads,
    flips,
):
    high, wide, span, frames, head_dim, factor, step = geometry
    cells = high * wide
    head_at = lax.axis_index("head")
    stretch_at = lax.axis_index("tm")
    for head in range(heads):
        cols = slice(head * head_dim, (head + 1) * head_dim)
        seen = (stretch_at > 0) & (mask_ref[stretch_at, 0, head] > 0)
        for flip, out_ref in zip(flips, outs):
            start = pl.multiple_of(jnp.bitwise_xor(head_at, flip) * step, step)
            rows = pl.ds(start, step)

            @pl.when(seen)
            def _(start=start, rows=rows, out_ref=out_ref):
                near = dist_ref[pl.ds(pl.multiple_of(lax.rem(start, cells), step), step)]
                acc, total, m = merge(
                    reach_ref[head],
                    rows,
                    near,
                    cols,
                    q_ref,
                    kv_ref[0, :, cols],
                    kv_ref[1, :, cols],
                    (acc_ref, sum_ref, max_ref),
                    factor,
                    head_dim,
                )
                out_ref[:, cols] = (acc / total).astype(jnp.bfloat16)

            @pl.when(jnp.logical_not(seen))
            def _(rows=rows, out_ref=out_ref):
                out_ref[:, cols] = (acc_ref[rows, cols] / sum_ref[rows, cols]).astype(jnp.bfloat16)


def stack_kernel(*refs):
    *parts, out_ref = refs
    tile_at = lax.axis_index("tile")
    for flip, part in enumerate(parts):
        tall = part.shape[0]
        top = pl.multiple_of(jnp.bitwise_xor(tile_at, flip) * tall, 16)
        out_ref[pl.ds(top, tall)] = part[...]


def project_kernel(w_ref, here_ref, there_ref, own_ref, got_ref, out_ref):
    broad = here_ref.shape[1]
    core = lax.axis_index("tm")
    for mine, ref in ((core, here_ref), (1 - core, there_ref)):
        cols = pl.ds(pl.multiple_of(mine * broad, 128), broad)
        total = jnp.dot(own_ref[...], w_ref[:, cols], preferred_element_type=jnp.float32)
        total += jnp.dot(got_ref[...], ref[...], preferred_element_type=jnp.float32)
        out_ref[:, cols] = total.astype(out_ref.dtype)


def add_kernel(mine_ref, got_ref, out_ref):
    out_ref[...] = (mine_ref[...] + got_ref[...].astype(jnp.float32)).astype(jnp.bfloat16)


def two_by_two(query, keys, values, out_weight, radius, block_mask):
    span = RMAX
    frames, high, wide, channels = query.shape[2:]
    heads = radius.shape[0]
    head_dim = channels // heads
    cells = high * wide
    tokens = frames * cells
    groups = lax.axis_size("head")
    tiles = lax.axis_size("tile")
    depth, width = out_weight.shape
    step = tokens // groups
    geometry = (high, wide, span, frames, head_dim, LOG2E / math.sqrt(head_dim), step)
    count = frames * (cells + span * (wide + high + span))
    smem = pl.BlockSpec(memory_space=pltpu.SMEM)
    vmem = pl.BlockSpec(memory_space=pltpu.VMEM)
    bf16, f32 = jnp.bfloat16, jnp.float32
    shape = jax.ShapeDtypeStruct
    state_shape = [shape((tokens, channels), f32)] * 3

    def call(kernel, out_shape, specs, *args, name, **keys_of):
        return pl.pallas_call(
            functools.partial(kernel, **keys_of) if keys_of else kernel,
            out_shape=out_shape,
            in_specs=specs,
            out_specs=jax.tree.map(lambda _: vmem, out_shape),
            compiler_params=pltpu.CompilerParams(vmem_limit_bytes=VMEM_LIMIT),
            name=name,
        )(*args)

    def flipped(value, axis, flip):
        return lax.ppermute(value, axis, [(i, i ^ flip) for i in range(lax.axis_size(axis))])

    q = query.reshape(tokens, channels)
    k = keys.reshape(tokens, channels)
    v = values.reshape(tokens, channels)

    tall, broad = depth // tiles, width // 2
    part = lax.dynamic_slice(
        out_weight, (lax.axis_index("tile") * tall, lax.axis_index("tm") * broad), (tall, broad)
    )
    lone = flipped(part, "head", 2)
    faces = call(
        face_kernel,
        [
            shape((2, frames, span * wide, channels), bf16),
            shape((2, frames, span * high, channels), bf16),
            shape((2, frames, span * span, channels), bf16),
        ],
        [vmem] * 2,
        k,
        v,
        name="faces",
        geometry=geometry,
    )
    faces = [flipped(face, "tile", flip) for face, flip in zip(faces, (2, 1, 3))]
    *state, dist = call(
        tile_kernel,
        state_shape + [shape((cells, count), jnp.int32)],
        [smem] + [vmem] * 3,
        radius,
        q,
        k,
        v,
        name="tile",
        geometry=geometry,
        heads=heads,
    )
    lone, state, faces = lax.optimization_barrier((lone, state, faces))
    kv = call(
        join_kernel, shape((2, count, channels), bf16), [vmem] * 5, k, v, *faces, name="join"
    )
    kv_first = lax.ppermute(kv, "tm", [(0, 1)])
    parts = [lone] + [flipped(lone, "tile", flip) for flip in range(1, tiles)]
    state = call(
        edge_kernel,
        state_shape,
        [smem] + [vmem] * 6,
        radius,
        q,
        kv,
        dist,
        *state,
        name="edges",
        geometry=geometry,
        heads=heads,
    )
    mask = block_mask.transpose(1, 2, 0)

    def first(state, *flips):
        return call(
            first_kernel,
            [shape((step, channels), bf16)] * len(flips),
            [smem] * 2 + [vmem] * 6,
            radius,
            mask,
            q,
            kv_first,
            dist,
            *state,
            name="first",
            geometry=geometry,
            heads=heads,
            flips=flips,
        )

    (for_side,) = first(state, 3)
    got_side = flipped(for_side, "head", 2)
    state, parts, for_side = lax.optimization_barrier((state, parts, for_side))
    here = call(
        stack_kernel, shape((depth, broad), bf16), [vmem] * tiles, *parts, name="stack"
    )
    (for_far,) = first(state, 2)
    got_far = flipped(for_far, "head", 2)
    state, for_far = lax.optimization_barrier((state, for_far))
    own_side, own = first(state, 1, 0)
    there = flipped(here, "tm", 1)

    def project(mine, got, kind):
        return call(
            project_kernel,
            shape((step, width), kind),
            [vmem] * 5,
            out_weight,
            here,
            there,
            mine,
            got,
            name="project",
        )

    from_side = flipped(project(own_side, got_side, bf16), "head", 1)
    mixed = call(
        add_kernel,
        shape((step, width), bf16),
        [vmem] * 2,
        project(own, got_far, f32),
        from_side,
        name="add",
    )
    return mixed.reshape(1, 1, step, width)


def solution(mesh):
    in_specs = (
        P("tm", "tile", None, None, None, "head"),
        P("tm", "tile", None, None, None, "head"),
        P("tm", "tile", None, None, None, "head"),
        P("head", None),
        P("head"),
        P("head", None, None),
    )
    out_specs = P("tm", "tile", "head", None)
    small = dict(mesh.shape) == {"tm": 2, "tile": 4, "head": 4}
    return jax.shard_map(
        two_by_two if small else any_grid,
        mesh=mesh,
        in_specs=in_specs,
        out_specs=out_specs,
        check_vma=False,
    )
```

```python
import functools
import math

import jax
import jax.numpy as jnp
from jax import lax
from jax.experimental import pallas as pl
from jax.experimental.pallas import tpu as pltpu
from jax.sharding import PartitionSpec as P

RMAX = 4
FAR = -1e30
LOG2E = 1.4426950408889634
VMEM_LIMIT = 24 * 1024 * 1024


def passed_along(value, axis, by):
    peers = lax.axis_size(axis)
    pairs = [(i, i + by) for i in range(peers) if 0 <= i + by < peers]
    return lax.ppermute(value, axis, pairs)


def widen(key_part, value_part, span, row_move, col_move):
    grid = math.isqrt(lax.axis_size("tile"))
    above = None
    below = None
    for offset in (grid, -grid):
        if offset > 0:
            face_key = key_part[:, :, key_part.shape[2] - span :]
            face_value = value_part[:, :, value_part.shape[2] - span :]
        else:
            face_key = key_part[:, :, :span]
            face_value = value_part[:, :, :span]
        got = row_move(face_key, face_value, offset)
        if offset > 0:
            above = got
        else:
            below = got
    key_rows = jnp.concatenate([above[0], key_part, below[0]], axis=2)
    value_rows = jnp.concatenate([above[1], value_part, below[1]], axis=2)
    left = None
    right = None
    for offset in (1, -1):
        if offset > 0:
            face_key = key_rows[:, :, :, key_rows.shape[3] - span :]
            face_value = value_rows[:, :, :, value_rows.shape[3] - span :]
        else:
            face_key = key_rows[:, :, :, :span]
            face_value = value_rows[:, :, :, :span]
        got = col_move(face_key, face_value, offset)
        if offset > 0:
            left = got
        else:
            right = got
    key_full = jnp.concatenate([left[0], key_rows, right[0]], axis=3)
    value_full = jnp.concatenate([left[1], value_rows, right[1]], axis=3)
    return (key_full, value_full)


def windows_of(block, half_high, half_wide, win_high, win_wide, heads_here, head_dim):
    parts = []
    for band in (0, 1):
        for strip in (0, 1):
            parts.append(
                block[
                    :,
                    band * half_high : band * half_high + win_high,
                    strip * half_wide : strip * half_wide + win_wide,
                ]
            )
    stacked = jnp.stack(parts)
    return stacked.reshape(4, -1, heads_here, head_dim)


def any_grid(query, keys, values, out_weight, radius, block_mask):
    span = RMAX
    grid = math.isqrt(lax.axis_size("tile"))
    tile_at = lax.axis_index("tile")
    row_at = tile_at // grid
    col_at = tile_at % grid
    stretch_at = lax.axis_index("tm")
    frames, high, wide, channels = query.shape[2:]
    heads_here = radius.shape[0]
    head_dim = channels // heads_here
    tokens_here = frames * high * wide
    half_high = high // 2
    half_wide = wide // 2
    win_high = half_high + 2 * span
    win_wide = half_wide + 2 * span
    quarter = frames * half_high * half_wide
    queries = query[0, 0].reshape(frames, 2, half_high, 2, half_wide, channels)
    queries = queries.transpose(1, 3, 0, 2, 4, 5).reshape(4, quarter, heads_here, head_dim)
    query_y = jnp.broadcast_to(
        jnp.arange(half_high, dtype=jnp.int32)[None, :, None], (frames, half_high, half_wide)
    ).reshape(-1)
    query_x = jnp.broadcast_to(
        jnp.arange(half_wide, dtype=jnp.int32)[None, None, :], (frames, half_high, half_wide)
    ).reshape(-1)
    key_y = jnp.broadcast_to(
        jnp.arange(win_high, dtype=jnp.int32)[None, :, None] - span, (frames, win_high, win_wide)
    ).reshape(-1)
    key_x = jnp.broadcast_to(
        jnp.arange(win_wide, dtype=jnp.int32)[None, None, :] - span, (frames, win_high, win_wide)
    ).reshape(-1)
    band_at = jnp.array([0, 0, 1, 1], dtype=jnp.int32)
    strip_at = jnp.array([0, 1, 0, 1], dtype=jnp.int32)
    global_y = row_at * high + band_at[:, None] * half_high + key_y[None, :]
    global_x = col_at * wide + strip_at[:, None] * half_wide + key_x[None, :]
    inside = (global_y >= 0) & (global_y < grid * high) & (global_x >= 0) & (global_x < grid * wide)
    distance = jnp.maximum(
        jnp.abs(query_y[:, None] - key_y[None, :]), jnp.abs(query_x[:, None] - key_x[None, :])
    )
    near = distance[None, :, :] <= radius[:, None, None]
    allowed = near[None, :, :, :] & inside[:, None, None, :]
    scale = 1.0 / math.sqrt(head_dim)
    initial = (
        jnp.full((4, heads_here, quarter), -1e30, jnp.float32),
        jnp.zeros((4, heads_here, quarter), jnp.float32),
        jnp.zeros((4, heads_here, quarter, head_dim), jnp.float32),
    )

    def tile_move(face_key, face_value, offset):
        return passed_along((face_key, face_value), "tile", offset)

    key_all, value_all = (
        lax.all_gather(keys[0], "tm", axis=0, tiled=True),
        lax.all_gather(values[0], "tm", axis=0, tiled=True),
    )
    key_full, value_full = widen(key_all, value_all, span, tile_move, tile_move)
    stretch_ids = jnp.arange(key_full.shape[0], dtype=jnp.int32)

    def one_stretch(state, item):
        key_block, value_block, stretch_id = item
        visible = (
            lax.dynamic_slice_in_dim(
                lax.dynamic_index_in_dim(block_mask, stretch_at, 1, False), stretch_id, 1, 1
            )[:, 0]
            > 0
        )
        best, total, acc = state
        key_win = windows_of(
            key_block, half_high, half_wide, win_high, win_wide, heads_here, head_dim
        )
        value_win = windows_of(
            value_block, half_high, half_wide, win_high, win_wide, heads_here, head_dim
        )
        usable = allowed & visible[None, :, None, None]
        scores = (
            jnp.einsum("nqhd,nkhd->nhqk", queries, key_win, preferred_element_type=jnp.float32)
            * scale
        )
        masked = jnp.where(usable, scores, jnp.float32(-1e30))
        fresh = jnp.maximum(best, jnp.max(masked, axis=3))
        probs = jnp.where(usable, jnp.exp(scores - fresh[..., None]), jnp.float32(0.0))
        shrink = jnp.exp(best - fresh)
        total = total * shrink + jnp.sum(probs, axis=3)
        acc = acc * shrink[..., None] + jnp.einsum(
            "nhqk,nkhd->nhqd",
            probs.astype(jnp.bfloat16),
            value_win,
            preferred_element_type=jnp.float32,
        )
        return ((fresh, total, acc), None)

    final, unused = lax.scan(one_stretch, initial, (key_full, value_full, stretch_ids))
    best, total, acc = final
    attn = (acc / total[..., None]).astype(jnp.bfloat16)
    attn = attn.transpose(0, 2, 1, 3).reshape(
        2, 2, frames, half_high, half_wide, heads_here * head_dim
    )
    attn = attn.transpose(2, 0, 3, 1, 4, 5).reshape(tokens_here, heads_here * head_dim)
    mixed = lax.psum_scatter(
        jnp.dot(attn, out_weight, preferred_element_type=jnp.float32).astype(jnp.bfloat16),
        "head",
        scatter_dimension=0,
        tiled=True,
    )
    return mixed.reshape(1, 1, -1, out_weight.shape[1])


def tile_place():
    tile_at = lax.axis_index("tile")
    return tile_at // 2, tile_at % 2


def face_kernel(
    k_ref, v_ref, w_ref, row_ref, col_ref, corner_ref, tile_ref, part_ref, sems, *, geometry
):
    high, wide, span, frames = geometry[:4]
    cells = high * wide
    row_at, col_at = tile_place()
    y0 = jnp.where(row_at == 0, high - span, 0)
    x0 = jnp.where(col_at == 0, wide - span, 0)
    tall, broad = part_ref.shape
    top = pl.multiple_of(lax.axis_index("tile") * tall, 16)
    edge = pl.multiple_of(lax.axis_index("tm") * broad, 128)
    copies = [
        pltpu.make_async_copy(ref, tile_ref.at[which], sems.at[which])
        for which, ref in enumerate((k_ref, v_ref))
    ]
    copies.append(
        pltpu.make_async_copy(
            w_ref.at[pl.ds(top, tall), pl.ds(edge, broad)], part_ref, sems.at[2]
        )
    )
    for copy in copies:
        copy.start()

    def picker(count, cell_of):
        row = lax.broadcasted_iota(jnp.int32, (count, cells), 0)
        col = lax.broadcasted_iota(jnp.int32, (count, cells), 1)
        return (col == cell_of(row)).astype(jnp.bfloat16)

    beside = picker(high * span, lambda i: (i // span) * wide + x0 + i % span)
    across = picker(span * span, lambda i: (y0 + i // span) * wide + x0 + i % span)
    for which in range(2):
        copies[which].wait()
        for f in range(frames):
            start = pl.multiple_of(f * cells + y0 * wide, 16)
            row_ref[which, f] = tile_ref[which, pl.ds(start, span * wide)]
            whole = tile_ref[which, f * cells : (f + 1) * cells]
            col_ref[which, f] = jnp.dot(
                beside, whole, preferred_element_type=jnp.float32
            ).astype(jnp.bfloat16)
            corner_ref[which, f] = jnp.dot(
                across, whole, preferred_element_type=jnp.float32
            ).astype(jnp.bfloat16)
    copies[2].wait()


def join_kernel(tile_ref, row_ref, col_ref, corner_ref, kv_ref):
    for which in range(2):
        at = 0
        for part in (row_ref, col_ref, corner_ref):
            for f in range(part.shape[1]):
                size = part.shape[2]
                kv_ref[which, at : at + size] = part[which, f]
                at += size
        kv_ref[which, at:] = tile_ref[which]


def distances(high, wide, span, frames):
    row_at, col_at = tile_place()
    cells = high * wide
    count = frames * (cells + span * (wide + high + span))
    j = lax.broadcasted_iota(jnp.int32, (1, count), 1)
    y_off = jnp.where(row_at == 0, high, -span)
    x_off = jnp.where(col_at == 0, wide, -span)
    c = j % (span * wide)
    ky, kx = y_off + c // wide, c % wide
    base = frames * span * wide
    c = (j - base) % (span * high)
    ky = jnp.where(j >= base, c // span, ky)
    kx = jnp.where(j >= base, x_off + c % span, kx)
    base += frames * span * high
    c = (j - base) % (span * span)
    ky = jnp.where(j >= base, y_off + c // span, ky)
    kx = jnp.where(j >= base, x_off + c % span, kx)
    base += frames * span * span
    c = (j - base) % cells
    ky = jnp.where(j >= base, c // wide, ky)
    kx = jnp.where(j >= base, c % wide, kx)
    i = lax.broadcasted_iota(jnp.int32, (cells, 1), 0)
    return jnp.maximum(jnp.abs(i // wide - ky), jnp.abs(i % wide - kx))


def attend(q, pieces, factor, before):
    scores = []
    m = before
    for k, v, dist, reach in pieces:
        s = lax.dot_general(q, k, (((1,), (1,)), ((), ())), preferred_element_type=jnp.float32)
        s = jnp.where(dist <= reach, s * factor, FAR)
        top = jnp.max(s, axis=1, keepdims=True)
        m = top if m is None else jnp.maximum(m, top)
        scores.append(s)
    total = None
    for s, (k, v, dist, reach) in zip(scores, pieces):
        p = jnp.exp2(s - m).astype(jnp.bfloat16)
        both = jnp.concatenate([v, jnp.ones_like(v)], axis=1)
        got = jnp.dot(p, both, preferred_element_type=jnp.float32)
        total = got if total is None else total + got
    return m, total


def tile_kernel(
    reach_ref, q_ref, tile_ref, acc_ref, sum_ref, max_ref, dist_ref, *, geometry, heads
):
    high, wide, span, frames, head_dim, factor, step = geometry
    cells = high * wide
    dist_ref[...] = distances(high, wide, span, frames)
    base = dist_ref.shape[1] - tile_ref.shape[1]
    for head in range(heads):
        cols = slice(head * head_dim, (head + 1) * head_dim)
        for start in range(0, q_ref.shape[0], step):
            rows = slice(start, start + step)
            near = dist_ref[start % cells : start % cells + step, base:]
            piece = (tile_ref[0, :, cols], tile_ref[1, :, cols], near, reach_ref[head])
            m, got = attend(q_ref[rows, cols], [piece], factor, None)
            acc_ref[rows, cols] = got[:, :head_dim]
            sum_ref[rows, cols] = got[:, head_dim:]
            max_ref[rows, cols] = jnp.broadcast_to(m, (step, head_dim))


def rest_kernel(
    reach_ref,
    mask_ref,
    q_ref,
    kv_ref,
    first_ref,
    dist_ref,
    acc_ref,
    sum_ref,
    max_ref,
    *outs,
    geometry,
    heads,
    flips,
):
    high, wide, span, frames, head_dim, factor, step = geometry
    cells = high * wide
    base = kv_ref.shape[1] - frames * cells
    head_at = lax.axis_index("head")
    stretch_at = lax.axis_index("tm")

    def run(with_first):
        for flip, out_ref in zip(flips, outs):
            start = pl.multiple_of(jnp.bitwise_xor(head_at, flip) * step, step)
            rows = pl.ds(start, step)
            near = dist_ref[pl.ds(pl.multiple_of(lax.rem(start, cells), step), step)]
            for head in range(heads):
                cols = slice(head * head_dim, (head + 1) * head_dim)
                reach = reach_ref[head]
                pieces = [
                    (kv_ref[0, :base, cols], kv_ref[1, :base, cols], near[:, :base], reach)
                ]
                if with_first:
                    seen = mask_ref[stretch_at, 0, head] > 0
                    pieces.append(
                        (
                            first_ref[0, :, cols],
                            first_ref[1, :, cols],
                            near,
                            jnp.where(seen, reach, -1),
                        )
                    )
                old = max_ref[rows, cols]
                m, got = attend(q_ref[rows, cols], pieces, factor, old[:, :1])
                shrink = jnp.exp2(old - m)
                acc = acc_ref[rows, cols] * shrink + got[:, :head_dim]
                total = sum_ref[rows, cols] * shrink + got[:, head_dim:]
                out_ref[:, cols] = (acc / total).astype(jnp.bfloat16)

    @pl.when(stretch_at > 0)
    def _():
        run(True)

    @pl.when(stretch_at == 0)
    def _():
        run(False)


def stack_kernel(*refs):
    *parts, out_ref = refs
    tile_at = lax.axis_index("tile")
    for flip, part in enumerate(parts):
        tall = part.shape[0]
        top = pl.multiple_of(jnp.bitwise_xor(tile_at, flip) * tall, 16)
        out_ref[pl.ds(top, tall)] = part[...]


def half_sum(w_ref, part_ref, own_ref, got_ref, core):
    broad = part_ref.shape[1]
    cols = pl.ds(pl.multiple_of(core * broad, 128), broad)
    total = jnp.dot(own_ref[...], w_ref[:, cols], preferred_element_type=jnp.float32)
    return cols, total + jnp.dot(
        got_ref[...], part_ref[...], preferred_element_type=jnp.float32
    )


def half_kernel(w_ref, here_ref, own_ref, got_ref, out_ref):
    core = lax.axis_index("tm")
    out_ref[...] = half_sum(w_ref, here_ref, own_ref, got_ref, core)[1].astype(out_ref.dtype)


def whole_kernel(w_ref, there_ref, own_ref, got_ref, half_ref, out_ref):
    core = lax.axis_index("tm")
    cols, total = half_sum(w_ref, there_ref, own_ref, got_ref, 1 - core)
    out_ref[:, cols] = total.astype(out_ref.dtype)
    broad = half_ref.shape[1]
    out_ref[:, pl.ds(pl.multiple_of(core * broad, 128), broad)] = half_ref[...]


def add_kernel(mine_ref, got_ref, out_ref):
    out_ref[...] = (mine_ref[...] + got_ref[...].astype(jnp.float32)).astype(jnp.bfloat16)


def two_by_two(query, keys, values, out_weight, radius, block_mask):
    span = RMAX
    frames, high, wide, channels = query.shape[2:]
    heads = radius.shape[0]
    head_dim = channels // heads
    cells = high * wide
    tokens = frames * cells
    groups = lax.axis_size("head")
    tiles = lax.axis_size("tile")
    depth, width = out_weight.shape
    step = tokens // groups
    geometry = (high, wide, span, frames, head_dim, LOG2E / math.sqrt(head_dim), step)
    count = frames * (cells + span * (wide + high + span))
    smem = pl.BlockSpec(memory_space=pltpu.SMEM)
    vmem = pl.BlockSpec(memory_space=pltpu.VMEM)
    hbm = pl.BlockSpec(memory_space=pltpu.HBM)
    bf16, f32 = jnp.bfloat16, jnp.float32
    shape = jax.ShapeDtypeStruct
    state_shape = [shape((tokens, channels), f32)] * 3

    def call(kernel, out_shape, specs, *args, name, scratch=(), flops=0, **keys_of):
        return pl.pallas_call(
            functools.partial(kernel, **keys_of) if keys_of else kernel,
            out_shape=out_shape,
            in_specs=specs,
            out_specs=jax.tree.map(lambda _: vmem, out_shape),
            scratch_shapes=scratch,
            cost_estimate=pl.CostEstimate(flops=flops, bytes_accessed=0, transcendentals=0),
            compiler_params=pltpu.CompilerParams(vmem_limit_bytes=VMEM_LIMIT),
            name=name,
        )(*args)

    def flipped(value, axis, flip):
        return lax.ppermute(value, axis, [(i, i ^ flip) for i in range(lax.axis_size(axis))])

    q = query.reshape(tokens, channels)
    k = keys.reshape(tokens, channels)
    v = values.reshape(tokens, channels)

    tall, broad = depth // tiles, width // 2
    *faces, tile, part = call(
        face_kernel,
        [
            shape((2, frames, span * wide, channels), bf16),
            shape((2, frames, span * high, channels), bf16),
            shape((2, frames, span * span, channels), bf16),
            shape((2, tokens, channels), bf16),
            shape((tall, broad), bf16),
        ],
        [hbm] * 3,
        *[pltpu.with_memory_space_constraint(x, pltpu.HBM) for x in (k, v, out_weight)],
        name="faces",
        scratch=[pltpu.SemaphoreType.DMA((3,))],
        geometry=geometry,
    )
    faces = [flipped(face, "tile", flip) for face, flip in zip(faces, (2, 1, 3))]
    lone = flipped(part, "head", 2)
    *state, dist = call(
        tile_kernel,
        state_shape + [shape((cells, count), jnp.int32)],
        [smem] + [vmem] * 2,
        radius,
        q,
        tile,
        name="tile",
        geometry=geometry,
        heads=heads,
    )
    lone, state, faces = lax.optimization_barrier((lone, state, faces))
    kv = call(
        join_kernel, shape((2, count, channels), bf16), [vmem] * 4, tile, *faces, name="join"
    )
    kv_first = lax.ppermute(kv, "tm", [(0, 1)])
    parts = [lone] + [flipped(lone, "tile", flip) for flip in range(1, tiles)]
    mask = block_mask.transpose(1, 2, 0)

    def rest(state, *flips):
        return call(
            rest_kernel,
            [shape((step, channels), bf16)] * len(flips),
            [smem] * 2 + [vmem] * 7,
            radius,
            mask,
            q,
            kv,
            kv_first,
            dist,
            *state,
            name="rest",
            geometry=geometry,
            heads=heads,
            flips=flips,
        )

    (for_side,) = rest(state, 3)
    got_side = flipped(for_side, "head", 2)
    state, for_side = lax.optimization_barrier((state, for_side))
    (for_far,) = rest(state, 2)
    got_far = flipped(for_far, "head", 2)
    state, for_far = lax.optimization_barrier((state, for_far))
    (own_side,) = rest(state, 1)
    parts, own_side = lax.optimization_barrier((parts, own_side))
    here = call(
        stack_kernel, shape((depth, broad), bf16), [vmem] * tiles, *parts, name="stack"
    )
    there = flipped(here, "tm", 1)

    def project(mine, got, kind, flops):
        half = call(
            half_kernel,
            shape((step, broad), kind),
            [vmem] * 4,
            out_weight,
            here,
            mine,
            got,
            name="half",
            flops=flops,
        )
        return call(
            whole_kernel,
            shape((step, width), kind),
            [vmem] * 5,
            out_weight,
            there,
            mine,
            got,
            half,
            name="whole",
        )

    for_side = project(own_side, got_side, bf16, 20 * 10**9)
    from_side = flipped(for_side, "head", 1)
    state, for_side = lax.optimization_barrier((state, for_side))
    (own,) = rest(state, 0)
    mixed = call(
        add_kernel,
        shape((step, width), bf16),
        [vmem] * 2,
        project(own, got_far, f32, 20 * 10**9),
        from_side,
        name="add",
    )
    return mixed.reshape(1, 1, step, width)


def solution(mesh):
    in_specs = (
        P("tm", "tile", None, None, None, "head"),
        P("tm", "tile", None, None, None, "head"),
        P("tm", "tile", None, None, None, "head"),
        P("head", None),
        P("head"),
        P("head", None, None),
    )
    out_specs = P("tm", "tile", "head", None)
    small = dict(mesh.shape) == {"tm": 2, "tile": 4, "head": 4}
    return jax.shard_map(
        two_by_two if small else any_grid,
        mesh=mesh,
        in_specs=in_specs,
        out_specs=out_specs,
        check_vma=False,
    )
```

```python
import functools
import math

import jax
import jax.numpy as jnp
from jax import lax
from jax.experimental import pallas as pl
from jax.experimental.pallas import tpu as pltpu
from jax.sharding import PartitionSpec as P

RMAX = 4
FAR = -1e30
LOG2E = 1.4426950408889634
VMEM_LIMIT = 24 * 1024 * 1024


def passed_along(value, axis, by):
    peers = lax.axis_size(axis)
    pairs = [(i, i + by) for i in range(peers) if 0 <= i + by < peers]
    return lax.ppermute(value, axis, pairs)


def widen(key_part, value_part, span, row_move, col_move):
    grid = math.isqrt(lax.axis_size("tile"))
    above = None
    below = None
    for offset in (grid, -grid):
        if offset > 0:
            face_key = key_part[:, :, key_part.shape[2] - span :]
            face_value = value_part[:, :, value_part.shape[2] - span :]
        else:
            face_key = key_part[:, :, :span]
            face_value = value_part[:, :, :span]
        got = row_move(face_key, face_value, offset)
        if offset > 0:
            above = got
        else:
            below = got
    key_rows = jnp.concatenate([above[0], key_part, below[0]], axis=2)
    value_rows = jnp.concatenate([above[1], value_part, below[1]], axis=2)
    left = None
    right = None
    for offset in (1, -1):
        if offset > 0:
            face_key = key_rows[:, :, :, key_rows.shape[3] - span :]
            face_value = value_rows[:, :, :, value_rows.shape[3] - span :]
        else:
            face_key = key_rows[:, :, :, :span]
            face_value = value_rows[:, :, :, :span]
        got = col_move(face_key, face_value, offset)
        if offset > 0:
            left = got
        else:
            right = got
    key_full = jnp.concatenate([left[0], key_rows, right[0]], axis=3)
    value_full = jnp.concatenate([left[1], value_rows, right[1]], axis=3)
    return (key_full, value_full)


def windows_of(block, half_high, half_wide, win_high, win_wide, heads_here, head_dim):
    parts = []
    for band in (0, 1):
        for strip in (0, 1):
            parts.append(
                block[
                    :,
                    band * half_high : band * half_high + win_high,
                    strip * half_wide : strip * half_wide + win_wide,
                ]
            )
    stacked = jnp.stack(parts)
    return stacked.reshape(4, -1, heads_here, head_dim)


def any_grid(query, keys, values, out_weight, radius, block_mask):
    span = RMAX
    grid = math.isqrt(lax.axis_size("tile"))
    tile_at = lax.axis_index("tile")
    row_at = tile_at // grid
    col_at = tile_at % grid
    stretch_at = lax.axis_index("tm")
    frames, high, wide, channels = query.shape[2:]
    heads_here = radius.shape[0]
    head_dim = channels // heads_here
    tokens_here = frames * high * wide
    half_high = high // 2
    half_wide = wide // 2
    win_high = half_high + 2 * span
    win_wide = half_wide + 2 * span
    quarter = frames * half_high * half_wide
    queries = query[0, 0].reshape(frames, 2, half_high, 2, half_wide, channels)
    queries = queries.transpose(1, 3, 0, 2, 4, 5).reshape(4, quarter, heads_here, head_dim)
    query_y = jnp.broadcast_to(
        jnp.arange(half_high, dtype=jnp.int32)[None, :, None], (frames, half_high, half_wide)
    ).reshape(-1)
    query_x = jnp.broadcast_to(
        jnp.arange(half_wide, dtype=jnp.int32)[None, None, :], (frames, half_high, half_wide)
    ).reshape(-1)
    key_y = jnp.broadcast_to(
        jnp.arange(win_high, dtype=jnp.int32)[None, :, None] - span, (frames, win_high, win_wide)
    ).reshape(-1)
    key_x = jnp.broadcast_to(
        jnp.arange(win_wide, dtype=jnp.int32)[None, None, :] - span, (frames, win_high, win_wide)
    ).reshape(-1)
    band_at = jnp.array([0, 0, 1, 1], dtype=jnp.int32)
    strip_at = jnp.array([0, 1, 0, 1], dtype=jnp.int32)
    global_y = row_at * high + band_at[:, None] * half_high + key_y[None, :]
    global_x = col_at * wide + strip_at[:, None] * half_wide + key_x[None, :]
    inside = (global_y >= 0) & (global_y < grid * high) & (global_x >= 0) & (global_x < grid * wide)
    distance = jnp.maximum(
        jnp.abs(query_y[:, None] - key_y[None, :]), jnp.abs(query_x[:, None] - key_x[None, :])
    )
    near = distance[None, :, :] <= radius[:, None, None]
    allowed = near[None, :, :, :] & inside[:, None, None, :]
    scale = 1.0 / math.sqrt(head_dim)
    initial = (
        jnp.full((4, heads_here, quarter), -1e30, jnp.float32),
        jnp.zeros((4, heads_here, quarter), jnp.float32),
        jnp.zeros((4, heads_here, quarter, head_dim), jnp.float32),
    )

    def tile_move(face_key, face_value, offset):
        return passed_along((face_key, face_value), "tile", offset)

    key_all, value_all = (
        lax.all_gather(keys[0], "tm", axis=0, tiled=True),
        lax.all_gather(values[0], "tm", axis=0, tiled=True),
    )
    key_full, value_full = widen(key_all, value_all, span, tile_move, tile_move)
    stretch_ids = jnp.arange(key_full.shape[0], dtype=jnp.int32)

    def one_stretch(state, item):
        key_block, value_block, stretch_id = item
        visible = (
            lax.dynamic_slice_in_dim(
                lax.dynamic_index_in_dim(block_mask, stretch_at, 1, False), stretch_id, 1, 1
            )[:, 0]
            > 0
        )
        best, total, acc = state
        key_win = windows_of(
            key_block, half_high, half_wide, win_high, win_wide, heads_here, head_dim
        )
        value_win = windows_of(
            value_block, half_high, half_wide, win_high, win_wide, heads_here, head_dim
        )
        usable = allowed & visible[None, :, None, None]
        scores = (
            jnp.einsum("nqhd,nkhd->nhqk", queries, key_win, preferred_element_type=jnp.float32)
            * scale
        )
        masked = jnp.where(usable, scores, jnp.float32(-1e30))
        fresh = jnp.maximum(best, jnp.max(masked, axis=3))
        probs = jnp.where(usable, jnp.exp(scores - fresh[..., None]), jnp.float32(0.0))
        shrink = jnp.exp(best - fresh)
        total = total * shrink + jnp.sum(probs, axis=3)
        acc = acc * shrink[..., None] + jnp.einsum(
            "nhqk,nkhd->nhqd",
            probs.astype(jnp.bfloat16),
            value_win,
            preferred_element_type=jnp.float32,
        )
        return ((fresh, total, acc), None)

    final, unused = lax.scan(one_stretch, initial, (key_full, value_full, stretch_ids))
    best, total, acc = final
    attn = (acc / total[..., None]).astype(jnp.bfloat16)
    attn = attn.transpose(0, 2, 1, 3).reshape(
        2, 2, frames, half_high, half_wide, heads_here * head_dim
    )
    attn = attn.transpose(2, 0, 3, 1, 4, 5).reshape(tokens_here, heads_here * head_dim)
    mixed = lax.psum_scatter(
        jnp.dot(attn, out_weight, preferred_element_type=jnp.float32).astype(jnp.bfloat16),
        "head",
        scatter_dimension=0,
        tiled=True,
    )
    return mixed.reshape(1, 1, -1, out_weight.shape[1])


def tile_place():
    tile_at = lax.axis_index("tile")
    return tile_at // 2, tile_at % 2


def face_kernel(
    k_ref, v_ref, w_ref, row_ref, col_ref, corner_ref, tile_ref, part_ref, sems, *, geometry
):
    high, wide, span, frames = geometry[:4]
    cells = high * wide
    row_at, col_at = tile_place()
    y0 = jnp.where(row_at == 0, high - span, 0)
    x0 = jnp.where(col_at == 0, wide - span, 0)
    tall, broad = part_ref.shape
    top = pl.multiple_of(lax.axis_index("tile") * tall, 16)
    edge = pl.multiple_of(lax.axis_index("tm") * broad, 128)
    copies = [
        pltpu.make_async_copy(ref, tile_ref.at[which], sems.at[which])
        for which, ref in enumerate((k_ref, v_ref))
    ]
    copies.append(
        pltpu.make_async_copy(
            w_ref.at[pl.ds(top, tall), pl.ds(edge, broad)], part_ref, sems.at[2]
        )
    )
    for copy in copies:
        copy.start()

    def picker(count, cell_of):
        row = lax.broadcasted_iota(jnp.int32, (count, cells), 0)
        col = lax.broadcasted_iota(jnp.int32, (count, cells), 1)
        return (col == cell_of(row)).astype(jnp.bfloat16)

    beside = picker(high * span, lambda i: (i // span) * wide + x0 + i % span)
    across = picker(span * span, lambda i: (y0 + i // span) * wide + x0 + i % span)
    for which in range(2):
        copies[which].wait()
        for f in range(frames):
            start = pl.multiple_of(f * cells + y0 * wide, 16)
            row_ref[which, f] = tile_ref[which, pl.ds(start, span * wide)]
            whole = tile_ref[which, f * cells : (f + 1) * cells]
            col_ref[which, f] = jnp.dot(
                beside, whole, preferred_element_type=jnp.float32
            ).astype(jnp.bfloat16)
            corner_ref[which, f] = jnp.dot(
                across, whole, preferred_element_type=jnp.float32
            ).astype(jnp.bfloat16)
    copies[2].wait()


def join_kernel(tile_ref, row_ref, col_ref, corner_ref, kv_ref):
    for which in range(2):
        at = tile_ref.shape[1]
        kv_ref[which, :at] = tile_ref[which]
        for part in (row_ref, col_ref, corner_ref):
            for f in range(part.shape[1]):
                size = part.shape[2]
                kv_ref[which, at : at + size] = part[which, f]
                at += size


def distances(high, wide, span, frames):
    row_at, col_at = tile_place()
    cells = high * wide
    count = frames * (cells + span * (wide + high + span))
    j = lax.broadcasted_iota(jnp.int32, (1, count), 1)
    y_off = jnp.where(row_at == 0, high, -span)
    x_off = jnp.where(col_at == 0, wide, -span)
    c = j % cells
    ky, kx = c // wide, c % wide
    base = frames * cells
    c = (j - base) % (span * wide)
    ky = jnp.where(j >= base, y_off + c // wide, ky)
    kx = jnp.where(j >= base, c % wide, kx)
    base += frames * span * wide
    c = (j - base) % (span * high)
    ky = jnp.where(j >= base, c // span, ky)
    kx = jnp.where(j >= base, x_off + c % span, kx)
    base += frames * span * high
    c = (j - base) % (span * span)
    ky = jnp.where(j >= base, y_off + c // span, ky)
    kx = jnp.where(j >= base, x_off + c % span, kx)
    i = lax.broadcasted_iota(jnp.int32, (cells, 1), 0)
    return jnp.maximum(jnp.abs(i // wide - ky), jnp.abs(i % wide - kx))


def attend(q, pieces, factor, before):
    scores = []
    m = before
    for k, v, dist, reach in pieces:
        s = lax.dot_general(q, k, (((1,), (1,)), ((), ())), preferred_element_type=jnp.float32)
        s = jnp.where(dist <= reach, s * factor, FAR)
        top = jnp.max(s, axis=1, keepdims=True)
        m = top if m is None else jnp.maximum(m, top)
        scores.append(s)
    total = None
    for s, (k, v, dist, reach) in zip(scores, pieces):
        p = jnp.exp2(s - m).astype(jnp.bfloat16)
        both = jnp.concatenate([v, jnp.ones_like(v)], axis=1)
        got = jnp.dot(p, both, preferred_element_type=jnp.float32)
        total = got if total is None else total + got
    return m, total


def attend_tile(q_ref, tile_ref, dist_ref, reach_of, heads, state, geometry):
    high, wide, span, frames, head_dim, factor, step = geometry
    cells = high * wide
    acc_ref, sum_ref, max_ref = state
    for at, head in enumerate(heads):
        cols = slice(head * head_dim, (head + 1) * head_dim)
        outs = slice(at * head_dim, (at + 1) * head_dim)
        for start in range(0, q_ref.shape[0], step):
            rows = slice(start, start + step)
            near = dist_ref[start % cells : start % cells + step, : tile_ref.shape[1]]
            piece = (tile_ref[0, :, cols], tile_ref[1, :, cols], near, reach_of(head))
            m, got = attend(q_ref[rows, cols], [piece], factor, None)
            acc_ref[rows, outs] = got[:, :head_dim]
            sum_ref[rows, outs] = got[:, head_dim:]
            max_ref[rows, outs] = jnp.broadcast_to(m, (step, head_dim))


def begin_kernel(radius_ref, mask_ref, q_ref, tile_ref, *outs, geometry, heads):
    *state, dist_ref, reach_ref = outs
    high, wide, span, frames = geometry[:4]
    dist_ref[...] = distances(high, wide, span, frames)
    stretch_at = lax.axis_index("tm")
    line = (1, reach_ref.shape[1])
    for head in range(heads):
        radius = radius_ref[head]
        seen = mask_ref[stretch_at, 0, head] > 0
        reach_ref[head : head + 1] = jnp.full(line, radius, jnp.int32)
        reach_ref[heads + head : heads + head + 1] = jnp.full(
            line, jnp.where(seen, radius, -1), jnp.int32
        )
    attend_tile(q_ref, tile_ref, dist_ref, lambda h: radius_ref[h], (0,), state, geometry)


def tile_kernel(q_ref, tile_ref, dist_ref, reach_ref, *state, geometry, heads):
    attend_tile(
        q_ref,
        tile_ref,
        dist_ref,
        lambda h: reach_ref[h : h + 1, :1],
        range(1, heads),
        state,
        geometry,
    )


def rest_kernel(
    q_ref,
    kv_ref,
    first_ref,
    *rest,
    geometry,
    heads,
    flips,
):
    head_state, dist_ref, reach_ref, state, outs = rest[:3], rest[3], rest[4], rest[5:8], rest[8:]
    high, wide, span, frames, head_dim, factor, step = geometry
    cells = high * wide
    base = frames * cells
    head_at = lax.axis_index("head")
    stretch_at = lax.axis_index("tm")

    def run(with_first):
        for flip, out_ref in zip(flips, outs):
            start = pl.multiple_of(jnp.bitwise_xor(head_at, flip) * step, step)
            rows = pl.ds(start, step)
            near = dist_ref[pl.ds(pl.multiple_of(lax.rem(start, cells), step), step)]
            for head in range(heads):
                cols = slice(head * head_dim, (head + 1) * head_dim)
                reach = reach_ref[head : head + 1, :1]
                seen = reach_ref[heads + head : heads + head + 1, :1]
                pieces = [
                    (kv_ref[0, base:, cols], kv_ref[1, base:, cols], near[:, base:], reach)
                ]
                if with_first:
                    pieces.append((first_ref[0, :, cols], first_ref[1, :, cols], near, seen))
                refs = head_state if head == 0 else state
                at = max(head - 1, 0) * head_dim
                old_acc, old_total, old = (ref[rows, at : at + head_dim] for ref in refs)
                m, got = attend(q_ref[rows, cols], pieces, factor, old[:, :1])
                shrink = jnp.exp2(old - m)
                acc = old_acc * shrink + got[:, :head_dim]
                total = old_total * shrink + got[:, head_dim:]
                out_ref[:, cols] = (acc / total).astype(jnp.bfloat16)

    @pl.when(stretch_at > 0)
    def _():
        run(True)

    @pl.when(stretch_at == 0)
    def _():
        run(False)


def stack_kernel(*refs):
    *parts, out_ref = refs
    tile_at = lax.axis_index("tile")
    for flip, part in enumerate(parts):
        tall = part.shape[0]
        top = pl.multiple_of(jnp.bitwise_xor(tile_at, flip) * tall, 16)
        out_ref[pl.ds(top, tall)] = part[...]


def half_sum(w_ref, part_ref, own_ref, got_ref, core):
    broad = part_ref.shape[1]
    cols = pl.ds(pl.multiple_of(core * broad, 128), broad)
    total = jnp.dot(own_ref[...], w_ref[:, cols], preferred_element_type=jnp.float32)
    return cols, total + jnp.dot(
        got_ref[...], part_ref[...], preferred_element_type=jnp.float32
    )


def half_kernel(w_ref, here_ref, own_ref, got_ref, out_ref):
    core = lax.axis_index("tm")
    out_ref[...] = half_sum(w_ref, here_ref, own_ref, got_ref, core)[1].astype(out_ref.dtype)


def whole_kernel(w_ref, there_ref, own_ref, got_ref, half_ref, out_ref):
    core = lax.axis_index("tm")
    cols, total = half_sum(w_ref, there_ref, own_ref, got_ref, 1 - core)
    out_ref[:, cols] = total.astype(out_ref.dtype)
    broad = half_ref.shape[1]
    out_ref[:, pl.ds(pl.multiple_of(core * broad, 128), broad)] = half_ref[...]


def add_kernel(mine_ref, got_ref, out_ref, sum_ref, sems):
    parts = sum_ref.shape[0]
    tall = sum_ref.shape[1]
    copies = []
    for i in range(parts):
        rows = slice(i * tall, (i + 1) * tall)
        sum_ref[i] = (mine_ref[rows] + got_ref[rows].astype(jnp.float32)).astype(jnp.bfloat16)
        copies.append(pltpu.make_async_copy(sum_ref.at[i], out_ref.at[rows], sems.at[i]))
        copies[-1].start()
    for copy in copies:
        copy.wait()


def two_by_two(query, keys, values, out_weight, radius, block_mask):
    span = RMAX
    frames, high, wide, channels = query.shape[2:]
    heads = radius.shape[0]
    head_dim = channels // heads
    cells = high * wide
    tokens = frames * cells
    groups = lax.axis_size("head")
    tiles = lax.axis_size("tile")
    depth, width = out_weight.shape
    step = tokens // groups
    geometry = (high, wide, span, frames, head_dim, LOG2E / math.sqrt(head_dim), step)
    count = frames * (cells + span * (wide + high + span))
    smem = pl.BlockSpec(memory_space=pltpu.SMEM)
    vmem = pl.BlockSpec(memory_space=pltpu.VMEM)
    hbm = pl.BlockSpec(memory_space=pltpu.HBM)
    bf16, f32 = jnp.bfloat16, jnp.float32
    shape = jax.ShapeDtypeStruct

    def call(kernel, out_shape, specs, *args, name, scratch=(), flops=0, **keys_of):
        return pl.pallas_call(
            functools.partial(kernel, **keys_of) if keys_of else kernel,
            out_shape=out_shape,
            in_specs=specs,
            out_specs=jax.tree.map(lambda _: vmem, out_shape),
            scratch_shapes=scratch,
            cost_estimate=pl.CostEstimate(flops=flops, bytes_accessed=0, transcendentals=0),
            compiler_params=pltpu.CompilerParams(vmem_limit_bytes=VMEM_LIMIT),
            name=name,
        )(*args)

    def flipped(value, axis, flip):
        return lax.ppermute(value, axis, [(i, i ^ flip) for i in range(lax.axis_size(axis))])

    q = query.reshape(tokens, channels)
    k = keys.reshape(tokens, channels)
    v = values.reshape(tokens, channels)

    tall, broad = depth // tiles, width // 2
    *faces, tile, part = call(
        face_kernel,
        [
            shape((2, frames, span * wide, channels), bf16),
            shape((2, frames, span * high, channels), bf16),
            shape((2, frames, span * span, channels), bf16),
            shape((2, tokens, channels), bf16),
            shape((tall, broad), bf16),
        ],
        [hbm] * 3,
        *[pltpu.with_memory_space_constraint(x, pltpu.HBM) for x in (k, v, out_weight)],
        name="faces",
        scratch=[pltpu.SemaphoreType.DMA((3,))],
        geometry=geometry,
    )
    faces = [flipped(face, "tile", flip) for face, flip in zip(faces, (2, 1, 3))]
    lone = flipped(part, "head", 2)
    begun = call(
        begin_kernel,
        [shape((tokens, head_dim), f32)] * 3
        + [shape((cells, count), jnp.int32), shape((2 * heads, head_dim), jnp.int32)],
        [smem] * 2 + [vmem] * 2,
        radius,
        block_mask.transpose(1, 2, 0),
        q,
        tile,
        name="begin",
        geometry=geometry,
        heads=heads,
    )
    lone, begun = lax.optimization_barrier((lone, begun))
    state = begun + call(
        tile_kernel,
        [shape((tokens, channels - head_dim), f32)] * 3,
        [vmem] * 4,
        q,
        tile,
        *begun[3:],
        name="tile",
        flops=20 * 10**9,
        geometry=geometry,
        heads=heads,
    )
    state, faces = lax.optimization_barrier((state, faces))
    kv = call(
        join_kernel, shape((2, count, channels), bf16), [vmem] * 4, tile, *faces, name="join"
    )
    kv_first = lax.ppermute(kv, "tm", [(0, 1)])
    parts = [lone] + [flipped(lone, "tile", flip) for flip in range(1, tiles)]

    def rest(state, *flips):
        return call(
            rest_kernel,
            [shape((step, channels), bf16)] * len(flips),
            [vmem] * 11,
            q,
            kv,
            kv_first,
            *state,
            name="rest",
            geometry=geometry,
            heads=heads,
            flips=flips,
        )

    (for_side,) = rest(state, 3)
    got_side = flipped(for_side, "head", 2)
    state, for_side = lax.optimization_barrier((state, for_side))
    (for_far,) = rest(state, 2)
    got_far = flipped(for_far, "head", 2)
    state, for_far = lax.optimization_barrier((state, for_far))
    (own_side,) = rest(state, 1)
    parts, own_side = lax.optimization_barrier((parts, own_side))
    here = call(
        stack_kernel, shape((depth, broad), bf16), [vmem] * tiles, *parts, name="stack"
    )
    there = flipped(here, "tm", 1)

    def project(mine, got, kind, flops):
        half = call(
            half_kernel,
            shape((step, broad), kind),
            [vmem] * 4,
            out_weight,
            here,
            mine,
            got,
            name="half",
            flops=flops,
        )
        return call(
            whole_kernel,
            shape((step, width), kind),
            [vmem] * 5,
            out_weight,
            there,
            mine,
            got,
            half,
            name="whole",
        )

    for_side = project(own_side, got_side, bf16, 20 * 10**9)
    from_side = flipped(for_side, "head", 1)
    state, for_side = lax.optimization_barrier((state, for_side))
    (own,) = rest(state, 0)
    mine = project(own, got_far, f32, 20 * 10**9)
    quarters = 4
    mixed = pl.pallas_call(
        add_kernel,
        out_shape=shape((step, width), bf16),
        in_specs=[vmem] * 2,
        out_specs=hbm,
        scratch_shapes=[
            pltpu.VMEM((quarters, step // quarters, width), bf16),
            pltpu.SemaphoreType.DMA((quarters,)),
        ],
        compiler_params=pltpu.CompilerParams(vmem_limit_bytes=VMEM_LIMIT),
        name="add",
    )(mine, from_side)
    return mixed.reshape(1, 1, step, width)


def solution(mesh):
    in_specs = (
        P("tm", "tile", None, None, None, "head"),
        P("tm", "tile", None, None, None, "head"),
        P("tm", "tile", None, None, None, "head"),
        P("head", None),
        P("head"),
        P("head", None, None),
    )
    out_specs = P("tm", "tile", "head", None)
    small = dict(mesh.shape) == {"tm": 2, "tile": 4, "head": 4}
    return jax.shard_map(
        two_by_two if small else any_grid,
        mesh=mesh,
        in_specs=in_specs,
        out_specs=out_specs,
        check_vma=False,
    )
```

```python
import functools
import math

import jax
import jax.numpy as jnp
from jax import lax
from jax.experimental import pallas as pl
from jax.experimental.pallas import tpu as pltpu
from jax.sharding import PartitionSpec as P

RMAX = 4
FAR = -1e30
LOG2E = 1.4426950408889634
VMEM_LIMIT = 24 * 1024 * 1024


def passed_along(value, axis, by):
    peers = lax.axis_size(axis)
    pairs = [(i, i + by) for i in range(peers) if 0 <= i + by < peers]
    return lax.ppermute(value, axis, pairs)


def widen(key_part, value_part, span, row_move, col_move):
    grid = math.isqrt(lax.axis_size("tile"))
    above = None
    below = None
    for offset in (grid, -grid):
        if offset > 0:
            face_key = key_part[:, :, key_part.shape[2] - span :]
            face_value = value_part[:, :, value_part.shape[2] - span :]
        else:
            face_key = key_part[:, :, :span]
            face_value = value_part[:, :, :span]
        got = row_move(face_key, face_value, offset)
        if offset > 0:
            above = got
        else:
            below = got
    key_rows = jnp.concatenate([above[0], key_part, below[0]], axis=2)
    value_rows = jnp.concatenate([above[1], value_part, below[1]], axis=2)
    left = None
    right = None
    for offset in (1, -1):
        if offset > 0:
            face_key = key_rows[:, :, :, key_rows.shape[3] - span :]
            face_value = value_rows[:, :, :, value_rows.shape[3] - span :]
        else:
            face_key = key_rows[:, :, :, :span]
            face_value = value_rows[:, :, :, :span]
        got = col_move(face_key, face_value, offset)
        if offset > 0:
            left = got
        else:
            right = got
    key_full = jnp.concatenate([left[0], key_rows, right[0]], axis=3)
    value_full = jnp.concatenate([left[1], value_rows, right[1]], axis=3)
    return (key_full, value_full)


def windows_of(block, half_high, half_wide, win_high, win_wide, heads_here, head_dim):
    parts = []
    for band in (0, 1):
        for strip in (0, 1):
            parts.append(
                block[
                    :,
                    band * half_high : band * half_high + win_high,
                    strip * half_wide : strip * half_wide + win_wide,
                ]
            )
    stacked = jnp.stack(parts)
    return stacked.reshape(4, -1, heads_here, head_dim)


def any_grid(query, keys, values, out_weight, radius, block_mask):
    span = RMAX
    grid = math.isqrt(lax.axis_size("tile"))
    tile_at = lax.axis_index("tile")
    row_at = tile_at // grid
    col_at = tile_at % grid
    stretch_at = lax.axis_index("tm")
    frames, high, wide, channels = query.shape[2:]
    heads_here = radius.shape[0]
    head_dim = channels // heads_here
    tokens_here = frames * high * wide
    half_high = high // 2
    half_wide = wide // 2
    win_high = half_high + 2 * span
    win_wide = half_wide + 2 * span
    quarter = frames * half_high * half_wide
    queries = query[0, 0].reshape(frames, 2, half_high, 2, half_wide, channels)
    queries = queries.transpose(1, 3, 0, 2, 4, 5).reshape(4, quarter, heads_here, head_dim)
    query_y = jnp.broadcast_to(
        jnp.arange(half_high, dtype=jnp.int32)[None, :, None], (frames, half_high, half_wide)
    ).reshape(-1)
    query_x = jnp.broadcast_to(
        jnp.arange(half_wide, dtype=jnp.int32)[None, None, :], (frames, half_high, half_wide)
    ).reshape(-1)
    key_y = jnp.broadcast_to(
        jnp.arange(win_high, dtype=jnp.int32)[None, :, None] - span, (frames, win_high, win_wide)
    ).reshape(-1)
    key_x = jnp.broadcast_to(
        jnp.arange(win_wide, dtype=jnp.int32)[None, None, :] - span, (frames, win_high, win_wide)
    ).reshape(-1)
    band_at = jnp.array([0, 0, 1, 1], dtype=jnp.int32)
    strip_at = jnp.array([0, 1, 0, 1], dtype=jnp.int32)
    global_y = row_at * high + band_at[:, None] * half_high + key_y[None, :]
    global_x = col_at * wide + strip_at[:, None] * half_wide + key_x[None, :]
    inside = (global_y >= 0) & (global_y < grid * high) & (global_x >= 0) & (global_x < grid * wide)
    distance = jnp.maximum(
        jnp.abs(query_y[:, None] - key_y[None, :]), jnp.abs(query_x[:, None] - key_x[None, :])
    )
    near = distance[None, :, :] <= radius[:, None, None]
    allowed = near[None, :, :, :] & inside[:, None, None, :]
    scale = 1.0 / math.sqrt(head_dim)
    initial = (
        jnp.full((4, heads_here, quarter), -1e30, jnp.float32),
        jnp.zeros((4, heads_here, quarter), jnp.float32),
        jnp.zeros((4, heads_here, quarter, head_dim), jnp.float32),
    )

    def tile_move(face_key, face_value, offset):
        return passed_along((face_key, face_value), "tile", offset)

    key_all, value_all = (
        lax.all_gather(keys[0], "tm", axis=0, tiled=True),
        lax.all_gather(values[0], "tm", axis=0, tiled=True),
    )
    key_full, value_full = widen(key_all, value_all, span, tile_move, tile_move)
    stretch_ids = jnp.arange(key_full.shape[0], dtype=jnp.int32)

    def one_stretch(state, item):
        key_block, value_block, stretch_id = item
        visible = (
            lax.dynamic_slice_in_dim(
                lax.dynamic_index_in_dim(block_mask, stretch_at, 1, False), stretch_id, 1, 1
            )[:, 0]
            > 0
        )
        best, total, acc = state
        key_win = windows_of(
            key_block, half_high, half_wide, win_high, win_wide, heads_here, head_dim
        )
        value_win = windows_of(
            value_block, half_high, half_wide, win_high, win_wide, heads_here, head_dim
        )
        usable = allowed & visible[None, :, None, None]
        scores = (
            jnp.einsum("nqhd,nkhd->nhqk", queries, key_win, preferred_element_type=jnp.float32)
            * scale
        )
        masked = jnp.where(usable, scores, jnp.float32(-1e30))
        fresh = jnp.maximum(best, jnp.max(masked, axis=3))
        probs = jnp.where(usable, jnp.exp(scores - fresh[..., None]), jnp.float32(0.0))
        shrink = jnp.exp(best - fresh)
        total = total * shrink + jnp.sum(probs, axis=3)
        acc = acc * shrink[..., None] + jnp.einsum(
            "nhqk,nkhd->nhqd",
            probs.astype(jnp.bfloat16),
            value_win,
            preferred_element_type=jnp.float32,
        )
        return ((fresh, total, acc), None)

    final, unused = lax.scan(one_stretch, initial, (key_full, value_full, stretch_ids))
    best, total, acc = final
    attn = (acc / total[..., None]).astype(jnp.bfloat16)
    attn = attn.transpose(0, 2, 1, 3).reshape(
        2, 2, frames, half_high, half_wide, heads_here * head_dim
    )
    attn = attn.transpose(2, 0, 3, 1, 4, 5).reshape(tokens_here, heads_here * head_dim)
    mixed = lax.psum_scatter(
        jnp.dot(attn, out_weight, preferred_element_type=jnp.float32).astype(jnp.bfloat16),
        "head",
        scatter_dimension=0,
        tiled=True,
    )
    return mixed.reshape(1, 1, -1, out_weight.shape[1])


def tile_place():
    tile_at = lax.axis_index("tile")
    return tile_at // 2, tile_at % 2


def face_kernel(
    k_ref, v_ref, w_ref, row_ref, col_ref, corner_ref, tile_ref, part_ref, sems, *, geometry
):
    high, wide, span, frames = geometry[:4]
    cells = high * wide
    row_at, col_at = tile_place()
    y0 = jnp.where(row_at == 0, high - span, 0)
    x0 = jnp.where(col_at == 0, wide - span, 0)
    tall, broad = part_ref.shape
    top = pl.multiple_of(lax.axis_index("tile") * tall, 16)
    edge = pl.multiple_of(lax.axis_index("tm") * broad, 128)
    copies = [
        pltpu.make_async_copy(ref, tile_ref.at[which], sems.at[which])
        for which, ref in enumerate((k_ref, v_ref))
    ]
    copies.append(
        pltpu.make_async_copy(
            w_ref.at[pl.ds(top, tall), pl.ds(edge, broad)], part_ref, sems.at[2]
        )
    )
    for copy in copies:
        copy.start()

    def picker(count, cell_of):
        row = lax.broadcasted_iota(jnp.int32, (count, cells), 0)
        col = lax.broadcasted_iota(jnp.int32, (count, cells), 1)
        return (col == cell_of(row)).astype(jnp.bfloat16)

    beside = picker(high * span, lambda i: (i // span) * wide + x0 + i % span)
    across = picker(span * span, lambda i: (y0 + i // span) * wide + x0 + i % span)
    for which in range(2):
        copies[which].wait()
        for f in range(frames):
            start = pl.multiple_of(f * cells + y0 * wide, 16)
            row_ref[which, f] = tile_ref[which, pl.ds(start, span * wide)]
            whole = tile_ref[which, f * cells : (f + 1) * cells]
            col_ref[which, f] = jnp.dot(
                beside, whole, preferred_element_type=jnp.float32
            ).astype(jnp.bfloat16)
            corner_ref[which, f] = jnp.dot(
                across, whole, preferred_element_type=jnp.float32
            ).astype(jnp.bfloat16)
    copies[2].wait()


def edge_kernel(row_ref, col_ref, corner_ref, out_ref):
    for which in range(2):
        at = 0
        for part in (row_ref, col_ref, corner_ref):
            for f in range(part.shape[1]):
                size = part.shape[2]
                out_ref[which, at : at + size] = part[which, f]
                at += size


def distances(high, wide, span, frames):
    row_at, col_at = tile_place()
    cells = high * wide
    count = frames * (cells + span * (wide + high + span))
    j = lax.broadcasted_iota(jnp.int32, (1, count), 1)
    y_off = jnp.where(row_at == 0, high, -span)
    x_off = jnp.where(col_at == 0, wide, -span)
    c = j % cells
    ky, kx = c // wide, c % wide
    base = frames * cells
    c = (j - base) % (span * wide)
    ky = jnp.where(j >= base, y_off + c // wide, ky)
    kx = jnp.where(j >= base, c % wide, kx)
    base += frames * span * wide
    c = (j - base) % (span * high)
    ky = jnp.where(j >= base, c // span, ky)
    kx = jnp.where(j >= base, x_off + c % span, kx)
    base += frames * span * high
    c = (j - base) % (span * span)
    ky = jnp.where(j >= base, y_off + c // span, ky)
    kx = jnp.where(j >= base, x_off + c % span, kx)
    i = lax.broadcasted_iota(jnp.int32, (cells, 1), 0)
    return jnp.maximum(jnp.abs(i // wide - ky), jnp.abs(i % wide - kx))


def attend(q, pieces, factor, before):
    scores = []
    m = before
    for k, v, dist, reach in pieces:
        s = lax.dot_general(q, k, (((1,), (1,)), ((), ())), preferred_element_type=jnp.float32)
        s = jnp.where(dist <= reach, s * factor, FAR)
        top = jnp.max(s, axis=1, keepdims=True)
        m = top if m is None else jnp.maximum(m, top)
        scores.append(s)
    total = None
    for s, (k, v, dist, reach) in zip(scores, pieces):
        p = jnp.exp2(s - m).astype(jnp.bfloat16)
        both = jnp.concatenate([v, jnp.ones_like(v)], axis=1)
        got = jnp.dot(p, both, preferred_element_type=jnp.float32)
        total = got if total is None else total + got
    return m, total


def attend_tile(q_ref, tile_ref, dist_ref, reach_of, heads, state, geometry):
    high, wide, span, frames, head_dim, factor, step = geometry
    cells = high * wide
    acc_ref, sum_ref, max_ref = state
    for at, head in enumerate(heads):
        cols = slice(head * head_dim, (head + 1) * head_dim)
        outs = slice(at * head_dim, (at + 1) * head_dim)
        for start in range(0, q_ref.shape[0], step):
            rows = slice(start, start + step)
            near = dist_ref[start % cells : start % cells + step, : tile_ref.shape[1]]
            piece = (tile_ref[0, :, cols], tile_ref[1, :, cols], near, reach_of(head))
            m, got = attend(q_ref[rows, cols], [piece], factor, None)
            acc_ref[rows, outs] = got[:, :head_dim]
            sum_ref[rows, outs] = got[:, head_dim:]
            max_ref[rows, outs] = jnp.broadcast_to(m, (step, head_dim))


def begin_kernel(radius_ref, mask_ref, q_ref, tile_ref, *outs, geometry, heads):
    *state, dist_ref, reach_ref = outs
    high, wide, span, frames = geometry[:4]
    dist_ref[...] = distances(high, wide, span, frames)
    stretch_at = lax.axis_index("tm")
    line = (1, reach_ref.shape[1])
    for head in range(heads):
        radius = radius_ref[head]
        seen = mask_ref[stretch_at, 0, head] > 0
        reach_ref[head : head + 1] = jnp.full(line, radius, jnp.int32)
        reach_ref[heads + head : heads + head + 1] = jnp.full(
            line, jnp.where(seen, radius, -1), jnp.int32
        )
    attend_tile(q_ref, tile_ref, dist_ref, lambda h: radius_ref[h], (0,), state, geometry)


def tile_kernel(q_ref, tile_ref, dist_ref, reach_ref, *state, geometry, heads):
    attend_tile(
        q_ref,
        tile_ref,
        dist_ref,
        lambda h: reach_ref[h : h + 1, :1],
        range(1, heads),
        state,
        geometry,
    )


def pick_state(head_state, state, head, rows, head_dim):
    refs = head_state if head == 0 else state
    at = max(head - 1, 0) * head_dim
    return [ref[rows, at : at + head_dim] for ref in refs]


def merge(q, pieces, factor, old):
    old_acc, old_total, old_max = old
    m, got = attend(q, pieces, factor, old_max[:, :1])
    shrink = jnp.exp2(old_max - m)
    head_dim = old_acc.shape[1]
    acc = old_acc * shrink + got[:, :head_dim]
    total = old_total * shrink + got[:, head_dim:]
    return acc, total, jnp.broadcast_to(m, old_max.shape)


def rest_kernel(
    q_ref,
    edge_ref,
    first_tile_ref,
    first_edge_ref,
    *rest,
    geometry,
    heads,
    flips,
):
    head_state, dist_ref, reach_ref, state, outs = rest[:3], rest[3], rest[4], rest[5:8], rest[8:]
    high, wide, span, frames, head_dim, factor, step = geometry
    cells = high * wide
    base = frames * cells
    head_at = lax.axis_index("head")
    stretch_at = lax.axis_index("tm")

    def run(with_first):
        for flip, out_ref in zip(flips, outs):
            start = pl.multiple_of(jnp.bitwise_xor(head_at, flip) * step, step)
            rows = pl.ds(start, step)
            near = dist_ref[pl.ds(pl.multiple_of(lax.rem(start, cells), step), step)]
            beyond = near[:, base:]
            for head in range(heads):
                cols = slice(head * head_dim, (head + 1) * head_dim)
                sources = [(edge_ref, beyond, head)]
                if with_first:
                    sources.append((first_tile_ref, near[:, :base], heads + head))
                    sources.append((first_edge_ref, beyond, heads + head))
                pieces = [
                    (ref[0, :, cols], ref[1, :, cols], dist, reach_ref[row : row + 1, :1])
                    for ref, dist, row in sources
                ]
                old = pick_state(head_state, state, head, rows, head_dim)
                acc, total, m = merge(q_ref[rows, cols], pieces, factor, old)
                out_ref[:, cols] = (acc / total).astype(jnp.bfloat16)

    @pl.when(stretch_at > 0)
    def _():
        run(True)

    @pl.when(stretch_at == 0)
    def _():
        run(False)


def copy_kernel(in_ref, out_ref):
    out_ref[...] = in_ref[...]


def stack_kernel(*refs):
    *parts, out_ref = refs
    tile_at = lax.axis_index("tile")
    for flip, part in enumerate(parts):
        tall = part.shape[0]
        top = pl.multiple_of(jnp.bitwise_xor(tile_at, flip) * tall, 16)
        out_ref[pl.ds(top, tall)] = part[...]


def half_sum(w_ref, part_ref, own_ref, got_ref, core):
    broad = part_ref.shape[1]
    cols = pl.ds(pl.multiple_of(core * broad, 128), broad)
    total = jnp.dot(own_ref[...], w_ref[:, cols], preferred_element_type=jnp.float32)
    return cols, total + jnp.dot(
        got_ref[...], part_ref[...], preferred_element_type=jnp.float32
    )


def half_kernel(w_ref, here_ref, own_ref, got_ref, out_ref):
    core = lax.axis_index("tm")
    out_ref[...] = half_sum(w_ref, here_ref, own_ref, got_ref, core)[1].astype(out_ref.dtype)


def whole_kernel(w_ref, there_ref, own_ref, got_ref, half_ref, out_ref):
    core = lax.axis_index("tm")
    cols, total = half_sum(w_ref, there_ref, own_ref, got_ref, 1 - core)
    out_ref[:, cols] = total.astype(out_ref.dtype)
    broad = half_ref.shape[1]
    out_ref[:, pl.ds(pl.multiple_of(core * broad, 128), broad)] = half_ref[...]


def add_kernel(mine_ref, got_ref, out_ref, sum_ref, sems):
    parts = sum_ref.shape[0]
    tall = sum_ref.shape[1]
    copies = []
    for i in range(parts):
        rows = slice(i * tall, (i + 1) * tall)
        sum_ref[i] = (mine_ref[rows] + got_ref[rows].astype(jnp.float32)).astype(jnp.bfloat16)
        copies.append(pltpu.make_async_copy(sum_ref.at[i], out_ref.at[rows], sems.at[i]))
        copies[-1].start()
    for copy in copies:
        copy.wait()


def two_by_two(query, keys, values, out_weight, radius, block_mask):
    span = RMAX
    frames, high, wide, channels = query.shape[2:]
    heads = radius.shape[0]
    head_dim = channels // heads
    cells = high * wide
    tokens = frames * cells
    groups = lax.axis_size("head")
    tiles = lax.axis_size("tile")
    depth, width = out_weight.shape
    step = tokens // groups
    geometry = (high, wide, span, frames, head_dim, LOG2E / math.sqrt(head_dim), step)
    count = frames * (cells + span * (wide + high + span))
    smem = pl.BlockSpec(memory_space=pltpu.SMEM)
    vmem = pl.BlockSpec(memory_space=pltpu.VMEM)
    hbm = pl.BlockSpec(memory_space=pltpu.HBM)
    bf16, f32 = jnp.bfloat16, jnp.float32
    shape = jax.ShapeDtypeStruct

    def call(kernel, out_shape, specs, *args, name, scratch=(), flops=0, **keys_of):
        return pl.pallas_call(
            functools.partial(kernel, **keys_of) if keys_of else kernel,
            out_shape=out_shape,
            in_specs=specs,
            out_specs=jax.tree.map(lambda _: vmem, out_shape),
            scratch_shapes=scratch,
            cost_estimate=pl.CostEstimate(flops=flops, bytes_accessed=0, transcendentals=0),
            compiler_params=pltpu.CompilerParams(vmem_limit_bytes=VMEM_LIMIT),
            name=name,
        )(*args)

    def flipped(value, axis, flip):
        return lax.ppermute(value, axis, [(i, i ^ flip) for i in range(lax.axis_size(axis))])

    q = query.reshape(tokens, channels)
    k = keys.reshape(tokens, channels)
    v = values.reshape(tokens, channels)

    tall, broad = depth // tiles, width // 2
    part_shape = shape((tall, broad), bf16)
    *faces, tile, part = call(
        face_kernel,
        [
            shape((2, frames, span * wide, channels), bf16),
            shape((2, frames, span * high, channels), bf16),
            shape((2, frames, span * span, channels), bf16),
            shape((2, tokens, channels), bf16),
            part_shape,
        ],
        [hbm] * 3,
        *[pltpu.with_memory_space_constraint(x, pltpu.HBM) for x in (k, v, out_weight)],
        name="faces",
        scratch=[pltpu.SemaphoreType.DMA((3,))],
        geometry=geometry,
    )
    faces = [flipped(face, "tile", flip) for face, flip in zip(faces, (2, 1, 3))]
    lone = flipped(part, "head", 2)
    begun = call(
        begin_kernel,
        [shape((tokens, head_dim), f32)] * 3
        + [shape((cells, count), jnp.int32), shape((2 * heads, head_dim), jnp.int32)],
        [smem] * 2 + [vmem] * 2,
        radius,
        block_mask.transpose(1, 2, 0),
        q,
        tile,
        name="begin",
        geometry=geometry,
        heads=heads,
    )
    begun, tile = lax.optimization_barrier((begun, tile))
    first_tile = lax.ppermute(tile, "tm", [(0, 1)])
    state = call(
        tile_kernel,
        [shape((tokens, channels - head_dim), f32)] * 3,
        [vmem] * 4,
        q,
        tile,
        *begun[3:],
        name="tile",
        geometry=geometry,
        heads=heads,
    )
    lone, state = lax.optimization_barrier((lone, state))
    lone = call(copy_kernel, part_shape, [vmem], lone, name="lone", flops=20 * 10**9)
    lone, state, faces = lax.optimization_barrier((lone, state, faces))
    edge = call(
        edge_kernel, shape((2, count - tokens, channels), bf16), [vmem] * 3, *faces, name="edges"
    )
    first_edge = lax.ppermute(edge, "tm", [(0, 1)])
    parts = [lone] + [flipped(lone, "tile", flip) for flip in range(1, tiles)]

    def rest(state, *flips):
        return call(
            rest_kernel,
            [shape((step, channels), bf16)] * len(flips),
            [vmem] * 12,
            q,
            edge,
            first_tile,
            first_edge,
            *begun,
            *state,
            name="rest",
            geometry=geometry,
            heads=heads,
            flips=flips,
        )

    (for_side,) = rest(state, 3)
    got_side = flipped(for_side, "head", 2)
    state, for_side = lax.optimization_barrier((state, for_side))
    (for_far,) = rest(state, 2)
    got_far = flipped(for_far, "head", 2)
    state, for_far = lax.optimization_barrier((state, for_far))
    (own_side,) = rest(state, 1)
    parts, own_side = lax.optimization_barrier((parts, own_side))
    here = call(
        stack_kernel, shape((depth, broad), bf16), [vmem] * tiles, *parts, name="stack"
    )
    there = flipped(here, "tm", 1)

    def project(mine, got, kind, flops):
        half = call(
            half_kernel,
            shape((step, broad), kind),
            [vmem] * 4,
            out_weight,
            here,
            mine,
            got,
            name="half",
            flops=flops,
        )
        return call(
            whole_kernel,
            shape((step, width), kind),
            [vmem] * 5,
            out_weight,
            there,
            mine,
            got,
            half,
            name="whole",
        )

    for_side = project(own_side, got_side, bf16, 20 * 10**9)
    from_side = flipped(for_side, "head", 1)
    state, for_side = lax.optimization_barrier((state, for_side))
    (own,) = rest(state, 0)
    mine = project(own, got_far, f32, 20 * 10**9)
    quarters = 4
    mixed = pl.pallas_call(
        add_kernel,
        out_shape=shape((step, width), bf16),
        in_specs=[vmem] * 2,
        out_specs=hbm,
        scratch_shapes=[
            pltpu.VMEM((quarters, step // quarters, width), bf16),
            pltpu.SemaphoreType.DMA((quarters,)),
        ],
        compiler_params=pltpu.CompilerParams(vmem_limit_bytes=VMEM_LIMIT),
        name="add",
    )(mine, from_side)
    return mixed.reshape(1, 1, step, width)


def solution(mesh):
    in_specs = (
        P("tm", "tile", None, None, None, "head"),
        P("tm", "tile", None, None, None, "head"),
        P("tm", "tile", None, None, None, "head"),
        P("head", None),
        P("head"),
        P("head", None, None),
    )
    out_specs = P("tm", "tile", "head", None)
    small = dict(mesh.shape) == {"tm": 2, "tile": 4, "head": 4}
    return jax.shard_map(
        two_by_two if small else any_grid,
        mesh=mesh,
        in_specs=in_specs,
        out_specs=out_specs,
        check_vma=False,
    )
```

```python
import functools
import math

import jax
import jax.numpy as jnp
from jax import lax
from jax.experimental import pallas as pl
from jax.experimental.pallas import tpu as pltpu
from jax.sharding import PartitionSpec as P

RMAX = 4
FAR = -1e30
LOG2E = 1.4426950408889634
VMEM_LIMIT = 24 * 1024 * 1024


def passed_along(value, axis, by):
    peers = lax.axis_size(axis)
    pairs = [(i, i + by) for i in range(peers) if 0 <= i + by < peers]
    return lax.ppermute(value, axis, pairs)


def widen(key_part, value_part, span, row_move, col_move):
    grid = math.isqrt(lax.axis_size("tile"))
    above = None
    below = None
    for offset in (grid, -grid):
        if offset > 0:
            face_key = key_part[:, :, key_part.shape[2] - span :]
            face_value = value_part[:, :, value_part.shape[2] - span :]
        else:
            face_key = key_part[:, :, :span]
            face_value = value_part[:, :, :span]
        got = row_move(face_key, face_value, offset)
        if offset > 0:
            above = got
        else:
            below = got
    key_rows = jnp.concatenate([above[0], key_part, below[0]], axis=2)
    value_rows = jnp.concatenate([above[1], value_part, below[1]], axis=2)
    left = None
    right = None
    for offset in (1, -1):
        if offset > 0:
            face_key = key_rows[:, :, :, key_rows.shape[3] - span :]
            face_value = value_rows[:, :, :, value_rows.shape[3] - span :]
        else:
            face_key = key_rows[:, :, :, :span]
            face_value = value_rows[:, :, :, :span]
        got = col_move(face_key, face_value, offset)
        if offset > 0:
            left = got
        else:
            right = got
    key_full = jnp.concatenate([left[0], key_rows, right[0]], axis=3)
    value_full = jnp.concatenate([left[1], value_rows, right[1]], axis=3)
    return (key_full, value_full)


def windows_of(block, half_high, half_wide, win_high, win_wide, heads_here, head_dim):
    parts = []
    for band in (0, 1):
        for strip in (0, 1):
            parts.append(
                block[
                    :,
                    band * half_high : band * half_high + win_high,
                    strip * half_wide : strip * half_wide + win_wide,
                ]
            )
    stacked = jnp.stack(parts)
    return stacked.reshape(4, -1, heads_here, head_dim)


def any_grid(query, keys, values, out_weight, radius, block_mask):
    span = RMAX
    grid = math.isqrt(lax.axis_size("tile"))
    tile_at = lax.axis_index("tile")
    row_at = tile_at // grid
    col_at = tile_at % grid
    stretch_at = lax.axis_index("tm")
    frames, high, wide, channels = query.shape[2:]
    heads_here = radius.shape[0]
    head_dim = channels // heads_here
    tokens_here = frames * high * wide
    half_high = high // 2
    half_wide = wide // 2
    win_high = half_high + 2 * span
    win_wide = half_wide + 2 * span
    quarter = frames * half_high * half_wide
    queries = query[0, 0].reshape(frames, 2, half_high, 2, half_wide, channels)
    queries = queries.transpose(1, 3, 0, 2, 4, 5).reshape(4, quarter, heads_here, head_dim)
    query_y = jnp.broadcast_to(
        jnp.arange(half_high, dtype=jnp.int32)[None, :, None], (frames, half_high, half_wide)
    ).reshape(-1)
    query_x = jnp.broadcast_to(
        jnp.arange(half_wide, dtype=jnp.int32)[None, None, :], (frames, half_high, half_wide)
    ).reshape(-1)
    key_y = jnp.broadcast_to(
        jnp.arange(win_high, dtype=jnp.int32)[None, :, None] - span, (frames, win_high, win_wide)
    ).reshape(-1)
    key_x = jnp.broadcast_to(
        jnp.arange(win_wide, dtype=jnp.int32)[None, None, :] - span, (frames, win_high, win_wide)
    ).reshape(-1)
    band_at = jnp.array([0, 0, 1, 1], dtype=jnp.int32)
    strip_at = jnp.array([0, 1, 0, 1], dtype=jnp.int32)
    global_y = row_at * high + band_at[:, None] * half_high + key_y[None, :]
    global_x = col_at * wide + strip_at[:, None] * half_wide + key_x[None, :]
    inside = (global_y >= 0) & (global_y < grid * high) & (global_x >= 0) & (global_x < grid * wide)
    distance = jnp.maximum(
        jnp.abs(query_y[:, None] - key_y[None, :]), jnp.abs(query_x[:, None] - key_x[None, :])
    )
    near = distance[None, :, :] <= radius[:, None, None]
    allowed = near[None, :, :, :] & inside[:, None, None, :]
    scale = 1.0 / math.sqrt(head_dim)
    initial = (
        jnp.full((4, heads_here, quarter), -1e30, jnp.float32),
        jnp.zeros((4, heads_here, quarter), jnp.float32),
        jnp.zeros((4, heads_here, quarter, head_dim), jnp.float32),
    )

    def tile_move(face_key, face_value, offset):
        return passed_along((face_key, face_value), "tile", offset)

    key_all, value_all = (
        lax.all_gather(keys[0], "tm", axis=0, tiled=True),
        lax.all_gather(values[0], "tm", axis=0, tiled=True),
    )
    key_full, value_full = widen(key_all, value_all, span, tile_move, tile_move)
    stretch_ids = jnp.arange(key_full.shape[0], dtype=jnp.int32)

    def one_stretch(state, item):
        key_block, value_block, stretch_id = item
        visible = (
            lax.dynamic_slice_in_dim(
                lax.dynamic_index_in_dim(block_mask, stretch_at, 1, False), stretch_id, 1, 1
            )[:, 0]
            > 0
        )
        best, total, acc = state
        key_win = windows_of(
            key_block, half_high, half_wide, win_high, win_wide, heads_here, head_dim
        )
        value_win = windows_of(
            value_block, half_high, half_wide, win_high, win_wide, heads_here, head_dim
        )
        usable = allowed & visible[None, :, None, None]
        scores = (
            jnp.einsum("nqhd,nkhd->nhqk", queries, key_win, preferred_element_type=jnp.float32)
            * scale
        )
        masked = jnp.where(usable, scores, jnp.float32(-1e30))
        fresh = jnp.maximum(best, jnp.max(masked, axis=3))
        probs = jnp.where(usable, jnp.exp(scores - fresh[..., None]), jnp.float32(0.0))
        shrink = jnp.exp(best - fresh)
        total = total * shrink + jnp.sum(probs, axis=3)
        acc = acc * shrink[..., None] + jnp.einsum(
            "nhqk,nkhd->nhqd",
            probs.astype(jnp.bfloat16),
            value_win,
            preferred_element_type=jnp.float32,
        )
        return ((fresh, total, acc), None)

    final, unused = lax.scan(one_stretch, initial, (key_full, value_full, stretch_ids))
    best, total, acc = final
    attn = (acc / total[..., None]).astype(jnp.bfloat16)
    attn = attn.transpose(0, 2, 1, 3).reshape(
        2, 2, frames, half_high, half_wide, heads_here * head_dim
    )
    attn = attn.transpose(2, 0, 3, 1, 4, 5).reshape(tokens_here, heads_here * head_dim)
    mixed = lax.psum_scatter(
        jnp.dot(attn, out_weight, preferred_element_type=jnp.float32).astype(jnp.bfloat16),
        "head",
        scatter_dimension=0,
        tiled=True,
    )
    return mixed.reshape(1, 1, -1, out_weight.shape[1])


def tile_place():
    tile_at = lax.axis_index("tile")
    return tile_at // 2, tile_at % 2


def face_kernel(
    k_ref, v_ref, w_ref, row_ref, col_ref, corner_ref, tile_ref, part_ref, sems, *, geometry
):
    high, wide, span, frames = geometry[:4]
    cells = high * wide
    row_at, col_at = tile_place()
    y0 = jnp.where(row_at == 0, high - span, 0)
    x0 = jnp.where(col_at == 0, wide - span, 0)
    tall, broad = part_ref.shape
    top = pl.multiple_of(lax.axis_index("tile") * tall, 16)
    edge = pl.multiple_of(lax.axis_index("tm") * broad, 128)
    copies = [
        pltpu.make_async_copy(ref, tile_ref.at[which], sems.at[which])
        for which, ref in enumerate((k_ref, v_ref))
    ]
    copies.append(
        pltpu.make_async_copy(
            w_ref.at[pl.ds(top, tall), pl.ds(edge, broad)], part_ref, sems.at[2]
        )
    )
    for copy in copies:
        copy.start()

    def picker(count, cell_of):
        row = lax.broadcasted_iota(jnp.int32, (count, cells), 0)
        col = lax.broadcasted_iota(jnp.int32, (count, cells), 1)
        return (col == cell_of(row)).astype(jnp.bfloat16)

    beside = picker(high * span, lambda i: (i // span) * wide + x0 + i % span)
    across = picker(span * span, lambda i: (y0 + i // span) * wide + x0 + i % span)
    for which in range(2):
        copies[which].wait()
        for f in range(frames):
            start = pl.multiple_of(f * cells + y0 * wide, 16)
            row_ref[which, f] = tile_ref[which, pl.ds(start, span * wide)]
            whole = tile_ref[which, f * cells : (f + 1) * cells]
            col_ref[which, f] = jnp.dot(
                beside, whole, preferred_element_type=jnp.float32
            ).astype(jnp.bfloat16)
            corner_ref[which, f] = jnp.dot(
                across, whole, preferred_element_type=jnp.float32
            ).astype(jnp.bfloat16)
    copies[2].wait()


def edge_kernel(row_ref, col_ref, corner_ref, out_ref):
    for which in range(2):
        at = 0
        for part in (row_ref, col_ref, corner_ref):
            for f in range(part.shape[1]):
                size = part.shape[2]
                out_ref[which, at : at + size] = part[which, f]
                at += size


def distances(high, wide, span, frames):
    row_at, col_at = tile_place()
    cells = high * wide
    count = frames * (cells + span * (wide + high + span))
    j = lax.broadcasted_iota(jnp.int32, (1, count), 1)
    y_off = jnp.where(row_at == 0, high, -span)
    x_off = jnp.where(col_at == 0, wide, -span)
    c = j % cells
    ky, kx = c // wide, c % wide
    base = frames * cells
    c = (j - base) % (span * wide)
    ky = jnp.where(j >= base, y_off + c // wide, ky)
    kx = jnp.where(j >= base, c % wide, kx)
    base += frames * span * wide
    c = (j - base) % (span * high)
    ky = jnp.where(j >= base, c // span, ky)
    kx = jnp.where(j >= base, x_off + c % span, kx)
    base += frames * span * high
    c = (j - base) % (span * span)
    ky = jnp.where(j >= base, y_off + c // span, ky)
    kx = jnp.where(j >= base, x_off + c % span, kx)
    i = lax.broadcasted_iota(jnp.int32, (cells, 1), 0)
    return jnp.maximum(jnp.abs(i // wide - ky), jnp.abs(i % wide - kx))


def attend(q, pieces, factor, before):
    scores = []
    m = before
    for k, v, dist, reach in pieces:
        s = lax.dot_general(q, k, (((1,), (1,)), ((), ())), preferred_element_type=jnp.float32)
        s = jnp.where(dist <= reach, s * factor, FAR)
        top = jnp.max(s, axis=1, keepdims=True)
        m = top if m is None else jnp.maximum(m, top)
        scores.append(s)
    total = None
    for s, (k, v, dist, reach) in zip(scores, pieces):
        p = jnp.exp2(s - m).astype(jnp.bfloat16)
        both = jnp.concatenate([v, jnp.ones_like(v)], axis=1)
        got = jnp.dot(p, both, preferred_element_type=jnp.float32)
        total = got if total is None else total + got
    return m, total


def attend_tile(q_ref, tile_ref, dist_ref, reach_of, heads, state, geometry):
    high, wide, span, frames, head_dim, factor, step = geometry
    cells = high * wide
    acc_ref, sum_ref, max_ref = state
    for at, head in enumerate(heads):
        cols = slice(head * head_dim, (head + 1) * head_dim)
        outs = slice(at * head_dim, (at + 1) * head_dim)
        for start in range(0, q_ref.shape[0], step):
            rows = slice(start, start + step)
            near = dist_ref[start % cells : start % cells + step, : tile_ref.shape[1]]
            piece = (tile_ref[0, :, cols], tile_ref[1, :, cols], near, reach_of(head))
            m, got = attend(q_ref[rows, cols], [piece], factor, None)
            acc_ref[rows, outs] = got[:, :head_dim]
            sum_ref[rows, outs] = got[:, head_dim:]
            max_ref[rows, outs] = jnp.broadcast_to(m, (step, head_dim))


def begin_kernel(radius_ref, mask_ref, q_ref, tile_ref, *outs, geometry, heads):
    *state, dist_ref, reach_ref = outs
    high, wide, span, frames = geometry[:4]
    dist_ref[...] = distances(high, wide, span, frames)
    stretch_at = lax.axis_index("tm")
    line = (1, reach_ref.shape[1])
    for head in range(heads):
        radius = radius_ref[head]
        seen = mask_ref[stretch_at, 0, head] > 0
        reach_ref[head : head + 1] = jnp.full(line, radius, jnp.int32)
        reach_ref[heads + head : heads + head + 1] = jnp.full(
            line, jnp.where(seen, radius, -1), jnp.int32
        )
    attend_tile(q_ref, tile_ref, dist_ref, lambda h: radius_ref[h], (0,), state, geometry)


def tile_kernel(q_ref, tile_ref, dist_ref, reach_ref, *state, geometry, heads):
    attend_tile(
        q_ref,
        tile_ref,
        dist_ref,
        lambda h: reach_ref[h : h + 1, :1],
        range(1, heads),
        state,
        geometry,
    )


def pick_state(head_state, state, head, rows, head_dim):
    refs = head_state if head == 0 else state
    at = max(head - 1, 0) * head_dim
    return [ref[rows, at : at + head_dim] for ref in refs]


def merge(q, pieces, factor, old):
    old_acc, old_total, old_max = old
    m, got = attend(q, pieces, factor, old_max[:, :1])
    shrink = jnp.exp2(old_max - m)
    head_dim = old_acc.shape[1]
    acc = old_acc * shrink + got[:, :head_dim]
    total = old_total * shrink + got[:, head_dim:]
    return acc, total, jnp.broadcast_to(m, old_max.shape)


def rest_kernel(
    q_ref,
    edge_ref,
    first_tile_ref,
    first_edge_ref,
    *rest,
    geometry,
    heads,
    flips,
):
    head_state, dist_ref, reach_ref, state, outs = rest[:3], rest[3], rest[4], rest[5:8], rest[8:]
    high, wide, span, frames, head_dim, factor, step = geometry
    cells = high * wide
    base = frames * cells
    head_at = lax.axis_index("head")
    stretch_at = lax.axis_index("tm")

    def run(with_first):
        for flip, out_ref in zip(flips, outs):
            start = pl.multiple_of(jnp.bitwise_xor(head_at, flip) * step, step)
            rows = pl.ds(start, step)
            near = dist_ref[pl.ds(pl.multiple_of(lax.rem(start, cells), step), step)]
            beyond = near[:, base:]
            for head in range(heads):
                cols = slice(head * head_dim, (head + 1) * head_dim)
                sources = [(edge_ref, beyond, head)]
                if with_first:
                    sources.append((first_tile_ref, near[:, :base], heads + head))
                    sources.append((first_edge_ref, beyond, heads + head))
                pieces = [
                    (ref[0, :, cols], ref[1, :, cols], dist, reach_ref[row : row + 1, :1])
                    for ref, dist, row in sources
                ]
                old = pick_state(head_state, state, head, rows, head_dim)
                acc, total, m = merge(q_ref[rows, cols], pieces, factor, old)
                out_ref[:, cols] = (acc / total).astype(jnp.bfloat16)

    @pl.when(stretch_at > 0)
    def _():
        run(True)

    @pl.when(stretch_at == 0)
    def _():
        run(False)


def copy_kernel(in_ref, out_ref):
    out_ref[...] = in_ref[...]


def stack_kernel(*refs):
    *parts, out_ref = refs
    tile_at = lax.axis_index("tile")
    for flip, part in enumerate(parts):
        tall = part.shape[0]
        top = pl.multiple_of(jnp.bitwise_xor(tile_at, flip) * tall, 16)
        out_ref[pl.ds(top, tall)] = part[...]


def project_kernel(w_ref, part_ref, own_ref, got_ref, out_ref, *, flip):
    broad = part_ref.shape[1]
    half = jnp.bitwise_xor(lax.axis_index("tm"), flip)
    cols = pl.ds(pl.multiple_of(half * broad, 128), broad)
    total = jnp.dot(own_ref[...], w_ref[:, cols], preferred_element_type=jnp.float32)
    total += jnp.dot(got_ref[...], part_ref[...], preferred_element_type=jnp.float32)
    out_ref[...] = total.astype(out_ref.dtype)


def add_kernel(*refs):
    *halves, out_ref, sum_ref, sems = refs
    pieces, tall, broad = sum_ref.shape
    copies = []
    for i in range(pieces):
        flip, row = divmod(i, pieces // 2)
        mine_ref, got_ref = halves[flip], halves[2 + flip]
        rows = slice(row * tall, (row + 1) * tall)
        sum_ref[i] = (mine_ref[rows] + got_ref[rows].astype(jnp.float32)).astype(jnp.bfloat16)
        half = jnp.bitwise_xor(lax.axis_index("tm"), flip)
        cols = pl.ds(pl.multiple_of(half * broad, 128), broad)
        copies.append(pltpu.make_async_copy(sum_ref.at[i], out_ref.at[rows, cols], sems.at[i]))
        copies[-1].start()
    for copy in copies:
        copy.wait()


def two_by_two(query, keys, values, out_weight, radius, block_mask):
    span = RMAX
    frames, high, wide, channels = query.shape[2:]
    heads = radius.shape[0]
    head_dim = channels // heads
    cells = high * wide
    tokens = frames * cells
    groups = lax.axis_size("head")
    tiles = lax.axis_size("tile")
    depth, width = out_weight.shape
    step = tokens // groups
    geometry = (high, wide, span, frames, head_dim, LOG2E / math.sqrt(head_dim), step)
    count = frames * (cells + span * (wide + high + span))
    smem = pl.BlockSpec(memory_space=pltpu.SMEM)
    vmem = pl.BlockSpec(memory_space=pltpu.VMEM)
    hbm = pl.BlockSpec(memory_space=pltpu.HBM)
    bf16, f32 = jnp.bfloat16, jnp.float32
    shape = jax.ShapeDtypeStruct

    def call(kernel, out_shape, specs, *args, name, scratch=(), flops=0, **keys_of):
        return pl.pallas_call(
            functools.partial(kernel, **keys_of) if keys_of else kernel,
            out_shape=out_shape,
            in_specs=specs,
            out_specs=jax.tree.map(lambda _: vmem, out_shape),
            scratch_shapes=scratch,
            cost_estimate=pl.CostEstimate(flops=flops, bytes_accessed=0, transcendentals=0),
            compiler_params=pltpu.CompilerParams(vmem_limit_bytes=VMEM_LIMIT),
            name=name,
        )(*args)

    def flipped(value, axis, flip):
        return lax.ppermute(value, axis, [(i, i ^ flip) for i in range(lax.axis_size(axis))])

    q = query.reshape(tokens, channels)
    k = keys.reshape(tokens, channels)
    v = values.reshape(tokens, channels)

    tall, broad = depth // tiles, width // 2
    part_shape = shape((tall, broad), bf16)
    *faces, tile, part = call(
        face_kernel,
        [
            shape((2, frames, span * wide, channels), bf16),
            shape((2, frames, span * high, channels), bf16),
            shape((2, frames, span * span, channels), bf16),
            shape((2, tokens, channels), bf16),
            part_shape,
        ],
        [hbm] * 3,
        *[pltpu.with_memory_space_constraint(x, pltpu.HBM) for x in (k, v, out_weight)],
        name="faces",
        scratch=[pltpu.SemaphoreType.DMA((3,))],
        geometry=geometry,
    )
    faces = [flipped(face, "tile", flip) for face, flip in zip(faces, (2, 1, 3))]
    lone = flipped(part, "head", 2)
    begun = call(
        begin_kernel,
        [shape((tokens, head_dim), f32)] * 3
        + [shape((cells, count), jnp.int32), shape((2 * heads, head_dim), jnp.int32)],
        [smem] * 2 + [vmem] * 2,
        radius,
        block_mask.transpose(1, 2, 0),
        q,
        tile,
        name="begin",
        geometry=geometry,
        heads=heads,
    )
    begun, tile = lax.optimization_barrier((begun, tile))
    first_tile = lax.ppermute(tile, "tm", [(0, 1)])
    state = call(
        tile_kernel,
        [shape((tokens, channels - head_dim), f32)] * 3,
        [vmem] * 4,
        q,
        tile,
        *begun[3:],
        name="tile",
        geometry=geometry,
        heads=heads,
    )
    lone, state = lax.optimization_barrier((lone, state))
    lone = call(copy_kernel, part_shape, [vmem], lone, name="lone", flops=20 * 10**9)
    lone, state, faces = lax.optimization_barrier((lone, state, faces))
    edge = call(
        edge_kernel, shape((2, count - tokens, channels), bf16), [vmem] * 3, *faces, name="edges"
    )
    first_edge = lax.ppermute(edge, "tm", [(0, 1)])
    parts = [lone] + [flipped(lone, "tile", flip) for flip in range(1, tiles)]

    def rest(state, *flips):
        return call(
            rest_kernel,
            [shape((step, channels), bf16)] * len(flips),
            [vmem] * 12,
            q,
            edge,
            first_tile,
            first_edge,
            *begun,
            *state,
            name="rest",
            geometry=geometry,
            heads=heads,
            flips=flips,
        )

    (for_side,) = rest(state, 3)
    got_side = flipped(for_side, "head", 2)
    state, for_side = lax.optimization_barrier((state, for_side))
    for_far, own_side = rest(state, 2, 1)
    got_far = flipped(for_far, "head", 2)
    parts, own_side = lax.optimization_barrier((parts, own_side))
    here = call(
        stack_kernel, shape((depth, broad), bf16), [vmem] * tiles, *parts, name="stack"
    )
    there = flipped(here, "tm", 1)

    def project(mine, got, kind, flip, flops=0):
        return call(
            project_kernel,
            shape((step, broad), kind),
            [vmem] * 4,
            out_weight,
            there if flip else here,
            mine,
            got,
            name="project",
            flops=flops,
            flip=flip,
        )

    for_side = [project(own_side, got_side, bf16, 0, 20 * 10**9)]
    from_side = [flipped(for_side[0], "head", 1)]
    for_side.append(project(own_side, got_side, bf16, 1))
    from_side.append(flipped(for_side[1], "head", 1))
    state, for_side = lax.optimization_barrier((state, for_side))
    (own,) = rest(state, 0)
    mine = [project(own, got_far, f32, 0), project(own, got_far, f32, 1, 20 * 10**9)]
    pieces = 4
    mixed = pl.pallas_call(
        add_kernel,
        out_shape=shape((step, width), bf16),
        in_specs=[vmem] * 4,
        out_specs=hbm,
        scratch_shapes=[
            pltpu.VMEM((pieces, step * 2 // pieces, broad), bf16),
            pltpu.SemaphoreType.DMA((pieces,)),
        ],
        compiler_params=pltpu.CompilerParams(vmem_limit_bytes=VMEM_LIMIT),
        name="add",
    )(*mine, *from_side)
    return mixed.reshape(1, 1, step, width)


def solution(mesh):
    in_specs = (
        P("tm", "tile", None, None, None, "head"),
        P("tm", "tile", None, None, None, "head"),
        P("tm", "tile", None, None, None, "head"),
        P("head", None),
        P("head"),
        P("head", None, None),
    )
    out_specs = P("tm", "tile", "head", None)
    small = dict(mesh.shape) == {"tm": 2, "tile": 4, "head": 4}
    return jax.shard_map(
        two_by_two if small else any_grid,
        mesh=mesh,
        in_specs=in_specs,
        out_specs=out_specs,
        check_vma=False,
    )
```

```python
import functools
import math

import jax
import jax.numpy as jnp
from jax import lax
from jax.experimental import pallas as pl
from jax.experimental.pallas import tpu as pltpu
from jax.sharding import PartitionSpec as P

RMAX = 4
FAR = -1e30
LOG2E = 1.4426950408889634
VMEM_LIMIT = 24 * 1024 * 1024


def passed_along(value, axis, by):
    peers = lax.axis_size(axis)
    pairs = [(i, i + by) for i in range(peers) if 0 <= i + by < peers]
    return lax.ppermute(value, axis, pairs)


def widen(key_part, value_part, span, row_move, col_move):
    grid = math.isqrt(lax.axis_size("tile"))
    above = None
    below = None
    for offset in (grid, -grid):
        if offset > 0:
            face_key = key_part[:, :, key_part.shape[2] - span :]
            face_value = value_part[:, :, value_part.shape[2] - span :]
        else:
            face_key = key_part[:, :, :span]
            face_value = value_part[:, :, :span]
        got = row_move(face_key, face_value, offset)
        if offset > 0:
            above = got
        else:
            below = got
    key_rows = jnp.concatenate([above[0], key_part, below[0]], axis=2)
    value_rows = jnp.concatenate([above[1], value_part, below[1]], axis=2)
    left = None
    right = None
    for offset in (1, -1):
        if offset > 0:
            face_key = key_rows[:, :, :, key_rows.shape[3] - span :]
            face_value = value_rows[:, :, :, value_rows.shape[3] - span :]
        else:
            face_key = key_rows[:, :, :, :span]
            face_value = value_rows[:, :, :, :span]
        got = col_move(face_key, face_value, offset)
        if offset > 0:
            left = got
        else:
            right = got
    key_full = jnp.concatenate([left[0], key_rows, right[0]], axis=3)
    value_full = jnp.concatenate([left[1], value_rows, right[1]], axis=3)
    return (key_full, value_full)


def windows_of(block, half_high, half_wide, win_high, win_wide, heads_here, head_dim):
    parts = []
    for band in (0, 1):
        for strip in (0, 1):
            parts.append(
                block[
                    :,
                    band * half_high : band * half_high + win_high,
                    strip * half_wide : strip * half_wide + win_wide,
                ]
            )
    stacked = jnp.stack(parts)
    return stacked.reshape(4, -1, heads_here, head_dim)


def any_grid(query, keys, values, out_weight, radius, block_mask):
    span = RMAX
    grid = math.isqrt(lax.axis_size("tile"))
    tile_at = lax.axis_index("tile")
    row_at = tile_at // grid
    col_at = tile_at % grid
    stretch_at = lax.axis_index("tm")
    frames, high, wide, channels = query.shape[2:]
    heads_here = radius.shape[0]
    head_dim = channels // heads_here
    tokens_here = frames * high * wide
    half_high = high // 2
    half_wide = wide // 2
    win_high = half_high + 2 * span
    win_wide = half_wide + 2 * span
    quarter = frames * half_high * half_wide
    queries = query[0, 0].reshape(frames, 2, half_high, 2, half_wide, channels)
    queries = queries.transpose(1, 3, 0, 2, 4, 5).reshape(4, quarter, heads_here, head_dim)
    query_y = jnp.broadcast_to(
        jnp.arange(half_high, dtype=jnp.int32)[None, :, None], (frames, half_high, half_wide)
    ).reshape(-1)
    query_x = jnp.broadcast_to(
        jnp.arange(half_wide, dtype=jnp.int32)[None, None, :], (frames, half_high, half_wide)
    ).reshape(-1)
    key_y = jnp.broadcast_to(
        jnp.arange(win_high, dtype=jnp.int32)[None, :, None] - span, (frames, win_high, win_wide)
    ).reshape(-1)
    key_x = jnp.broadcast_to(
        jnp.arange(win_wide, dtype=jnp.int32)[None, None, :] - span, (frames, win_high, win_wide)
    ).reshape(-1)
    band_at = jnp.array([0, 0, 1, 1], dtype=jnp.int32)
    strip_at = jnp.array([0, 1, 0, 1], dtype=jnp.int32)
    global_y = row_at * high + band_at[:, None] * half_high + key_y[None, :]
    global_x = col_at * wide + strip_at[:, None] * half_wide + key_x[None, :]
    inside = (global_y >= 0) & (global_y < grid * high) & (global_x >= 0) & (global_x < grid * wide)
    distance = jnp.maximum(
        jnp.abs(query_y[:, None] - key_y[None, :]), jnp.abs(query_x[:, None] - key_x[None, :])
    )
    near = distance[None, :, :] <= radius[:, None, None]
    allowed = near[None, :, :, :] & inside[:, None, None, :]
    scale = 1.0 / math.sqrt(head_dim)
    initial = (
        jnp.full((4, heads_here, quarter), -1e30, jnp.float32),
        jnp.zeros((4, heads_here, quarter), jnp.float32),
        jnp.zeros((4, heads_here, quarter, head_dim), jnp.float32),
    )

    def tile_move(face_key, face_value, offset):
        return passed_along((face_key, face_value), "tile", offset)

    key_all, value_all = (
        lax.all_gather(keys[0], "tm", axis=0, tiled=True),
        lax.all_gather(values[0], "tm", axis=0, tiled=True),
    )
    key_full, value_full = widen(key_all, value_all, span, tile_move, tile_move)
    stretch_ids = jnp.arange(key_full.shape[0], dtype=jnp.int32)

    def one_stretch(state, item):
        key_block, value_block, stretch_id = item
        visible = (
            lax.dynamic_slice_in_dim(
                lax.dynamic_index_in_dim(block_mask, stretch_at, 1, False), stretch_id, 1, 1
            )[:, 0]
            > 0
        )
        best, total, acc = state
        key_win = windows_of(
            key_block, half_high, half_wide, win_high, win_wide, heads_here, head_dim
        )
        value_win = windows_of(
            value_block, half_high, half_wide, win_high, win_wide, heads_here, head_dim
        )
        usable = allowed & visible[None, :, None, None]
        scores = (
            jnp.einsum("nqhd,nkhd->nhqk", queries, key_win, preferred_element_type=jnp.float32)
            * scale
        )
        masked = jnp.where(usable, scores, jnp.float32(-1e30))
        fresh = jnp.maximum(best, jnp.max(masked, axis=3))
        probs = jnp.where(usable, jnp.exp(scores - fresh[..., None]), jnp.float32(0.0))
        shrink = jnp.exp(best - fresh)
        total = total * shrink + jnp.sum(probs, axis=3)
        acc = acc * shrink[..., None] + jnp.einsum(
            "nhqk,nkhd->nhqd",
            probs.astype(jnp.bfloat16),
            value_win,
            preferred_element_type=jnp.float32,
        )
        return ((fresh, total, acc), None)

    final, unused = lax.scan(one_stretch, initial, (key_full, value_full, stretch_ids))
    best, total, acc = final
    attn = (acc / total[..., None]).astype(jnp.bfloat16)
    attn = attn.transpose(0, 2, 1, 3).reshape(
        2, 2, frames, half_high, half_wide, heads_here * head_dim
    )
    attn = attn.transpose(2, 0, 3, 1, 4, 5).reshape(tokens_here, heads_here * head_dim)
    mixed = lax.psum_scatter(
        jnp.dot(attn, out_weight, preferred_element_type=jnp.float32).astype(jnp.bfloat16),
        "head",
        scatter_dimension=0,
        tiled=True,
    )
    return mixed.reshape(1, 1, -1, out_weight.shape[1])


def tile_place():
    tile_at = lax.axis_index("tile")
    return tile_at // 2, tile_at % 2


def face_kernel(
    k_ref, v_ref, w_ref, row_ref, col_ref, corner_ref, tile_ref, part_ref, sems, *, geometry
):
    high, wide, span, frames = geometry[:4]
    cells = high * wide
    row_at, col_at = tile_place()
    y0 = jnp.where(row_at == 0, high - span, 0)
    x0 = jnp.where(col_at == 0, wide - span, 0)
    tall, broad = part_ref.shape
    top = pl.multiple_of(lax.axis_index("tile") * tall, 16)
    edge = pl.multiple_of(lax.axis_index("tm") * broad, 128)
    copies = [
        pltpu.make_async_copy(ref, tile_ref.at[which], sems.at[which])
        for which, ref in enumerate((k_ref, v_ref))
    ]
    copies.append(
        pltpu.make_async_copy(
            w_ref.at[pl.ds(top, tall), pl.ds(edge, broad)], part_ref, sems.at[2]
        )
    )
    for copy in copies:
        copy.start()

    def picker(count, cell_of):
        row = lax.broadcasted_iota(jnp.int32, (count, cells), 0)
        col = lax.broadcasted_iota(jnp.int32, (count, cells), 1)
        return (col == cell_of(row)).astype(jnp.bfloat16)

    beside = picker(high * span, lambda i: (i // span) * wide + x0 + i % span)
    across = picker(span * span, lambda i: (y0 + i // span) * wide + x0 + i % span)
    for which in range(2):
        copies[which].wait()
        for f in range(frames):
            start = pl.multiple_of(f * cells + y0 * wide, 16)
            row_ref[which, f] = tile_ref[which, pl.ds(start, span * wide)]
            whole = tile_ref[which, f * cells : (f + 1) * cells]
            col_ref[which, f] = jnp.dot(
                beside, whole, preferred_element_type=jnp.float32
            ).astype(jnp.bfloat16)
            corner_ref[which, f] = jnp.dot(
                across, whole, preferred_element_type=jnp.float32
            ).astype(jnp.bfloat16)
    copies[2].wait()


def edge_kernel(row_ref, col_ref, corner_ref, out_ref):
    for which in range(2):
        at = 0
        for part in (row_ref, col_ref, corner_ref):
            for f in range(part.shape[1]):
                size = part.shape[2]
                out_ref[which, at : at + size] = part[which, f]
                at += size


def distances(high, wide, span, frames):
    row_at, col_at = tile_place()
    cells = high * wide
    count = frames * (cells + span * (wide + high + span))
    j = lax.broadcasted_iota(jnp.int32, (1, count), 1)
    y_off = jnp.where(row_at == 0, high, -span)
    x_off = jnp.where(col_at == 0, wide, -span)
    c = j % cells
    ky, kx = c // wide, c % wide
    base = frames * cells
    c = (j - base) % (span * wide)
    ky = jnp.where(j >= base, y_off + c // wide, ky)
    kx = jnp.where(j >= base, c % wide, kx)
    base += frames * span * wide
    c = (j - base) % (span * high)
    ky = jnp.where(j >= base, c // span, ky)
    kx = jnp.where(j >= base, x_off + c % span, kx)
    base += frames * span * high
    c = (j - base) % (span * span)
    ky = jnp.where(j >= base, y_off + c // span, ky)
    kx = jnp.where(j >= base, x_off + c % span, kx)
    i = lax.broadcasted_iota(jnp.int32, (cells, 1), 0)
    return jnp.maximum(jnp.abs(i // wide - ky), jnp.abs(i % wide - kx))


def attend(q, pieces, factor, before):
    scores = []
    m = before
    for k, v, dist, reach in pieces:
        s = lax.dot_general(q, k, (((1,), (1,)), ((), ())), preferred_element_type=jnp.float32)
        s = jnp.where(dist <= reach, s * factor, FAR)
        top = jnp.max(s, axis=1, keepdims=True)
        m = top if m is None else jnp.maximum(m, top)
        scores.append(s)
    total = None
    for s, (k, v, dist, reach) in zip(scores, pieces):
        p = jnp.exp2(s - m).astype(jnp.bfloat16)
        both = jnp.concatenate([v, jnp.ones_like(v)], axis=1)
        got = jnp.dot(p, both, preferred_element_type=jnp.float32)
        total = got if total is None else total + got
    return m, total


def attend_tile(q_ref, tile_ref, dist_ref, reach_of, heads, state, geometry):
    high, wide, span, frames, head_dim, factor, step = geometry
    cells = high * wide
    acc_ref, sum_ref, max_ref = state
    for at, head in enumerate(heads):
        cols = slice(head * head_dim, (head + 1) * head_dim)
        outs = slice(at * head_dim, (at + 1) * head_dim)
        for start in range(0, q_ref.shape[0], step):
            rows = slice(start, start + step)
            near = dist_ref[start % cells : start % cells + step, : tile_ref.shape[1]]
            piece = (tile_ref[0, :, cols], tile_ref[1, :, cols], near, reach_of(head))
            m, got = attend(q_ref[rows, cols], [piece], factor, None)
            acc_ref[rows, outs] = got[:, :head_dim]
            sum_ref[rows, outs] = got[:, head_dim:]
            max_ref[rows, outs] = jnp.broadcast_to(m, (step, head_dim))


def begin_kernel(radius_ref, mask_ref, q_ref, tile_ref, *outs, geometry, heads):
    *state, dist_ref, reach_ref = outs
    high, wide, span, frames = geometry[:4]
    dist_ref[...] = distances(high, wide, span, frames)
    stretch_at = lax.axis_index("tm")
    line = (1, reach_ref.shape[1])
    for head in range(heads):
        radius = radius_ref[head]
        seen = mask_ref[stretch_at, 0, head] > 0
        reach_ref[head : head + 1] = jnp.full(line, radius, jnp.int32)
        reach_ref[heads + head : heads + head + 1] = jnp.full(
            line, jnp.where(seen, radius, -1), jnp.int32
        )
    attend_tile(q_ref, tile_ref, dist_ref, lambda h: radius_ref[h], (0,), state, geometry)


def tile_kernel(q_ref, tile_ref, dist_ref, reach_ref, *state, geometry, heads):
    attend_tile(
        q_ref,
        tile_ref,
        dist_ref,
        lambda h: reach_ref[h : h + 1, :1],
        range(1, heads),
        state,
        geometry,
    )


def pick_state(head_state, state, head, rows, head_dim):
    refs = head_state if head == 0 else state
    at = max(head - 1, 0) * head_dim
    return [ref[rows, at : at + head_dim] for ref in refs]


def merge(q, pieces, factor, old):
    old_acc, old_total, old_max = old
    m, got = attend(q, pieces, factor, old_max[:, :1])
    shrink = jnp.exp2(old_max - m)
    head_dim = old_acc.shape[1]
    acc = old_acc * shrink + got[:, :head_dim]
    total = old_total * shrink + got[:, head_dim:]
    return acc, total, jnp.broadcast_to(m, old_max.shape)


def rest_kernel(
    q_ref,
    edge_ref,
    first_tile_ref,
    first_edge_ref,
    *rest,
    geometry,
    heads,
    flips,
):
    head_state, dist_ref, reach_ref, state, outs = rest[:3], rest[3], rest[4], rest[5:8], rest[8:]
    high, wide, span, frames, head_dim, factor, step = geometry
    cells = high * wide
    base = frames * cells
    head_at = lax.axis_index("head")
    stretch_at = lax.axis_index("tm")

    def run(with_first):
        for flip, out_ref in zip(flips, outs):
            start = pl.multiple_of(jnp.bitwise_xor(head_at, flip) * step, step)
            rows = pl.ds(start, step)
            near = dist_ref[pl.ds(pl.multiple_of(lax.rem(start, cells), step), step)]
            beyond = near[:, base:]
            for head in range(heads):
                cols = slice(head * head_dim, (head + 1) * head_dim)
                sources = [(edge_ref, beyond, head)]
                if with_first:
                    sources.append((first_tile_ref, near[:, :base], heads + head))
                    sources.append((first_edge_ref, beyond, heads + head))
                pieces = [
                    (ref[0, :, cols], ref[1, :, cols], dist, reach_ref[row : row + 1, :1])
                    for ref, dist, row in sources
                ]
                old = pick_state(head_state, state, head, rows, head_dim)
                acc, total, m = merge(q_ref[rows, cols], pieces, factor, old)
                out_ref[:, cols] = (acc / total).astype(jnp.bfloat16)

    @pl.when(stretch_at > 0)
    def _():
        run(True)

    @pl.when(stretch_at == 0)
    def _():
        run(False)


def copy_kernel(in_ref, out_ref):
    out_ref[...] = in_ref[...]


def stack_kernel(*refs):
    *parts, out_ref = refs
    tile_at = lax.axis_index("tile")
    for flip, part in enumerate(parts):
        tall = part.shape[0]
        top = pl.multiple_of(jnp.bitwise_xor(tile_at, flip) * tall, 16)
        out_ref[pl.ds(top, tall)] = part[...]


def project_kernel(w_ref, part_ref, own_ref, got_ref, out_ref, *, flip):
    broad = part_ref.shape[1]
    half = jnp.bitwise_xor(lax.axis_index("tm"), flip)
    cols = pl.ds(pl.multiple_of(half * broad, 128), broad)
    total = jnp.dot(own_ref[...], w_ref[:, cols], preferred_element_type=jnp.float32)
    total += jnp.dot(got_ref[...], part_ref[...], preferred_element_type=jnp.float32)
    out_ref[...] = total.astype(out_ref.dtype)


def add_kernel(mine_ref, got_ref, *rest, flip):
    out_ref, sum_ref, sems = rest[-3:]
    pieces, tall, broad = sum_ref.shape
    half = jnp.bitwise_xor(lax.axis_index("tm"), flip)
    cols = pl.ds(pl.multiple_of(half * broad, 128), broad)
    copies = []
    for i in range(pieces):
        rows = slice(i * tall, (i + 1) * tall)
        sum_ref[i] = (mine_ref[rows] + got_ref[rows].astype(jnp.float32)).astype(jnp.bfloat16)
        copies.append(pltpu.make_async_copy(sum_ref.at[i], out_ref.at[rows, cols], sems.at[i]))
        copies[-1].start()
    for copy in copies:
        copy.wait()


def two_by_two(query, keys, values, out_weight, radius, block_mask):
    span = RMAX
    frames, high, wide, channels = query.shape[2:]
    heads = radius.shape[0]
    head_dim = channels // heads
    cells = high * wide
    tokens = frames * cells
    groups = lax.axis_size("head")
    tiles = lax.axis_size("tile")
    depth, width = out_weight.shape
    step = tokens // groups
    geometry = (high, wide, span, frames, head_dim, LOG2E / math.sqrt(head_dim), step)
    count = frames * (cells + span * (wide + high + span))
    smem = pl.BlockSpec(memory_space=pltpu.SMEM)
    vmem = pl.BlockSpec(memory_space=pltpu.VMEM)
    hbm = pl.BlockSpec(memory_space=pltpu.HBM)
    bf16, f32 = jnp.bfloat16, jnp.float32
    shape = jax.ShapeDtypeStruct

    def call(kernel, out_shape, specs, *args, name, scratch=(), flops=0, **keys_of):
        return pl.pallas_call(
            functools.partial(kernel, **keys_of) if keys_of else kernel,
            out_shape=out_shape,
            in_specs=specs,
            out_specs=jax.tree.map(lambda _: vmem, out_shape),
            scratch_shapes=scratch,
            cost_estimate=pl.CostEstimate(flops=flops, bytes_accessed=0, transcendentals=0),
            compiler_params=pltpu.CompilerParams(vmem_limit_bytes=VMEM_LIMIT),
            name=name,
        )(*args)

    def flipped(value, axis, flip):
        return lax.ppermute(value, axis, [(i, i ^ flip) for i in range(lax.axis_size(axis))])

    q = query.reshape(tokens, channels)
    k = keys.reshape(tokens, channels)
    v = values.reshape(tokens, channels)

    tall, broad = depth // tiles, width // 2
    part_shape = shape((tall, broad), bf16)
    *faces, tile, part = call(
        face_kernel,
        [
            shape((2, frames, span * wide, channels), bf16),
            shape((2, frames, span * high, channels), bf16),
            shape((2, frames, span * span, channels), bf16),
            shape((2, tokens, channels), bf16),
            part_shape,
        ],
        [hbm] * 3,
        *[pltpu.with_memory_space_constraint(x, pltpu.HBM) for x in (k, v, out_weight)],
        name="faces",
        scratch=[pltpu.SemaphoreType.DMA((3,))],
        geometry=geometry,
    )
    faces = [flipped(face, "tile", flip) for face, flip in zip(faces, (2, 1, 3))]
    lone = flipped(part, "head", 2)
    begun = call(
        begin_kernel,
        [shape((tokens, head_dim), f32)] * 3
        + [shape((cells, count), jnp.int32), shape((2 * heads, head_dim), jnp.int32)],
        [smem] * 2 + [vmem] * 2,
        radius,
        block_mask.transpose(1, 2, 0),
        q,
        tile,
        name="begin",
        geometry=geometry,
        heads=heads,
    )
    begun, tile = lax.optimization_barrier((begun, tile))
    first_tile = lax.ppermute(tile, "tm", [(0, 1)])
    state = call(
        tile_kernel,
        [shape((tokens, channels - head_dim), f32)] * 3,
        [vmem] * 4,
        q,
        tile,
        *begun[3:],
        name="tile",
        geometry=geometry,
        heads=heads,
    )
    lone, state = lax.optimization_barrier((lone, state))
    lone = call(copy_kernel, part_shape, [vmem], lone, name="lone", flops=20 * 10**9)
    lone, state, faces = lax.optimization_barrier((lone, state, faces))
    edge = call(
        edge_kernel, shape((2, count - tokens, channels), bf16), [vmem] * 3, *faces, name="edges"
    )
    first_edge = lax.ppermute(edge, "tm", [(0, 1)])
    parts = [lone] + [flipped(lone, "tile", flip) for flip in range(1, tiles)]

    def rest(state, *flips, flops=0):
        return call(
            rest_kernel,
            [shape((step, channels), bf16)] * len(flips),
            [vmem] * 12,
            q,
            edge,
            first_tile,
            first_edge,
            *begun,
            *state,
            name="rest",
            geometry=geometry,
            heads=heads,
            flips=flips,
            flops=flops,
        )

    (for_side,) = rest(state, 3)
    got_side = flipped(for_side, "head", 2)
    state, for_side = lax.optimization_barrier((state, for_side))
    for_far, own_side = rest(state, 2, 1)
    got_far = flipped(for_far, "head", 2)
    parts, own_side = lax.optimization_barrier((parts, own_side))
    here = call(
        stack_kernel, shape((depth, broad), bf16), [vmem] * tiles, *parts, name="stack"
    )

    def project(part, mine, got, kind, flip, flops=0):
        return call(
            project_kernel,
            shape((step, broad), kind),
            [vmem] * 4,
            out_weight,
            part,
            mine,
            got,
            name="project",
            flops=flops,
            flip=flip,
        )

    for_side = [project(here, own_side, got_side, bf16, 0, 20 * 10**9)]
    from_side = [flipped(for_side[0], "head", 1)]
    state, here, for_side[0] = lax.optimization_barrier((state, here, for_side[0]))
    there = flipped(here, "tm", 1)
    (own,) = rest(state, 0, flops=20 * 10**9)
    own_side, own = lax.optimization_barrier((own_side, own))
    for_side.append(project(there, own_side, got_side, bf16, 1))
    from_side.append(flipped(for_side[1], "head", 1))
    own, for_side[1] = lax.optimization_barrier((own, for_side[1]))
    mine = [
        project(here, own, got_far, f32, 0),
        project(there, own, got_far, f32, 1, 20 * 10**9),
    ]
    pieces = 2
    mixed = []
    for flip in range(2):
        mixed = [
            pl.pallas_call(
                functools.partial(add_kernel, flip=flip),
                out_shape=shape((step, width), bf16),
                in_specs=[vmem] * 2 + [hbm] * flip,
                out_specs=hbm,
                input_output_aliases={2: 0} if flip else {},
                scratch_shapes=[
                    pltpu.VMEM((pieces, step // pieces, broad), bf16),
                    pltpu.SemaphoreType.DMA((pieces,)),
                ],
                compiler_params=pltpu.CompilerParams(vmem_limit_bytes=VMEM_LIMIT),
                name="add",
            )(mine[flip], from_side[flip], *mixed)
        ]
    (mixed,) = mixed
    return mixed.reshape(1, 1, step, width)


def solution(mesh):
    in_specs = (
        P("tm", "tile", None, None, None, "head"),
        P("tm", "tile", None, None, None, "head"),
        P("tm", "tile", None, None, None, "head"),
        P("head", None),
        P("head"),
        P("head", None, None),
    )
    out_specs = P("tm", "tile", "head", None)
    small = dict(mesh.shape) == {"tm": 2, "tile": 4, "head": 4}
    return jax.shard_map(
        two_by_two if small else any_grid,
        mesh=mesh,
        in_specs=in_specs,
        out_specs=out_specs,
        check_vma=False,
    )
```

```python
import functools
import math

import jax
import jax.numpy as jnp
from jax import lax
from jax.experimental import pallas as pl
from jax.experimental.pallas import tpu as pltpu
from jax.sharding import PartitionSpec as P

RMAX = 4
FAR = -1e30
LOG2E = 1.4426950408889634
VMEM_LIMIT = 24 * 1024 * 1024


def passed_along(value, axis, by):
    peers = lax.axis_size(axis)
    pairs = [(i, i + by) for i in range(peers) if 0 <= i + by < peers]
    return lax.ppermute(value, axis, pairs)


def widen(key_part, value_part, span, row_move, col_move):
    grid = math.isqrt(lax.axis_size("tile"))
    above = None
    below = None
    for offset in (grid, -grid):
        if offset > 0:
            face_key = key_part[:, :, key_part.shape[2] - span :]
            face_value = value_part[:, :, value_part.shape[2] - span :]
        else:
            face_key = key_part[:, :, :span]
            face_value = value_part[:, :, :span]
        got = row_move(face_key, face_value, offset)
        if offset > 0:
            above = got
        else:
            below = got
    key_rows = jnp.concatenate([above[0], key_part, below[0]], axis=2)
    value_rows = jnp.concatenate([above[1], value_part, below[1]], axis=2)
    left = None
    right = None
    for offset in (1, -1):
        if offset > 0:
            face_key = key_rows[:, :, :, key_rows.shape[3] - span :]
            face_value = value_rows[:, :, :, value_rows.shape[3] - span :]
        else:
            face_key = key_rows[:, :, :, :span]
            face_value = value_rows[:, :, :, :span]
        got = col_move(face_key, face_value, offset)
        if offset > 0:
            left = got
        else:
            right = got
    key_full = jnp.concatenate([left[0], key_rows, right[0]], axis=3)
    value_full = jnp.concatenate([left[1], value_rows, right[1]], axis=3)
    return (key_full, value_full)


def windows_of(block, half_high, half_wide, win_high, win_wide, heads_here, head_dim):
    parts = []
    for band in (0, 1):
        for strip in (0, 1):
            parts.append(
                block[
                    :,
                    band * half_high : band * half_high + win_high,
                    strip * half_wide : strip * half_wide + win_wide,
                ]
            )
    stacked = jnp.stack(parts)
    return stacked.reshape(4, -1, heads_here, head_dim)


def any_grid(query, keys, values, out_weight, radius, block_mask):
    span = RMAX
    grid = math.isqrt(lax.axis_size("tile"))
    tile_at = lax.axis_index("tile")
    row_at = tile_at // grid
    col_at = tile_at % grid
    stretch_at = lax.axis_index("tm")
    frames, high, wide, channels = query.shape[2:]
    heads_here = radius.shape[0]
    head_dim = channels // heads_here
    tokens_here = frames * high * wide
    half_high = high // 2
    half_wide = wide // 2
    win_high = half_high + 2 * span
    win_wide = half_wide + 2 * span
    quarter = frames * half_high * half_wide
    queries = query[0, 0].reshape(frames, 2, half_high, 2, half_wide, channels)
    queries = queries.transpose(1, 3, 0, 2, 4, 5).reshape(4, quarter, heads_here, head_dim)
    query_y = jnp.broadcast_to(
        jnp.arange(half_high, dtype=jnp.int32)[None, :, None], (frames, half_high, half_wide)
    ).reshape(-1)
    query_x = jnp.broadcast_to(
        jnp.arange(half_wide, dtype=jnp.int32)[None, None, :], (frames, half_high, half_wide)
    ).reshape(-1)
    key_y = jnp.broadcast_to(
        jnp.arange(win_high, dtype=jnp.int32)[None, :, None] - span, (frames, win_high, win_wide)
    ).reshape(-1)
    key_x = jnp.broadcast_to(
        jnp.arange(win_wide, dtype=jnp.int32)[None, None, :] - span, (frames, win_high, win_wide)
    ).reshape(-1)
    band_at = jnp.array([0, 0, 1, 1], dtype=jnp.int32)
    strip_at = jnp.array([0, 1, 0, 1], dtype=jnp.int32)
    global_y = row_at * high + band_at[:, None] * half_high + key_y[None, :]
    global_x = col_at * wide + strip_at[:, None] * half_wide + key_x[None, :]
    inside = (global_y >= 0) & (global_y < grid * high) & (global_x >= 0) & (global_x < grid * wide)
    distance = jnp.maximum(
        jnp.abs(query_y[:, None] - key_y[None, :]), jnp.abs(query_x[:, None] - key_x[None, :])
    )
    near = distance[None, :, :] <= radius[:, None, None]
    allowed = near[None, :, :, :] & inside[:, None, None, :]
    scale = 1.0 / math.sqrt(head_dim)
    initial = (
        jnp.full((4, heads_here, quarter), -1e30, jnp.float32),
        jnp.zeros((4, heads_here, quarter), jnp.float32),
        jnp.zeros((4, heads_here, quarter, head_dim), jnp.float32),
    )

    def tile_move(face_key, face_value, offset):
        return passed_along((face_key, face_value), "tile", offset)

    key_all, value_all = (
        lax.all_gather(keys[0], "tm", axis=0, tiled=True),
        lax.all_gather(values[0], "tm", axis=0, tiled=True),
    )
    key_full, value_full = widen(key_all, value_all, span, tile_move, tile_move)
    stretch_ids = jnp.arange(key_full.shape[0], dtype=jnp.int32)

    def one_stretch(state, item):
        key_block, value_block, stretch_id = item
        visible = (
            lax.dynamic_slice_in_dim(
                lax.dynamic_index_in_dim(block_mask, stretch_at, 1, False), stretch_id, 1, 1
            )[:, 0]
            > 0
        )
        best, total, acc = state
        key_win = windows_of(
            key_block, half_high, half_wide, win_high, win_wide, heads_here, head_dim
        )
        value_win = windows_of(
            value_block, half_high, half_wide, win_high, win_wide, heads_here, head_dim
        )
        usable = allowed & visible[None, :, None, None]
        scores = (
            jnp.einsum("nqhd,nkhd->nhqk", queries, key_win, preferred_element_type=jnp.float32)
            * scale
        )
        masked = jnp.where(usable, scores, jnp.float32(-1e30))
        fresh = jnp.maximum(best, jnp.max(masked, axis=3))
        probs = jnp.where(usable, jnp.exp(scores - fresh[..., None]), jnp.float32(0.0))
        shrink = jnp.exp(best - fresh)
        total = total * shrink + jnp.sum(probs, axis=3)
        acc = acc * shrink[..., None] + jnp.einsum(
            "nhqk,nkhd->nhqd",
            probs.astype(jnp.bfloat16),
            value_win,
            preferred_element_type=jnp.float32,
        )
        return ((fresh, total, acc), None)

    final, unused = lax.scan(one_stretch, initial, (key_full, value_full, stretch_ids))
    best, total, acc = final
    attn = (acc / total[..., None]).astype(jnp.bfloat16)
    attn = attn.transpose(0, 2, 1, 3).reshape(
        2, 2, frames, half_high, half_wide, heads_here * head_dim
    )
    attn = attn.transpose(2, 0, 3, 1, 4, 5).reshape(tokens_here, heads_here * head_dim)
    mixed = lax.psum_scatter(
        jnp.dot(attn, out_weight, preferred_element_type=jnp.float32).astype(jnp.bfloat16),
        "head",
        scatter_dimension=0,
        tiled=True,
    )
    return mixed.reshape(1, 1, -1, out_weight.shape[1])


def tile_place():
    tile_at = lax.axis_index("tile")
    return tile_at // 2, tile_at % 2


def load_kernel(k_ref, v_ref, w_ref, tile_ref, part_ref, sems):
    tall, broad = part_ref.shape
    top = pl.multiple_of(lax.axis_index("tile") * tall, 16)
    left = pl.multiple_of(lax.axis_index("tm") * broad, 128)
    copies = [
        pltpu.make_async_copy(
            w_ref.at[pl.ds(top, tall), pl.ds(left, broad)], part_ref, sems.at[2]
        )
    ]
    for which, ref in enumerate((k_ref, v_ref)):
        copies.append(pltpu.make_async_copy(ref, tile_ref.at[which], sems.at[which]))
    for copy in copies:
        copy.start()
    for copy in copies:
        copy.wait()


def face_kernel(tile_ref, row_ref, col_ref, corner_ref, *, geometry):
    high, wide, span, frames = geometry[:4]
    cells = high * wide
    row_at, col_at = tile_place()
    y0 = jnp.where(row_at == 0, high - span, 0)
    x0 = jnp.where(col_at == 0, wide - span, 0)

    def picker(count, cell_of):
        row = lax.broadcasted_iota(jnp.int32, (count, cells), 0)
        col = lax.broadcasted_iota(jnp.int32, (count, cells), 1)
        return (col == cell_of(row)).astype(jnp.bfloat16)

    beside = picker(high * span, lambda i: (i // span) * wide + x0 + i % span)
    across = picker(span * span, lambda i: (y0 + i // span) * wide + x0 + i % span)
    for which in range(2):
        for f in range(frames):
            start = pl.multiple_of(f * cells + y0 * wide, 16)
            row_ref[which, f] = tile_ref[which, pl.ds(start, span * wide)]
            whole = tile_ref[which, f * cells : (f + 1) * cells]
            col_ref[which, f] = jnp.dot(
                beside, whole, preferred_element_type=jnp.float32
            ).astype(jnp.bfloat16)
            corner_ref[which, f] = jnp.dot(
                across, whole, preferred_element_type=jnp.float32
            ).astype(jnp.bfloat16)


def edge_kernel(row_ref, col_ref, corner_ref, out_ref):
    for which in range(2):
        at = 0
        for part in (row_ref, col_ref, corner_ref):
            for f in range(part.shape[1]):
                size = part.shape[2]
                out_ref[which, at : at + size] = part[which, f]
                at += size


def distances(high, wide, span, frames):
    row_at, col_at = tile_place()
    cells = high * wide
    count = frames * (cells + span * (wide + high + span))
    j = lax.broadcasted_iota(jnp.int32, (1, count), 1)
    y_off = jnp.where(row_at == 0, high, -span)
    x_off = jnp.where(col_at == 0, wide, -span)
    c = j % cells
    ky, kx = c // wide, c % wide
    base = frames * cells
    c = (j - base) % (span * wide)
    ky = jnp.where(j >= base, y_off + c // wide, ky)
    kx = jnp.where(j >= base, c % wide, kx)
    base += frames * span * wide
    c = (j - base) % (span * high)
    ky = jnp.where(j >= base, c // span, ky)
    kx = jnp.where(j >= base, x_off + c % span, kx)
    base += frames * span * high
    c = (j - base) % (span * span)
    ky = jnp.where(j >= base, y_off + c // span, ky)
    kx = jnp.where(j >= base, x_off + c % span, kx)
    i = lax.broadcasted_iota(jnp.int32, (cells, 1), 0)
    return jnp.maximum(jnp.abs(i // wide - ky), jnp.abs(i % wide - kx))


def attend(q, pieces, factor, before):
    scores = []
    m = before
    for k, v, dist, reach in pieces:
        s = lax.dot_general(q, k, (((1,), (1,)), ((), ())), preferred_element_type=jnp.float32)
        s = jnp.where(dist <= reach, s * factor, FAR)
        top = jnp.max(s, axis=1, keepdims=True)
        m = top if m is None else jnp.maximum(m, top)
        scores.append(s)
    total = None
    for s, (k, v, dist, reach) in zip(scores, pieces):
        p = jnp.exp2(s - m).astype(jnp.bfloat16)
        both = jnp.concatenate([v, jnp.ones_like(v)], axis=1)
        got = jnp.dot(p, both, preferred_element_type=jnp.float32)
        total = got if total is None else total + got
    return m, total


def attend_tile(q_ref, tile_ref, dist_ref, reach_of, heads, state, geometry):
    high, wide, span, frames, head_dim, factor, step = geometry
    cells = high * wide
    acc_ref, sum_ref, max_ref = state
    for at, head in enumerate(heads):
        cols = slice(head * head_dim, (head + 1) * head_dim)
        outs = slice(at * head_dim, (at + 1) * head_dim)
        for start in range(0, q_ref.shape[0], step):
            rows = slice(start, start + step)
            near = dist_ref[start % cells : start % cells + step, : tile_ref.shape[1]]
            piece = (tile_ref[0, :, cols], tile_ref[1, :, cols], near, reach_of(head))
            m, got = attend(q_ref[rows, cols], [piece], factor, None)
            acc_ref[rows, outs] = got[:, :head_dim]
            sum_ref[rows, outs] = got[:, head_dim:]
            max_ref[rows, outs] = jnp.broadcast_to(m, (step, head_dim))


def begin_kernel(radius_ref, mask_ref, q_ref, tile_ref, *outs, geometry, heads):
    *state, dist_ref, reach_ref = outs
    high, wide, span, frames = geometry[:4]
    dist_ref[...] = distances(high, wide, span, frames)
    stretch_at = lax.axis_index("tm")
    line = (1, reach_ref.shape[1])
    for head in range(heads):
        radius = radius_ref[head]
        seen = mask_ref[stretch_at, 0, head] > 0
        reach_ref[head : head + 1] = jnp.full(line, radius, jnp.int32)
        reach_ref[heads + head : heads + head + 1] = jnp.full(
            line, jnp.where(seen, radius, -1), jnp.int32
        )
    attend_tile(q_ref, tile_ref, dist_ref, lambda h: radius_ref[h], (0,), state, geometry)


def tile_kernel(q_ref, tile_ref, dist_ref, reach_ref, *state, geometry, heads):
    attend_tile(
        q_ref,
        tile_ref,
        dist_ref,
        lambda h: reach_ref[h : h + 1, :1],
        range(1, heads),
        state,
        geometry,
    )


def pick_state(head_state, state, head, rows, head_dim):
    refs = head_state if head == 0 else state
    at = max(head - 1, 0) * head_dim
    return [ref[rows, at : at + head_dim] for ref in refs]


def merge(q, pieces, factor, old):
    old_acc, old_total, old_max = old
    m, got = attend(q, pieces, factor, old_max[:, :1])
    shrink = jnp.exp2(old_max - m)
    head_dim = old_acc.shape[1]
    acc = old_acc * shrink + got[:, :head_dim]
    total = old_total * shrink + got[:, head_dim:]
    return acc, total, jnp.broadcast_to(m, old_max.shape)


def rest_kernel(
    q_ref,
    edge_ref,
    first_tile_ref,
    first_edge_ref,
    *rest,
    geometry,
    heads,
    flips,
):
    head_state, dist_ref, reach_ref, state, outs = rest[:3], rest[3], rest[4], rest[5:8], rest[8:]
    high, wide, span, frames, head_dim, factor, step = geometry
    cells = high * wide
    base = frames * cells
    head_at = lax.axis_index("head")
    stretch_at = lax.axis_index("tm")

    def run(with_first):
        for flip, out_ref in zip(flips, outs):
            start = pl.multiple_of(jnp.bitwise_xor(head_at, flip) * step, step)
            rows = pl.ds(start, step)
            near = dist_ref[pl.ds(pl.multiple_of(lax.rem(start, cells), step), step)]
            beyond = near[:, base:]
            for head in range(heads):
                cols = slice(head * head_dim, (head + 1) * head_dim)
                sources = [(edge_ref, beyond, head)]
                if with_first:
                    sources.append((first_tile_ref, near[:, :base], heads + head))
                    sources.append((first_edge_ref, beyond, heads + head))
                pieces = [
                    (ref[0, :, cols], ref[1, :, cols], dist, reach_ref[row : row + 1, :1])
                    for ref, dist, row in sources
                ]
                old = pick_state(head_state, state, head, rows, head_dim)
                acc, total, m = merge(q_ref[rows, cols], pieces, factor, old)
                out_ref[:, cols] = (acc / total).astype(jnp.bfloat16)

    @pl.when(stretch_at > 0)
    def _():
        run(True)

    @pl.when(stretch_at == 0)
    def _():
        run(False)


def copy_kernel(in_ref, out_ref):
    out_ref[...] = in_ref[...]


def stack_kernel(*refs):
    *parts, out_ref = refs
    tile_at = lax.axis_index("tile")
    for flip, part in enumerate(parts):
        tall = part.shape[0]
        top = pl.multiple_of(jnp.bitwise_xor(tile_at, flip) * tall, 16)
        out_ref[pl.ds(top, tall)] = part[...]


def project_kernel(w_ref, part_ref, own_ref, got_ref, out_ref, *, flip):
    broad = part_ref.shape[1]
    half = jnp.bitwise_xor(lax.axis_index("tm"), flip)
    cols = pl.ds(pl.multiple_of(half * broad, 128), broad)
    total = jnp.dot(own_ref[...], w_ref[:, cols], preferred_element_type=jnp.float32)
    total += jnp.dot(got_ref[...], part_ref[...], preferred_element_type=jnp.float32)
    out_ref[...] = total.astype(out_ref.dtype)


def add_kernel(mine_ref, got_ref, *rest, flip):
    out_ref, sum_ref, sems = rest[-3:]
    pieces, tall, broad = sum_ref.shape
    half = jnp.bitwise_xor(lax.axis_index("tm"), flip)
    cols = pl.ds(pl.multiple_of(half * broad, 128), broad)
    copies = []
    for i in range(pieces):
        rows = slice(i * tall, (i + 1) * tall)
        sum_ref[i] = (mine_ref[rows] + got_ref[rows].astype(jnp.float32)).astype(jnp.bfloat16)
        copies.append(pltpu.make_async_copy(sum_ref.at[i], out_ref.at[rows, cols], sems.at[i]))
        copies[-1].start()
    for copy in copies:
        copy.wait()


def two_by_two(query, keys, values, out_weight, radius, block_mask):
    span = RMAX
    frames, high, wide, channels = query.shape[2:]
    heads = radius.shape[0]
    head_dim = channels // heads
    cells = high * wide
    tokens = frames * cells
    groups = lax.axis_size("head")
    tiles = lax.axis_size("tile")
    depth, width = out_weight.shape
    step = tokens // groups
    geometry = (high, wide, span, frames, head_dim, LOG2E / math.sqrt(head_dim), step)
    count = frames * (cells + span * (wide + high + span))
    smem = pl.BlockSpec(memory_space=pltpu.SMEM)
    vmem = pl.BlockSpec(memory_space=pltpu.VMEM)
    hbm = pl.BlockSpec(memory_space=pltpu.HBM)
    bf16, f32 = jnp.bfloat16, jnp.float32
    shape = jax.ShapeDtypeStruct

    def call(kernel, out_shape, specs, *args, name, scratch=(), flops=0, **keys_of):
        return pl.pallas_call(
            functools.partial(kernel, **keys_of) if keys_of else kernel,
            out_shape=out_shape,
            in_specs=specs,
            out_specs=jax.tree.map(lambda _: vmem, out_shape),
            scratch_shapes=scratch,
            cost_estimate=pl.CostEstimate(flops=flops, bytes_accessed=0, transcendentals=0),
            compiler_params=pltpu.CompilerParams(vmem_limit_bytes=VMEM_LIMIT),
            name=name,
        )(*args)

    def flipped(value, axis, flip):
        return lax.ppermute(value, axis, [(i, i ^ flip) for i in range(lax.axis_size(axis))])

    q = query.reshape(tokens, channels)
    k = keys.reshape(tokens, channels)
    v = values.reshape(tokens, channels)

    tall, broad = depth // tiles, width // 2
    part_shape = shape((tall, broad), bf16)
    tile, part = call(
        load_kernel,
        [shape((2, tokens, channels), bf16), part_shape],
        [hbm] * 3,
        *[pltpu.with_memory_space_constraint(x, pltpu.HBM) for x in (k, v, out_weight)],
        name="load",
        scratch=[pltpu.SemaphoreType.DMA((3,))],
    )
    faces = call(
        face_kernel,
        [
            shape((2, frames, span * wide, channels), bf16),
            shape((2, frames, span * high, channels), bf16),
            shape((2, frames, span * span, channels), bf16),
        ],
        [vmem],
        tile,
        name="faces",
        geometry=geometry,
    )
    faces = [flipped(face, "tile", flip) for face, flip in zip(faces, (2, 1, 3))]
    lone = flipped(part, "head", 2)
    begun = call(
        begin_kernel,
        [shape((tokens, head_dim), f32)] * 3
        + [shape((cells, count), jnp.int32), shape((2 * heads, head_dim), jnp.int32)],
        [smem] * 2 + [vmem] * 2,
        radius,
        block_mask.transpose(1, 2, 0),
        q,
        tile,
        name="begin",
        geometry=geometry,
        heads=heads,
    )
    begun, tile = lax.optimization_barrier((begun, tile))
    first_tile = lax.ppermute(tile, "tm", [(0, 1)])
    state = call(
        tile_kernel,
        [shape((tokens, channels - head_dim), f32)] * 3,
        [vmem] * 4,
        q,
        tile,
        *begun[3:],
        name="tile",
        geometry=geometry,
        heads=heads,
    )
    lone, state = lax.optimization_barrier((lone, state))
    lone = call(copy_kernel, part_shape, [vmem], lone, name="lone", flops=20 * 10**9)
    lone, state, faces = lax.optimization_barrier((lone, state, faces))
    edge = call(
        edge_kernel, shape((2, count - tokens, channels), bf16), [vmem] * 3, *faces, name="edges"
    )
    first_edge = lax.ppermute(edge, "tm", [(0, 1)])
    parts = [lone] + [flipped(lone, "tile", flip) for flip in range(1, tiles)]

    def rest(state, *flips, flops=0):
        return call(
            rest_kernel,
            [shape((step, channels), bf16)] * len(flips),
            [vmem] * 12,
            q,
            edge,
            first_tile,
            first_edge,
            *begun,
            *state,
            name="rest",
            geometry=geometry,
            heads=heads,
            flips=flips,
            flops=flops,
        )

    (for_side,) = rest(state, 3)
    got_side = flipped(for_side, "head", 2)
    state, for_side = lax.optimization_barrier((state, for_side))
    for_far, own_side = rest(state, 2, 1)
    got_far = flipped(for_far, "head", 2)
    parts, own_side = lax.optimization_barrier((parts, own_side))
    here = call(
        stack_kernel, shape((depth, broad), bf16), [vmem] * tiles, *parts, name="stack"
    )

    def project(part, mine, got, kind, flip, flops=0):
        return call(
            project_kernel,
            shape((step, broad), kind),
            [vmem] * 4,
            out_weight,
            part,
            mine,
            got,
            name="project",
            flops=flops,
            flip=flip,
        )

    for_side = [project(here, own_side, got_side, bf16, 0, 20 * 10**9)]
    from_side = [flipped(for_side[0], "head", 1)]
    state, here, for_side[0] = lax.optimization_barrier((state, here, for_side[0]))
    there = flipped(here, "tm", 1)
    (own,) = rest(state, 0, flops=20 * 10**9)
    own_side, own = lax.optimization_barrier((own_side, own))
    for_side.append(project(there, own_side, got_side, bf16, 1))
    from_side.append(flipped(for_side[1], "head", 1))
    own, for_side[1] = lax.optimization_barrier((own, for_side[1]))
    mine = [
        project(here, own, got_far, f32, 0),
        project(there, own, got_far, f32, 1, 20 * 10**9),
    ]
    pieces = 2
    mixed = []
    for flip in range(2):
        mixed = [
            pl.pallas_call(
                functools.partial(add_kernel, flip=flip),
                out_shape=shape((step, width), bf16),
                in_specs=[vmem] * 2 + [hbm] * flip,
                out_specs=hbm,
                input_output_aliases={2: 0} if flip else {},
                scratch_shapes=[
                    pltpu.VMEM((pieces, step // pieces, broad), bf16),
                    pltpu.SemaphoreType.DMA((pieces,)),
                ],
                compiler_params=pltpu.CompilerParams(vmem_limit_bytes=VMEM_LIMIT),
                name="add",
            )(mine[flip], from_side[flip], *mixed)
        ]
    (mixed,) = mixed
    return mixed.reshape(1, 1, step, width)


def solution(mesh):
    in_specs = (
        P("tm", "tile", None, None, None, "head"),
        P("tm", "tile", None, None, None, "head"),
        P("tm", "tile", None, None, None, "head"),
        P("head", None),
        P("head"),
        P("head", None, None),
    )
    out_specs = P("tm", "tile", "head", None)
    small = dict(mesh.shape) == {"tm": 2, "tile": 4, "head": 4}
    return jax.shard_map(
        two_by_two if small else any_grid,
        mesh=mesh,
        in_specs=in_specs,
        out_specs=out_specs,
        check_vma=False,
    )
```

```python
import functools
import math

import jax
import jax.numpy as jnp
from jax import lax
from jax.experimental import pallas as pl
from jax.experimental.pallas import tpu as pltpu
from jax.sharding import PartitionSpec as P

RMAX = 4
FAR = -1e30
LOG2E = 1.4426950408889634
VMEM_LIMIT = 24 * 1024 * 1024


def passed_along(value, axis, by):
    peers = lax.axis_size(axis)
    pairs = [(i, i + by) for i in range(peers) if 0 <= i + by < peers]
    return lax.ppermute(value, axis, pairs)


def widen(key_part, value_part, span, row_move, col_move):
    grid = math.isqrt(lax.axis_size("tile"))
    above = None
    below = None
    for offset in (grid, -grid):
        if offset > 0:
            face_key = key_part[:, :, key_part.shape[2] - span :]
            face_value = value_part[:, :, value_part.shape[2] - span :]
        else:
            face_key = key_part[:, :, :span]
            face_value = value_part[:, :, :span]
        got = row_move(face_key, face_value, offset)
        if offset > 0:
            above = got
        else:
            below = got
    key_rows = jnp.concatenate([above[0], key_part, below[0]], axis=2)
    value_rows = jnp.concatenate([above[1], value_part, below[1]], axis=2)
    left = None
    right = None
    for offset in (1, -1):
        if offset > 0:
            face_key = key_rows[:, :, :, key_rows.shape[3] - span :]
            face_value = value_rows[:, :, :, value_rows.shape[3] - span :]
        else:
            face_key = key_rows[:, :, :, :span]
            face_value = value_rows[:, :, :, :span]
        got = col_move(face_key, face_value, offset)
        if offset > 0:
            left = got
        else:
            right = got
    key_full = jnp.concatenate([left[0], key_rows, right[0]], axis=3)
    value_full = jnp.concatenate([left[1], value_rows, right[1]], axis=3)
    return (key_full, value_full)


def windows_of(block, half_high, half_wide, win_high, win_wide, heads_here, head_dim):
    parts = []
    for band in (0, 1):
        for strip in (0, 1):
            parts.append(
                block[
                    :,
                    band * half_high : band * half_high + win_high,
                    strip * half_wide : strip * half_wide + win_wide,
                ]
            )
    stacked = jnp.stack(parts)
    return stacked.reshape(4, -1, heads_here, head_dim)


def any_grid(query, keys, values, out_weight, radius, block_mask):
    span = RMAX
    grid = math.isqrt(lax.axis_size("tile"))
    tile_at = lax.axis_index("tile")
    row_at = tile_at // grid
    col_at = tile_at % grid
    stretch_at = lax.axis_index("tm")
    frames, high, wide, channels = query.shape[2:]
    heads_here = radius.shape[0]
    head_dim = channels // heads_here
    tokens_here = frames * high * wide
    half_high = high // 2
    half_wide = wide // 2
    win_high = half_high + 2 * span
    win_wide = half_wide + 2 * span
    quarter = frames * half_high * half_wide
    queries = query[0, 0].reshape(frames, 2, half_high, 2, half_wide, channels)
    queries = queries.transpose(1, 3, 0, 2, 4, 5).reshape(4, quarter, heads_here, head_dim)
    query_y = jnp.broadcast_to(
        jnp.arange(half_high, dtype=jnp.int32)[None, :, None], (frames, half_high, half_wide)
    ).reshape(-1)
    query_x = jnp.broadcast_to(
        jnp.arange(half_wide, dtype=jnp.int32)[None, None, :], (frames, half_high, half_wide)
    ).reshape(-1)
    key_y = jnp.broadcast_to(
        jnp.arange(win_high, dtype=jnp.int32)[None, :, None] - span, (frames, win_high, win_wide)
    ).reshape(-1)
    key_x = jnp.broadcast_to(
        jnp.arange(win_wide, dtype=jnp.int32)[None, None, :] - span, (frames, win_high, win_wide)
    ).reshape(-1)
    band_at = jnp.array([0, 0, 1, 1], dtype=jnp.int32)
    strip_at = jnp.array([0, 1, 0, 1], dtype=jnp.int32)
    global_y = row_at * high + band_at[:, None] * half_high + key_y[None, :]
    global_x = col_at * wide + strip_at[:, None] * half_wide + key_x[None, :]
    inside = (global_y >= 0) & (global_y < grid * high) & (global_x >= 0) & (global_x < grid * wide)
    distance = jnp.maximum(
        jnp.abs(query_y[:, None] - key_y[None, :]), jnp.abs(query_x[:, None] - key_x[None, :])
    )
    near = distance[None, :, :] <= radius[:, None, None]
    allowed = near[None, :, :, :] & inside[:, None, None, :]
    scale = 1.0 / math.sqrt(head_dim)
    initial = (
        jnp.full((4, heads_here, quarter), -1e30, jnp.float32),
        jnp.zeros((4, heads_here, quarter), jnp.float32),
        jnp.zeros((4, heads_here, quarter, head_dim), jnp.float32),
    )

    def tile_move(face_key, face_value, offset):
        return passed_along((face_key, face_value), "tile", offset)

    key_all, value_all = (
        lax.all_gather(keys[0], "tm", axis=0, tiled=True),
        lax.all_gather(values[0], "tm", axis=0, tiled=True),
    )
    key_full, value_full = widen(key_all, value_all, span, tile_move, tile_move)
    stretch_ids = jnp.arange(key_full.shape[0], dtype=jnp.int32)

    def one_stretch(state, item):
        key_block, value_block, stretch_id = item
        visible = (
            lax.dynamic_slice_in_dim(
                lax.dynamic_index_in_dim(block_mask, stretch_at, 1, False), stretch_id, 1, 1
            )[:, 0]
            > 0
        )
        best, total, acc = state
        key_win = windows_of(
            key_block, half_high, half_wide, win_high, win_wide, heads_here, head_dim
        )
        value_win = windows_of(
            value_block, half_high, half_wide, win_high, win_wide, heads_here, head_dim
        )
        usable = allowed & visible[None, :, None, None]
        scores = (
            jnp.einsum("nqhd,nkhd->nhqk", queries, key_win, preferred_element_type=jnp.float32)
            * scale
        )
        masked = jnp.where(usable, scores, jnp.float32(-1e30))
        fresh = jnp.maximum(best, jnp.max(masked, axis=3))
        probs = jnp.where(usable, jnp.exp(scores - fresh[..., None]), jnp.float32(0.0))
        shrink = jnp.exp(best - fresh)
        total = total * shrink + jnp.sum(probs, axis=3)
        acc = acc * shrink[..., None] + jnp.einsum(
            "nhqk,nkhd->nhqd",
            probs.astype(jnp.bfloat16),
            value_win,
            preferred_element_type=jnp.float32,
        )
        return ((fresh, total, acc), None)

    final, unused = lax.scan(one_stretch, initial, (key_full, value_full, stretch_ids))
    best, total, acc = final
    attn = (acc / total[..., None]).astype(jnp.bfloat16)
    attn = attn.transpose(0, 2, 1, 3).reshape(
        2, 2, frames, half_high, half_wide, heads_here * head_dim
    )
    attn = attn.transpose(2, 0, 3, 1, 4, 5).reshape(tokens_here, heads_here * head_dim)
    mixed = lax.psum_scatter(
        jnp.dot(attn, out_weight, preferred_element_type=jnp.float32).astype(jnp.bfloat16),
        "head",
        scatter_dimension=0,
        tiled=True,
    )
    return mixed.reshape(1, 1, -1, out_weight.shape[1])


def tile_place():
    tile_at = lax.axis_index("tile")
    return tile_at // 2, tile_at % 2


def load_kernel(k_ref, v_ref, w_ref, tile_ref, part_ref, sems):
    tall, broad = part_ref.shape
    top = pl.multiple_of(lax.axis_index("tile") * tall, 16)
    left = pl.multiple_of(lax.axis_index("tm") * broad, 128)
    copies = [
        pltpu.make_async_copy(
            w_ref.at[pl.ds(top, tall), pl.ds(left, broad)], part_ref, sems.at[2]
        )
    ]
    for which, ref in enumerate((k_ref, v_ref)):
        copies.append(pltpu.make_async_copy(ref, tile_ref.at[which], sems.at[which]))
    for copy in copies:
        copy.start()
    for copy in copies:
        copy.wait()


def face_kernel(tile_ref, row_ref, col_ref, corner_ref, *, geometry):
    high, wide, span, frames = geometry[:4]
    cells = high * wide
    row_at, col_at = tile_place()
    y0 = jnp.where(row_at == 0, high - span, 0)
    x0 = jnp.where(col_at == 0, wide - span, 0)

    def picker(count, cell_of):
        row = lax.broadcasted_iota(jnp.int32, (count, cells), 0)
        col = lax.broadcasted_iota(jnp.int32, (count, cells), 1)
        return (col == cell_of(row)).astype(jnp.bfloat16)

    beside = picker(high * span, lambda i: (i // span) * wide + x0 + i % span)
    across = picker(span * span, lambda i: (y0 + i // span) * wide + x0 + i % span)
    for which in range(2):
        for f in range(frames):
            start = pl.multiple_of(f * cells + y0 * wide, 16)
            row_ref[which, f] = tile_ref[which, pl.ds(start, span * wide)]
            whole = tile_ref[which, f * cells : (f + 1) * cells]
            col_ref[which, f] = jnp.dot(
                beside, whole, preferred_element_type=jnp.float32
            ).astype(jnp.bfloat16)
            corner_ref[which, f] = jnp.dot(
                across, whole, preferred_element_type=jnp.float32
            ).astype(jnp.bfloat16)


def edge_kernel(row_ref, col_ref, corner_ref, out_ref):
    for which in range(2):
        at = 0
        for part in (row_ref, col_ref, corner_ref):
            for f in range(part.shape[1]):
                size = part.shape[2]
                out_ref[which, at : at + size] = part[which, f]
                at += size


def distances(high, wide, span, frames):
    row_at, col_at = tile_place()
    cells = high * wide
    count = frames * (cells + span * (wide + high + span))
    j = lax.broadcasted_iota(jnp.int32, (1, count), 1)
    y_off = jnp.where(row_at == 0, high, -span)
    x_off = jnp.where(col_at == 0, wide, -span)
    c = j % cells
    ky, kx = c // wide, c % wide
    base = frames * cells
    c = (j - base) % (span * wide)
    ky = jnp.where(j >= base, y_off + c // wide, ky)
    kx = jnp.where(j >= base, c % wide, kx)
    base += frames * span * wide
    c = (j - base) % (span * high)
    ky = jnp.where(j >= base, c // span, ky)
    kx = jnp.where(j >= base, x_off + c % span, kx)
    base += frames * span * high
    c = (j - base) % (span * span)
    ky = jnp.where(j >= base, y_off + c // span, ky)
    kx = jnp.where(j >= base, x_off + c % span, kx)
    i = lax.broadcasted_iota(jnp.int32, (cells, 1), 0)
    return jnp.maximum(jnp.abs(i // wide - ky), jnp.abs(i % wide - kx))


def attend(q, pieces, factor, before):
    scores = []
    m = before
    for k, v, dist, reach in pieces:
        s = lax.dot_general(q, k, (((1,), (1,)), ((), ())), preferred_element_type=jnp.float32)
        s = jnp.where(dist <= reach, s * factor, FAR)
        top = jnp.max(s, axis=1, keepdims=True)
        m = top if m is None else jnp.maximum(m, top)
        scores.append(s)
    total = None
    for s, (k, v, dist, reach) in zip(scores, pieces):
        p = jnp.exp2(s - m).astype(jnp.bfloat16)
        both = jnp.concatenate([v, jnp.ones_like(v)], axis=1)
        got = jnp.dot(p, both, preferred_element_type=jnp.float32)
        total = got if total is None else total + got
    return m, total


def attend_tile(q_ref, tile_ref, dist_ref, reach_of, heads, state, geometry):
    high, wide, span, frames, head_dim, factor, step = geometry
    cells = high * wide
    acc_ref, sum_ref, max_ref = state
    for at, head in enumerate(heads):
        cols = slice(head * head_dim, (head + 1) * head_dim)
        outs = slice(at * head_dim, (at + 1) * head_dim)
        for start in range(0, q_ref.shape[0], step):
            rows = slice(start, start + step)
            near = dist_ref[start % cells : start % cells + step, : tile_ref.shape[1]]
            piece = (tile_ref[0, :, cols], tile_ref[1, :, cols], near, reach_of(head))
            m, got = attend(q_ref[rows, cols], [piece], factor, None)
            acc_ref[rows, outs] = got[:, :head_dim]
            sum_ref[rows, outs] = got[:, head_dim:]
            max_ref[rows, outs] = jnp.broadcast_to(m, (step, head_dim))


def begin_kernel(radius_ref, mask_ref, q_ref, tile_ref, *outs, geometry, heads):
    *state, dist_ref, reach_ref = outs
    high, wide, span, frames = geometry[:4]
    dist_ref[...] = distances(high, wide, span, frames)
    stretch_at = lax.axis_index("tm")
    line = (1, reach_ref.shape[1])
    for head in range(heads):
        radius = radius_ref[head]
        seen = mask_ref[stretch_at, 0, head] > 0
        reach_ref[head : head + 1] = jnp.full(line, radius, jnp.int32)
        reach_ref[heads + head : heads + head + 1] = jnp.full(
            line, jnp.where(seen, radius, -1), jnp.int32
        )
    attend_tile(q_ref, tile_ref, dist_ref, lambda h: radius_ref[h], (0,), state, geometry)


def tile_kernel(q_ref, tile_ref, dist_ref, reach_ref, *state, geometry, heads):
    attend_tile(
        q_ref,
        tile_ref,
        dist_ref,
        lambda h: reach_ref[h : h + 1, :1],
        range(1, heads),
        state,
        geometry,
    )


def pick_state(head_state, state, head, rows, head_dim):
    refs = head_state if head == 0 else state
    at = max(head - 1, 0) * head_dim
    return [ref[rows, at : at + head_dim] for ref in refs]


def merge(q, pieces, factor, old):
    old_acc, old_total, old_max = old
    m, got = attend(q, pieces, factor, old_max[:, :1])
    shrink = jnp.exp2(old_max - m)
    head_dim = old_acc.shape[1]
    acc = old_acc * shrink + got[:, :head_dim]
    total = old_total * shrink + got[:, head_dim:]
    return acc, total, jnp.broadcast_to(m, old_max.shape)


def rest_kernel(
    q_ref,
    edge_ref,
    first_tile_ref,
    first_edge_ref,
    *rest,
    geometry,
    heads,
    flips,
):
    head_state, dist_ref, reach_ref, state, outs = rest[:3], rest[3], rest[4], rest[5:8], rest[8:]
    high, wide, span, frames, head_dim, factor, step = geometry
    cells = high * wide
    base = frames * cells
    head_at = lax.axis_index("head")
    stretch_at = lax.axis_index("tm")

    def run(with_first):
        for flip, out_ref in zip(flips, outs):
            start = pl.multiple_of(jnp.bitwise_xor(head_at, flip) * step, step)
            rows = pl.ds(start, step)
            near = dist_ref[pl.ds(pl.multiple_of(lax.rem(start, cells), step), step)]
            beyond = near[:, base:]
            for head in range(heads):
                cols = slice(head * head_dim, (head + 1) * head_dim)
                sources = [(edge_ref, beyond, head)]
                if with_first:
                    sources.append((first_tile_ref, near[:, :base], heads + head))
                    sources.append((first_edge_ref, beyond, heads + head))
                pieces = [
                    (ref[0, :, cols], ref[1, :, cols], dist, reach_ref[row : row + 1, :1])
                    for ref, dist, row in sources
                ]
                old = pick_state(head_state, state, head, rows, head_dim)
                acc, total, m = merge(q_ref[rows, cols], pieces, factor, old)
                out_ref[:, cols] = (acc / total).astype(jnp.bfloat16)

    @pl.when(stretch_at > 0)
    def _():
        run(True)

    @pl.when(stretch_at == 0)
    def _():
        run(False)


def copy_kernel(in_ref, out_ref):
    out_ref[...] = in_ref[...]


def stack_kernel(*refs):
    *parts, out_ref = refs
    tile_at = lax.axis_index("tile")
    for flip, part in enumerate(parts):
        tall = part.shape[0]
        top = pl.multiple_of(jnp.bitwise_xor(tile_at, flip) * tall, 16)
        out_ref[pl.ds(top, tall)] = part[...]


def project_kernel(w_ref, part_ref, own_ref, got_ref, out_ref, *, flip):
    broad = part_ref.shape[1]
    half = jnp.bitwise_xor(lax.axis_index("tm"), flip)
    cols = pl.ds(pl.multiple_of(half * broad, 128), broad)
    total = jnp.dot(own_ref[...], w_ref[:, cols], preferred_element_type=jnp.float32)
    total += jnp.dot(got_ref[...], part_ref[...], preferred_element_type=jnp.float32)
    out_ref[...] = total.astype(out_ref.dtype)


def add_kernel(mine_ref, got_ref, *rest, flip):
    out_ref, sum_ref, sems = rest[-3:]
    pieces, tall, broad = sum_ref.shape
    half = jnp.bitwise_xor(lax.axis_index("tm"), flip)
    cols = pl.ds(pl.multiple_of(half * broad, 128), broad)
    copies = []
    for i in range(pieces):
        rows = slice(i * tall, (i + 1) * tall)
        sum_ref[i] = (mine_ref[rows] + got_ref[rows].astype(jnp.float32)).astype(jnp.bfloat16)
        copies.append(pltpu.make_async_copy(sum_ref.at[i], out_ref.at[rows, cols], sems.at[i]))
        copies[-1].start()
    for copy in copies:
        copy.wait()


def two_by_two(query, keys, values, out_weight, radius, block_mask):
    span = RMAX
    frames, high, wide, channels = query.shape[2:]
    heads = radius.shape[0]
    head_dim = channels // heads
    cells = high * wide
    tokens = frames * cells
    groups = lax.axis_size("head")
    tiles = lax.axis_size("tile")
    depth, width = out_weight.shape
    step = tokens // groups
    geometry = (high, wide, span, frames, head_dim, LOG2E / math.sqrt(head_dim), step)
    count = frames * (cells + span * (wide + high + span))
    smem = pl.BlockSpec(memory_space=pltpu.SMEM)
    vmem = pl.BlockSpec(memory_space=pltpu.VMEM)
    hbm = pl.BlockSpec(memory_space=pltpu.HBM)
    bf16, f32 = jnp.bfloat16, jnp.float32
    shape = jax.ShapeDtypeStruct

    def call(kernel, out_shape, specs, *args, name, scratch=(), flops=0, **keys_of):
        return pl.pallas_call(
            functools.partial(kernel, **keys_of) if keys_of else kernel,
            out_shape=out_shape,
            in_specs=specs,
            out_specs=jax.tree.map(lambda _: vmem, out_shape),
            scratch_shapes=scratch,
            cost_estimate=pl.CostEstimate(flops=flops, bytes_accessed=0, transcendentals=0),
            compiler_params=pltpu.CompilerParams(vmem_limit_bytes=VMEM_LIMIT),
            name=name,
        )(*args)

    def flipped(value, axis, flip):
        return lax.ppermute(value, axis, [(i, i ^ flip) for i in range(lax.axis_size(axis))])

    q = query.reshape(tokens, channels)
    k = keys.reshape(tokens, channels)
    v = values.reshape(tokens, channels)

    tall, broad = depth // tiles, width // 2
    part_shape = shape((tall, broad), bf16)
    tile, part = call(
        load_kernel,
        [shape((2, tokens, channels), bf16), part_shape],
        [hbm] * 3,
        *[pltpu.with_memory_space_constraint(x, pltpu.HBM) for x in (k, v, out_weight)],
        name="load",
        scratch=[pltpu.SemaphoreType.DMA((3,))],
    )
    faces = call(
        face_kernel,
        [
            shape((2, frames, span * wide, channels), bf16),
            shape((2, frames, span * high, channels), bf16),
            shape((2, frames, span * span, channels), bf16),
        ],
        [vmem],
        tile,
        name="faces",
        geometry=geometry,
    )
    faces = [flipped(face, "tile", flip) for face, flip in zip(faces, (2, 1, 3))]
    lone = flipped(part, "head", 2)
    begun = call(
        begin_kernel,
        [shape((tokens, head_dim), f32)] * 3
        + [shape((cells, count), jnp.int32), shape((2 * heads, head_dim), jnp.int32)],
        [smem] * 2 + [vmem] * 2,
        radius,
        block_mask.transpose(1, 2, 0),
        q,
        tile,
        name="begin",
        geometry=geometry,
        heads=heads,
    )
    begun, tile = lax.optimization_barrier((begun, tile))
    first_tile = lax.ppermute(tile, "tm", [(0, 1)])
    state = call(
        tile_kernel,
        [shape((tokens, channels - head_dim), f32)] * 3,
        [vmem] * 4,
        q,
        tile,
        *begun[3:],
        name="tile",
        geometry=geometry,
        heads=heads,
    )
    lone, state = lax.optimization_barrier((lone, state))
    lone = call(copy_kernel, part_shape, [vmem], lone, name="lone", flops=2 * 10**9)
    lone, state, faces = lax.optimization_barrier((lone, state, faces))
    edge = call(
        edge_kernel, shape((2, count - tokens, channels), bf16), [vmem] * 3, *faces, name="edges", flops=20 * 10**9
    )
    first_edge = lax.ppermute(edge, "tm", [(0, 1)])
    parts = [lone] + [flipped(lone, "tile", flip) for flip in range(1, tiles)]

    def rest(state, *flips, flops=0):
        return call(
            rest_kernel,
            [shape((step, channels), bf16)] * len(flips),
            [vmem] * 12,
            q,
            edge,
            first_tile,
            first_edge,
            *begun,
            *state,
            name="rest",
            geometry=geometry,
            heads=heads,
            flips=flips,
            flops=flops,
        )

    (for_side,) = rest(state, 3)
    got_side = flipped(for_side, "head", 2)
    state, for_side = lax.optimization_barrier((state, for_side))
    for_far, own_side = rest(state, 2, 1)
    got_far = flipped(for_far, "head", 2)
    parts, own_side = lax.optimization_barrier((parts[::-1], own_side))
    parts = parts[::-1]
    here = call(
        stack_kernel, shape((depth, broad), bf16), [vmem] * tiles, *parts, name="stack"
    )

    def project(part, mine, got, kind, flip, flops=0):
        return call(
            project_kernel,
            shape((step, broad), kind),
            [vmem] * 4,
            out_weight,
            part,
            mine,
            got,
            name="project",
            flops=flops,
            flip=flip,
        )

    for_side = [project(here, own_side, got_side, bf16, 0, 20 * 10**9)]
    from_side = [flipped(for_side[0], "head", 1)]
    state, here, for_side[0] = lax.optimization_barrier((state, here, for_side[0]))
    there = flipped(here, "tm", 1)
    (own,) = rest(state, 0, flops=20 * 10**9)
    own_side, own = lax.optimization_barrier((own_side, own))
    for_side.append(project(there, own_side, got_side, bf16, 1))
    from_side.append(flipped(for_side[1], "head", 1))
    own, for_side[1] = lax.optimization_barrier((own, for_side[1]))
    mine = [
        project(here, own, got_far, f32, 0),
        project(there, own, got_far, f32, 1, 20 * 10**9),
    ]
    pieces = 2
    mixed = []
    for flip in range(2):
        mixed = [
            pl.pallas_call(
                functools.partial(add_kernel, flip=flip),
                out_shape=shape((step, width), bf16),
                in_specs=[vmem] * 2 + [hbm] * flip,
                out_specs=hbm,
                input_output_aliases={2: 0} if flip else {},
                scratch_shapes=[
                    pltpu.VMEM((pieces, step // pieces, broad), bf16),
                    pltpu.SemaphoreType.DMA((pieces,)),
                ],
                compiler_params=pltpu.CompilerParams(vmem_limit_bytes=VMEM_LIMIT),
                name="add",
            )(mine[flip], from_side[flip], *mixed)
        ]
    (mixed,) = mixed
    return mixed.reshape(1, 1, step, width)


def solution(mesh):
    in_specs = (
        P("tm", "tile", None, None, None, "head"),
        P("tm", "tile", None, None, None, "head"),
        P("tm", "tile", None, None, None, "head"),
        P("head", None),
        P("head"),
        P("head", None, None),
    )
    out_specs = P("tm", "tile", "head", None)
    small = dict(mesh.shape) == {"tm": 2, "tile": 4, "head": 4}
    return jax.shard_map(
        two_by_two if small else any_grid,
        mesh=mesh,
        in_specs=in_specs,
        out_specs=out_specs,
        check_vma=False,
    )
```

```python
import functools
import math

import jax
import jax.numpy as jnp
from jax import lax
from jax.experimental import pallas as pl
from jax.experimental.pallas import tpu as pltpu
from jax.sharding import PartitionSpec as P

RMAX = 4
FAR = -1e30
LOG2E = 1.4426950408889634
VMEM_LIMIT = 24 * 1024 * 1024


def passed_along(value, axis, by):
    peers = lax.axis_size(axis)
    pairs = [(i, i + by) for i in range(peers) if 0 <= i + by < peers]
    return lax.ppermute(value, axis, pairs)


def widen(key_part, value_part, span, row_move, col_move):
    grid = math.isqrt(lax.axis_size("tile"))
    above = None
    below = None
    for offset in (grid, -grid):
        if offset > 0:
            face_key = key_part[:, :, key_part.shape[2] - span :]
            face_value = value_part[:, :, value_part.shape[2] - span :]
        else:
            face_key = key_part[:, :, :span]
            face_value = value_part[:, :, :span]
        got = row_move(face_key, face_value, offset)
        if offset > 0:
            above = got
        else:
            below = got
    key_rows = jnp.concatenate([above[0], key_part, below[0]], axis=2)
    value_rows = jnp.concatenate([above[1], value_part, below[1]], axis=2)
    left = None
    right = None
    for offset in (1, -1):
        if offset > 0:
            face_key = key_rows[:, :, :, key_rows.shape[3] - span :]
            face_value = value_rows[:, :, :, value_rows.shape[3] - span :]
        else:
            face_key = key_rows[:, :, :, :span]
            face_value = value_rows[:, :, :, :span]
        got = col_move(face_key, face_value, offset)
        if offset > 0:
            left = got
        else:
            right = got
    key_full = jnp.concatenate([left[0], key_rows, right[0]], axis=3)
    value_full = jnp.concatenate([left[1], value_rows, right[1]], axis=3)
    return (key_full, value_full)


def windows_of(block, half_high, half_wide, win_high, win_wide, heads_here, head_dim):
    parts = []
    for band in (0, 1):
        for strip in (0, 1):
            parts.append(
                block[
                    :,
                    band * half_high : band * half_high + win_high,
                    strip * half_wide : strip * half_wide + win_wide,
                ]
            )
    stacked = jnp.stack(parts)
    return stacked.reshape(4, -1, heads_here, head_dim)


def any_grid(query, keys, values, out_weight, radius, block_mask):
    span = RMAX
    grid = math.isqrt(lax.axis_size("tile"))
    tile_at = lax.axis_index("tile")
    row_at = tile_at // grid
    col_at = tile_at % grid
    stretch_at = lax.axis_index("tm")
    frames, high, wide, channels = query.shape[2:]
    heads_here = radius.shape[0]
    head_dim = channels // heads_here
    tokens_here = frames * high * wide
    half_high = high // 2
    half_wide = wide // 2
    win_high = half_high + 2 * span
    win_wide = half_wide + 2 * span
    quarter = frames * half_high * half_wide
    queries = query[0, 0].reshape(frames, 2, half_high, 2, half_wide, channels)
    queries = queries.transpose(1, 3, 0, 2, 4, 5).reshape(4, quarter, heads_here, head_dim)
    query_y = jnp.broadcast_to(
        jnp.arange(half_high, dtype=jnp.int32)[None, :, None], (frames, half_high, half_wide)
    ).reshape(-1)
    query_x = jnp.broadcast_to(
        jnp.arange(half_wide, dtype=jnp.int32)[None, None, :], (frames, half_high, half_wide)
    ).reshape(-1)
    key_y = jnp.broadcast_to(
        jnp.arange(win_high, dtype=jnp.int32)[None, :, None] - span, (frames, win_high, win_wide)
    ).reshape(-1)
    key_x = jnp.broadcast_to(
        jnp.arange(win_wide, dtype=jnp.int32)[None, None, :] - span, (frames, win_high, win_wide)
    ).reshape(-1)
    band_at = jnp.array([0, 0, 1, 1], dtype=jnp.int32)
    strip_at = jnp.array([0, 1, 0, 1], dtype=jnp.int32)
    global_y = row_at * high + band_at[:, None] * half_high + key_y[None, :]
    global_x = col_at * wide + strip_at[:, None] * half_wide + key_x[None, :]
    inside = (global_y >= 0) & (global_y < grid * high) & (global_x >= 0) & (global_x < grid * wide)
    distance = jnp.maximum(
        jnp.abs(query_y[:, None] - key_y[None, :]), jnp.abs(query_x[:, None] - key_x[None, :])
    )
    near = distance[None, :, :] <= radius[:, None, None]
    allowed = near[None, :, :, :] & inside[:, None, None, :]
    scale = 1.0 / math.sqrt(head_dim)
    initial = (
        jnp.full((4, heads_here, quarter), -1e30, jnp.float32),
        jnp.zeros((4, heads_here, quarter), jnp.float32),
        jnp.zeros((4, heads_here, quarter, head_dim), jnp.float32),
    )

    def tile_move(face_key, face_value, offset):
        return passed_along((face_key, face_value), "tile", offset)

    key_all, value_all = (
        lax.all_gather(keys[0], "tm", axis=0, tiled=True),
        lax.all_gather(values[0], "tm", axis=0, tiled=True),
    )
    key_full, value_full = widen(key_all, value_all, span, tile_move, tile_move)
    stretch_ids = jnp.arange(key_full.shape[0], dtype=jnp.int32)

    def one_stretch(state, item):
        key_block, value_block, stretch_id = item
        visible = (
            lax.dynamic_slice_in_dim(
                lax.dynamic_index_in_dim(block_mask, stretch_at, 1, False), stretch_id, 1, 1
            )[:, 0]
            > 0
        )
        best, total, acc = state
        key_win = windows_of(
            key_block, half_high, half_wide, win_high, win_wide, heads_here, head_dim
        )
        value_win = windows_of(
            value_block, half_high, half_wide, win_high, win_wide, heads_here, head_dim
        )
        usable = allowed & visible[None, :, None, None]
        scores = (
            jnp.einsum("nqhd,nkhd->nhqk", queries, key_win, preferred_element_type=jnp.float32)
            * scale
        )
        masked = jnp.where(usable, scores, jnp.float32(-1e30))
        fresh = jnp.maximum(best, jnp.max(masked, axis=3))
        probs = jnp.where(usable, jnp.exp(scores - fresh[..., None]), jnp.float32(0.0))
        shrink = jnp.exp(best - fresh)
        total = total * shrink + jnp.sum(probs, axis=3)
        acc = acc * shrink[..., None] + jnp.einsum(
            "nhqk,nkhd->nhqd",
            probs.astype(jnp.bfloat16),
            value_win,
            preferred_element_type=jnp.float32,
        )
        return ((fresh, total, acc), None)

    final, unused = lax.scan(one_stretch, initial, (key_full, value_full, stretch_ids))
    best, total, acc = final
    attn = (acc / total[..., None]).astype(jnp.bfloat16)
    attn = attn.transpose(0, 2, 1, 3).reshape(
        2, 2, frames, half_high, half_wide, heads_here * head_dim
    )
    attn = attn.transpose(2, 0, 3, 1, 4, 5).reshape(tokens_here, heads_here * head_dim)
    mixed = lax.psum_scatter(
        jnp.dot(attn, out_weight, preferred_element_type=jnp.float32).astype(jnp.bfloat16),
        "head",
        scatter_dimension=0,
        tiled=True,
    )
    return mixed.reshape(1, 1, -1, out_weight.shape[1])


def tile_place():
    tile_at = lax.axis_index("tile")
    return tile_at // 2, tile_at % 2


def part_kernel(w_ref, part_ref, sem):
    tall, broad = part_ref.shape
    top = pl.multiple_of(lax.axis_index("tile") * tall, 16)
    left = pl.multiple_of(lax.axis_index("tm") * broad, 128)
    copy = pltpu.make_async_copy(w_ref.at[pl.ds(top, tall), pl.ds(left, broad)], part_ref, sem)
    copy.start()
    copy.wait()


def face_kernel(
    k_ref, v_ref, part_ref, row_ref, col_ref, corner_ref, tile_ref, sems, *, geometry
):
    high, wide, span, frames = geometry[:4]
    cells = high * wide
    row_at, col_at = tile_place()
    y0 = jnp.where(row_at == 0, high - span, 0)
    x0 = jnp.where(col_at == 0, wide - span, 0)
    copies = [
        pltpu.make_async_copy(ref, tile_ref.at[which], sems.at[which])
        for which, ref in enumerate((k_ref, v_ref))
    ]
    for copy in copies:
        copy.start()

    def picker(count, cell_of):
        row = lax.broadcasted_iota(jnp.int32, (count, cells), 0)
        col = lax.broadcasted_iota(jnp.int32, (count, cells), 1)
        return (col == cell_of(row)).astype(jnp.bfloat16)

    beside = picker(high * span, lambda i: (i // span) * wide + x0 + i % span)
    across = picker(span * span, lambda i: (y0 + i // span) * wide + x0 + i % span)
    for which in range(2):
        copies[which].wait()
        for f in range(frames):
            start = pl.multiple_of(f * cells + y0 * wide, 16)
            row_ref[which, f] = tile_ref[which, pl.ds(start, span * wide)]
            whole = tile_ref[which, f * cells : (f + 1) * cells]
            col_ref[which, f] = jnp.dot(
                beside, whole, preferred_element_type=jnp.float32
            ).astype(jnp.bfloat16)
            corner_ref[which, f] = jnp.dot(
                across, whole, preferred_element_type=jnp.float32
            ).astype(jnp.bfloat16)


def edge_kernel(row_ref, col_ref, corner_ref, out_ref):
    for which in range(2):
        at = 0
        for part in (row_ref, col_ref, corner_ref):
            for f in range(part.shape[1]):
                size = part.shape[2]
                out_ref[which, at : at + size] = part[which, f]
                at += size


def distances(high, wide, span, frames):
    row_at, col_at = tile_place()
    cells = high * wide
    count = frames * (cells + span * (wide + high + span))
    j = lax.broadcasted_iota(jnp.int32, (1, count), 1)
    y_off = jnp.where(row_at == 0, high, -span)
    x_off = jnp.where(col_at == 0, wide, -span)
    c = j % cells
    ky, kx = c // wide, c % wide
    base = frames * cells
    c = (j - base) % (span * wide)
    ky = jnp.where(j >= base, y_off + c // wide, ky)
    kx = jnp.where(j >= base, c % wide, kx)
    base += frames * span * wide
    c = (j - base) % (span * high)
    ky = jnp.where(j >= base, c // span, ky)
    kx = jnp.where(j >= base, x_off + c % span, kx)
    base += frames * span * high
    c = (j - base) % (span * span)
    ky = jnp.where(j >= base, y_off + c // span, ky)
    kx = jnp.where(j >= base, x_off + c % span, kx)
    i = lax.broadcasted_iota(jnp.int32, (cells, 1), 0)
    return jnp.maximum(jnp.abs(i // wide - ky), jnp.abs(i % wide - kx))


def attend(q, pieces, factor, before):
    scores = []
    m = before
    for k, v, dist, reach in pieces:
        s = lax.dot_general(q, k, (((1,), (1,)), ((), ())), preferred_element_type=jnp.float32)
        s = jnp.where(dist <= reach, s * factor, FAR)
        top = jnp.max(s, axis=1, keepdims=True)
        m = top if m is None else jnp.maximum(m, top)
        scores.append(s)
    total = None
    for s, (k, v, dist, reach) in zip(scores, pieces):
        p = jnp.exp2(s - m).astype(jnp.bfloat16)
        both = jnp.concatenate([v, jnp.ones_like(v)], axis=1)
        got = jnp.dot(p, both, preferred_element_type=jnp.float32)
        total = got if total is None else total + got
    return m, total


def attend_tile(q_ref, tile_ref, dist_ref, reach_of, heads, state, geometry):
    high, wide, span, frames, head_dim, factor, step = geometry
    cells = high * wide
    acc_ref, sum_ref, max_ref = state
    for at, head in enumerate(heads):
        cols = slice(head * head_dim, (head + 1) * head_dim)
        outs = slice(at * head_dim, (at + 1) * head_dim)
        for start in range(0, q_ref.shape[0], step):
            rows = slice(start, start + step)
            near = dist_ref[start % cells : start % cells + step, : tile_ref.shape[1]]
            piece = (tile_ref[0, :, cols], tile_ref[1, :, cols], near, reach_of(head))
            m, got = attend(q_ref[rows, cols], [piece], factor, None)
            acc_ref[rows, outs] = got[:, :head_dim]
            sum_ref[rows, outs] = got[:, head_dim:]
            max_ref[rows, outs] = jnp.broadcast_to(m, (step, head_dim))


def begin_kernel(radius_ref, mask_ref, q_ref, tile_ref, *outs, geometry, heads):
    *state, dist_ref, reach_ref = outs
    high, wide, span, frames = geometry[:4]
    dist_ref[...] = distances(high, wide, span, frames)
    stretch_at = lax.axis_index("tm")
    line = (1, reach_ref.shape[1])
    for head in range(heads):
        radius = radius_ref[head]
        seen = mask_ref[stretch_at, 0, head] > 0
        reach_ref[head : head + 1] = jnp.full(line, radius, jnp.int32)
        reach_ref[heads + head : heads + head + 1] = jnp.full(
            line, jnp.where(seen, radius, -1), jnp.int32
        )
    attend_tile(q_ref, tile_ref, dist_ref, lambda h: radius_ref[h], (0,), state, geometry)


def tile_kernel(q_ref, tile_ref, dist_ref, reach_ref, *state, geometry, heads):
    attend_tile(
        q_ref,
        tile_ref,
        dist_ref,
        lambda h: reach_ref[h : h + 1, :1],
        range(1, heads),
        state,
        geometry,
    )


def pick_state(head_state, state, head, rows, head_dim):
    refs = head_state if head == 0 else state
    at = max(head - 1, 0) * head_dim
    return [ref[rows, at : at + head_dim] for ref in refs]


def merge(q, pieces, factor, old):
    old_acc, old_total, old_max = old
    m, got = attend(q, pieces, factor, old_max[:, :1])
    shrink = jnp.exp2(old_max - m)
    head_dim = old_acc.shape[1]
    acc = old_acc * shrink + got[:, :head_dim]
    total = old_total * shrink + got[:, head_dim:]
    return acc, total, jnp.broadcast_to(m, old_max.shape)


def rest_kernel(
    q_ref,
    edge_ref,
    first_tile_ref,
    first_edge_ref,
    *rest,
    geometry,
    heads,
    flips,
):
    head_state, dist_ref, reach_ref, state, outs = rest[:3], rest[3], rest[4], rest[5:8], rest[8:]
    high, wide, span, frames, head_dim, factor, step = geometry
    cells = high * wide
    base = frames * cells
    head_at = lax.axis_index("head")
    stretch_at = lax.axis_index("tm")

    def run(with_first):
        for flip, out_ref in zip(flips, outs):
            start = pl.multiple_of(jnp.bitwise_xor(head_at, flip) * step, step)
            rows = pl.ds(start, step)
            near = dist_ref[pl.ds(pl.multiple_of(lax.rem(start, cells), step), step)]
            beyond = near[:, base:]
            for head in range(heads):
                cols = slice(head * head_dim, (head + 1) * head_dim)
                sources = [(edge_ref, beyond, head)]
                if with_first:
                    sources.append((first_tile_ref, near[:, :base], heads + head))
                    sources.append((first_edge_ref, beyond, heads + head))
                pieces = [
                    (ref[0, :, cols], ref[1, :, cols], dist, reach_ref[row : row + 1, :1])
                    for ref, dist, row in sources
                ]
                old = pick_state(head_state, state, head, rows, head_dim)
                acc, total, m = merge(q_ref[rows, cols], pieces, factor, old)
                out_ref[:, cols] = (acc / total).astype(jnp.bfloat16)

    @pl.when(stretch_at > 0)
    def _():
        run(True)

    @pl.when(stretch_at == 0)
    def _():
        run(False)


def copy_kernel(in_ref, out_ref):
    out_ref[...] = in_ref[...]


def stack_kernel(*refs):
    *parts, out_ref = refs
    tile_at = lax.axis_index("tile")
    for flip, part in enumerate(parts):
        tall = part.shape[0]
        top = pl.multiple_of(jnp.bitwise_xor(tile_at, flip) * tall, 16)
        out_ref[pl.ds(top, tall)] = part[...]


def project_kernel(w_ref, part_ref, own_ref, got_ref, out_ref, *, flip):
    broad = part_ref.shape[1]
    half = jnp.bitwise_xor(lax.axis_index("tm"), flip)
    cols = pl.ds(pl.multiple_of(half * broad, 128), broad)
    total = jnp.dot(own_ref[...], w_ref[:, cols], preferred_element_type=jnp.float32)
    total += jnp.dot(got_ref[...], part_ref[...], preferred_element_type=jnp.float32)
    out_ref[...] = total.astype(out_ref.dtype)


def add_kernel(mine_ref, got_ref, *rest, flip):
    out_ref, sum_ref, sems = rest[-3:]
    pieces, tall, broad = sum_ref.shape
    half = jnp.bitwise_xor(lax.axis_index("tm"), flip)
    cols = pl.ds(pl.multiple_of(half * broad, 128), broad)
    copies = []
    for i in range(pieces):
        rows = slice(i * tall, (i + 1) * tall)
        sum_ref[i] = (mine_ref[rows] + got_ref[rows].astype(jnp.float32)).astype(jnp.bfloat16)
        copies.append(pltpu.make_async_copy(sum_ref.at[i], out_ref.at[rows, cols], sems.at[i]))
        copies[-1].start()
    for copy in copies:
        copy.wait()


def two_by_two(query, keys, values, out_weight, radius, block_mask):
    span = RMAX
    frames, high, wide, channels = query.shape[2:]
    heads = radius.shape[0]
    head_dim = channels // heads
    cells = high * wide
    tokens = frames * cells
    groups = lax.axis_size("head")
    tiles = lax.axis_size("tile")
    depth, width = out_weight.shape
    step = tokens // groups
    geometry = (high, wide, span, frames, head_dim, LOG2E / math.sqrt(head_dim), step)
    count = frames * (cells + span * (wide + high + span))
    smem = pl.BlockSpec(memory_space=pltpu.SMEM)
    vmem = pl.BlockSpec(memory_space=pltpu.VMEM)
    hbm = pl.BlockSpec(memory_space=pltpu.HBM)
    bf16, f32 = jnp.bfloat16, jnp.float32
    shape = jax.ShapeDtypeStruct

    def call(kernel, out_shape, specs, *args, name, scratch=(), flops=0, **keys_of):
        return pl.pallas_call(
            functools.partial(kernel, **keys_of) if keys_of else kernel,
            out_shape=out_shape,
            in_specs=specs,
            out_specs=jax.tree.map(lambda _: vmem, out_shape),
            scratch_shapes=scratch,
            cost_estimate=pl.CostEstimate(flops=flops, bytes_accessed=0, transcendentals=0),
            compiler_params=pltpu.CompilerParams(vmem_limit_bytes=VMEM_LIMIT),
            name=name,
        )(*args)

    def flipped(value, axis, flip):
        return lax.ppermute(value, axis, [(i, i ^ flip) for i in range(lax.axis_size(axis))])

    q = query.reshape(tokens, channels)
    k = keys.reshape(tokens, channels)
    v = values.reshape(tokens, channels)

    tall, broad = depth // tiles, width // 2
    part_shape = shape((tall, broad), bf16)
    k, v, far_weight = (
        pltpu.with_memory_space_constraint(x, pltpu.HBM) for x in (k, v, out_weight)
    )
    part = call(
        part_kernel,
        part_shape,
        [hbm],
        far_weight,
        name="part",
        scratch=[pltpu.SemaphoreType.DMA],
    )
    *faces, tile = call(
        face_kernel,
        [
            shape((2, frames, span * wide, channels), bf16),
            shape((2, frames, span * high, channels), bf16),
            shape((2, frames, span * span, channels), bf16),
            shape((2, tokens, channels), bf16),
        ],
        [hbm] * 2 + [vmem],
        k,
        v,
        part,
        name="faces",
        scratch=[pltpu.SemaphoreType.DMA((2,))],
        geometry=geometry,
    )
    faces = [flipped(face, "tile", flip) for face, flip in zip(faces, (2, 1, 3))]
    lone = flipped(part, "head", 2)
    begun = call(
        begin_kernel,
        [shape((tokens, head_dim), f32)] * 3
        + [shape((cells, count), jnp.int32), shape((2 * heads, head_dim), jnp.int32)],
        [smem] * 2 + [vmem] * 2,
        radius,
        block_mask.transpose(1, 2, 0),
        q,
        tile,
        name="begin",
        geometry=geometry,
        heads=heads,
    )
    begun, tile = lax.optimization_barrier((begun, tile))
    first_tile = lax.ppermute(tile, "tm", [(0, 1)])
    state = call(
        tile_kernel,
        [shape((tokens, channels - head_dim), f32)] * 3,
        [vmem] * 4,
        q,
        tile,
        *begun[3:],
        name="tile",
        geometry=geometry,
        heads=heads,
    )
    lone, state = lax.optimization_barrier((lone, state))
    lone = call(copy_kernel, part_shape, [vmem], lone, name="lone", flops=2 * 10**9)
    lone, state, faces = lax.optimization_barrier((lone, state, faces))
    edge = call(
        edge_kernel, shape((2, count - tokens, channels), bf16), [vmem] * 3, *faces, name="edges", flops=20 * 10**9
    )
    first_edge = lax.ppermute(edge, "tm", [(0, 1)])
    parts = [lone] + [flipped(lone, "tile", flip) for flip in range(1, tiles)]

    def rest(state, *flips, flops=0):
        return call(
            rest_kernel,
            [shape((step, channels), bf16)] * len(flips),
            [vmem] * 12,
            q,
            edge,
            first_tile,
            first_edge,
            *begun,
            *state,
            name="rest",
            geometry=geometry,
            heads=heads,
            flips=flips,
            flops=flops,
        )

    (for_side,) = rest(state, 3)
    got_side = flipped(for_side, "head", 2)
    state, for_side = lax.optimization_barrier((state, for_side))
    for_far, own_side = rest(state, 2, 1)
    got_far = flipped(for_far, "head", 2)
    parts, own_side = lax.optimization_barrier((parts[::-1], own_side))
    parts = parts[::-1]
    here = call(
        stack_kernel, shape((depth, broad), bf16), [vmem] * tiles, *parts, name="stack"
    )

    def project(part, mine, got, kind, flip, flops=0):
        return call(
            project_kernel,
            shape((step, broad), kind),
            [vmem] * 4,
            out_weight,
            part,
            mine,
            got,
            name="project",
            flops=flops,
            flip=flip,
        )

    for_side = [project(here, own_side, got_side, bf16, 0, 20 * 10**9)]
    from_side = [flipped(for_side[0], "head", 1)]
    state, here, for_side[0] = lax.optimization_barrier((state, here, for_side[0]))
    there = flipped(here, "tm", 1)
    (own,) = rest(state, 0, flops=20 * 10**9)
    own_side, own = lax.optimization_barrier((own_side, own))
    for_side.append(project(there, own_side, got_side, bf16, 1))
    from_side.append(flipped(for_side[1], "head", 1))
    own, for_side[1] = lax.optimization_barrier((own, for_side[1]))
    mine = [
        project(here, own, got_far, f32, 0),
        project(there, own, got_far, f32, 1, 20 * 10**9),
    ]
    pieces = 2
    mixed = []
    for flip in range(2):
        mixed = [
            pl.pallas_call(
                functools.partial(add_kernel, flip=flip),
                out_shape=shape((step, width), bf16),
                in_specs=[vmem] * 2 + [hbm] * flip,
                out_specs=hbm,
                input_output_aliases={2: 0} if flip else {},
                scratch_shapes=[
                    pltpu.VMEM((pieces, step // pieces, broad), bf16),
                    pltpu.SemaphoreType.DMA((pieces,)),
                ],
                compiler_params=pltpu.CompilerParams(vmem_limit_bytes=VMEM_LIMIT),
                name="add",
            )(mine[flip], from_side[flip], *mixed)
        ]
    (mixed,) = mixed
    return mixed.reshape(1, 1, step, width)


def solution(mesh):
    in_specs = (
        P("tm", "tile", None, None, None, "head"),
        P("tm", "tile", None, None, None, "head"),
        P("tm", "tile", None, None, None, "head"),
        P("head", None),
        P("head"),
        P("head", None, None),
    )
    out_specs = P("tm", "tile", "head", None)
    small = dict(mesh.shape) == {"tm": 2, "tile": 4, "head": 4}
    return jax.shard_map(
        two_by_two if small else any_grid,
        mesh=mesh,
        in_specs=in_specs,
        out_specs=out_specs,
        check_vma=False,
    )
```

```python
import functools
import math

import jax
import jax.numpy as jnp
from jax import lax
from jax.experimental import pallas as pl
from jax.experimental.pallas import tpu as pltpu
from jax.sharding import PartitionSpec as P

RMAX = 4
FAR = -1e30
LOG2E = 1.4426950408889634
VMEM_LIMIT = 24 * 1024 * 1024


def passed_along(value, axis, by):
    peers = lax.axis_size(axis)
    pairs = [(i, i + by) for i in range(peers) if 0 <= i + by < peers]
    return lax.ppermute(value, axis, pairs)


def widen(key_part, value_part, span, row_move, col_move):
    grid = math.isqrt(lax.axis_size("tile"))
    above = None
    below = None
    for offset in (grid, -grid):
        if offset > 0:
            face_key = key_part[:, :, key_part.shape[2] - span :]
            face_value = value_part[:, :, value_part.shape[2] - span :]
        else:
            face_key = key_part[:, :, :span]
            face_value = value_part[:, :, :span]
        got = row_move(face_key, face_value, offset)
        if offset > 0:
            above = got
        else:
            below = got
    key_rows = jnp.concatenate([above[0], key_part, below[0]], axis=2)
    value_rows = jnp.concatenate([above[1], value_part, below[1]], axis=2)
    left = None
    right = None
    for offset in (1, -1):
        if offset > 0:
            face_key = key_rows[:, :, :, key_rows.shape[3] - span :]
            face_value = value_rows[:, :, :, value_rows.shape[3] - span :]
        else:
            face_key = key_rows[:, :, :, :span]
            face_value = value_rows[:, :, :, :span]
        got = col_move(face_key, face_value, offset)
        if offset > 0:
            left = got
        else:
            right = got
    key_full = jnp.concatenate([left[0], key_rows, right[0]], axis=3)
    value_full = jnp.concatenate([left[1], value_rows, right[1]], axis=3)
    return (key_full, value_full)


def windows_of(block, half_high, half_wide, win_high, win_wide, heads_here, head_dim):
    parts = []
    for band in (0, 1):
        for strip in (0, 1):
            parts.append(
                block[
                    :,
                    band * half_high : band * half_high + win_high,
                    strip * half_wide : strip * half_wide + win_wide,
                ]
            )
    stacked = jnp.stack(parts)
    return stacked.reshape(4, -1, heads_here, head_dim)


def any_grid(query, keys, values, out_weight, radius, block_mask):
    span = RMAX
    grid = math.isqrt(lax.axis_size("tile"))
    tile_at = lax.axis_index("tile")
    row_at = tile_at // grid
    col_at = tile_at % grid
    stretch_at = lax.axis_index("tm")
    frames, high, wide, channels = query.shape[2:]
    heads_here = radius.shape[0]
    head_dim = channels // heads_here
    tokens_here = frames * high * wide
    half_high = high // 2
    half_wide = wide // 2
    win_high = half_high + 2 * span
    win_wide = half_wide + 2 * span
    quarter = frames * half_high * half_wide
    queries = query[0, 0].reshape(frames, 2, half_high, 2, half_wide, channels)
    queries = queries.transpose(1, 3, 0, 2, 4, 5).reshape(4, quarter, heads_here, head_dim)
    query_y = jnp.broadcast_to(
        jnp.arange(half_high, dtype=jnp.int32)[None, :, None], (frames, half_high, half_wide)
    ).reshape(-1)
    query_x = jnp.broadcast_to(
        jnp.arange(half_wide, dtype=jnp.int32)[None, None, :], (frames, half_high, half_wide)
    ).reshape(-1)
    key_y = jnp.broadcast_to(
        jnp.arange(win_high, dtype=jnp.int32)[None, :, None] - span, (frames, win_high, win_wide)
    ).reshape(-1)
    key_x = jnp.broadcast_to(
        jnp.arange(win_wide, dtype=jnp.int32)[None, None, :] - span, (frames, win_high, win_wide)
    ).reshape(-1)
    band_at = jnp.array([0, 0, 1, 1], dtype=jnp.int32)
    strip_at = jnp.array([0, 1, 0, 1], dtype=jnp.int32)
    global_y = row_at * high + band_at[:, None] * half_high + key_y[None, :]
    global_x = col_at * wide + strip_at[:, None] * half_wide + key_x[None, :]
    inside = (global_y >= 0) & (global_y < grid * high) & (global_x >= 0) & (global_x < grid * wide)
    distance = jnp.maximum(
        jnp.abs(query_y[:, None] - key_y[None, :]), jnp.abs(query_x[:, None] - key_x[None, :])
    )
    near = distance[None, :, :] <= radius[:, None, None]
    allowed = near[None, :, :, :] & inside[:, None, None, :]
    scale = 1.0 / math.sqrt(head_dim)
    initial = (
        jnp.full((4, heads_here, quarter), -1e30, jnp.float32),
        jnp.zeros((4, heads_here, quarter), jnp.float32),
        jnp.zeros((4, heads_here, quarter, head_dim), jnp.float32),
    )

    def tile_move(face_key, face_value, offset):
        return passed_along((face_key, face_value), "tile", offset)

    key_all, value_all = (
        lax.all_gather(keys[0], "tm", axis=0, tiled=True),
        lax.all_gather(values[0], "tm", axis=0, tiled=True),
    )
    key_full, value_full = widen(key_all, value_all, span, tile_move, tile_move)
    stretch_ids = jnp.arange(key_full.shape[0], dtype=jnp.int32)

    def one_stretch(state, item):
        key_block, value_block, stretch_id = item
        visible = (
            lax.dynamic_slice_in_dim(
                lax.dynamic_index_in_dim(block_mask, stretch_at, 1, False), stretch_id, 1, 1
            )[:, 0]
            > 0
        )
        best, total, acc = state
        key_win = windows_of(
            key_block, half_high, half_wide, win_high, win_wide, heads_here, head_dim
        )
        value_win = windows_of(
            value_block, half_high, half_wide, win_high, win_wide, heads_here, head_dim
        )
        usable = allowed & visible[None, :, None, None]
        scores = (
            jnp.einsum("nqhd,nkhd->nhqk", queries, key_win, preferred_element_type=jnp.float32)
            * scale
        )
        masked = jnp.where(usable, scores, jnp.float32(-1e30))
        fresh = jnp.maximum(best, jnp.max(masked, axis=3))
        probs = jnp.where(usable, jnp.exp(scores - fresh[..., None]), jnp.float32(0.0))
        shrink = jnp.exp(best - fresh)
        total = total * shrink + jnp.sum(probs, axis=3)
        acc = acc * shrink[..., None] + jnp.einsum(
            "nhqk,nkhd->nhqd",
            probs.astype(jnp.bfloat16),
            value_win,
            preferred_element_type=jnp.float32,
        )
        return ((fresh, total, acc), None)

    final, unused = lax.scan(one_stretch, initial, (key_full, value_full, stretch_ids))
    best, total, acc = final
    attn = (acc / total[..., None]).astype(jnp.bfloat16)
    attn = attn.transpose(0, 2, 1, 3).reshape(
        2, 2, frames, half_high, half_wide, heads_here * head_dim
    )
    attn = attn.transpose(2, 0, 3, 1, 4, 5).reshape(tokens_here, heads_here * head_dim)
    mixed = lax.psum_scatter(
        jnp.dot(attn, out_weight, preferred_element_type=jnp.float32).astype(jnp.bfloat16),
        "head",
        scatter_dimension=0,
        tiled=True,
    )
    return mixed.reshape(1, 1, -1, out_weight.shape[1])


def tile_place():
    tile_at = lax.axis_index("tile")
    return tile_at // 2, tile_at % 2


def load_kernel(k_ref, v_ref, w_ref, tile_ref, part_ref, sems):
    tall, broad = part_ref.shape
    top = pl.multiple_of(lax.axis_index("tile") * tall, 16)
    left = pl.multiple_of(lax.axis_index("tm") * broad, 128)
    copies = [
        pltpu.make_async_copy(
            w_ref.at[pl.ds(top, tall), pl.ds(left, broad)], part_ref, sems.at[2]
        )
    ]
    for which, ref in enumerate((k_ref, v_ref)):
        copies.append(pltpu.make_async_copy(ref, tile_ref.at[which], sems.at[which]))
    for copy in copies:
        copy.start()
    for copy in copies:
        copy.wait()


def face_kernel(tile_ref, row_ref, col_ref, corner_ref, *, geometry):
    high, wide, span, frames = geometry[:4]
    cells = high * wide
    row_at, col_at = tile_place()
    y0 = jnp.where(row_at == 0, high - span, 0)
    x0 = jnp.where(col_at == 0, wide - span, 0)

    def picker(count, cell_of):
        row = lax.broadcasted_iota(jnp.int32, (count, cells), 0)
        col = lax.broadcasted_iota(jnp.int32, (count, cells), 1)
        return (col == cell_of(row)).astype(jnp.bfloat16)

    beside = picker(high * span, lambda i: (i // span) * wide + x0 + i % span)
    across = picker(span * span, lambda i: (y0 + i // span) * wide + x0 + i % span)
    for which in range(2):
        for f in range(frames):
            start = pl.multiple_of(f * cells + y0 * wide, 16)
            row_ref[which, f] = tile_ref[which, pl.ds(start, span * wide)]
            whole = tile_ref[which, f * cells : (f + 1) * cells]
            col_ref[which, f] = jnp.dot(
                beside, whole, preferred_element_type=jnp.float32
            ).astype(jnp.bfloat16)
            corner_ref[which, f] = jnp.dot(
                across, whole, preferred_element_type=jnp.float32
            ).astype(jnp.bfloat16)


def edge_kernel(row_ref, col_ref, corner_ref, out_ref):
    for which in range(2):
        at = 0
        for part in (row_ref, col_ref, corner_ref):
            for f in range(part.shape[1]):
                size = part.shape[2]
                out_ref[which, at : at + size] = part[which, f]
                at += size


def distances(high, wide, span, frames):
    row_at, col_at = tile_place()
    cells = high * wide
    count = frames * (cells + span * (wide + high + span))
    j = lax.broadcasted_iota(jnp.int32, (1, count), 1)
    y_off = jnp.where(row_at == 0, high, -span)
    x_off = jnp.where(col_at == 0, wide, -span)
    c = j % cells
    ky, kx = c // wide, c % wide
    base = frames * cells
    c = (j - base) % (span * wide)
    ky = jnp.where(j >= base, y_off + c // wide, ky)
    kx = jnp.where(j >= base, c % wide, kx)
    base += frames * span * wide
    c = (j - base) % (span * high)
    ky = jnp.where(j >= base, c // span, ky)
    kx = jnp.where(j >= base, x_off + c % span, kx)
    base += frames * span * high
    c = (j - base) % (span * span)
    ky = jnp.where(j >= base, y_off + c // span, ky)
    kx = jnp.where(j >= base, x_off + c % span, kx)
    i = lax.broadcasted_iota(jnp.int32, (cells, 1), 0)
    return jnp.maximum(jnp.abs(i // wide - ky), jnp.abs(i % wide - kx))


def attend(units, factor):
    scores = [
        [
            jnp.where(
                dist <= reach,
                lax.dot_general(
                    q, k, (((1,), (1,)), ((), ())), preferred_element_type=jnp.float32
                )
                * factor,
                FAR,
            )
            for k, v, dist, reach in pieces
        ]
        for q, pieces, before in units
    ]
    tops = []
    for parts, (q, pieces, before) in zip(scores, units):
        found = [jnp.max(s, axis=1, keepdims=True) for s in parts]
        if before is not None:
            found.append(before)
        tops.append(functools.reduce(jnp.maximum, found))
    probs = [
        [jnp.exp2(s - m).astype(jnp.bfloat16) for s in parts] for parts, m in zip(scores, tops)
    ]
    sums = []
    for parts, (q, pieces, before) in zip(probs, units):
        total = None
        for p, (k, v, dist, reach) in zip(parts, pieces):
            both = jnp.concatenate([v, jnp.ones_like(v)], axis=1)
            got = jnp.dot(p, both, preferred_element_type=jnp.float32)
            total = got if total is None else total + got
        sums.append(total)
    return tops, sums


def attend_tile(q_ref, tile_ref, dist_ref, reach_of, heads, state, geometry):
    high, wide, span, frames, head_dim, factor, step = geometry
    cells = high * wide
    acc_ref, sum_ref, max_ref = state
    for at, head in enumerate(heads):
        cols = slice(head * head_dim, (head + 1) * head_dim)
        outs = slice(at * head_dim, (at + 1) * head_dim)
        starts = range(0, q_ref.shape[0], step)
        units = []
        for start in starts:
            near = dist_ref[start % cells : start % cells + step, : tile_ref.shape[1]]
            piece = (tile_ref[0, :, cols], tile_ref[1, :, cols], near, reach_of(head))
            units.append((q_ref[start : start + step, cols], [piece], None))
        for start, m, got in zip(starts, *attend(units, factor)):
            rows = slice(start, start + step)
            acc_ref[rows, outs] = got[:, :head_dim]
            sum_ref[rows, outs] = got[:, head_dim:]
            max_ref[rows, outs] = jnp.broadcast_to(m, (step, head_dim))


def begin_kernel(radius_ref, mask_ref, q_ref, tile_ref, *outs, geometry, heads):
    *state, dist_ref, reach_ref = outs
    high, wide, span, frames = geometry[:4]
    dist_ref[...] = distances(high, wide, span, frames)
    stretch_at = lax.axis_index("tm")
    line = (1, reach_ref.shape[1])
    for head in range(heads):
        radius = radius_ref[head]
        seen = mask_ref[stretch_at, 0, head] > 0
        reach_ref[head : head + 1] = jnp.full(line, radius, jnp.int32)
        reach_ref[heads + head : heads + head + 1] = jnp.full(
            line, jnp.where(seen, radius, -1), jnp.int32
        )
    attend_tile(q_ref, tile_ref, dist_ref, lambda h: radius_ref[h], (0,), state, geometry)


def tile_kernel(q_ref, tile_ref, dist_ref, reach_ref, *state, geometry, heads):
    attend_tile(
        q_ref,
        tile_ref,
        dist_ref,
        lambda h: reach_ref[h : h + 1, :1],
        range(1, heads),
        state,
        geometry,
    )


def pick_state(head_state, state, head, rows, head_dim):
    refs = head_state if head == 0 else state
    at = max(head - 1, 0) * head_dim
    return [ref[rows, at : at + head_dim] for ref in refs]


def rest_kernel(
    q_ref,
    edge_ref,
    first_tile_ref,
    first_edge_ref,
    *rest,
    geometry,
    heads,
    flips,
):
    head_state, dist_ref, reach_ref, state, outs = rest[:3], rest[3], rest[4], rest[5:8], rest[8:]
    high, wide, span, frames, head_dim, factor, step = geometry
    cells = high * wide
    base = frames * cells
    head_at = lax.axis_index("head")
    stretch_at = lax.axis_index("tm")

    def run(with_first):
        for flip, out_ref in zip(flips, outs):
            start = pl.multiple_of(jnp.bitwise_xor(head_at, flip) * step, step)
            rows = pl.ds(start, step)
            near = dist_ref[pl.ds(pl.multiple_of(lax.rem(start, cells), step), step)]
            beyond = near[:, base:]
            units = []
            olds = []
            for head in range(heads):
                cols = slice(head * head_dim, (head + 1) * head_dim)
                sources = [(edge_ref, beyond, head)]
                if with_first:
                    sources.append((first_tile_ref, near[:, :base], heads + head))
                    sources.append((first_edge_ref, beyond, heads + head))
                pieces = [
                    (ref[0, :, cols], ref[1, :, cols], dist, reach_ref[row : row + 1, :1])
                    for ref, dist, row in sources
                ]
                olds.append(pick_state(head_state, state, head, rows, head_dim))
                units.append((q_ref[rows, cols], pieces, olds[-1][2][:, :1]))
            for head, (m, got) in enumerate(zip(*attend(units, factor))):
                old_acc, old_total, old_max = olds[head]
                shrink = jnp.exp2(old_max - m)
                acc = old_acc * shrink + got[:, :head_dim]
                total = old_total * shrink + got[:, head_dim:]
                cols = slice(head * head_dim, (head + 1) * head_dim)
                out_ref[:, cols] = (acc / total).astype(jnp.bfloat16)

    @pl.when(stretch_at > 0)
    def _():
        run(True)

    @pl.when(stretch_at == 0)
    def _():
        run(False)


def copy_kernel(in_ref, out_ref):
    out_ref[...] = in_ref[...]


def stack_kernel(*refs):
    *parts, out_ref = refs
    tile_at = lax.axis_index("tile")
    for flip, part in enumerate(parts):
        tall = part.shape[0]
        top = pl.multiple_of(jnp.bitwise_xor(tile_at, flip) * tall, 16)
        out_ref[pl.ds(top, tall)] = part[...]


def project_kernel(w_ref, part_ref, own_ref, got_ref, out_ref, *, flip):
    broad = part_ref.shape[1]
    half = jnp.bitwise_xor(lax.axis_index("tm"), flip)
    cols = pl.ds(pl.multiple_of(half * broad, 128), broad)
    total = jnp.dot(own_ref[...], w_ref[:, cols], preferred_element_type=jnp.float32)
    total += jnp.dot(got_ref[...], part_ref[...], preferred_element_type=jnp.float32)
    out_ref[...] = total.astype(out_ref.dtype)


def add_kernel(mine_ref, got_ref, *rest, flip):
    out_ref, sum_ref, sems = rest[-3:]
    pieces, tall, broad = sum_ref.shape
    half = jnp.bitwise_xor(lax.axis_index("tm"), flip)
    cols = pl.ds(pl.multiple_of(half * broad, 128), broad)
    copies = []
    for i in range(pieces):
        rows = slice(i * tall, (i + 1) * tall)
        sum_ref[i] = (mine_ref[rows] + got_ref[rows].astype(jnp.float32)).astype(jnp.bfloat16)
        copies.append(pltpu.make_async_copy(sum_ref.at[i], out_ref.at[rows, cols], sems.at[i]))
        copies[-1].start()
    for copy in copies:
        copy.wait()


def two_by_two(query, keys, values, out_weight, radius, block_mask):
    span = RMAX
    frames, high, wide, channels = query.shape[2:]
    heads = radius.shape[0]
    head_dim = channels // heads
    cells = high * wide
    tokens = frames * cells
    groups = lax.axis_size("head")
    tiles = lax.axis_size("tile")
    depth, width = out_weight.shape
    step = tokens // groups
    geometry = (high, wide, span, frames, head_dim, LOG2E / math.sqrt(head_dim), step)
    count = frames * (cells + span * (wide + high + span))
    smem = pl.BlockSpec(memory_space=pltpu.SMEM)
    vmem = pl.BlockSpec(memory_space=pltpu.VMEM)
    hbm = pl.BlockSpec(memory_space=pltpu.HBM)
    bf16, f32 = jnp.bfloat16, jnp.float32
    shape = jax.ShapeDtypeStruct

    def call(kernel, out_shape, specs, *args, name, scratch=(), flops=0, **keys_of):
        return pl.pallas_call(
            functools.partial(kernel, **keys_of) if keys_of else kernel,
            out_shape=out_shape,
            in_specs=specs,
            out_specs=jax.tree.map(lambda _: vmem, out_shape),
            scratch_shapes=scratch,
            cost_estimate=pl.CostEstimate(flops=flops, bytes_accessed=0, transcendentals=0),
            compiler_params=pltpu.CompilerParams(vmem_limit_bytes=VMEM_LIMIT),
            name=name,
        )(*args)

    def flipped(value, axis, flip):
        return lax.ppermute(value, axis, [(i, i ^ flip) for i in range(lax.axis_size(axis))])

    q = query.reshape(tokens, channels)
    k = keys.reshape(tokens, channels)
    v = values.reshape(tokens, channels)

    tall, broad = depth // tiles, width // 2
    part_shape = shape((tall, broad), bf16)
    tile, part = call(
        load_kernel,
        [shape((2, tokens, channels), bf16), part_shape],
        [hbm] * 3,
        *[pltpu.with_memory_space_constraint(x, pltpu.HBM) for x in (k, v, out_weight)],
        name="load",
        scratch=[pltpu.SemaphoreType.DMA((3,))],
    )
    faces = call(
        face_kernel,
        [
            shape((2, frames, span * wide, channels), bf16),
            shape((2, frames, span * high, channels), bf16),
            shape((2, frames, span * span, channels), bf16),
        ],
        [vmem],
        tile,
        name="faces",
        geometry=geometry,
    )
    faces = [flipped(face, "tile", flip) for face, flip in zip(faces, (2, 1, 3))]
    lone = flipped(part, "head", 2)
    begun = call(
        begin_kernel,
        [shape((tokens, head_dim), f32)] * 3
        + [shape((cells, count), jnp.int32), shape((2 * heads, head_dim), jnp.int32)],
        [smem] * 2 + [vmem] * 2,
        radius,
        block_mask.transpose(1, 2, 0),
        q,
        tile,
        name="begin",
        geometry=geometry,
        heads=heads,
    )
    begun, tile = lax.optimization_barrier((begun, tile))
    first_tile = lax.ppermute(tile, "tm", [(0, 1)])
    state = call(
        tile_kernel,
        [shape((tokens, channels - head_dim), f32)] * 3,
        [vmem] * 4,
        q,
        tile,
        *begun[3:],
        name="tile",
        geometry=geometry,
        heads=heads,
    )
    lone, state = lax.optimization_barrier((lone, state))
    lone = call(copy_kernel, part_shape, [vmem], lone, name="lone", flops=2 * 10**9)
    lone, state, faces = lax.optimization_barrier((lone, state, faces))
    edge = call(
        edge_kernel, shape((2, count - tokens, channels), bf16), [vmem] * 3, *faces, name="edges", flops=20 * 10**9
    )
    first_edge = lax.ppermute(edge, "tm", [(0, 1)])
    parts = [lone] + [flipped(lone, "tile", flip) for flip in range(1, tiles)]

    def rest(state, *flips, flops=0):
        return call(
            rest_kernel,
            [shape((step, channels), bf16)] * len(flips),
            [vmem] * 12,
            q,
            edge,
            first_tile,
            first_edge,
            *begun,
            *state,
            name="rest",
            geometry=geometry,
            heads=heads,
            flips=flips,
            flops=flops,
        )

    (for_side,) = rest(state, 3)
    got_side = flipped(for_side, "head", 2)
    state, for_side = lax.optimization_barrier((state, for_side))
    for_far, own_side = rest(state, 2, 1)
    got_far = flipped(for_far, "head", 2)
    parts, own_side = lax.optimization_barrier((parts, own_side))
    here = call(
        stack_kernel, shape((depth, broad), bf16), [vmem] * tiles, *parts, name="stack"
    )

    def project(part, mine, got, kind, flip, flops=0):
        return call(
            project_kernel,
            shape((step, broad), kind),
            [vmem] * 4,
            out_weight,
            part,
            mine,
            got,
            name="project",
            flops=flops,
            flip=flip,
        )

    for_side = [project(here, own_side, got_side, bf16, 0, 20 * 10**9)]
    from_side = [flipped(for_side[0], "head", 1)]
    state, here, for_side[0] = lax.optimization_barrier((state, here, for_side[0]))
    there = flipped(here, "tm", 1)
    (own,) = rest(state, 0, flops=20 * 10**9)
    own_side, own = lax.optimization_barrier((own_side, own))
    for_side.append(project(there, own_side, got_side, bf16, 1))
    from_side.append(flipped(for_side[1], "head", 1))
    own, for_side[1] = lax.optimization_barrier((own, for_side[1]))
    mine = [
        project(here, own, got_far, f32, 0),
        project(there, own, got_far, f32, 1, 20 * 10**9),
    ]
    pieces = 2
    mixed = []
    for flip in range(2):
        mixed = [
            pl.pallas_call(
                functools.partial(add_kernel, flip=flip),
                out_shape=shape((step, width), bf16),
                in_specs=[vmem] * 2 + [hbm] * flip,
                out_specs=hbm,
                input_output_aliases={2: 0} if flip else {},
                scratch_shapes=[
                    pltpu.VMEM((pieces, step // pieces, broad), bf16),
                    pltpu.SemaphoreType.DMA((pieces,)),
                ],
                compiler_params=pltpu.CompilerParams(vmem_limit_bytes=VMEM_LIMIT),
                name="add",
            )(mine[flip], from_side[flip], *mixed)
        ]
    (mixed,) = mixed
    return mixed.reshape(1, 1, step, width)


def solution(mesh):
    in_specs = (
        P("tm", "tile", None, None, None, "head"),
        P("tm", "tile", None, None, None, "head"),
        P("tm", "tile", None, None, None, "head"),
        P("head", None),
        P("head"),
        P("head", None, None),
    )
    out_specs = P("tm", "tile", "head", None)
    small = dict(mesh.shape) == {"tm": 2, "tile": 4, "head": 4}
    return jax.shard_map(
        two_by_two if small else any_grid,
        mesh=mesh,
        in_specs=in_specs,
        out_specs=out_specs,
        check_vma=False,
    )
```

```python
import functools
import math

import jax
import jax.numpy as jnp
from jax import lax
from jax.experimental import pallas as pl
from jax.experimental.pallas import tpu as pltpu
from jax.sharding import PartitionSpec as P

RMAX = 4
FAR = -1e30
LOG2E = 1.4426950408889634
VMEM_LIMIT = 24 * 1024 * 1024


def passed_along(value, axis, by):
    peers = lax.axis_size(axis)
    pairs = [(i, i + by) for i in range(peers) if 0 <= i + by < peers]
    return lax.ppermute(value, axis, pairs)


def widen(key_part, value_part, span, row_move, col_move):
    grid = math.isqrt(lax.axis_size("tile"))
    above = None
    below = None
    for offset in (grid, -grid):
        if offset > 0:
            face_key = key_part[:, :, key_part.shape[2] - span :]
            face_value = value_part[:, :, value_part.shape[2] - span :]
        else:
            face_key = key_part[:, :, :span]
            face_value = value_part[:, :, :span]
        got = row_move(face_key, face_value, offset)
        if offset > 0:
            above = got
        else:
            below = got
    key_rows = jnp.concatenate([above[0], key_part, below[0]], axis=2)
    value_rows = jnp.concatenate([above[1], value_part, below[1]], axis=2)
    left = None
    right = None
    for offset in (1, -1):
        if offset > 0:
            face_key = key_rows[:, :, :, key_rows.shape[3] - span :]
            face_value = value_rows[:, :, :, value_rows.shape[3] - span :]
        else:
            face_key = key_rows[:, :, :, :span]
            face_value = value_rows[:, :, :, :span]
        got = col_move(face_key, face_value, offset)
        if offset > 0:
            left = got
        else:
            right = got
    key_full = jnp.concatenate([left[0], key_rows, right[0]], axis=3)
    value_full = jnp.concatenate([left[1], value_rows, right[1]], axis=3)
    return (key_full, value_full)


def windows_of(block, half_high, half_wide, win_high, win_wide, heads_here, head_dim):
    parts = []
    for band in (0, 1):
        for strip in (0, 1):
            parts.append(
                block[
                    :,
                    band * half_high : band * half_high + win_high,
                    strip * half_wide : strip * half_wide + win_wide,
                ]
            )
    stacked = jnp.stack(parts)
    return stacked.reshape(4, -1, heads_here, head_dim)


def any_grid(query, keys, values, out_weight, radius, block_mask):
    span = RMAX
    grid = math.isqrt(lax.axis_size("tile"))
    tile_at = lax.axis_index("tile")
    row_at = tile_at // grid
    col_at = tile_at % grid
    stretch_at = lax.axis_index("tm")
    frames, high, wide, channels = query.shape[2:]
    heads_here = radius.shape[0]
    head_dim = channels // heads_here
    tokens_here = frames * high * wide
    half_high = high // 2
    half_wide = wide // 2
    win_high = half_high + 2 * span
    win_wide = half_wide + 2 * span
    quarter = frames * half_high * half_wide
    queries = query[0, 0].reshape(frames, 2, half_high, 2, half_wide, channels)
    queries = queries.transpose(1, 3, 0, 2, 4, 5).reshape(4, quarter, heads_here, head_dim)
    query_y = jnp.broadcast_to(
        jnp.arange(half_high, dtype=jnp.int32)[None, :, None], (frames, half_high, half_wide)
    ).reshape(-1)
    query_x = jnp.broadcast_to(
        jnp.arange(half_wide, dtype=jnp.int32)[None, None, :], (frames, half_high, half_wide)
    ).reshape(-1)
    key_y = jnp.broadcast_to(
        jnp.arange(win_high, dtype=jnp.int32)[None, :, None] - span, (frames, win_high, win_wide)
    ).reshape(-1)
    key_x = jnp.broadcast_to(
        jnp.arange(win_wide, dtype=jnp.int32)[None, None, :] - span, (frames, win_high, win_wide)
    ).reshape(-1)
    band_at = jnp.array([0, 0, 1, 1], dtype=jnp.int32)
    strip_at = jnp.array([0, 1, 0, 1], dtype=jnp.int32)
    global_y = row_at * high + band_at[:, None] * half_high + key_y[None, :]
    global_x = col_at * wide + strip_at[:, None] * half_wide + key_x[None, :]
    inside = (global_y >= 0) & (global_y < grid * high) & (global_x >= 0) & (global_x < grid * wide)
    distance = jnp.maximum(
        jnp.abs(query_y[:, None] - key_y[None, :]), jnp.abs(query_x[:, None] - key_x[None, :])
    )
    near = distance[None, :, :] <= radius[:, None, None]
    allowed = near[None, :, :, :] & inside[:, None, None, :]
    scale = 1.0 / math.sqrt(head_dim)
    initial = (
        jnp.full((4, heads_here, quarter), -1e30, jnp.float32),
        jnp.zeros((4, heads_here, quarter), jnp.float32),
        jnp.zeros((4, heads_here, quarter, head_dim), jnp.float32),
    )

    def tile_move(face_key, face_value, offset):
        return passed_along((face_key, face_value), "tile", offset)

    key_all, value_all = (
        lax.all_gather(keys[0], "tm", axis=0, tiled=True),
        lax.all_gather(values[0], "tm", axis=0, tiled=True),
    )
    key_full, value_full = widen(key_all, value_all, span, tile_move, tile_move)
    stretch_ids = jnp.arange(key_full.shape[0], dtype=jnp.int32)

    def one_stretch(state, item):
        key_block, value_block, stretch_id = item
        visible = (
            lax.dynamic_slice_in_dim(
                lax.dynamic_index_in_dim(block_mask, stretch_at, 1, False), stretch_id, 1, 1
            )[:, 0]
            > 0
        )
        best, total, acc = state
        key_win = windows_of(
            key_block, half_high, half_wide, win_high, win_wide, heads_here, head_dim
        )
        value_win = windows_of(
            value_block, half_high, half_wide, win_high, win_wide, heads_here, head_dim
        )
        usable = allowed & visible[None, :, None, None]
        scores = (
            jnp.einsum("nqhd,nkhd->nhqk", queries, key_win, preferred_element_type=jnp.float32)
            * scale
        )
        masked = jnp.where(usable, scores, jnp.float32(-1e30))
        fresh = jnp.maximum(best, jnp.max(masked, axis=3))
        probs = jnp.where(usable, jnp.exp(scores - fresh[..., None]), jnp.float32(0.0))
        shrink = jnp.exp(best - fresh)
        total = total * shrink + jnp.sum(probs, axis=3)
        acc = acc * shrink[..., None] + jnp.einsum(
            "nhqk,nkhd->nhqd",
            probs.astype(jnp.bfloat16),
            value_win,
            preferred_element_type=jnp.float32,
        )
        return ((fresh, total, acc), None)

    final, unused = lax.scan(one_stretch, initial, (key_full, value_full, stretch_ids))
    best, total, acc = final
    attn = (acc / total[..., None]).astype(jnp.bfloat16)
    attn = attn.transpose(0, 2, 1, 3).reshape(
        2, 2, frames, half_high, half_wide, heads_here * head_dim
    )
    attn = attn.transpose(2, 0, 3, 1, 4, 5).reshape(tokens_here, heads_here * head_dim)
    mixed = lax.psum_scatter(
        jnp.dot(attn, out_weight, preferred_element_type=jnp.float32).astype(jnp.bfloat16),
        "head",
        scatter_dimension=0,
        tiled=True,
    )
    return mixed.reshape(1, 1, -1, out_weight.shape[1])


def tile_place():
    tile_at = lax.axis_index("tile")
    return tile_at // 2, tile_at % 2


def load_kernel(k_ref, v_ref, w_ref, tile_ref, part_ref, sems):
    tall, broad = part_ref.shape
    top = pl.multiple_of(lax.axis_index("tile") * tall, 16)
    left = pl.multiple_of(lax.axis_index("tm") * broad, 128)
    copies = [
        pltpu.make_async_copy(
            w_ref.at[pl.ds(top, tall), pl.ds(left, broad)], part_ref, sems.at[2]
        )
    ]
    for which, ref in enumerate((k_ref, v_ref)):
        copies.append(pltpu.make_async_copy(ref, tile_ref.at[which], sems.at[which]))
    for copy in copies:
        copy.start()
    for copy in copies:
        copy.wait()


def face_kernel(tile_ref, row_ref, col_ref, corner_ref, *, geometry):
    high, wide, span, frames = geometry[:4]
    cells = high * wide
    row_at, col_at = tile_place()
    y0 = jnp.where(row_at == 0, high - span, 0)
    x0 = jnp.where(col_at == 0, wide - span, 0)

    def picker(count, cell_of):
        row = lax.broadcasted_iota(jnp.int32, (count, cells), 0)
        col = lax.broadcasted_iota(jnp.int32, (count, cells), 1)
        return (col == cell_of(row)).astype(jnp.bfloat16)

    beside = picker(high * span, lambda i: (i // span) * wide + x0 + i % span)
    across = picker(span * span, lambda i: (y0 + i // span) * wide + x0 + i % span)
    for which in range(2):
        for f in range(frames):
            start = pl.multiple_of(f * cells + y0 * wide, 16)
            row_ref[which, f] = tile_ref[which, pl.ds(start, span * wide)]
            whole = tile_ref[which, f * cells : (f + 1) * cells]
            col_ref[which, f] = jnp.dot(
                beside, whole, preferred_element_type=jnp.float32
            ).astype(jnp.bfloat16)
            corner_ref[which, f] = jnp.dot(
                across, whole, preferred_element_type=jnp.float32
            ).astype(jnp.bfloat16)


def edge_kernel(row_ref, col_ref, corner_ref, out_ref):
    for which in range(2):
        at = 0
        for part in (row_ref, col_ref, corner_ref):
            for f in range(part.shape[1]):
                size = part.shape[2]
                out_ref[which, at : at + size] = part[which, f]
                at += size


def distances(high, wide, span, frames):
    row_at, col_at = tile_place()
    cells = high * wide
    count = frames * (cells + span * (wide + high + span))
    j = lax.broadcasted_iota(jnp.int32, (1, count), 1)
    y_off = jnp.where(row_at == 0, high, -span)
    x_off = jnp.where(col_at == 0, wide, -span)
    c = j % cells
    ky, kx = c // wide, c % wide
    base = frames * cells
    c = (j - base) % (span * wide)
    ky = jnp.where(j >= base, y_off + c // wide, ky)
    kx = jnp.where(j >= base, c % wide, kx)
    base += frames * span * wide
    c = (j - base) % (span * high)
    ky = jnp.where(j >= base, c // span, ky)
    kx = jnp.where(j >= base, x_off + c % span, kx)
    base += frames * span * high
    c = (j - base) % (span * span)
    ky = jnp.where(j >= base, y_off + c // span, ky)
    kx = jnp.where(j >= base, x_off + c % span, kx)
    i = lax.broadcasted_iota(jnp.int32, (cells, 1), 0)
    return jnp.maximum(jnp.abs(i // wide - ky), jnp.abs(i % wide - kx))


def attend(units, factor):
    scores = [
        [
            jnp.where(
                dist <= reach,
                lax.dot_general(
                    q, k, (((1,), (1,)), ((), ())), preferred_element_type=jnp.float32
                )
                * factor,
                FAR,
            )
            for k, v, dist, reach in pieces
        ]
        for q, pieces, before in units
    ]
    tops = []
    for parts, (q, pieces, before) in zip(scores, units):
        found = [jnp.max(s, axis=1, keepdims=True) for s in parts]
        if before is not None:
            found.append(before)
        tops.append(functools.reduce(jnp.maximum, found))
    probs = [
        [jnp.exp2(s - m).astype(jnp.bfloat16) for s in parts] for parts, m in zip(scores, tops)
    ]
    sums = []
    for parts, (q, pieces, before) in zip(probs, units):
        total = None
        for p, (k, v, dist, reach) in zip(parts, pieces):
            both = jnp.concatenate([v, jnp.ones_like(v)], axis=1)
            got = jnp.dot(p, both, preferred_element_type=jnp.float32)
            total = got if total is None else total + got
        sums.append(total)
    return tops, sums


def attend_tile(q_ref, tile_ref, dist_ref, reach_of, heads, state, geometry):
    high, wide, span, frames, head_dim, factor, step = geometry
    cells = high * wide
    acc_ref, sum_ref, max_ref = state
    for at, head in enumerate(heads):
        cols = slice(head * head_dim, (head + 1) * head_dim)
        outs = slice(at * head_dim, (at + 1) * head_dim)
        starts = range(0, q_ref.shape[0], step)
        units = []
        for start in starts:
            near = dist_ref[start % cells : start % cells + step, : tile_ref.shape[1]]
            piece = (tile_ref[0, :, cols], tile_ref[1, :, cols], near, reach_of(head))
            units.append((q_ref[start : start + step, cols], [piece], None))
        for start, m, got in zip(starts, *attend(units, factor)):
            rows = slice(start, start + step)
            acc_ref[rows, outs] = got[:, :head_dim]
            sum_ref[rows, outs] = got[:, head_dim:]
            max_ref[rows, outs] = jnp.broadcast_to(m, (step, head_dim))


def begin_kernel(radius_ref, mask_ref, q_ref, tile_ref, *outs, geometry, heads):
    *state, dist_ref, reach_ref = outs
    high, wide, span, frames = geometry[:4]
    dist_ref[...] = distances(high, wide, span, frames)
    stretch_at = lax.axis_index("tm")
    line = (1, reach_ref.shape[1])
    for head in range(heads):
        radius = radius_ref[head]
        seen = mask_ref[stretch_at, 0, head] > 0
        reach_ref[head : head + 1] = jnp.full(line, radius, jnp.int32)
        reach_ref[heads + head : heads + head + 1] = jnp.full(
            line, jnp.where(seen, radius, -1), jnp.int32
        )
    attend_tile(q_ref, tile_ref, dist_ref, lambda h: radius_ref[h], (0,), state, geometry)


def tile_kernel(q_ref, tile_ref, dist_ref, reach_ref, *state, geometry, heads):
    attend_tile(
        q_ref,
        tile_ref,
        dist_ref,
        lambda h: reach_ref[h : h + 1, :1],
        range(1, heads),
        state,
        geometry,
    )


def pick_state(head_state, state, head, rows, head_dim):
    refs = head_state if head == 0 else state
    at = max(head - 1, 0) * head_dim
    return [ref[rows, at : at + head_dim] for ref in refs]


def rest_kernel(
    q_ref,
    edge_ref,
    first_tile_ref,
    first_edge_ref,
    *rest,
    geometry,
    heads,
    flips,
):
    head_state, dist_ref, reach_ref, state, outs = rest[:3], rest[3], rest[4], rest[5:8], rest[8:]
    high, wide, span, frames, head_dim, factor, step = geometry
    cells = high * wide
    base = frames * cells
    head_at = lax.axis_index("head")
    stretch_at = lax.axis_index("tm")

    def run(with_first):
        for flip, out_ref in zip(flips, outs):
            start = pl.multiple_of(jnp.bitwise_xor(head_at, flip) * step, step)
            rows = pl.ds(start, step)
            near = dist_ref[pl.ds(pl.multiple_of(lax.rem(start, cells), step), step)]
            beyond = near[:, base:]
            units = []
            olds = []
            for head in range(heads):
                cols = slice(head * head_dim, (head + 1) * head_dim)
                sources = [(edge_ref, beyond, head)]
                if with_first:
                    sources.append((first_tile_ref, near[:, :base], heads + head))
                    sources.append((first_edge_ref, beyond, heads + head))
                pieces = [
                    (ref[0, :, cols], ref[1, :, cols], dist, reach_ref[row : row + 1, :1])
                    for ref, dist, row in sources
                ]
                olds.append(pick_state(head_state, state, head, rows, head_dim))
                units.append((q_ref[rows, cols], pieces, olds[-1][2][:, :1]))
            for head, (m, got) in enumerate(zip(*attend(units, factor))):
                old_acc, old_total, old_max = olds[head]
                shrink = jnp.exp2(old_max - m)
                acc = old_acc * shrink + got[:, :head_dim]
                total = old_total * shrink + got[:, head_dim:]
                cols = slice(head * head_dim, (head + 1) * head_dim)
                out_ref[:, cols] = (acc / total).astype(jnp.bfloat16)

    @pl.when(stretch_at > 0)
    def _():
        run(True)

    @pl.when(stretch_at == 0)
    def _():
        run(False)


def copy_kernel(in_ref, out_ref):
    out_ref[...] = in_ref[...]


def stack_kernel(*refs):
    *parts, out_ref = refs
    tile_at = lax.axis_index("tile")
    for flip, part in enumerate(parts):
        tall = part.shape[0]
        top = pl.multiple_of(jnp.bitwise_xor(tile_at, flip) * tall, 16)
        out_ref[pl.ds(top, tall)] = part[...]


def project_kernel(w_ref, part_ref, own_ref, got_ref, out_ref, *, flip):
    broad = part_ref.shape[1]
    half = jnp.bitwise_xor(lax.axis_index("tm"), flip)
    cols = pl.ds(pl.multiple_of(half * broad, 128), broad)
    total = jnp.dot(own_ref[...], w_ref[:, cols], preferred_element_type=jnp.float32)
    total += jnp.dot(got_ref[...], part_ref[...], preferred_element_type=jnp.float32)
    out_ref[...] = total.astype(out_ref.dtype)


def add_kernel(mine_ref, got_ref, *rest, flip):
    out_ref, sum_ref, sems = rest[-3:]
    pieces, tall, broad = sum_ref.shape
    half = jnp.bitwise_xor(lax.axis_index("tm"), flip)
    cols = pl.ds(pl.multiple_of(half * broad, 128), broad)
    copies = []
    for i in range(pieces):
        rows = slice(i * tall, (i + 1) * tall)
        sum_ref[i] = (mine_ref[rows] + got_ref[rows].astype(jnp.float32)).astype(jnp.bfloat16)
        copies.append(pltpu.make_async_copy(sum_ref.at[i], out_ref.at[rows, cols], sems.at[i]))
        copies[-1].start()
    for copy in copies:
        copy.wait()


def two_by_two(query, keys, values, out_weight, radius, block_mask):
    span = RMAX
    frames, high, wide, channels = query.shape[2:]
    heads = radius.shape[0]
    head_dim = channels // heads
    cells = high * wide
    tokens = frames * cells
    groups = lax.axis_size("head")
    tiles = lax.axis_size("tile")
    depth, width = out_weight.shape
    step = tokens // groups
    geometry = (high, wide, span, frames, head_dim, LOG2E / math.sqrt(head_dim), step)
    count = frames * (cells + span * (wide + high + span))
    smem = pl.BlockSpec(memory_space=pltpu.SMEM)
    vmem = pl.BlockSpec(memory_space=pltpu.VMEM)
    hbm = pl.BlockSpec(memory_space=pltpu.HBM)
    bf16, f32 = jnp.bfloat16, jnp.float32
    shape = jax.ShapeDtypeStruct

    def call(kernel, out_shape, specs, *args, name, scratch=(), flops=0, **keys_of):
        return pl.pallas_call(
            functools.partial(kernel, **keys_of) if keys_of else kernel,
            out_shape=out_shape,
            in_specs=specs,
            out_specs=jax.tree.map(lambda _: vmem, out_shape),
            scratch_shapes=scratch,
            cost_estimate=pl.CostEstimate(flops=flops, bytes_accessed=0, transcendentals=0),
            compiler_params=pltpu.CompilerParams(vmem_limit_bytes=VMEM_LIMIT),
            name=name,
        )(*args)

    def flipped(value, axis, flip):
        return lax.ppermute(value, axis, [(i, i ^ flip) for i in range(lax.axis_size(axis))])

    q = query.reshape(tokens, channels)
    k = keys.reshape(tokens, channels)
    v = values.reshape(tokens, channels)

    tall, broad = depth // tiles, width // 2
    part_shape = shape((tall, broad), bf16)
    tile, part = call(
        load_kernel,
        [shape((2, tokens, channels), bf16), part_shape],
        [hbm] * 3,
        *[pltpu.with_memory_space_constraint(x, pltpu.HBM) for x in (k, v, out_weight)],
        name="load",
        scratch=[pltpu.SemaphoreType.DMA((3,))],
    )
    faces = call(
        face_kernel,
        [
            shape((2, frames, span * wide, channels), bf16),
            shape((2, frames, span * high, channels), bf16),
            shape((2, frames, span * span, channels), bf16),
        ],
        [vmem],
        tile,
        name="faces",
        geometry=geometry,
    )
    faces = [flipped(face, "tile", flip) for face, flip in zip(faces, (2, 1, 3))]
    lone = flipped(part, "head", 2)
    begun = call(
        begin_kernel,
        [shape((tokens, head_dim), f32)] * 3
        + [shape((cells, count), jnp.int32), shape((2 * heads, head_dim), jnp.int32)],
        [smem] * 2 + [vmem] * 2,
        radius,
        block_mask.transpose(1, 2, 0),
        q,
        tile,
        name="begin",
        geometry=geometry,
        heads=heads,
    )
    begun, tile = lax.optimization_barrier((begun, tile))
    first_tile = lax.ppermute(tile, "tm", [(0, 1)])
    state = call(
        tile_kernel,
        [shape((tokens, channels - head_dim), f32)] * 3,
        [vmem] * 4,
        q,
        tile,
        *begun[3:],
        name="tile",
        geometry=geometry,
        heads=heads,
    )
    lone, state = lax.optimization_barrier((lone, state))
    lone = call(copy_kernel, part_shape, [vmem], lone, name="lone", flops=2 * 10**9)
    lone, state, faces = lax.optimization_barrier((lone, state, faces))
    edge = call(
        edge_kernel, shape((2, count - tokens, channels), bf16), [vmem] * 3, *faces, name="edges", flops=20 * 10**9
    )
    first_edge = lax.ppermute(edge, "tm", [(0, 1)])
    parts = [lone] + [flipped(lone, "tile", flip) for flip in range(1, tiles)]

    def rest(state, *flips, flops=0):
        return call(
            rest_kernel,
            [shape((step, channels), bf16)] * len(flips),
            [vmem] * 12,
            q,
            edge,
            first_tile,
            first_edge,
            *begun,
            *state,
            name="rest",
            geometry=geometry,
            heads=heads,
            flips=flips,
            flops=flops,
        )

    (for_side,) = rest(state, 3)
    got_side = flipped(for_side, "head", 2)
    state, for_side = lax.optimization_barrier((state, for_side))
    for_far, own_side = rest(state, 2, 1)
    parts, own_side = lax.optimization_barrier((parts, own_side))
    here = call(
        stack_kernel, shape((depth, broad), bf16), [vmem] * tiles, *parts, name="stack"
    )

    def project(part, mine, got, kind, flip, flops=0):
        return call(
            project_kernel,
            shape((step, broad), kind),
            [vmem] * 4,
            out_weight,
            part,
            mine,
            got,
            name="project",
            flops=flops,
            flip=flip,
        )

    for_side = [project(here, own_side, got_side, bf16, 0, 20 * 10**9)]
    from_side = [flipped(for_side[0], "head", 1)]
    state, here, for_far, for_side[0] = lax.optimization_barrier(
        (state, here, for_far, for_side[0])
    )
    got_far = flipped(for_far, "head", 2)
    there = flipped(here, "tm", 1)
    (own,) = rest(state, 0, flops=20 * 10**9)
    own_side, own = lax.optimization_barrier((own_side, own))
    for_side.append(project(there, own_side, got_side, bf16, 1))
    from_side.append(flipped(for_side[1], "head", 1))
    own, for_side[1] = lax.optimization_barrier((own, for_side[1]))
    mine = [
        project(here, own, got_far, f32, 0),
        project(there, own, got_far, f32, 1, 20 * 10**9),
    ]
    pieces = 2
    mixed = []
    for flip in range(2):
        mixed = [
            pl.pallas_call(
                functools.partial(add_kernel, flip=flip),
                out_shape=shape((step, width), bf16),
                in_specs=[vmem] * 2 + [hbm] * flip,
                out_specs=hbm,
                input_output_aliases={2: 0} if flip else {},
                scratch_shapes=[
                    pltpu.VMEM((pieces, step // pieces, broad), bf16),
                    pltpu.SemaphoreType.DMA((pieces,)),
                ],
                compiler_params=pltpu.CompilerParams(vmem_limit_bytes=VMEM_LIMIT),
                name="add",
            )(mine[flip], from_side[flip], *mixed)
        ]
    (mixed,) = mixed
    return mixed.reshape(1, 1, step, width)


def solution(mesh):
    in_specs = (
        P("tm", "tile", None, None, None, "head"),
        P("tm", "tile", None, None, None, "head"),
        P("tm", "tile", None, None, None, "head"),
        P("head", None),
        P("head"),
        P("head", None, None),
    )
    out_specs = P("tm", "tile", "head", None)
    small = dict(mesh.shape) == {"tm": 2, "tile": 4, "head": 4}
    return jax.shard_map(
        two_by_two if small else any_grid,
        mesh=mesh,
        in_specs=in_specs,
        out_specs=out_specs,
        check_vma=False,
    )
```

```python
import functools
import math

import jax
import jax.numpy as jnp
from jax import lax
from jax.experimental import pallas as pl
from jax.experimental.pallas import tpu as pltpu
from jax.sharding import PartitionSpec as P

RMAX = 4
FAR = -1e30
LOG2E = 1.4426950408889634
VMEM_LIMIT = 24 * 1024 * 1024


def passed_along(value, axis, by):
    peers = lax.axis_size(axis)
    pairs = [(i, i + by) for i in range(peers) if 0 <= i + by < peers]
    return lax.ppermute(value, axis, pairs)


def widen(key_part, value_part, span, row_move, col_move):
    grid = math.isqrt(lax.axis_size("tile"))
    above = None
    below = None
    for offset in (grid, -grid):
        if offset > 0:
            face_key = key_part[:, :, key_part.shape[2] - span :]
            face_value = value_part[:, :, value_part.shape[2] - span :]
        else:
            face_key = key_part[:, :, :span]
            face_value = value_part[:, :, :span]
        got = row_move(face_key, face_value, offset)
        if offset > 0:
            above = got
        else:
            below = got
    key_rows = jnp.concatenate([above[0], key_part, below[0]], axis=2)
    value_rows = jnp.concatenate([above[1], value_part, below[1]], axis=2)
    left = None
    right = None
    for offset in (1, -1):
        if offset > 0:
            face_key = key_rows[:, :, :, key_rows.shape[3] - span :]
            face_value = value_rows[:, :, :, value_rows.shape[3] - span :]
        else:
            face_key = key_rows[:, :, :, :span]
            face_value = value_rows[:, :, :, :span]
        got = col_move(face_key, face_value, offset)
        if offset > 0:
            left = got
        else:
            right = got
    key_full = jnp.concatenate([left[0], key_rows, right[0]], axis=3)
    value_full = jnp.concatenate([left[1], value_rows, right[1]], axis=3)
    return (key_full, value_full)


def windows_of(block, half_high, half_wide, win_high, win_wide, heads_here, head_dim):
    parts = []
    for band in (0, 1):
        for strip in (0, 1):
            parts.append(
                block[
                    :,
                    band * half_high : band * half_high + win_high,
                    strip * half_wide : strip * half_wide + win_wide,
                ]
            )
    stacked = jnp.stack(parts)
    return stacked.reshape(4, -1, heads_here, head_dim)


def any_grid(query, keys, values, out_weight, radius, block_mask):
    span = RMAX
    grid = math.isqrt(lax.axis_size("tile"))
    tile_at = lax.axis_index("tile")
    row_at = tile_at // grid
    col_at = tile_at % grid
    stretch_at = lax.axis_index("tm")
    frames, high, wide, channels = query.shape[2:]
    heads_here = radius.shape[0]
    head_dim = channels // heads_here
    tokens_here = frames * high * wide
    half_high = high // 2
    half_wide = wide // 2
    win_high = half_high + 2 * span
    win_wide = half_wide + 2 * span
    quarter = frames * half_high * half_wide
    queries = query[0, 0].reshape(frames, 2, half_high, 2, half_wide, channels)
    queries = queries.transpose(1, 3, 0, 2, 4, 5).reshape(4, quarter, heads_here, head_dim)
    query_y = jnp.broadcast_to(
        jnp.arange(half_high, dtype=jnp.int32)[None, :, None], (frames, half_high, half_wide)
    ).reshape(-1)
    query_x = jnp.broadcast_to(
        jnp.arange(half_wide, dtype=jnp.int32)[None, None, :], (frames, half_high, half_wide)
    ).reshape(-1)
    key_y = jnp.broadcast_to(
        jnp.arange(win_high, dtype=jnp.int32)[None, :, None] - span, (frames, win_high, win_wide)
    ).reshape(-1)
    key_x = jnp.broadcast_to(
        jnp.arange(win_wide, dtype=jnp.int32)[None, None, :] - span, (frames, win_high, win_wide)
    ).reshape(-1)
    band_at = jnp.array([0, 0, 1, 1], dtype=jnp.int32)
    strip_at = jnp.array([0, 1, 0, 1], dtype=jnp.int32)
    global_y = row_at * high + band_at[:, None] * half_high + key_y[None, :]
    global_x = col_at * wide + strip_at[:, None] * half_wide + key_x[None, :]
    inside = (global_y >= 0) & (global_y < grid * high) & (global_x >= 0) & (global_x < grid * wide)
    distance = jnp.maximum(
        jnp.abs(query_y[:, None] - key_y[None, :]), jnp.abs(query_x[:, None] - key_x[None, :])
    )
    near = distance[None, :, :] <= radius[:, None, None]
    allowed = near[None, :, :, :] & inside[:, None, None, :]
    scale = 1.0 / math.sqrt(head_dim)
    initial = (
        jnp.full((4, heads_here, quarter), -1e30, jnp.float32),
        jnp.zeros((4, heads_here, quarter), jnp.float32),
        jnp.zeros((4, heads_here, quarter, head_dim), jnp.float32),
    )

    def tile_move(face_key, face_value, offset):
        return passed_along((face_key, face_value), "tile", offset)

    key_all, value_all = (
        lax.all_gather(keys[0], "tm", axis=0, tiled=True),
        lax.all_gather(values[0], "tm", axis=0, tiled=True),
    )
    key_full, value_full = widen(key_all, value_all, span, tile_move, tile_move)
    stretch_ids = jnp.arange(key_full.shape[0], dtype=jnp.int32)

    def one_stretch(state, item):
        key_block, value_block, stretch_id = item
        visible = (
            lax.dynamic_slice_in_dim(
                lax.dynamic_index_in_dim(block_mask, stretch_at, 1, False), stretch_id, 1, 1
            )[:, 0]
            > 0
        )
        best, total, acc = state
        key_win = windows_of(
            key_block, half_high, half_wide, win_high, win_wide, heads_here, head_dim
        )
        value_win = windows_of(
            value_block, half_high, half_wide, win_high, win_wide, heads_here, head_dim
        )
        usable = allowed & visible[None, :, None, None]
        scores = (
            jnp.einsum("nqhd,nkhd->nhqk", queries, key_win, preferred_element_type=jnp.float32)
            * scale
        )
        masked = jnp.where(usable, scores, jnp.float32(-1e30))
        fresh = jnp.maximum(best, jnp.max(masked, axis=3))
        probs = jnp.where(usable, jnp.exp(scores - fresh[..., None]), jnp.float32(0.0))
        shrink = jnp.exp(best - fresh)
        total = total * shrink + jnp.sum(probs, axis=3)
        acc = acc * shrink[..., None] + jnp.einsum(
            "nhqk,nkhd->nhqd",
            probs.astype(jnp.bfloat16),
            value_win,
            preferred_element_type=jnp.float32,
        )
        return ((fresh, total, acc), None)

    final, unused = lax.scan(one_stretch, initial, (key_full, value_full, stretch_ids))
    best, total, acc = final
    attn = (acc / total[..., None]).astype(jnp.bfloat16)
    attn = attn.transpose(0, 2, 1, 3).reshape(
        2, 2, frames, half_high, half_wide, heads_here * head_dim
    )
    attn = attn.transpose(2, 0, 3, 1, 4, 5).reshape(tokens_here, heads_here * head_dim)
    mixed = lax.psum_scatter(
        jnp.dot(attn, out_weight, preferred_element_type=jnp.float32).astype(jnp.bfloat16),
        "head",
        scatter_dimension=0,
        tiled=True,
    )
    return mixed.reshape(1, 1, -1, out_weight.shape[1])


def tile_place():
    tile_at = lax.axis_index("tile")
    return tile_at // 2, tile_at % 2


def load_kernel(k_ref, v_ref, w_ref, tile_ref, part_ref, sems):
    tall, broad = part_ref.shape
    top = pl.multiple_of(lax.axis_index("tile") * tall, 16)
    left = pl.multiple_of(lax.axis_index("tm") * broad, 128)
    copies = [
        pltpu.make_async_copy(
            w_ref.at[pl.ds(top, tall), pl.ds(left, broad)], part_ref, sems.at[2]
        )
    ]
    for which, ref in enumerate((k_ref, v_ref)):
        copies.append(pltpu.make_async_copy(ref, tile_ref.at[which], sems.at[which]))
    for copy in copies:
        copy.start()
    for copy in copies:
        copy.wait()


def face_kernel(tile_ref, row_ref, col_ref, corner_ref, *, geometry):
    high, wide, span, frames = geometry[:4]
    cells = high * wide
    row_at, col_at = tile_place()
    y0 = jnp.where(row_at == 0, high - span, 0)
    x0 = jnp.where(col_at == 0, wide - span, 0)

    def picker(count, cell_of):
        row = lax.broadcasted_iota(jnp.int32, (count, cells), 0)
        col = lax.broadcasted_iota(jnp.int32, (count, cells), 1)
        return (col == cell_of(row)).astype(jnp.bfloat16)

    beside = picker(high * span, lambda i: (i // span) * wide + x0 + i % span)
    across = picker(span * span, lambda i: (y0 + i // span) * wide + x0 + i % span)
    for which in range(2):
        for f in range(frames):
            start = pl.multiple_of(f * cells + y0 * wide, 16)
            row_ref[which, f] = tile_ref[which, pl.ds(start, span * wide)]
            whole = tile_ref[which, f * cells : (f + 1) * cells]
            col_ref[which, f] = jnp.dot(
                beside, whole, preferred_element_type=jnp.float32
            ).astype(jnp.bfloat16)
            corner_ref[which, f] = jnp.dot(
                across, whole, preferred_element_type=jnp.float32
            ).astype(jnp.bfloat16)


def edge_kernel(row_ref, col_ref, corner_ref, out_ref):
    for which in range(2):
        at = 0
        for part in (row_ref, col_ref, corner_ref):
            for f in range(part.shape[1]):
                size = part.shape[2]
                out_ref[which, at : at + size] = part[which, f]
                at += size


def distances(high, wide, span, frames):
    row_at, col_at = tile_place()
    cells = high * wide
    count = frames * (cells + span * (wide + high + span))
    j = lax.broadcasted_iota(jnp.int32, (1, count), 1)
    y_off = jnp.where(row_at == 0, high, -span)
    x_off = jnp.where(col_at == 0, wide, -span)
    c = j % cells
    ky, kx = c // wide, c % wide
    base = frames * cells
    c = (j - base) % (span * wide)
    ky = jnp.where(j >= base, y_off + c // wide, ky)
    kx = jnp.where(j >= base, c % wide, kx)
    base += frames * span * wide
    c = (j - base) % (span * high)
    ky = jnp.where(j >= base, c // span, ky)
    kx = jnp.where(j >= base, x_off + c % span, kx)
    base += frames * span * high
    c = (j - base) % (span * span)
    ky = jnp.where(j >= base, y_off + c // span, ky)
    kx = jnp.where(j >= base, x_off + c % span, kx)
    i = lax.broadcasted_iota(jnp.int32, (cells, 1), 0)
    return jnp.maximum(jnp.abs(i // wide - ky), jnp.abs(i % wide - kx))


def attend(units, factor):
    scores = [
        [
            jnp.where(
                dist <= reach,
                lax.dot_general(
                    q, k, (((1,), (1,)), ((), ())), preferred_element_type=jnp.float32
                )
                * factor,
                FAR,
            )
            for k, v, dist, reach in pieces
        ]
        for q, pieces, before in units
    ]
    tops = []
    for parts, (q, pieces, before) in zip(scores, units):
        found = [jnp.max(s, axis=1, keepdims=True) for s in parts]
        if before is not None:
            found.append(before)
        tops.append(functools.reduce(jnp.maximum, found))
    probs = [
        [jnp.exp2(s - m).astype(jnp.bfloat16) for s in parts] for parts, m in zip(scores, tops)
    ]
    sums = []
    for parts, (q, pieces, before) in zip(probs, units):
        total = None
        for p, (k, v, dist, reach) in zip(parts, pieces):
            both = jnp.concatenate([v, jnp.ones_like(v)], axis=1)
            got = jnp.dot(p, both, preferred_element_type=jnp.float32)
            total = got if total is None else total + got
        sums.append(total)
    return tops, sums


def attend_tile(q_ref, tile_ref, dist_ref, reach_of, heads, state, geometry):
    high, wide, span, frames, head_dim, factor, step = geometry
    cells = high * wide
    acc_ref, sum_ref, max_ref = state
    for at, head in enumerate(heads):
        cols = slice(head * head_dim, (head + 1) * head_dim)
        outs = slice(at * head_dim, (at + 1) * head_dim)
        starts = range(0, q_ref.shape[0], step)
        units = []
        for start in starts:
            near = dist_ref[start % cells : start % cells + step, : tile_ref.shape[1]]
            piece = (tile_ref[0, :, cols], tile_ref[1, :, cols], near, reach_of(head))
            units.append((q_ref[start : start + step, cols], [piece], None))
        for start, m, got in zip(starts, *attend(units, factor)):
            rows = slice(start, start + step)
            acc_ref[rows, outs] = got[:, :head_dim]
            sum_ref[rows, outs] = got[:, head_dim:]
            max_ref[rows, outs] = jnp.broadcast_to(m, (step, head_dim))


def begin_kernel(radius_ref, mask_ref, q_ref, tile_ref, *outs, geometry, heads):
    *state, dist_ref, reach_ref = outs
    high, wide, span, frames = geometry[:4]
    dist_ref[...] = distances(high, wide, span, frames)
    stretch_at = lax.axis_index("tm")
    line = (1, reach_ref.shape[1])
    for head in range(heads):
        radius = radius_ref[head]
        seen = mask_ref[stretch_at, 0, head] > 0
        reach_ref[head : head + 1] = jnp.full(line, radius, jnp.int32)
        reach_ref[heads + head : heads + head + 1] = jnp.full(
            line, jnp.where(seen, radius, -1), jnp.int32
        )
    attend_tile(q_ref, tile_ref, dist_ref, lambda h: radius_ref[h], (0,), state, geometry)


def tile_kernel(q_ref, tile_ref, dist_ref, reach_ref, *state, geometry, heads):
    attend_tile(
        q_ref,
        tile_ref,
        dist_ref,
        lambda h: reach_ref[h : h + 1, :1],
        range(1, heads),
        state,
        geometry,
    )


def pick_state(head_state, state, head, rows, head_dim):
    refs = head_state if head == 0 else state
    at = max(head - 1, 0) * head_dim
    return [ref[rows, at : at + head_dim] for ref in refs]


def rest_kernel(
    q_ref,
    edge_ref,
    first_tile_ref,
    first_edge_ref,
    *rest,
    geometry,
    heads,
    flips,
):
    head_state, dist_ref, reach_ref, state, outs = rest[:3], rest[3], rest[4], rest[5:8], rest[8:]
    high, wide, span, frames, head_dim, factor, step = geometry
    cells = high * wide
    base = frames * cells
    head_at = lax.axis_index("head")
    stretch_at = lax.axis_index("tm")

    def run(with_first):
        for flip, out_ref in zip(flips, outs):
            start = pl.multiple_of(jnp.bitwise_xor(head_at, flip) * step, step)
            rows = pl.ds(start, step)
            near = dist_ref[pl.ds(pl.multiple_of(lax.rem(start, cells), step), step)]
            beyond = near[:, base:]
            units = []
            olds = []
            for head in range(heads):
                cols = slice(head * head_dim, (head + 1) * head_dim)
                sources = [(edge_ref, beyond, head)]
                if with_first:
                    sources.append((first_tile_ref, near[:, :base], heads + head))
                    sources.append((first_edge_ref, beyond, heads + head))
                pieces = [
                    (ref[0, :, cols], ref[1, :, cols], dist, reach_ref[row : row + 1, :1])
                    for ref, dist, row in sources
                ]
                olds.append(pick_state(head_state, state, head, rows, head_dim))
                units.append((q_ref[rows, cols], pieces, olds[-1][2][:, :1]))
            for head, (m, got) in enumerate(zip(*attend(units, factor))):
                old_acc, old_total, old_max = olds[head]
                shrink = jnp.exp2(old_max - m)
                acc = old_acc * shrink + got[:, :head_dim]
                total = old_total * shrink + got[:, head_dim:]
                cols = slice(head * head_dim, (head + 1) * head_dim)
                out_ref[:, cols] = (acc / total).astype(jnp.bfloat16)

    @pl.when(stretch_at > 0)
    def _():
        run(True)

    @pl.when(stretch_at == 0)
    def _():
        run(False)


def copy_kernel(in_ref, out_ref):
    out_ref[...] = in_ref[...]


def stack_kernel(*refs):
    *parts, out_ref = refs
    tile_at = lax.axis_index("tile")
    for flip, part in enumerate(parts):
        tall = part.shape[0]
        top = pl.multiple_of(jnp.bitwise_xor(tile_at, flip) * tall, 16)
        out_ref[pl.ds(top, tall)] = part[...]


def project_kernel(w_ref, part_ref, own_ref, got_ref, out_ref, *, flip):
    broad = part_ref.shape[1]
    half = jnp.bitwise_xor(lax.axis_index("tm"), flip)
    cols = pl.ds(pl.multiple_of(half * broad, 128), broad)
    total = jnp.dot(own_ref[...], w_ref[:, cols], preferred_element_type=jnp.float32)
    total += jnp.dot(got_ref[...], part_ref[...], preferred_element_type=jnp.float32)
    out_ref[...] = total.astype(out_ref.dtype)


def add_kernel(mine_ref, got_ref, *rest, flip):
    out_ref, sum_ref, sems = rest[-3:]
    pieces, tall, broad = sum_ref.shape
    half = jnp.bitwise_xor(lax.axis_index("tm"), flip)
    cols = pl.ds(pl.multiple_of(half * broad, 128), broad)
    copies = []
    for i in range(pieces):
        rows = slice(i * tall, (i + 1) * tall)
        sum_ref[i] = (mine_ref[rows] + got_ref[rows].astype(jnp.float32)).astype(jnp.bfloat16)
        copies.append(pltpu.make_async_copy(sum_ref.at[i], out_ref.at[rows, cols], sems.at[i]))
        copies[-1].start()
    for copy in copies:
        copy.wait()


def two_by_two(query, keys, values, out_weight, radius, block_mask):
    span = RMAX
    frames, high, wide, channels = query.shape[2:]
    heads = radius.shape[0]
    head_dim = channels // heads
    cells = high * wide
    tokens = frames * cells
    groups = lax.axis_size("head")
    tiles = lax.axis_size("tile")
    depth, width = out_weight.shape
    step = tokens // groups
    geometry = (high, wide, span, frames, head_dim, LOG2E / math.sqrt(head_dim), step)
    count = frames * (cells + span * (wide + high + span))
    smem = pl.BlockSpec(memory_space=pltpu.SMEM)
    vmem = pl.BlockSpec(memory_space=pltpu.VMEM)
    hbm = pl.BlockSpec(memory_space=pltpu.HBM)
    bf16, f32 = jnp.bfloat16, jnp.float32
    shape = jax.ShapeDtypeStruct

    def call(kernel, out_shape, specs, *args, name, scratch=(), flops=0, **keys_of):
        return pl.pallas_call(
            functools.partial(kernel, **keys_of) if keys_of else kernel,
            out_shape=out_shape,
            in_specs=specs,
            out_specs=jax.tree.map(lambda _: vmem, out_shape),
            scratch_shapes=scratch,
            cost_estimate=pl.CostEstimate(flops=flops, bytes_accessed=0, transcendentals=0),
            compiler_params=pltpu.CompilerParams(vmem_limit_bytes=VMEM_LIMIT),
            name=name,
        )(*args)

    def flipped(value, axis, flip):
        return lax.ppermute(value, axis, [(i, i ^ flip) for i in range(lax.axis_size(axis))])

    q = query.reshape(tokens, channels)
    k = keys.reshape(tokens, channels)
    v = values.reshape(tokens, channels)

    tall, broad = depth // tiles, width // 2
    part_shape = shape((tall, broad), bf16)
    tile, part = call(
        load_kernel,
        [shape((2, tokens, channels), bf16), part_shape],
        [hbm] * 3,
        *[pltpu.with_memory_space_constraint(x, pltpu.HBM) for x in (k, v, out_weight)],
        name="load",
        scratch=[pltpu.SemaphoreType.DMA((3,))],
    )
    faces = call(
        face_kernel,
        [
            shape((2, frames, span * wide, channels), bf16),
            shape((2, frames, span * high, channels), bf16),
            shape((2, frames, span * span, channels), bf16),
        ],
        [vmem],
        tile,
        name="faces",
        geometry=geometry,
    )
    faces = [flipped(face, "tile", flip) for face, flip in zip(faces, (2, 1, 3))]
    lone = flipped(part, "head", 2)
    begun = call(
        begin_kernel,
        [shape((tokens, head_dim), f32)] * 3
        + [shape((cells, count), jnp.int32), shape((2 * heads, head_dim), jnp.int32)],
        [smem] * 2 + [vmem] * 2,
        radius,
        block_mask.transpose(1, 2, 0),
        q,
        tile,
        name="begin",
        geometry=geometry,
        heads=heads,
    )
    begun, tile = lax.optimization_barrier((begun, tile))
    first_tile = lax.ppermute(tile, "tm", [(0, 1)])
    state = call(
        tile_kernel,
        [shape((tokens, channels - head_dim), f32)] * 3,
        [vmem] * 4,
        q,
        tile,
        *begun[3:],
        name="tile",
        geometry=geometry,
        heads=heads,
    )
    lone, state = lax.optimization_barrier((lone, state))
    lone = call(copy_kernel, part_shape, [vmem], lone, name="lone", flops=2 * 10**9)
    lone, state, faces = lax.optimization_barrier((lone, state, faces))
    edge = call(
        edge_kernel, shape((2, count - tokens, channels), bf16), [vmem] * 3, *faces, name="edges", flops=20 * 10**9
    )
    first_edge = lax.ppermute(edge, "tm", [(0, 1)])
    parts = [lone] + [flipped(lone, "tile", flip) for flip in range(1, tiles)]

    def rest(state, *flips, flops=0):
        return call(
            rest_kernel,
            [shape((step, channels), bf16)] * len(flips),
            [vmem] * 12,
            q,
            edge,
            first_tile,
            first_edge,
            *begun,
            *state,
            name="rest",
            geometry=geometry,
            heads=heads,
            flips=flips,
            flops=flops,
        )

    (for_side,) = rest(state, 3)
    got_side = flipped(for_side, "head", 2)
    state, for_side = lax.optimization_barrier((state, for_side))
    for_far, own_side = rest(state, 2, 1)
    got_far = flipped(for_far, "head", 2)
    parts, own_side = lax.optimization_barrier((parts, own_side))
    here = call(
        stack_kernel, shape((depth, broad), bf16), [vmem] * tiles, *parts, name="stack"
    )

    there = flipped(here, "tm", 1)

    def project(part, mine, got, kind, flip, flops=0):
        return call(
            project_kernel,
            shape((step, broad), kind),
            [vmem] * 4,
            out_weight,
            part,
            mine,
            got,
            name="project",
            flops=flops,
            flip=flip,
        )

    for_side = [project(here, own_side, got_side, bf16, 0, 20 * 10**9)]
    from_side = [flipped(for_side[0], "head", 1)]
    state, for_side[0] = lax.optimization_barrier((state, for_side[0]))
    for_side.append(project(there, own_side, got_side, bf16, 1))
    from_side.append(flipped(for_side[1], "head", 1))
    state, for_side[1] = lax.optimization_barrier((state, for_side[1]))
    (own,) = rest(state, 0, flops=20 * 10**9)
    mine = [
        project(here, own, got_far, f32, 0),
        project(there, own, got_far, f32, 1, 20 * 10**9),
    ]
    pieces = 2
    mixed = []
    for flip in range(2):
        mixed = [
            pl.pallas_call(
                functools.partial(add_kernel, flip=flip),
                out_shape=shape((step, width), bf16),
                in_specs=[vmem] * 2 + [hbm] * flip,
                out_specs=hbm,
                input_output_aliases={2: 0} if flip else {},
                scratch_shapes=[
                    pltpu.VMEM((pieces, step // pieces, broad), bf16),
                    pltpu.SemaphoreType.DMA((pieces,)),
                ],
                compiler_params=pltpu.CompilerParams(vmem_limit_bytes=VMEM_LIMIT),
                name="add",
            )(mine[flip], from_side[flip], *mixed)
        ]
    (mixed,) = mixed
    return mixed.reshape(1, 1, step, width)


def solution(mesh):
    in_specs = (
        P("tm", "tile", None, None, None, "head"),
        P("tm", "tile", None, None, None, "head"),
        P("tm", "tile", None, None, None, "head"),
        P("head", None),
        P("head"),
        P("head", None, None),
    )
    out_specs = P("tm", "tile", "head", None)
    small = dict(mesh.shape) == {"tm": 2, "tile": 4, "head": 4}
    return jax.shard_map(
        two_by_two if small else any_grid,
        mesh=mesh,
        in_specs=in_specs,
        out_specs=out_specs,
        check_vma=False,
    )
```

```python
import functools
import math

import jax
import jax.numpy as jnp
from jax import lax
from jax.experimental import pallas as pl
from jax.experimental.pallas import tpu as pltpu
from jax.sharding import PartitionSpec as P

RMAX = 4
FAR = -1e30
LOG2E = 1.4426950408889634
VMEM_LIMIT = 24 * 1024 * 1024


def passed_along(value, axis, by):
    peers = lax.axis_size(axis)
    pairs = [(i, i + by) for i in range(peers) if 0 <= i + by < peers]
    return lax.ppermute(value, axis, pairs)


def widen(key_part, value_part, span, row_move, col_move):
    grid = math.isqrt(lax.axis_size("tile"))
    above = None
    below = None
    for offset in (grid, -grid):
        if offset > 0:
            face_key = key_part[:, :, key_part.shape[2] - span :]
            face_value = value_part[:, :, value_part.shape[2] - span :]
        else:
            face_key = key_part[:, :, :span]
            face_value = value_part[:, :, :span]
        got = row_move(face_key, face_value, offset)
        if offset > 0:
            above = got
        else:
            below = got
    key_rows = jnp.concatenate([above[0], key_part, below[0]], axis=2)
    value_rows = jnp.concatenate([above[1], value_part, below[1]], axis=2)
    left = None
    right = None
    for offset in (1, -1):
        if offset > 0:
            face_key = key_rows[:, :, :, key_rows.shape[3] - span :]
            face_value = value_rows[:, :, :, value_rows.shape[3] - span :]
        else:
            face_key = key_rows[:, :, :, :span]
            face_value = value_rows[:, :, :, :span]
        got = col_move(face_key, face_value, offset)
        if offset > 0:
            left = got
        else:
            right = got
    key_full = jnp.concatenate([left[0], key_rows, right[0]], axis=3)
    value_full = jnp.concatenate([left[1], value_rows, right[1]], axis=3)
    return (key_full, value_full)


def windows_of(block, half_high, half_wide, win_high, win_wide, heads_here, head_dim):
    parts = []
    for band in (0, 1):
        for strip in (0, 1):
            parts.append(
                block[
                    :,
                    band * half_high : band * half_high + win_high,
                    strip * half_wide : strip * half_wide + win_wide,
                ]
            )
    stacked = jnp.stack(parts)
    return stacked.reshape(4, -1, heads_here, head_dim)


def any_grid(query, keys, values, out_weight, radius, block_mask):
    span = RMAX
    grid = math.isqrt(lax.axis_size("tile"))
    tile_at = lax.axis_index("tile")
    row_at = tile_at // grid
    col_at = tile_at % grid
    stretch_at = lax.axis_index("tm")
    frames, high, wide, channels = query.shape[2:]
    heads_here = radius.shape[0]
    head_dim = channels // heads_here
    tokens_here = frames * high * wide
    half_high = high // 2
    half_wide = wide // 2
    win_high = half_high + 2 * span
    win_wide = half_wide + 2 * span
    quarter = frames * half_high * half_wide
    queries = query[0, 0].reshape(frames, 2, half_high, 2, half_wide, channels)
    queries = queries.transpose(1, 3, 0, 2, 4, 5).reshape(4, quarter, heads_here, head_dim)
    query_y = jnp.broadcast_to(
        jnp.arange(half_high, dtype=jnp.int32)[None, :, None], (frames, half_high, half_wide)
    ).reshape(-1)
    query_x = jnp.broadcast_to(
        jnp.arange(half_wide, dtype=jnp.int32)[None, None, :], (frames, half_high, half_wide)
    ).reshape(-1)
    key_y = jnp.broadcast_to(
        jnp.arange(win_high, dtype=jnp.int32)[None, :, None] - span, (frames, win_high, win_wide)
    ).reshape(-1)
    key_x = jnp.broadcast_to(
        jnp.arange(win_wide, dtype=jnp.int32)[None, None, :] - span, (frames, win_high, win_wide)
    ).reshape(-1)
    band_at = jnp.array([0, 0, 1, 1], dtype=jnp.int32)
    strip_at = jnp.array([0, 1, 0, 1], dtype=jnp.int32)
    global_y = row_at * high + band_at[:, None] * half_high + key_y[None, :]
    global_x = col_at * wide + strip_at[:, None] * half_wide + key_x[None, :]
    inside = (global_y >= 0) & (global_y < grid * high) & (global_x >= 0) & (global_x < grid * wide)
    distance = jnp.maximum(
        jnp.abs(query_y[:, None] - key_y[None, :]), jnp.abs(query_x[:, None] - key_x[None, :])
    )
    near = distance[None, :, :] <= radius[:, None, None]
    allowed = near[None, :, :, :] & inside[:, None, None, :]
    scale = 1.0 / math.sqrt(head_dim)
    initial = (
        jnp.full((4, heads_here, quarter), -1e30, jnp.float32),
        jnp.zeros((4, heads_here, quarter), jnp.float32),
        jnp.zeros((4, heads_here, quarter, head_dim), jnp.float32),
    )

    def tile_move(face_key, face_value, offset):
        return passed_along((face_key, face_value), "tile", offset)

    key_all, value_all = (
        lax.all_gather(keys[0], "tm", axis=0, tiled=True),
        lax.all_gather(values[0], "tm", axis=0, tiled=True),
    )
    key_full, value_full = widen(key_all, value_all, span, tile_move, tile_move)
    stretch_ids = jnp.arange(key_full.shape[0], dtype=jnp.int32)

    def one_stretch(state, item):
        key_block, value_block, stretch_id = item
        visible = (
            lax.dynamic_slice_in_dim(
                lax.dynamic_index_in_dim(block_mask, stretch_at, 1, False), stretch_id, 1, 1
            )[:, 0]
            > 0
        )
        best, total, acc = state
        key_win = windows_of(
            key_block, half_high, half_wide, win_high, win_wide, heads_here, head_dim
        )
        value_win = windows_of(
            value_block, half_high, half_wide, win_high, win_wide, heads_here, head_dim
        )
        usable = allowed & visible[None, :, None, None]
        scores = (
            jnp.einsum("nqhd,nkhd->nhqk", queries, key_win, preferred_element_type=jnp.float32)
            * scale
        )
        masked = jnp.where(usable, scores, jnp.float32(-1e30))
        fresh = jnp.maximum(best, jnp.max(masked, axis=3))
        probs = jnp.where(usable, jnp.exp(scores - fresh[..., None]), jnp.float32(0.0))
        shrink = jnp.exp(best - fresh)
        total = total * shrink + jnp.sum(probs, axis=3)
        acc = acc * shrink[..., None] + jnp.einsum(
            "nhqk,nkhd->nhqd",
            probs.astype(jnp.bfloat16),
            value_win,
            preferred_element_type=jnp.float32,
        )
        return ((fresh, total, acc), None)

    final, unused = lax.scan(one_stretch, initial, (key_full, value_full, stretch_ids))
    best, total, acc = final
    attn = (acc / total[..., None]).astype(jnp.bfloat16)
    attn = attn.transpose(0, 2, 1, 3).reshape(
        2, 2, frames, half_high, half_wide, heads_here * head_dim
    )
    attn = attn.transpose(2, 0, 3, 1, 4, 5).reshape(tokens_here, heads_here * head_dim)
    mixed = lax.psum_scatter(
        jnp.dot(attn, out_weight, preferred_element_type=jnp.float32).astype(jnp.bfloat16),
        "head",
        scatter_dimension=0,
        tiled=True,
    )
    return mixed.reshape(1, 1, -1, out_weight.shape[1])


def tile_place():
    tile_at = lax.axis_index("tile")
    return tile_at // 2, tile_at % 2


def part_kernel(w_ref, part_ref, sem):
    tall, broad = part_ref.shape
    top = pl.multiple_of(lax.axis_index("tile") * tall, 16)
    left = pl.multiple_of(lax.axis_index("tm") * broad, 128)
    copy = pltpu.make_async_copy(w_ref.at[pl.ds(top, tall), pl.ds(left, broad)], part_ref, sem)
    copy.start()
    copy.wait()


def face_kernel(k_ref, v_ref, part_ref, row_ref, col_ref, corner_ref, tile_ref, *, geometry):
    high, wide, span, frames = geometry[:4]
    cells = high * wide
    row_at, col_at = tile_place()
    y0 = jnp.where(row_at == 0, high - span, 0)
    x0 = jnp.where(col_at == 0, wide - span, 0)

    def picker(count, cell_of):
        row = lax.broadcasted_iota(jnp.int32, (count, cells), 0)
        col = lax.broadcasted_iota(jnp.int32, (count, cells), 1)
        return (col == cell_of(row)).astype(jnp.bfloat16)

    beside = picker(high * span, lambda i: (i // span) * wide + x0 + i % span)
    across = picker(span * span, lambda i: (y0 + i // span) * wide + x0 + i % span)
    for which, ref in enumerate((k_ref, v_ref)):
        tile_ref[which] = ref[...]
        for f in range(frames):
            start = pl.multiple_of(f * cells + y0 * wide, 16)
            row_ref[which, f] = ref[pl.ds(start, span * wide)]
            whole = ref[f * cells : (f + 1) * cells]
            col_ref[which, f] = jnp.dot(
                beside, whole, preferred_element_type=jnp.float32
            ).astype(jnp.bfloat16)
            corner_ref[which, f] = jnp.dot(
                across, whole, preferred_element_type=jnp.float32
            ).astype(jnp.bfloat16)


def edge_kernel(row_ref, col_ref, corner_ref, out_ref):
    for which in range(2):
        at = 0
        for part in (row_ref, col_ref, corner_ref):
            for f in range(part.shape[1]):
                size = part.shape[2]
                out_ref[which, at : at + size] = part[which, f]
                at += size


def distances(high, wide, span, frames):
    row_at, col_at = tile_place()
    cells = high * wide
    count = frames * (cells + span * (wide + high + span))
    j = lax.broadcasted_iota(jnp.int32, (1, count), 1)
    y_off = jnp.where(row_at == 0, high, -span)
    x_off = jnp.where(col_at == 0, wide, -span)
    c = j % cells
    ky, kx = c // wide, c % wide
    base = frames * cells
    c = (j - base) % (span * wide)
    ky = jnp.where(j >= base, y_off + c // wide, ky)
    kx = jnp.where(j >= base, c % wide, kx)
    base += frames * span * wide
    c = (j - base) % (span * high)
    ky = jnp.where(j >= base, c // span, ky)
    kx = jnp.where(j >= base, x_off + c % span, kx)
    base += frames * span * high
    c = (j - base) % (span * span)
    ky = jnp.where(j >= base, y_off + c // span, ky)
    kx = jnp.where(j >= base, x_off + c % span, kx)
    i = lax.broadcasted_iota(jnp.int32, (cells, 1), 0)
    return jnp.maximum(jnp.abs(i // wide - ky), jnp.abs(i % wide - kx))


def attend(units, factor):
    scores = [
        [
            jnp.where(
                dist <= reach,
                lax.dot_general(
                    q, k, (((1,), (1,)), ((), ())), preferred_element_type=jnp.float32
                )
                * factor,
                FAR,
            )
            for k, v, dist, reach in pieces
        ]
        for q, pieces, before in units
    ]
    tops = []
    for parts, (q, pieces, before) in zip(scores, units):
        found = [jnp.max(s, axis=1, keepdims=True) for s in parts]
        if before is not None:
            found.append(before)
        tops.append(functools.reduce(jnp.maximum, found))
    probs = [
        [jnp.exp2(s - m).astype(jnp.bfloat16) for s in parts] for parts, m in zip(scores, tops)
    ]
    sums = []
    for parts, (q, pieces, before) in zip(probs, units):
        total = None
        for p, (k, v, dist, reach) in zip(parts, pieces):
            both = jnp.concatenate([v, jnp.ones_like(v)], axis=1)
            got = jnp.dot(p, both, preferred_element_type=jnp.float32)
            total = got if total is None else total + got
        sums.append(total)
    return tops, sums


def attend_tile(q_ref, tile_ref, dist_ref, reach_of, heads, state, geometry):
    high, wide, span, frames, head_dim, factor, step = geometry
    cells = high * wide
    acc_ref, sum_ref, max_ref = state
    for at, head in enumerate(heads):
        cols = slice(head * head_dim, (head + 1) * head_dim)
        outs = slice(at * head_dim, (at + 1) * head_dim)
        starts = range(0, q_ref.shape[0], step)
        units = []
        for start in starts:
            near = dist_ref[start % cells : start % cells + step, : tile_ref.shape[1]]
            piece = (tile_ref[0, :, cols], tile_ref[1, :, cols], near, reach_of(head))
            units.append((q_ref[start : start + step, cols], [piece], None))
        for start, m, got in zip(starts, *attend(units, factor)):
            rows = slice(start, start + step)
            acc_ref[rows, outs] = got[:, :head_dim]
            sum_ref[rows, outs] = got[:, head_dim:]
            max_ref[rows, outs] = jnp.broadcast_to(m, (step, head_dim))


def begin_kernel(radius_ref, mask_ref, q_ref, tile_ref, *outs, geometry, heads):
    *state, dist_ref, reach_ref = outs
    high, wide, span, frames = geometry[:4]
    dist_ref[...] = distances(high, wide, span, frames)
    stretch_at = lax.axis_index("tm")
    line = (1, reach_ref.shape[1])
    for head in range(heads):
        radius = radius_ref[head]
        seen = mask_ref[stretch_at, 0, head] > 0
        reach_ref[head : head + 1] = jnp.full(line, radius, jnp.int32)
        reach_ref[heads + head : heads + head + 1] = jnp.full(
            line, jnp.where(seen, radius, -1), jnp.int32
        )
    attend_tile(q_ref, tile_ref, dist_ref, lambda h: radius_ref[h], (0,), state, geometry)


def tile_kernel(q_ref, tile_ref, dist_ref, reach_ref, *state, geometry, heads):
    attend_tile(
        q_ref,
        tile_ref,
        dist_ref,
        lambda h: reach_ref[h : h + 1, :1],
        range(1, heads),
        state,
        geometry,
    )


def pick_state(head_state, state, head, rows, head_dim):
    refs = head_state if head == 0 else state
    at = max(head - 1, 0) * head_dim
    return [ref[rows, at : at + head_dim] for ref in refs]


def rest_kernel(
    q_ref,
    edge_ref,
    first_tile_ref,
    first_edge_ref,
    *rest,
    geometry,
    heads,
    flips,
):
    head_state, dist_ref, reach_ref, state, outs = rest[:3], rest[3], rest[4], rest[5:8], rest[8:]
    high, wide, span, frames, head_dim, factor, step = geometry
    cells = high * wide
    base = frames * cells
    head_at = lax.axis_index("head")
    stretch_at = lax.axis_index("tm")

    def run(with_first):
        for flip, out_ref in zip(flips, outs):
            start = pl.multiple_of(jnp.bitwise_xor(head_at, flip) * step, step)
            rows = pl.ds(start, step)
            near = dist_ref[pl.ds(pl.multiple_of(lax.rem(start, cells), step), step)]
            beyond = near[:, base:]
            units = []
            olds = []
            for head in range(heads):
                cols = slice(head * head_dim, (head + 1) * head_dim)
                sources = [(edge_ref, beyond, head)]
                if with_first:
                    sources.append((first_tile_ref, near[:, :base], heads + head))
                    sources.append((first_edge_ref, beyond, heads + head))
                pieces = [
                    (ref[0, :, cols], ref[1, :, cols], dist, reach_ref[row : row + 1, :1])
                    for ref, dist, row in sources
                ]
                olds.append(pick_state(head_state, state, head, rows, head_dim))
                units.append((q_ref[rows, cols], pieces, olds[-1][2][:, :1]))
            for head, (m, got) in enumerate(zip(*attend(units, factor))):
                old_acc, old_total, old_max = olds[head]
                shrink = jnp.exp2(old_max - m)
                acc = old_acc * shrink + got[:, :head_dim]
                total = old_total * shrink + got[:, head_dim:]
                cols = slice(head * head_dim, (head + 1) * head_dim)
                out_ref[:, cols] = (acc / total).astype(jnp.bfloat16)

    @pl.when(stretch_at > 0)
    def _():
        run(True)

    @pl.when(stretch_at == 0)
    def _():
        run(False)


def copy_kernel(in_ref, out_ref):
    out_ref[...] = in_ref[...]


def stack_kernel(*refs):
    *parts, out_ref = refs
    tile_at = lax.axis_index("tile")
    for flip, part in enumerate(parts):
        tall = part.shape[0]
        top = pl.multiple_of(jnp.bitwise_xor(tile_at, flip) * tall, 16)
        out_ref[pl.ds(top, tall)] = part[...]


def project_kernel(w_ref, part_ref, own_ref, got_ref, out_ref, *, flip):
    broad = part_ref.shape[1]
    half = jnp.bitwise_xor(lax.axis_index("tm"), flip)
    cols = pl.ds(pl.multiple_of(half * broad, 128), broad)
    total = jnp.dot(own_ref[...], w_ref[:, cols], preferred_element_type=jnp.float32)
    total += jnp.dot(got_ref[...], part_ref[...], preferred_element_type=jnp.float32)
    out_ref[...] = total.astype(out_ref.dtype)


def add_kernel(mine_ref, got_ref, *rest, flip):
    out_ref, sum_ref, sems = rest[-3:]
    pieces, tall, broad = sum_ref.shape
    half = jnp.bitwise_xor(lax.axis_index("tm"), flip)
    cols = pl.ds(pl.multiple_of(half * broad, 128), broad)
    copies = []
    for i in range(pieces):
        rows = slice(i * tall, (i + 1) * tall)
        sum_ref[i] = (mine_ref[rows] + got_ref[rows].astype(jnp.float32)).astype(jnp.bfloat16)
        copies.append(pltpu.make_async_copy(sum_ref.at[i], out_ref.at[rows, cols], sems.at[i]))
        copies[-1].start()
    for copy in copies:
        copy.wait()


def two_by_two(query, keys, values, out_weight, radius, block_mask):
    span = RMAX
    frames, high, wide, channels = query.shape[2:]
    heads = radius.shape[0]
    head_dim = channels // heads
    cells = high * wide
    tokens = frames * cells
    groups = lax.axis_size("head")
    tiles = lax.axis_size("tile")
    depth, width = out_weight.shape
    step = tokens // groups
    geometry = (high, wide, span, frames, head_dim, LOG2E / math.sqrt(head_dim), step)
    count = frames * (cells + span * (wide + high + span))
    smem = pl.BlockSpec(memory_space=pltpu.SMEM)
    vmem = pl.BlockSpec(memory_space=pltpu.VMEM)
    hbm = pl.BlockSpec(memory_space=pltpu.HBM)
    bf16, f32 = jnp.bfloat16, jnp.float32
    shape = jax.ShapeDtypeStruct

    def call(kernel, out_shape, specs, *args, name, scratch=(), flops=0, **keys_of):
        return pl.pallas_call(
            functools.partial(kernel, **keys_of) if keys_of else kernel,
            out_shape=out_shape,
            in_specs=specs,
            out_specs=jax.tree.map(lambda _: vmem, out_shape),
            scratch_shapes=scratch,
            cost_estimate=pl.CostEstimate(flops=flops, bytes_accessed=0, transcendentals=0),
            compiler_params=pltpu.CompilerParams(vmem_limit_bytes=VMEM_LIMIT),
            name=name,
        )(*args)

    def flipped(value, axis, flip):
        return lax.ppermute(value, axis, [(i, i ^ flip) for i in range(lax.axis_size(axis))])

    q = query.reshape(tokens, channels)
    k = keys.reshape(tokens, channels)
    v = values.reshape(tokens, channels)

    tall, broad = depth // tiles, width // 2
    part_shape = shape((tall, broad), bf16)
    part = call(
        part_kernel,
        part_shape,
        [hbm],
        pltpu.with_memory_space_constraint(out_weight, pltpu.HBM),
        name="part",
        scratch=[pltpu.SemaphoreType.DMA],
    )
    *faces, tile = call(
        face_kernel,
        [
            shape((2, frames, span * wide, channels), bf16),
            shape((2, frames, span * high, channels), bf16),
            shape((2, frames, span * span, channels), bf16),
            shape((2, tokens, channels), bf16),
        ],
        [vmem] * 3,
        k,
        v,
        part,
        name="faces",
        geometry=geometry,
    )
    faces = [flipped(face, "tile", flip) for face, flip in zip(faces, (2, 1, 3))]
    lone = flipped(part, "head", 2)
    begun = call(
        begin_kernel,
        [shape((tokens, head_dim), f32)] * 3
        + [shape((cells, count), jnp.int32), shape((2 * heads, head_dim), jnp.int32)],
        [smem] * 2 + [vmem] * 2,
        radius,
        block_mask.transpose(1, 2, 0),
        q,
        tile,
        name="begin",
        geometry=geometry,
        heads=heads,
    )
    begun, tile = lax.optimization_barrier((begun, tile))
    first_tile = lax.ppermute(tile, "tm", [(0, 1)])
    state = call(
        tile_kernel,
        [shape((tokens, channels - head_dim), f32)] * 3,
        [vmem] * 4,
        q,
        tile,
        *begun[3:],
        name="tile",
        geometry=geometry,
        heads=heads,
    )
    lone, state = lax.optimization_barrier((lone, state))
    lone = call(copy_kernel, part_shape, [vmem], lone, name="lone", flops=2 * 10**9)
    lone, state, faces = lax.optimization_barrier((lone, state, faces))
    edge = call(
        edge_kernel, shape((2, count - tokens, channels), bf16), [vmem] * 3, *faces, name="edges", flops=20 * 10**9
    )
    first_edge = lax.ppermute(edge, "tm", [(0, 1)])
    parts = [lone] + [flipped(lone, "tile", flip) for flip in range(1, tiles)]

    def rest(state, *flips, flops=0):
        return call(
            rest_kernel,
            [shape((step, channels), bf16)] * len(flips),
            [vmem] * 12,
            q,
            edge,
            first_tile,
            first_edge,
            *begun,
            *state,
            name="rest",
            geometry=geometry,
            heads=heads,
            flips=flips,
            flops=flops,
        )

    (for_side,) = rest(state, 3)
    got_side = flipped(for_side, "head", 2)
    state, for_side = lax.optimization_barrier((state, for_side))
    for_far, own_side = rest(state, 2, 1)
    got_far = flipped(for_far, "head", 2)
    parts, own_side = lax.optimization_barrier((parts, own_side))
    here = call(
        stack_kernel, shape((depth, broad), bf16), [vmem] * tiles, *parts, name="stack"
    )

    def project(part, mine, got, kind, flip, flops=0):
        return call(
            project_kernel,
            shape((step, broad), kind),
            [vmem] * 4,
            out_weight,
            part,
            mine,
            got,
            name="project",
            flops=flops,
            flip=flip,
        )

    for_side = [project(here, own_side, got_side, bf16, 0, 20 * 10**9)]
    from_side = [flipped(for_side[0], "head", 1)]
    state, here, for_side[0] = lax.optimization_barrier((state, here, for_side[0]))
    there = flipped(here, "tm", 1)
    (own,) = rest(state, 0, flops=20 * 10**9)
    own_side, own = lax.optimization_barrier((own_side, own))
    for_side.append(project(there, own_side, got_side, bf16, 1))
    from_side.append(flipped(for_side[1], "head", 1))
    own, for_side[1] = lax.optimization_barrier((own, for_side[1]))
    mine = [
        project(here, own, got_far, f32, 0),
        project(there, own, got_far, f32, 1, 20 * 10**9),
    ]
    pieces = 2
    mixed = []
    for flip in range(2):
        mixed = [
            pl.pallas_call(
                functools.partial(add_kernel, flip=flip),
                out_shape=shape((step, width), bf16),
                in_specs=[vmem] * 2 + [hbm] * flip,
                out_specs=hbm,
                input_output_aliases={2: 0} if flip else {},
                scratch_shapes=[
                    pltpu.VMEM((pieces, step // pieces, broad), bf16),
                    pltpu.SemaphoreType.DMA((pieces,)),
                ],
                compiler_params=pltpu.CompilerParams(vmem_limit_bytes=VMEM_LIMIT),
                name="add",
            )(mine[flip], from_side[flip], *mixed)
        ]
    (mixed,) = mixed
    return mixed.reshape(1, 1, step, width)


def solution(mesh):
    in_specs = (
        P("tm", "tile", None, None, None, "head"),
        P("tm", "tile", None, None, None, "head"),
        P("tm", "tile", None, None, None, "head"),
        P("head", None),
        P("head"),
        P("head", None, None),
    )
    out_specs = P("tm", "tile", "head", None)
    small = dict(mesh.shape) == {"tm": 2, "tile": 4, "head": 4}
    return jax.shard_map(
        two_by_two if small else any_grid,
        mesh=mesh,
        in_specs=in_specs,
        out_specs=out_specs,
        check_vma=False,
    )
```

```python
import functools
import math

import jax
import jax.numpy as jnp
from jax import lax
from jax.experimental import pallas as pl
from jax.experimental.pallas import tpu as pltpu
from jax.sharding import PartitionSpec as P

RMAX = 4
FAR = -1e30
LOG2E = 1.4426950408889634
VMEM_LIMIT = 24 * 1024 * 1024


def passed_along(value, axis, by):
    peers = lax.axis_size(axis)
    pairs = [(i, i + by) for i in range(peers) if 0 <= i + by < peers]
    return lax.ppermute(value, axis, pairs)


def widen(key_part, value_part, span, row_move, col_move):
    grid = math.isqrt(lax.axis_size("tile"))
    above = None
    below = None
    for offset in (grid, -grid):
        if offset > 0:
            face_key = key_part[:, :, key_part.shape[2] - span :]
            face_value = value_part[:, :, value_part.shape[2] - span :]
        else:
            face_key = key_part[:, :, :span]
            face_value = value_part[:, :, :span]
        got = row_move(face_key, face_value, offset)
        if offset > 0:
            above = got
        else:
            below = got
    key_rows = jnp.concatenate([above[0], key_part, below[0]], axis=2)
    value_rows = jnp.concatenate([above[1], value_part, below[1]], axis=2)
    left = None
    right = None
    for offset in (1, -1):
        if offset > 0:
            face_key = key_rows[:, :, :, key_rows.shape[3] - span :]
            face_value = value_rows[:, :, :, value_rows.shape[3] - span :]
        else:
            face_key = key_rows[:, :, :, :span]
            face_value = value_rows[:, :, :, :span]
        got = col_move(face_key, face_value, offset)
        if offset > 0:
            left = got
        else:
            right = got
    key_full = jnp.concatenate([left[0], key_rows, right[0]], axis=3)
    value_full = jnp.concatenate([left[1], value_rows, right[1]], axis=3)
    return (key_full, value_full)


def windows_of(block, half_high, half_wide, win_high, win_wide, heads_here, head_dim):
    parts = []
    for band in (0, 1):
        for strip in (0, 1):
            parts.append(
                block[
                    :,
                    band * half_high : band * half_high + win_high,
                    strip * half_wide : strip * half_wide + win_wide,
                ]
            )
    stacked = jnp.stack(parts)
    return stacked.reshape(4, -1, heads_here, head_dim)


def any_grid(query, keys, values, out_weight, radius, block_mask):
    span = RMAX
    grid = math.isqrt(lax.axis_size("tile"))
    tile_at = lax.axis_index("tile")
    row_at = tile_at // grid
    col_at = tile_at % grid
    stretch_at = lax.axis_index("tm")
    frames, high, wide, channels = query.shape[2:]
    heads_here = radius.shape[0]
    head_dim = channels // heads_here
    tokens_here = frames * high * wide
    half_high = high // 2
    half_wide = wide // 2
    win_high = half_high + 2 * span
    win_wide = half_wide + 2 * span
    quarter = frames * half_high * half_wide
    queries = query[0, 0].reshape(frames, 2, half_high, 2, half_wide, channels)
    queries = queries.transpose(1, 3, 0, 2, 4, 5).reshape(4, quarter, heads_here, head_dim)
    query_y = jnp.broadcast_to(
        jnp.arange(half_high, dtype=jnp.int32)[None, :, None], (frames, half_high, half_wide)
    ).reshape(-1)
    query_x = jnp.broadcast_to(
        jnp.arange(half_wide, dtype=jnp.int32)[None, None, :], (frames, half_high, half_wide)
    ).reshape(-1)
    key_y = jnp.broadcast_to(
        jnp.arange(win_high, dtype=jnp.int32)[None, :, None] - span, (frames, win_high, win_wide)
    ).reshape(-1)
    key_x = jnp.broadcast_to(
        jnp.arange(win_wide, dtype=jnp.int32)[None, None, :] - span, (frames, win_high, win_wide)
    ).reshape(-1)
    band_at = jnp.array([0, 0, 1, 1], dtype=jnp.int32)
    strip_at = jnp.array([0, 1, 0, 1], dtype=jnp.int32)
    global_y = row_at * high + band_at[:, None] * half_high + key_y[None, :]
    global_x = col_at * wide + strip_at[:, None] * half_wide + key_x[None, :]
    inside = (global_y >= 0) & (global_y < grid * high) & (global_x >= 0) & (global_x < grid * wide)
    distance = jnp.maximum(
        jnp.abs(query_y[:, None] - key_y[None, :]), jnp.abs(query_x[:, None] - key_x[None, :])
    )
    near = distance[None, :, :] <= radius[:, None, None]
    allowed = near[None, :, :, :] & inside[:, None, None, :]
    scale = 1.0 / math.sqrt(head_dim)
    initial = (
        jnp.full((4, heads_here, quarter), -1e30, jnp.float32),
        jnp.zeros((4, heads_here, quarter), jnp.float32),
        jnp.zeros((4, heads_here, quarter, head_dim), jnp.float32),
    )

    def tile_move(face_key, face_value, offset):
        return passed_along((face_key, face_value), "tile", offset)

    key_all, value_all = (
        lax.all_gather(keys[0], "tm", axis=0, tiled=True),
        lax.all_gather(values[0], "tm", axis=0, tiled=True),
    )
    key_full, value_full = widen(key_all, value_all, span, tile_move, tile_move)
    stretch_ids = jnp.arange(key_full.shape[0], dtype=jnp.int32)

    def one_stretch(state, item):
        key_block, value_block, stretch_id = item
        visible = (
            lax.dynamic_slice_in_dim(
                lax.dynamic_index_in_dim(block_mask, stretch_at, 1, False), stretch_id, 1, 1
            )[:, 0]
            > 0
        )
        best, total, acc = state
        key_win = windows_of(
            key_block, half_high, half_wide, win_high, win_wide, heads_here, head_dim
        )
        value_win = windows_of(
            value_block, half_high, half_wide, win_high, win_wide, heads_here, head_dim
        )
        usable = allowed & visible[None, :, None, None]
        scores = (
            jnp.einsum("nqhd,nkhd->nhqk", queries, key_win, preferred_element_type=jnp.float32)
            * scale
        )
        masked = jnp.where(usable, scores, jnp.float32(-1e30))
        fresh = jnp.maximum(best, jnp.max(masked, axis=3))
        probs = jnp.where(usable, jnp.exp(scores - fresh[..., None]), jnp.float32(0.0))
        shrink = jnp.exp(best - fresh)
        total = total * shrink + jnp.sum(probs, axis=3)
        acc = acc * shrink[..., None] + jnp.einsum(
            "nhqk,nkhd->nhqd",
            probs.astype(jnp.bfloat16),
            value_win,
            preferred_element_type=jnp.float32,
        )
        return ((fresh, total, acc), None)

    final, unused = lax.scan(one_stretch, initial, (key_full, value_full, stretch_ids))
    best, total, acc = final
    attn = (acc / total[..., None]).astype(jnp.bfloat16)
    attn = attn.transpose(0, 2, 1, 3).reshape(
        2, 2, frames, half_high, half_wide, heads_here * head_dim
    )
    attn = attn.transpose(2, 0, 3, 1, 4, 5).reshape(tokens_here, heads_here * head_dim)
    mixed = lax.psum_scatter(
        jnp.dot(attn, out_weight, preferred_element_type=jnp.float32).astype(jnp.bfloat16),
        "head",
        scatter_dimension=0,
        tiled=True,
    )
    return mixed.reshape(1, 1, -1, out_weight.shape[1])


def tile_place():
    tile_at = lax.axis_index("tile")
    return tile_at // 2, tile_at % 2


def part_kernel(w_ref, part_ref, sem):
    tall, broad = part_ref.shape
    top = pl.multiple_of(lax.axis_index("tile") * tall, 16)
    left = pl.multiple_of(lax.axis_index("tm") * broad, 128)
    copy = pltpu.make_async_copy(w_ref.at[pl.ds(top, tall), pl.ds(left, broad)], part_ref, sem)
    copy.start()
    copy.wait()


def face_kernel(k_ref, v_ref, part_ref, row_ref, col_ref, corner_ref, tile_ref, *, geometry):
    high, wide, span, frames = geometry[:4]
    cells = high * wide
    row_at, col_at = tile_place()
    y0 = jnp.where(row_at == 0, high - span, 0)
    x0 = jnp.where(col_at == 0, wide - span, 0)

    def picker(count, cell_of):
        row = lax.broadcasted_iota(jnp.int32, (count, cells), 0)
        col = lax.broadcasted_iota(jnp.int32, (count, cells), 1)
        return (col == cell_of(row)).astype(jnp.bfloat16)

    beside = picker(high * span, lambda i: (i // span) * wide + x0 + i % span)
    across = picker(span * span, lambda i: (y0 + i // span) * wide + x0 + i % span)
    for which, ref in enumerate((k_ref, v_ref)):
        tile_ref[which] = ref[...]
        for f in range(frames):
            start = pl.multiple_of(f * cells + y0 * wide, 16)
            row_ref[which, f] = ref[pl.ds(start, span * wide)]
            whole = ref[f * cells : (f + 1) * cells]
            col_ref[which, f] = jnp.dot(
                beside, whole, preferred_element_type=jnp.float32
            ).astype(jnp.bfloat16)
            corner_ref[which, f] = jnp.dot(
                across, whole, preferred_element_type=jnp.float32
            ).astype(jnp.bfloat16)


def edge_kernel(row_ref, col_ref, corner_ref, out_ref):
    for which in range(2):
        at = 0
        for part in (row_ref, col_ref, corner_ref):
            for f in range(part.shape[1]):
                size = part.shape[2]
                out_ref[which, at : at + size] = part[which, f]
                at += size


def distances(high, wide, span, frames):
    row_at, col_at = tile_place()
    cells = high * wide
    count = frames * (cells + span * (wide + high + span))
    j = lax.broadcasted_iota(jnp.int32, (1, count), 1)
    y_off = jnp.where(row_at == 0, high, -span)
    x_off = jnp.where(col_at == 0, wide, -span)
    c = j % cells
    ky, kx = c // wide, c % wide
    base = frames * cells
    c = (j - base) % (span * wide)
    ky = jnp.where(j >= base, y_off + c // wide, ky)
    kx = jnp.where(j >= base, c % wide, kx)
    base += frames * span * wide
    c = (j - base) % (span * high)
    ky = jnp.where(j >= base, c // span, ky)
    kx = jnp.where(j >= base, x_off + c % span, kx)
    base += frames * span * high
    c = (j - base) % (span * span)
    ky = jnp.where(j >= base, y_off + c // span, ky)
    kx = jnp.where(j >= base, x_off + c % span, kx)
    i = lax.broadcasted_iota(jnp.int32, (cells, 1), 0)
    return jnp.maximum(jnp.abs(i // wide - ky), jnp.abs(i % wide - kx))


def attend(units, factor):
    scores = [
        [
            jnp.where(
                dist <= reach,
                lax.dot_general(
                    q, k, (((1,), (1,)), ((), ())), preferred_element_type=jnp.float32
                )
                * factor,
                FAR,
            )
            for k, v, dist, reach in pieces
        ]
        for q, pieces, before in units
    ]
    tops = []
    for parts, (q, pieces, before) in zip(scores, units):
        found = [jnp.max(s, axis=1, keepdims=True) for s in parts]
        if before is not None:
            found.append(before)
        tops.append(functools.reduce(jnp.maximum, found))
    probs = [
        [jnp.exp2(s - m).astype(jnp.bfloat16) for s in parts] for parts, m in zip(scores, tops)
    ]
    sums = []
    for parts, (q, pieces, before) in zip(probs, units):
        total = None
        for p, (k, v, dist, reach) in zip(parts, pieces):
            both = jnp.concatenate([v, jnp.ones_like(v)], axis=1)
            got = jnp.dot(p, both, preferred_element_type=jnp.float32)
            total = got if total is None else total + got
        sums.append(total)
    return tops, sums


def attend_tile(q_ref, tile_ref, dist_ref, reach_of, heads, state, geometry):
    high, wide, span, frames, head_dim, factor, step = geometry
    cells = high * wide
    acc_ref, sum_ref, max_ref = state
    for at, head in enumerate(heads):
        cols = slice(head * head_dim, (head + 1) * head_dim)
        outs = slice(at * head_dim, (at + 1) * head_dim)
        starts = range(0, q_ref.shape[0], step)
        units = []
        for start in starts:
            near = dist_ref[start % cells : start % cells + step, : tile_ref.shape[1]]
            piece = (tile_ref[0, :, cols], tile_ref[1, :, cols], near, reach_of(head))
            units.append((q_ref[start : start + step, cols], [piece], None))
        for start, m, got in zip(starts, *attend(units, factor)):
            rows = slice(start, start + step)
            acc_ref[rows, outs] = got[:, :head_dim]
            sum_ref[rows, outs] = got[:, head_dim:]
            max_ref[rows, outs] = jnp.broadcast_to(m, (step, head_dim))


def begin_kernel(radius_ref, mask_ref, q_ref, tile_ref, *outs, geometry, heads):
    *state, dist_ref, reach_ref = outs
    high, wide, span, frames = geometry[:4]
    dist_ref[...] = distances(high, wide, span, frames)
    stretch_at = lax.axis_index("tm")
    line = (1, reach_ref.shape[1])
    for head in range(heads):
        radius = radius_ref[head]
        seen = mask_ref[stretch_at, 0, head] > 0
        reach_ref[head : head + 1] = jnp.full(line, radius, jnp.int32)
        reach_ref[heads + head : heads + head + 1] = jnp.full(
            line, jnp.where(seen, radius, -1), jnp.int32
        )
    attend_tile(q_ref, tile_ref, dist_ref, lambda h: radius_ref[h], (0,), state, geometry)


def tile_kernel(q_ref, tile_ref, dist_ref, reach_ref, *state, geometry, heads):
    attend_tile(
        q_ref,
        tile_ref,
        dist_ref,
        lambda h: reach_ref[h : h + 1, :1],
        range(1, heads),
        state,
        geometry,
    )


def pick_state(head_state, state, head, rows, head_dim):
    refs = head_state if head == 0 else state
    at = max(head - 1, 0) * head_dim
    return [ref[rows, at : at + head_dim] for ref in refs]


def rest_kernel(
    q_ref,
    edge_ref,
    first_tile_ref,
    first_edge_ref,
    *rest,
    geometry,
    heads,
    flips,
):
    head_state, dist_ref, reach_ref, state, outs = rest[:3], rest[3], rest[4], rest[5:8], rest[8:]
    high, wide, span, frames, head_dim, factor, step = geometry
    cells = high * wide
    base = frames * cells
    head_at = lax.axis_index("head")
    stretch_at = lax.axis_index("tm")

    def run(with_first):
        for flip, out_ref in zip(flips, outs):
            start = pl.multiple_of(jnp.bitwise_xor(head_at, flip) * step, step)
            rows = pl.ds(start, step)
            near = dist_ref[pl.ds(pl.multiple_of(lax.rem(start, cells), step), step)]
            beyond = near[:, base:]
            units = []
            olds = []
            for head in range(heads):
                cols = slice(head * head_dim, (head + 1) * head_dim)
                sources = [(edge_ref, beyond, head)]
                if with_first:
                    sources.append((first_tile_ref, near[:, :base], heads + head))
                    sources.append((first_edge_ref, beyond, heads + head))
                pieces = [
                    (ref[0, :, cols], ref[1, :, cols], dist, reach_ref[row : row + 1, :1])
                    for ref, dist, row in sources
                ]
                olds.append(pick_state(head_state, state, head, rows, head_dim))
                units.append((q_ref[rows, cols], pieces, olds[-1][2][:, :1]))
            for head, (m, got) in enumerate(zip(*attend(units, factor))):
                old_acc, old_total, old_max = olds[head]
                shrink = jnp.exp2(old_max - m)
                acc = old_acc * shrink + got[:, :head_dim]
                total = old_total * shrink + got[:, head_dim:]
                cols = slice(head * head_dim, (head + 1) * head_dim)
                out_ref[:, cols] = (acc / total).astype(jnp.bfloat16)

    @pl.when(stretch_at > 0)
    def _():
        run(True)

    @pl.when(stretch_at == 0)
    def _():
        run(False)


def copy_kernel(in_ref, out_ref):
    out_ref[...] = in_ref[...]


def stack_kernel(*refs):
    *parts, out_ref = refs
    tile_at = lax.axis_index("tile")
    for flip, part in enumerate(parts):
        tall = part.shape[0]
        top = pl.multiple_of(jnp.bitwise_xor(tile_at, flip) * tall, 16)
        out_ref[pl.ds(top, tall)] = part[...]


def project_kernel(w_ref, part_ref, own_ref, got_ref, out_ref, *, flip):
    broad = part_ref.shape[1]
    half = jnp.bitwise_xor(lax.axis_index("tm"), flip)
    cols = pl.ds(pl.multiple_of(half * broad, 128), broad)
    total = jnp.dot(own_ref[...], w_ref[:, cols], preferred_element_type=jnp.float32)
    total += jnp.dot(got_ref[...], part_ref[...], preferred_element_type=jnp.float32)
    out_ref[...] = total.astype(out_ref.dtype)


def add_kernel(mine_ref, got_ref, *rest, flip):
    out_ref, sum_ref, sems = rest[-3:]
    pieces, tall, broad = sum_ref.shape
    half = jnp.bitwise_xor(lax.axis_index("tm"), flip)
    cols = pl.ds(pl.multiple_of(half * broad, 128), broad)
    copies = []
    for i in range(pieces):
        rows = slice(i * tall, (i + 1) * tall)
        sum_ref[i] = (mine_ref[rows] + got_ref[rows].astype(jnp.float32)).astype(jnp.bfloat16)
        copies.append(pltpu.make_async_copy(sum_ref.at[i], out_ref.at[rows, cols], sems.at[i]))
        copies[-1].start()
    for copy in copies:
        copy.wait()


def two_by_two(query, keys, values, out_weight, radius, block_mask):
    span = RMAX
    frames, high, wide, channels = query.shape[2:]
    heads = radius.shape[0]
    head_dim = channels // heads
    cells = high * wide
    tokens = frames * cells
    groups = lax.axis_size("head")
    tiles = lax.axis_size("tile")
    depth, width = out_weight.shape
    step = tokens // groups
    geometry = (high, wide, span, frames, head_dim, LOG2E / math.sqrt(head_dim), step)
    count = frames * (cells + span * (wide + high + span))
    smem = pl.BlockSpec(memory_space=pltpu.SMEM)
    vmem = pl.BlockSpec(memory_space=pltpu.VMEM)
    hbm = pl.BlockSpec(memory_space=pltpu.HBM)
    bf16, f32 = jnp.bfloat16, jnp.float32
    shape = jax.ShapeDtypeStruct

    def call(kernel, out_shape, specs, *args, name, scratch=(), flops=0, **keys_of):
        return pl.pallas_call(
            functools.partial(kernel, **keys_of) if keys_of else kernel,
            out_shape=out_shape,
            in_specs=specs,
            out_specs=jax.tree.map(lambda _: vmem, out_shape),
            scratch_shapes=scratch,
            cost_estimate=pl.CostEstimate(flops=flops, bytes_accessed=0, transcendentals=0),
            compiler_params=pltpu.CompilerParams(vmem_limit_bytes=VMEM_LIMIT),
            name=name,
        )(*args)

    def flipped(value, axis, flip):
        return lax.ppermute(value, axis, [(i, i ^ flip) for i in range(lax.axis_size(axis))])

    q = query.reshape(tokens, channels)
    k = keys.reshape(tokens, channels)
    v = values.reshape(tokens, channels)

    tall, broad = depth // tiles, width // 2
    part_shape = shape((tall, broad), bf16)
    part = call(
        part_kernel,
        part_shape,
        [hbm],
        pltpu.with_memory_space_constraint(out_weight, pltpu.HBM),
        name="part",
        scratch=[pltpu.SemaphoreType.DMA],
    )
    *faces, tile = call(
        face_kernel,
        [
            shape((2, frames, span * wide, channels), bf16),
            shape((2, frames, span * high, channels), bf16),
            shape((2, frames, span * span, channels), bf16),
            shape((2, tokens, channels), bf16),
        ],
        [vmem] * 3,
        k,
        v,
        part,
        name="faces",
        geometry=geometry,
    )
    faces = [flipped(face, "tile", flip) for face, flip in zip(faces, (2, 1, 3))]
    lone = flipped(part, "head", 2)
    begun = call(
        begin_kernel,
        [shape((tokens, head_dim), f32)] * 3
        + [shape((cells, count), jnp.int32), shape((2 * heads, head_dim), jnp.int32)],
        [smem] * 2 + [vmem] * 2,
        radius,
        block_mask.transpose(1, 2, 0),
        q,
        tile,
        name="begin",
        geometry=geometry,
        heads=heads,
    )
    begun, tile = lax.optimization_barrier((begun, tile))
    first_tile = lax.ppermute(tile, "tm", [(0, 1)])
    state = call(
        tile_kernel,
        [shape((tokens, channels - head_dim), f32)] * 3,
        [vmem] * 4,
        q,
        tile,
        *begun[3:],
        name="tile",
        geometry=geometry,
        heads=heads,
    )
    lone, state = lax.optimization_barrier((lone, state))
    lone = call(copy_kernel, part_shape, [vmem], lone, name="lone", flops=2 * 10**9)
    lone, state, faces = lax.optimization_barrier((lone, state, faces))
    edge = call(
        edge_kernel, shape((2, count - tokens, channels), bf16), [vmem] * 3, *faces, name="edges", flops=20 * 10**9
    )
    first_edge = lax.ppermute(edge, "tm", [(0, 1)])
    parts = [lone] + [flipped(lone, "tile", flip) for flip in range(1, tiles)]

    def rest(state, *flips, flops=0):
        return call(
            rest_kernel,
            [shape((step, channels), bf16)] * len(flips),
            [vmem] * 12,
            q,
            edge,
            first_tile,
            first_edge,
            *begun,
            *state,
            name="rest",
            geometry=geometry,
            heads=heads,
            flips=flips,
            flops=flops,
        )

    (for_side,) = rest(state, 3)
    got_side = flipped(for_side, "head", 2)
    state, for_side = lax.optimization_barrier((state, for_side))
    for_far, own_side = rest(state, 2, 1)
    parts, own_side = lax.optimization_barrier((parts, own_side))
    here = call(
        stack_kernel, shape((depth, broad), bf16), [vmem] * tiles, *parts, name="stack"
    )

    there = flipped(here, "tm", 1)

    def project(part, mine, got, kind, flip, flops=0):
        return call(
            project_kernel,
            shape((step, broad), kind),
            [vmem] * 4,
            out_weight,
            part,
            mine,
            got,
            name="project",
            flops=flops,
            flip=flip,
        )

    for_side = [project(here, own_side, got_side, bf16, 0, 20 * 10**9)]
    from_side = [flipped(for_side[0], "head", 1)]
    for_side.append(project(there, own_side, got_side, bf16, 1))
    from_side.append(flipped(for_side[1], "head", 1))
    state, for_far, for_side[1] = lax.optimization_barrier((state, for_far, for_side[1]))
    got_far = flipped(for_far, "head", 2)
    (own,) = rest(state, 0, flops=20 * 10**9)
    mine = [
        project(here, own, got_far, f32, 0),
        project(there, own, got_far, f32, 1, 20 * 10**9),
    ]
    pieces = 2
    mixed = []
    for flip in range(2):
        mixed = [
            pl.pallas_call(
                functools.partial(add_kernel, flip=flip),
                out_shape=shape((step, width), bf16),
                in_specs=[vmem] * 2 + [hbm] * flip,
                out_specs=hbm,
                input_output_aliases={2: 0} if flip else {},
                scratch_shapes=[
                    pltpu.VMEM((pieces, step // pieces, broad), bf16),
                    pltpu.SemaphoreType.DMA((pieces,)),
                ],
                compiler_params=pltpu.CompilerParams(vmem_limit_bytes=VMEM_LIMIT),
                name="add",
            )(mine[flip], from_side[flip], *mixed)
        ]
    (mixed,) = mixed
    return mixed.reshape(1, 1, step, width)


def solution(mesh):
    in_specs = (
        P("tm", "tile", None, None, None, "head"),
        P("tm", "tile", None, None, None, "head"),
        P("tm", "tile", None, None, None, "head"),
        P("head", None),
        P("head"),
        P("head", None, None),
    )
    out_specs = P("tm", "tile", "head", None)
    small = dict(mesh.shape) == {"tm": 2, "tile": 4, "head": 4}
    return jax.shard_map(
        two_by_two if small else any_grid,
        mesh=mesh,
        in_specs=in_specs,
        out_specs=out_specs,
        check_vma=False,
    )
```

```python
import functools
import math

import jax
import jax.numpy as jnp
from jax import lax
from jax.experimental import pallas as pl
from jax.experimental.pallas import tpu as pltpu
from jax.sharding import PartitionSpec as P

RMAX = 4
FAR = -1e30
LOG2E = 1.4426950408889634
VMEM_LIMIT = 24 * 1024 * 1024


def passed_along(value, axis, by):
    peers = lax.axis_size(axis)
    pairs = [(i, i + by) for i in range(peers) if 0 <= i + by < peers]
    return lax.ppermute(value, axis, pairs)


def widen(key_part, value_part, span, row_move, col_move):
    grid = math.isqrt(lax.axis_size("tile"))
    above = None
    below = None
    for offset in (grid, -grid):
        if offset > 0:
            face_key = key_part[:, :, key_part.shape[2] - span :]
            face_value = value_part[:, :, value_part.shape[2] - span :]
        else:
            face_key = key_part[:, :, :span]
            face_value = value_part[:, :, :span]
        got = row_move(face_key, face_value, offset)
        if offset > 0:
            above = got
        else:
            below = got
    key_rows = jnp.concatenate([above[0], key_part, below[0]], axis=2)
    value_rows = jnp.concatenate([above[1], value_part, below[1]], axis=2)
    left = None
    right = None
    for offset in (1, -1):
        if offset > 0:
            face_key = key_rows[:, :, :, key_rows.shape[3] - span :]
            face_value = value_rows[:, :, :, value_rows.shape[3] - span :]
        else:
            face_key = key_rows[:, :, :, :span]
            face_value = value_rows[:, :, :, :span]
        got = col_move(face_key, face_value, offset)
        if offset > 0:
            left = got
        else:
            right = got
    key_full = jnp.concatenate([left[0], key_rows, right[0]], axis=3)
    value_full = jnp.concatenate([left[1], value_rows, right[1]], axis=3)
    return (key_full, value_full)


def windows_of(block, half_high, half_wide, win_high, win_wide, heads_here, head_dim):
    parts = []
    for band in (0, 1):
        for strip in (0, 1):
            parts.append(
                block[
                    :,
                    band * half_high : band * half_high + win_high,
                    strip * half_wide : strip * half_wide + win_wide,
                ]
            )
    stacked = jnp.stack(parts)
    return stacked.reshape(4, -1, heads_here, head_dim)


def any_grid(query, keys, values, out_weight, radius, block_mask):
    span = RMAX
    grid = math.isqrt(lax.axis_size("tile"))
    tile_at = lax.axis_index("tile")
    row_at = tile_at // grid
    col_at = tile_at % grid
    stretch_at = lax.axis_index("tm")
    frames, high, wide, channels = query.shape[2:]
    heads_here = radius.shape[0]
    head_dim = channels // heads_here
    tokens_here = frames * high * wide
    half_high = high // 2
    half_wide = wide // 2
    win_high = half_high + 2 * span
    win_wide = half_wide + 2 * span
    quarter = frames * half_high * half_wide
    queries = query[0, 0].reshape(frames, 2, half_high, 2, half_wide, channels)
    queries = queries.transpose(1, 3, 0, 2, 4, 5).reshape(4, quarter, heads_here, head_dim)
    query_y = jnp.broadcast_to(
        jnp.arange(half_high, dtype=jnp.int32)[None, :, None], (frames, half_high, half_wide)
    ).reshape(-1)
    query_x = jnp.broadcast_to(
        jnp.arange(half_wide, dtype=jnp.int32)[None, None, :], (frames, half_high, half_wide)
    ).reshape(-1)
    key_y = jnp.broadcast_to(
        jnp.arange(win_high, dtype=jnp.int32)[None, :, None] - span, (frames, win_high, win_wide)
    ).reshape(-1)
    key_x = jnp.broadcast_to(
        jnp.arange(win_wide, dtype=jnp.int32)[None, None, :] - span, (frames, win_high, win_wide)
    ).reshape(-1)
    band_at = jnp.array([0, 0, 1, 1], dtype=jnp.int32)
    strip_at = jnp.array([0, 1, 0, 1], dtype=jnp.int32)
    global_y = row_at * high + band_at[:, None] * half_high + key_y[None, :]
    global_x = col_at * wide + strip_at[:, None] * half_wide + key_x[None, :]
    inside = (global_y >= 0) & (global_y < grid * high) & (global_x >= 0) & (global_x < grid * wide)
    distance = jnp.maximum(
        jnp.abs(query_y[:, None] - key_y[None, :]), jnp.abs(query_x[:, None] - key_x[None, :])
    )
    near = distance[None, :, :] <= radius[:, None, None]
    allowed = near[None, :, :, :] & inside[:, None, None, :]
    scale = 1.0 / math.sqrt(head_dim)
    initial = (
        jnp.full((4, heads_here, quarter), -1e30, jnp.float32),
        jnp.zeros((4, heads_here, quarter), jnp.float32),
        jnp.zeros((4, heads_here, quarter, head_dim), jnp.float32),
    )

    def tile_move(face_key, face_value, offset):
        return passed_along((face_key, face_value), "tile", offset)

    key_all, value_all = (
        lax.all_gather(keys[0], "tm", axis=0, tiled=True),
        lax.all_gather(values[0], "tm", axis=0, tiled=True),
    )
    key_full, value_full = widen(key_all, value_all, span, tile_move, tile_move)
    stretch_ids = jnp.arange(key_full.shape[0], dtype=jnp.int32)

    def one_stretch(state, item):
        key_block, value_block, stretch_id = item
        visible = (
            lax.dynamic_slice_in_dim(
                lax.dynamic_index_in_dim(block_mask, stretch_at, 1, False), stretch_id, 1, 1
            )[:, 0]
            > 0
        )
        best, total, acc = state
        key_win = windows_of(
            key_block, half_high, half_wide, win_high, win_wide, heads_here, head_dim
        )
        value_win = windows_of(
            value_block, half_high, half_wide, win_high, win_wide, heads_here, head_dim
        )
        usable = allowed & visible[None, :, None, None]
        scores = (
            jnp.einsum("nqhd,nkhd->nhqk", queries, key_win, preferred_element_type=jnp.float32)
            * scale
        )
        masked = jnp.where(usable, scores, jnp.float32(-1e30))
        fresh = jnp.maximum(best, jnp.max(masked, axis=3))
        probs = jnp.where(usable, jnp.exp(scores - fresh[..., None]), jnp.float32(0.0))
        shrink = jnp.exp(best - fresh)
        total = total * shrink + jnp.sum(probs, axis=3)
        acc = acc * shrink[..., None] + jnp.einsum(
            "nhqk,nkhd->nhqd",
            probs.astype(jnp.bfloat16),
            value_win,
            preferred_element_type=jnp.float32,
        )
        return ((fresh, total, acc), None)

    final, unused = lax.scan(one_stretch, initial, (key_full, value_full, stretch_ids))
    best, total, acc = final
    attn = (acc / total[..., None]).astype(jnp.bfloat16)
    attn = attn.transpose(0, 2, 1, 3).reshape(
        2, 2, frames, half_high, half_wide, heads_here * head_dim
    )
    attn = attn.transpose(2, 0, 3, 1, 4, 5).reshape(tokens_here, heads_here * head_dim)
    mixed = lax.psum_scatter(
        jnp.dot(attn, out_weight, preferred_element_type=jnp.float32).astype(jnp.bfloat16),
        "head",
        scatter_dimension=0,
        tiled=True,
    )
    return mixed.reshape(1, 1, -1, out_weight.shape[1])


def tile_place():
    tile_at = lax.axis_index("tile")
    return tile_at // 2, tile_at % 2


def part_kernel(w_ref, part_ref, sem):
    tall, broad = part_ref.shape
    top = pl.multiple_of(lax.axis_index("tile") * tall, 16)
    left = pl.multiple_of(lax.axis_index("tm") * broad, 128)
    copy = pltpu.make_async_copy(w_ref.at[pl.ds(top, tall), pl.ds(left, broad)], part_ref, sem)
    copy.start()
    copy.wait()


def face_kernel(k_ref, v_ref, part_ref, row_ref, col_ref, corner_ref, tile_ref, *, geometry):
    high, wide, span, frames = geometry[:4]
    cells = high * wide
    row_at, col_at = tile_place()
    y0 = jnp.where(row_at == 0, high - span, 0)
    x0 = jnp.where(col_at == 0, wide - span, 0)

    def picker(count, cell_of):
        row = lax.broadcasted_iota(jnp.int32, (count, cells), 0)
        col = lax.broadcasted_iota(jnp.int32, (count, cells), 1)
        return (col == cell_of(row)).astype(jnp.bfloat16)

    beside = picker(high * span, lambda i: (i // span) * wide + x0 + i % span)
    across = picker(span * span, lambda i: (y0 + i // span) * wide + x0 + i % span)
    for which, ref in enumerate((k_ref, v_ref)):
        tile_ref[which] = ref[...]
        for f in range(frames):
            start = pl.multiple_of(f * cells + y0 * wide, 16)
            row_ref[which, f] = ref[pl.ds(start, span * wide)]
            whole = ref[f * cells : (f + 1) * cells]
            col_ref[which, f] = jnp.dot(
                beside, whole, preferred_element_type=jnp.float32
            ).astype(jnp.bfloat16)
            corner_ref[which, f] = jnp.dot(
                across, whole, preferred_element_type=jnp.float32
            ).astype(jnp.bfloat16)


def edge_kernel(row_ref, col_ref, corner_ref, out_ref):
    for which in range(2):
        at = 0
        for part in (row_ref, col_ref, corner_ref):
            for f in range(part.shape[1]):
                size = part.shape[2]
                out_ref[which, at : at + size] = part[which, f]
                at += size


def distances(high, wide, span, frames):
    row_at, col_at = tile_place()
    cells = high * wide
    count = frames * (cells + span * (wide + high + span))
    j = lax.broadcasted_iota(jnp.int32, (1, count), 1)
    y_off = jnp.where(row_at == 0, high, -span)
    x_off = jnp.where(col_at == 0, wide, -span)
    c = j % cells
    ky, kx = c // wide, c % wide
    base = frames * cells
    c = (j - base) % (span * wide)
    ky = jnp.where(j >= base, y_off + c // wide, ky)
    kx = jnp.where(j >= base, c % wide, kx)
    base += frames * span * wide
    c = (j - base) % (span * high)
    ky = jnp.where(j >= base, c // span, ky)
    kx = jnp.where(j >= base, x_off + c % span, kx)
    base += frames * span * high
    c = (j - base) % (span * span)
    ky = jnp.where(j >= base, y_off + c // span, ky)
    kx = jnp.where(j >= base, x_off + c % span, kx)
    i = lax.broadcasted_iota(jnp.int32, (cells, 1), 0)
    return jnp.maximum(jnp.abs(i // wide - ky), jnp.abs(i % wide - kx))


def attend(units, factor):
    scores = [
        [
            jnp.where(
                dist <= reach,
                lax.dot_general(
                    q, k, (((1,), (1,)), ((), ())), preferred_element_type=jnp.float32
                )
                * factor,
                FAR,
            )
            for k, v, dist, reach in pieces
        ]
        for q, pieces, before in units
    ]
    tops = []
    for parts, (q, pieces, before) in zip(scores, units):
        found = [jnp.max(s, axis=1, keepdims=True) for s in parts]
        if before is not None:
            found.append(before)
        tops.append(functools.reduce(jnp.maximum, found))
    probs = [
        [jnp.exp2(s - m).astype(jnp.bfloat16) for s in parts] for parts, m in zip(scores, tops)
    ]
    sums = []
    for parts, (q, pieces, before) in zip(probs, units):
        total = None
        for p, (k, v, dist, reach) in zip(parts, pieces):
            both = jnp.concatenate([v, jnp.ones_like(v)], axis=1)
            got = jnp.dot(p, both, preferred_element_type=jnp.float32)
            total = got if total is None else total + got
        sums.append(total)
    return tops, sums


def attend_tile(q_ref, tile_ref, dist_ref, reach_of, heads, state, geometry):
    high, wide, span, frames, head_dim, factor, step = geometry
    cells = high * wide
    acc_ref, sum_ref, max_ref = state
    for at, head in enumerate(heads):
        cols = slice(head * head_dim, (head + 1) * head_dim)
        outs = slice(at * head_dim, (at + 1) * head_dim)
        starts = range(0, q_ref.shape[0], step)
        units = []
        for start in starts:
            near = dist_ref[start % cells : start % cells + step, : tile_ref.shape[1]]
            piece = (tile_ref[0, :, cols], tile_ref[1, :, cols], near, reach_of(head))
            units.append((q_ref[start : start + step, cols], [piece], None))
        for start, m, got in zip(starts, *attend(units, factor)):
            rows = slice(start, start + step)
            acc_ref[rows, outs] = got[:, :head_dim]
            sum_ref[rows, outs] = got[:, head_dim:]
            max_ref[rows, outs] = jnp.broadcast_to(m, (step, head_dim))


def begin_kernel(radius_ref, mask_ref, q_ref, tile_ref, *outs, geometry, heads):
    *state, dist_ref, reach_ref = outs
    high, wide, span, frames = geometry[:4]
    dist_ref[...] = distances(high, wide, span, frames)
    stretch_at = lax.axis_index("tm")
    line = (1, reach_ref.shape[1])
    for head in range(heads):
        radius = radius_ref[head]
        seen = mask_ref[stretch_at, 0, head] > 0
        reach_ref[head : head + 1] = jnp.full(line, radius, jnp.int32)
        reach_ref[heads + head : heads + head + 1] = jnp.full(
            line, jnp.where(seen, radius, -1), jnp.int32
        )
    attend_tile(q_ref, tile_ref, dist_ref, lambda h: radius_ref[h], (0,), state, geometry)


def tile_kernel(q_ref, tile_ref, dist_ref, reach_ref, *state, geometry, heads):
    attend_tile(
        q_ref,
        tile_ref,
        dist_ref,
        lambda h: reach_ref[h : h + 1, :1],
        range(1, heads),
        state,
        geometry,
    )


def pick_state(head_state, state, head, rows, head_dim):
    refs = head_state if head == 0 else state
    at = max(head - 1, 0) * head_dim
    return [ref[rows, at : at + head_dim] for ref in refs]


def rest_kernel(
    q_ref,
    edge_ref,
    first_tile_ref,
    first_edge_ref,
    *rest,
    geometry,
    heads,
    flips,
):
    head_state, dist_ref, reach_ref, state, outs = rest[:3], rest[3], rest[4], rest[5:8], rest[8:]
    high, wide, span, frames, head_dim, factor, step = geometry
    cells = high * wide
    base = frames * cells
    head_at = lax.axis_index("head")
    stretch_at = lax.axis_index("tm")

    def run(with_first):
        for flip, out_ref in zip(flips, outs):
            start = pl.multiple_of(jnp.bitwise_xor(head_at, flip) * step, step)
            rows = pl.ds(start, step)
            near = dist_ref[pl.ds(pl.multiple_of(lax.rem(start, cells), step), step)]
            beyond = near[:, base:]
            units = []
            olds = []
            for head in range(heads):
                cols = slice(head * head_dim, (head + 1) * head_dim)
                sources = [(edge_ref, beyond, head)]
                if with_first:
                    sources.append((first_tile_ref, near[:, :base], heads + head))
                    sources.append((first_edge_ref, beyond, heads + head))
                pieces = [
                    (ref[0, :, cols], ref[1, :, cols], dist, reach_ref[row : row + 1, :1])
                    for ref, dist, row in sources
                ]
                olds.append(pick_state(head_state, state, head, rows, head_dim))
                units.append((q_ref[rows, cols], pieces, olds[-1][2][:, :1]))
            for head, (m, got) in enumerate(zip(*attend(units, factor))):
                old_acc, old_total, old_max = olds[head]
                shrink = jnp.exp2(old_max - m)
                acc = old_acc * shrink + got[:, :head_dim]
                total = old_total * shrink + got[:, head_dim:]
                cols = slice(head * head_dim, (head + 1) * head_dim)
                out_ref[:, cols] = (acc / total).astype(jnp.bfloat16)

    @pl.when(stretch_at > 0)
    def _():
        run(True)

    @pl.when(stretch_at == 0)
    def _():
        run(False)


def copy_kernel(in_ref, out_ref):
    out_ref[...] = in_ref[...]


def stack_kernel(*refs):
    *parts, out_ref = refs
    tile_at = lax.axis_index("tile")
    for flip, part in enumerate(parts):
        tall = part.shape[0]
        top = pl.multiple_of(jnp.bitwise_xor(tile_at, flip) * tall, 16)
        out_ref[pl.ds(top, tall)] = part[...]


def project_kernel(w_ref, part_ref, own_ref, got_ref, out_ref, *, flip):
    broad = part_ref.shape[1]
    half = jnp.bitwise_xor(lax.axis_index("tm"), flip)
    cols = pl.ds(pl.multiple_of(half * broad, 128), broad)
    total = jnp.dot(own_ref[...], w_ref[:, cols], preferred_element_type=jnp.float32)
    total += jnp.dot(got_ref[...], part_ref[...], preferred_element_type=jnp.float32)
    out_ref[...] = total.astype(out_ref.dtype)


def add_kernel(mine_ref, got_ref, *rest, flip):
    out_ref, sum_ref, sems = rest[-3:]
    pieces, tall, broad = sum_ref.shape
    half = jnp.bitwise_xor(lax.axis_index("tm"), flip)
    cols = pl.ds(pl.multiple_of(half * broad, 128), broad)
    copies = []
    for i in range(pieces):
        rows = slice(i * tall, (i + 1) * tall)
        sum_ref[i] = (mine_ref[rows] + got_ref[rows].astype(jnp.float32)).astype(jnp.bfloat16)
        copies.append(pltpu.make_async_copy(sum_ref.at[i], out_ref.at[rows, cols], sems.at[i]))
        copies[-1].start()
    for copy in copies:
        copy.wait()


def two_by_two(query, keys, values, out_weight, radius, block_mask):
    span = RMAX
    frames, high, wide, channels = query.shape[2:]
    heads = radius.shape[0]
    head_dim = channels // heads
    cells = high * wide
    tokens = frames * cells
    groups = lax.axis_size("head")
    tiles = lax.axis_size("tile")
    depth, width = out_weight.shape
    step = tokens // groups
    geometry = (high, wide, span, frames, head_dim, LOG2E / math.sqrt(head_dim), step)
    count = frames * (cells + span * (wide + high + span))
    smem = pl.BlockSpec(memory_space=pltpu.SMEM)
    vmem = pl.BlockSpec(memory_space=pltpu.VMEM)
    hbm = pl.BlockSpec(memory_space=pltpu.HBM)
    bf16, f32 = jnp.bfloat16, jnp.float32
    shape = jax.ShapeDtypeStruct

    def call(kernel, out_shape, specs, *args, name, scratch=(), flops=0, **keys_of):
        return pl.pallas_call(
            functools.partial(kernel, **keys_of) if keys_of else kernel,
            out_shape=out_shape,
            in_specs=specs,
            out_specs=jax.tree.map(lambda _: vmem, out_shape),
            scratch_shapes=scratch,
            cost_estimate=pl.CostEstimate(flops=flops, bytes_accessed=0, transcendentals=0),
            compiler_params=pltpu.CompilerParams(vmem_limit_bytes=VMEM_LIMIT),
            name=name,
        )(*args)

    def flipped(value, axis, flip):
        return lax.ppermute(value, axis, [(i, i ^ flip) for i in range(lax.axis_size(axis))])

    q = query.reshape(tokens, channels)
    k = keys.reshape(tokens, channels)
    v = values.reshape(tokens, channels)

    tall, broad = depth // tiles, width // 2
    part_shape = shape((tall, broad), bf16)
    part = call(
        part_kernel,
        part_shape,
        [hbm],
        pltpu.with_memory_space_constraint(out_weight, pltpu.HBM),
        name="part",
        scratch=[pltpu.SemaphoreType.DMA],
    )
    *faces, tile = call(
        face_kernel,
        [
            shape((2, frames, span * wide, channels), bf16),
            shape((2, frames, span * high, channels), bf16),
            shape((2, frames, span * span, channels), bf16),
            shape((2, tokens, channels), bf16),
        ],
        [vmem] * 3,
        k,
        v,
        part,
        name="faces",
        geometry=geometry,
    )
    faces = [flipped(face, "tile", flip) for face, flip in zip(faces, (2, 1, 3))]
    lone = flipped(part, "head", 2)
    begun = call(
        begin_kernel,
        [shape((tokens, head_dim), f32)] * 3
        + [shape((cells, count), jnp.int32), shape((2 * heads, head_dim), jnp.int32)],
        [smem] * 2 + [vmem] * 2,
        radius,
        block_mask.transpose(1, 2, 0),
        q,
        tile,
        name="begin",
        geometry=geometry,
        heads=heads,
    )
    begun, tile = lax.optimization_barrier((begun, tile))
    first_tile = lax.ppermute(tile, "tm", [(0, 1)])
    state = call(
        tile_kernel,
        [shape((tokens, channels - head_dim), f32)] * 3,
        [vmem] * 4,
        q,
        tile,
        *begun[3:],
        name="tile",
        geometry=geometry,
        heads=heads,
    )
    lone, state = lax.optimization_barrier((lone, state))
    lone = call(copy_kernel, part_shape, [vmem], lone, name="lone", flops=2 * 10**9)
    lone, state, faces = lax.optimization_barrier((lone, state, faces))
    edge = call(
        edge_kernel, shape((2, count - tokens, channels), bf16), [vmem] * 3, *faces, name="edges", flops=20 * 10**9
    )
    first_edge = lax.ppermute(edge, "tm", [(0, 1)])
    parts = [lone] + [flipped(lone, "tile", flip) for flip in range(1, tiles)]

    def rest(state, *flips, flops=0):
        return call(
            rest_kernel,
            [shape((step, channels), bf16)] * len(flips),
            [vmem] * 12,
            q,
            edge,
            first_tile,
            first_edge,
            *begun,
            *state,
            name="rest",
            geometry=geometry,
            heads=heads,
            flips=flips,
            flops=flops,
        )

    (for_side,) = rest(state, 3)
    got_side = flipped(for_side, "head", 2)
    state, for_side = lax.optimization_barrier((state, for_side))
    for_far, own_side = rest(state, 2, 1)
    parts, own_side = lax.optimization_barrier((parts, own_side))
    here = call(
        stack_kernel, shape((depth, broad), bf16), [vmem] * tiles, *parts, name="stack"
    )

    there = flipped(here, "tm", 1)

    def project(part, mine, got, kind, flip, flops=0):
        return call(
            project_kernel,
            shape((step, broad), kind),
            [vmem] * 4,
            out_weight,
            part,
            mine,
            got,
            name="project",
            flops=flops,
            flip=flip,
        )

    for_side = [project(here, own_side, got_side, bf16, 0, 20 * 10**9)]
    from_side = [flipped(for_side[0], "head", 1)]
    for_far, for_side[0] = lax.optimization_barrier((for_far, for_side[0]))
    got_far = flipped(for_far, "head", 2)
    for_side.append(project(there, own_side, got_side, bf16, 1))
    from_side.append(flipped(for_side[1], "head", 1))
    state, for_side[1] = lax.optimization_barrier((state, for_side[1]))
    (own,) = rest(state, 0, flops=20 * 10**9)
    mine = [
        project(here, own, got_far, f32, 0),
        project(there, own, got_far, f32, 1, 20 * 10**9),
    ]
    pieces = 2
    mixed = []
    for flip in range(2):
        mixed = [
            pl.pallas_call(
                functools.partial(add_kernel, flip=flip),
                out_shape=shape((step, width), bf16),
                in_specs=[vmem] * 2 + [hbm] * flip,
                out_specs=hbm,
                input_output_aliases={2: 0} if flip else {},
                scratch_shapes=[
                    pltpu.VMEM((pieces, step // pieces, broad), bf16),
                    pltpu.SemaphoreType.DMA((pieces,)),
                ],
                compiler_params=pltpu.CompilerParams(vmem_limit_bytes=VMEM_LIMIT),
                name="add",
            )(mine[flip], from_side[flip], *mixed)
        ]
    (mixed,) = mixed
    return mixed.reshape(1, 1, step, width)


def solution(mesh):
    in_specs = (
        P("tm", "tile", None, None, None, "head"),
        P("tm", "tile", None, None, None, "head"),
        P("tm", "tile", None, None, None, "head"),
        P("head", None),
        P("head"),
        P("head", None, None),
    )
    out_specs = P("tm", "tile", "head", None)
    small = dict(mesh.shape) == {"tm": 2, "tile": 4, "head": 4}
    return jax.shard_map(
        two_by_two if small else any_grid,
        mesh=mesh,
        in_specs=in_specs,
        out_specs=out_specs,
        check_vma=False,
    )
```

```python
import functools
import math

import jax
import jax.numpy as jnp
from jax import lax
from jax.experimental import pallas as pl
from jax.experimental.pallas import tpu as pltpu
from jax.sharding import PartitionSpec as P

RMAX = 4
FAR = -1e30
LOG2E = 1.4426950408889634
VMEM_LIMIT = 24 * 1024 * 1024


def passed_along(value, axis, by):
    peers = lax.axis_size(axis)
    pairs = [(i, i + by) for i in range(peers) if 0 <= i + by < peers]
    return lax.ppermute(value, axis, pairs)


def widen(key_part, value_part, span, row_move, col_move):
    grid = math.isqrt(lax.axis_size("tile"))
    above = None
    below = None
    for offset in (grid, -grid):
        if offset > 0:
            face_key = key_part[:, :, key_part.shape[2] - span :]
            face_value = value_part[:, :, value_part.shape[2] - span :]
        else:
            face_key = key_part[:, :, :span]
            face_value = value_part[:, :, :span]
        got = row_move(face_key, face_value, offset)
        if offset > 0:
            above = got
        else:
            below = got
    key_rows = jnp.concatenate([above[0], key_part, below[0]], axis=2)
    value_rows = jnp.concatenate([above[1], value_part, below[1]], axis=2)
    left = None
    right = None
    for offset in (1, -1):
        if offset > 0:
            face_key = key_rows[:, :, :, key_rows.shape[3] - span :]
            face_value = value_rows[:, :, :, value_rows.shape[3] - span :]
        else:
            face_key = key_rows[:, :, :, :span]
            face_value = value_rows[:, :, :, :span]
        got = col_move(face_key, face_value, offset)
        if offset > 0:
            left = got
        else:
            right = got
    key_full = jnp.concatenate([left[0], key_rows, right[0]], axis=3)
    value_full = jnp.concatenate([left[1], value_rows, right[1]], axis=3)
    return (key_full, value_full)


def windows_of(block, half_high, half_wide, win_high, win_wide, heads_here, head_dim):
    parts = []
    for band in (0, 1):
        for strip in (0, 1):
            parts.append(
                block[
                    :,
                    band * half_high : band * half_high + win_high,
                    strip * half_wide : strip * half_wide + win_wide,
                ]
            )
    stacked = jnp.stack(parts)
    return stacked.reshape(4, -1, heads_here, head_dim)


def any_grid(query, keys, values, out_weight, radius, block_mask):
    span = RMAX
    grid = math.isqrt(lax.axis_size("tile"))
    tile_at = lax.axis_index("tile")
    row_at = tile_at // grid
    col_at = tile_at % grid
    stretch_at = lax.axis_index("tm")
    frames, high, wide, channels = query.shape[2:]
    heads_here = radius.shape[0]
    head_dim = channels // heads_here
    tokens_here = frames * high * wide
    half_high = high // 2
    half_wide = wide // 2
    win_high = half_high + 2 * span
    win_wide = half_wide + 2 * span
    quarter = frames * half_high * half_wide
    queries = query[0, 0].reshape(frames, 2, half_high, 2, half_wide, channels)
    queries = queries.transpose(1, 3, 0, 2, 4, 5).reshape(4, quarter, heads_here, head_dim)
    query_y = jnp.broadcast_to(
        jnp.arange(half_high, dtype=jnp.int32)[None, :, None], (frames, half_high, half_wide)
    ).reshape(-1)
    query_x = jnp.broadcast_to(
        jnp.arange(half_wide, dtype=jnp.int32)[None, None, :], (frames, half_high, half_wide)
    ).reshape(-1)
    key_y = jnp.broadcast_to(
        jnp.arange(win_high, dtype=jnp.int32)[None, :, None] - span, (frames, win_high, win_wide)
    ).reshape(-1)
    key_x = jnp.broadcast_to(
        jnp.arange(win_wide, dtype=jnp.int32)[None, None, :] - span, (frames, win_high, win_wide)
    ).reshape(-1)
    band_at = jnp.array([0, 0, 1, 1], dtype=jnp.int32)
    strip_at = jnp.array([0, 1, 0, 1], dtype=jnp.int32)
    global_y = row_at * high + band_at[:, None] * half_high + key_y[None, :]
    global_x = col_at * wide + strip_at[:, None] * half_wide + key_x[None, :]
    inside = (global_y >= 0) & (global_y < grid * high) & (global_x >= 0) & (global_x < grid * wide)
    distance = jnp.maximum(
        jnp.abs(query_y[:, None] - key_y[None, :]), jnp.abs(query_x[:, None] - key_x[None, :])
    )
    near = distance[None, :, :] <= radius[:, None, None]
    allowed = near[None, :, :, :] & inside[:, None, None, :]
    scale = 1.0 / math.sqrt(head_dim)
    initial = (
        jnp.full((4, heads_here, quarter), -1e30, jnp.float32),
        jnp.zeros((4, heads_here, quarter), jnp.float32),
        jnp.zeros((4, heads_here, quarter, head_dim), jnp.float32),
    )

    def tile_move(face_key, face_value, offset):
        return passed_along((face_key, face_value), "tile", offset)

    key_all, value_all = (
        lax.all_gather(keys[0], "tm", axis=0, tiled=True),
        lax.all_gather(values[0], "tm", axis=0, tiled=True),
    )
    key_full, value_full = widen(key_all, value_all, span, tile_move, tile_move)
    stretch_ids = jnp.arange(key_full.shape[0], dtype=jnp.int32)

    def one_stretch(state, item):
        key_block, value_block, stretch_id = item
        visible = (
            lax.dynamic_slice_in_dim(
                lax.dynamic_index_in_dim(block_mask, stretch_at, 1, False), stretch_id, 1, 1
            )[:, 0]
            > 0
        )
        best, total, acc = state
        key_win = windows_of(
            key_block, half_high, half_wide, win_high, win_wide, heads_here, head_dim
        )
        value_win = windows_of(
            value_block, half_high, half_wide, win_high, win_wide, heads_here, head_dim
        )
        usable = allowed & visible[None, :, None, None]
        scores = (
            jnp.einsum("nqhd,nkhd->nhqk", queries, key_win, preferred_element_type=jnp.float32)
            * scale
        )
        masked = jnp.where(usable, scores, jnp.float32(-1e30))
        fresh = jnp.maximum(best, jnp.max(masked, axis=3))
        probs = jnp.where(usable, jnp.exp(scores - fresh[..., None]), jnp.float32(0.0))
        shrink = jnp.exp(best - fresh)
        total = total * shrink + jnp.sum(probs, axis=3)
        acc = acc * shrink[..., None] + jnp.einsum(
            "nhqk,nkhd->nhqd",
            probs.astype(jnp.bfloat16),
            value_win,
            preferred_element_type=jnp.float32,
        )
        return ((fresh, total, acc), None)

    final, unused = lax.scan(one_stretch, initial, (key_full, value_full, stretch_ids))
    best, total, acc = final
    attn = (acc / total[..., None]).astype(jnp.bfloat16)
    attn = attn.transpose(0, 2, 1, 3).reshape(
        2, 2, frames, half_high, half_wide, heads_here * head_dim
    )
    attn = attn.transpose(2, 0, 3, 1, 4, 5).reshape(tokens_here, heads_here * head_dim)
    mixed = lax.psum_scatter(
        jnp.dot(attn, out_weight, preferred_element_type=jnp.float32).astype(jnp.bfloat16),
        "head",
        scatter_dimension=0,
        tiled=True,
    )
    return mixed.reshape(1, 1, -1, out_weight.shape[1])


def tile_place():
    tile_at = lax.axis_index("tile")
    return tile_at // 2, tile_at % 2


def part_kernel(w_ref, part_ref, sem):
    tall, broad = part_ref.shape
    top = pl.multiple_of(lax.axis_index("tile") * tall, 16)
    left = pl.multiple_of(lax.axis_index("tm") * broad, 128)
    copy = pltpu.make_async_copy(w_ref.at[pl.ds(top, tall), pl.ds(left, broad)], part_ref, sem)
    copy.start()
    copy.wait()


def face_kernel(k_ref, v_ref, part_ref, row_ref, col_ref, corner_ref, tile_ref, *, geometry):
    high, wide, span, frames = geometry[:4]
    cells = high * wide
    row_at, col_at = tile_place()
    y0 = jnp.where(row_at == 0, high - span, 0)
    x0 = jnp.where(col_at == 0, wide - span, 0)

    def picker(count, cell_of):
        row = lax.broadcasted_iota(jnp.int32, (count, cells), 0)
        col = lax.broadcasted_iota(jnp.int32, (count, cells), 1)
        return (col == cell_of(row)).astype(jnp.bfloat16)

    beside = picker(high * span, lambda i: (i // span) * wide + x0 + i % span)
    across = picker(span * span, lambda i: (y0 + i // span) * wide + x0 + i % span)
    for which, ref in enumerate((k_ref, v_ref)):
        tile_ref[which] = ref[...]
        for f in range(frames):
            start = pl.multiple_of(f * cells + y0 * wide, 16)
            row_ref[which, f] = ref[pl.ds(start, span * wide)]
            whole = ref[f * cells : (f + 1) * cells]
            col_ref[which, f] = jnp.dot(
                beside, whole, preferred_element_type=jnp.float32
            ).astype(jnp.bfloat16)
            corner_ref[which, f] = jnp.dot(
                across, whole, preferred_element_type=jnp.float32
            ).astype(jnp.bfloat16)


def edge_kernel(row_ref, col_ref, corner_ref, out_ref):
    for which in range(2):
        at = 0
        for part in (row_ref, col_ref, corner_ref):
            for f in range(part.shape[1]):
                size = part.shape[2]
                out_ref[which, at : at + size] = part[which, f]
                at += size


def distances(high, wide, span, frames):
    row_at, col_at = tile_place()
    cells = high * wide
    count = frames * (cells + span * (wide + high + span))
    j = lax.broadcasted_iota(jnp.int32, (1, count), 1)
    y_off = jnp.where(row_at == 0, high, -span)
    x_off = jnp.where(col_at == 0, wide, -span)
    c = j % cells
    ky, kx = c // wide, c % wide
    base = frames * cells
    c = (j - base) % (span * wide)
    ky = jnp.where(j >= base, y_off + c // wide, ky)
    kx = jnp.where(j >= base, c % wide, kx)
    base += frames * span * wide
    c = (j - base) % (span * high)
    ky = jnp.where(j >= base, c // span, ky)
    kx = jnp.where(j >= base, x_off + c % span, kx)
    base += frames * span * high
    c = (j - base) % (span * span)
    ky = jnp.where(j >= base, y_off + c // span, ky)
    kx = jnp.where(j >= base, x_off + c % span, kx)
    i = lax.broadcasted_iota(jnp.int32, (cells, 1), 0)
    return jnp.maximum(jnp.abs(i // wide - ky), jnp.abs(i % wide - kx))


def attend(units, factor):
    scores = [
        [
            jnp.where(
                dist <= reach,
                lax.dot_general(
                    q, k, (((1,), (1,)), ((), ())), preferred_element_type=jnp.float32
                )
                * factor,
                FAR,
            )
            for k, v, dist, reach in pieces
        ]
        for q, pieces, before in units
    ]
    tops = []
    for parts, (q, pieces, before) in zip(scores, units):
        found = [jnp.max(s, axis=1, keepdims=True) for s in parts]
        if before is not None:
            found.append(before)
        tops.append(functools.reduce(jnp.maximum, found))
    probs = [
        [jnp.exp2(s - m).astype(jnp.bfloat16) for s in parts] for parts, m in zip(scores, tops)
    ]
    sums = []
    for parts, (q, pieces, before) in zip(probs, units):
        total = None
        for p, (k, v, dist, reach) in zip(parts, pieces):
            both = jnp.concatenate([v, jnp.ones_like(v)], axis=1)
            got = jnp.dot(p, both, preferred_element_type=jnp.float32)
            total = got if total is None else total + got
        sums.append(total)
    return tops, sums


def attend_tile(q_ref, tile_ref, dist_ref, reach_of, heads, state, geometry):
    high, wide, span, frames, head_dim, factor, step = geometry
    cells = high * wide
    acc_ref, sum_ref, max_ref = state
    for at, head in enumerate(heads):
        cols = slice(head * head_dim, (head + 1) * head_dim)
        outs = slice(at * head_dim, (at + 1) * head_dim)
        starts = range(0, q_ref.shape[0], step)
        units = []
        for start in starts:
            near = dist_ref[start % cells : start % cells + step, : tile_ref.shape[1]]
            piece = (tile_ref[0, :, cols], tile_ref[1, :, cols], near, reach_of(head))
            units.append((q_ref[start : start + step, cols], [piece], None))
        for start, m, got in zip(starts, *attend(units, factor)):
            rows = slice(start, start + step)
            acc_ref[rows, outs] = got[:, :head_dim]
            sum_ref[rows, outs] = got[:, head_dim:]
            max_ref[rows, outs] = jnp.broadcast_to(m, (step, head_dim))


def begin_kernel(radius_ref, mask_ref, q_ref, tile_ref, *outs, geometry, heads):
    *state, dist_ref, reach_ref = outs
    high, wide, span, frames = geometry[:4]
    dist_ref[...] = distances(high, wide, span, frames)
    stretch_at = lax.axis_index("tm")
    line = (1, reach_ref.shape[1])
    for head in range(heads):
        radius = radius_ref[head]
        seen = mask_ref[stretch_at, 0, head] > 0
        reach_ref[head : head + 1] = jnp.full(line, radius, jnp.int32)
        reach_ref[heads + head : heads + head + 1] = jnp.full(
            line, jnp.where(seen, radius, -1), jnp.int32
        )
    attend_tile(q_ref, tile_ref, dist_ref, lambda h: radius_ref[h], (0,), state, geometry)


def tile_kernel(q_ref, tile_ref, dist_ref, reach_ref, *state, geometry, heads):
    attend_tile(
        q_ref,
        tile_ref,
        dist_ref,
        lambda h: reach_ref[h : h + 1, :1],
        range(1, heads),
        state,
        geometry,
    )


def pick_state(head_state, state, head, rows, head_dim):
    refs = head_state if head == 0 else state
    at = max(head - 1, 0) * head_dim
    return [ref[rows, at : at + head_dim] for ref in refs]


def rest_kernel(
    q_ref,
    edge_ref,
    first_tile_ref,
    first_edge_ref,
    *rest,
    geometry,
    heads,
    flips,
):
    head_state, dist_ref, reach_ref, state, outs = rest[:3], rest[3], rest[4], rest[5:8], rest[8:]
    high, wide, span, frames, head_dim, factor, step = geometry
    cells = high * wide
    base = frames * cells
    head_at = lax.axis_index("head")
    stretch_at = lax.axis_index("tm")

    def run(with_first):
        for flip, out_ref in zip(flips, outs):
            start = pl.multiple_of(jnp.bitwise_xor(head_at, flip) * step, step)
            rows = pl.ds(start, step)
            near = dist_ref[pl.ds(pl.multiple_of(lax.rem(start, cells), step), step)]
            beyond = near[:, base:]
            units = []
            olds = []
            for head in range(heads):
                cols = slice(head * head_dim, (head + 1) * head_dim)
                sources = [(edge_ref, beyond, head)]
                if with_first:
                    sources.append((first_tile_ref, near[:, :base], heads + head))
                    sources.append((first_edge_ref, beyond, heads + head))
                pieces = [
                    (ref[0, :, cols], ref[1, :, cols], dist, reach_ref[row : row + 1, :1])
                    for ref, dist, row in sources
                ]
                olds.append(pick_state(head_state, state, head, rows, head_dim))
                units.append((q_ref[rows, cols], pieces, olds[-1][2][:, :1]))
            for head, (m, got) in enumerate(zip(*attend(units, factor))):
                old_acc, old_total, old_max = olds[head]
                shrink = jnp.exp2(old_max - m)
                acc = old_acc * shrink + got[:, :head_dim]
                total = old_total * shrink + got[:, head_dim:]
                cols = slice(head * head_dim, (head + 1) * head_dim)
                out_ref[:, cols] = (acc / total).astype(jnp.bfloat16)

    @pl.when(stretch_at > 0)
    def _():
        run(True)

    @pl.when(stretch_at == 0)
    def _():
        run(False)


def copy_kernel(in_ref, out_ref):
    out_ref[...] = in_ref[...]


def stack_kernel(*refs):
    *parts, out_ref = refs
    tile_at = lax.axis_index("tile")
    for flip, part in enumerate(parts):
        tall = part.shape[0]
        top = pl.multiple_of(jnp.bitwise_xor(tile_at, flip) * tall, 16)
        out_ref[pl.ds(top, tall)] = part[...]


def project_kernel(w_ref, part_ref, own_ref, *rest, flip):
    *got_refs, out_ref = rest
    broad = part_ref.shape[1]
    core = lax.axis_index("tm")
    half = jnp.bitwise_xor(core, flip)
    cols = pl.ds(pl.multiple_of(half * broad, 128), broad)
    got = got_refs[0][...]
    for at, ref in enumerate(got_refs[1:], 1):
        got = jnp.where(core == at, ref[...], got)
    total = jnp.dot(own_ref[...], w_ref[:, cols], preferred_element_type=jnp.float32)
    total += jnp.dot(got, part_ref[...], preferred_element_type=jnp.float32)
    out_ref[...] = total.astype(out_ref.dtype)


def add_kernel(mine_ref, got_ref, *rest, flip):
    out_ref, sum_ref, sems = rest[-3:]
    pieces, tall, broad = sum_ref.shape
    half = jnp.bitwise_xor(lax.axis_index("tm"), flip)
    cols = pl.ds(pl.multiple_of(half * broad, 128), broad)
    copies = []
    for i in range(pieces):
        rows = slice(i * tall, (i + 1) * tall)
        sum_ref[i] = (mine_ref[rows] + got_ref[rows].astype(jnp.float32)).astype(jnp.bfloat16)
        copies.append(pltpu.make_async_copy(sum_ref.at[i], out_ref.at[rows, cols], sems.at[i]))
        copies[-1].start()
    for copy in copies:
        copy.wait()


def two_by_two(query, keys, values, out_weight, radius, block_mask):
    span = RMAX
    frames, high, wide, channels = query.shape[2:]
    heads = radius.shape[0]
    head_dim = channels // heads
    cells = high * wide
    tokens = frames * cells
    groups = lax.axis_size("head")
    tiles = lax.axis_size("tile")
    depth, width = out_weight.shape
    step = tokens // groups
    geometry = (high, wide, span, frames, head_dim, LOG2E / math.sqrt(head_dim), step)
    count = frames * (cells + span * (wide + high + span))
    smem = pl.BlockSpec(memory_space=pltpu.SMEM)
    vmem = pl.BlockSpec(memory_space=pltpu.VMEM)
    hbm = pl.BlockSpec(memory_space=pltpu.HBM)
    bf16, f32 = jnp.bfloat16, jnp.float32
    shape = jax.ShapeDtypeStruct

    def call(kernel, out_shape, specs, *args, name, scratch=(), flops=0, **keys_of):
        return pl.pallas_call(
            functools.partial(kernel, **keys_of) if keys_of else kernel,
            out_shape=out_shape,
            in_specs=specs,
            out_specs=jax.tree.map(lambda _: vmem, out_shape),
            scratch_shapes=scratch,
            cost_estimate=pl.CostEstimate(flops=flops, bytes_accessed=0, transcendentals=0),
            compiler_params=pltpu.CompilerParams(vmem_limit_bytes=VMEM_LIMIT),
            name=name,
        )(*args)

    def flipped(value, axis, flip):
        return lax.ppermute(value, axis, [(i, i ^ flip) for i in range(lax.axis_size(axis))])

    def flipped_head(value, flip, stretch):
        at = [stretch * groups + i for i in range(groups)]
        pairs = [(at[i], at[i ^ flip]) for i in range(groups)]
        return lax.ppermute(value, ("tm", "head"), pairs)

    q = query.reshape(tokens, channels)
    k = keys.reshape(tokens, channels)
    v = values.reshape(tokens, channels)

    tall, broad = depth // tiles, width // 2
    part_shape = shape((tall, broad), bf16)
    part = call(
        part_kernel,
        part_shape,
        [hbm],
        pltpu.with_memory_space_constraint(out_weight, pltpu.HBM),
        name="part",
        scratch=[pltpu.SemaphoreType.DMA],
    )
    *faces, tile = call(
        face_kernel,
        [
            shape((2, frames, span * wide, channels), bf16),
            shape((2, frames, span * high, channels), bf16),
            shape((2, frames, span * span, channels), bf16),
            shape((2, tokens, channels), bf16),
        ],
        [vmem] * 3,
        k,
        v,
        part,
        name="faces",
        geometry=geometry,
    )
    faces = [flipped(face, "tile", flip) for face, flip in zip(faces, (2, 1, 3))]
    lone = flipped(part, "head", 2)
    begun = call(
        begin_kernel,
        [shape((tokens, head_dim), f32)] * 3
        + [shape((cells, count), jnp.int32), shape((2 * heads, head_dim), jnp.int32)],
        [smem] * 2 + [vmem] * 2,
        radius,
        block_mask.transpose(1, 2, 0),
        q,
        tile,
        name="begin",
        geometry=geometry,
        heads=heads,
    )
    begun, tile = lax.optimization_barrier((begun, tile))
    first_tile = lax.ppermute(tile, "tm", [(0, 1)])
    state = call(
        tile_kernel,
        [shape((tokens, channels - head_dim), f32)] * 3,
        [vmem] * 4,
        q,
        tile,
        *begun[3:],
        name="tile",
        geometry=geometry,
        heads=heads,
    )
    lone, state = lax.optimization_barrier((lone, state))
    lone = call(copy_kernel, part_shape, [vmem], lone, name="lone", flops=2 * 10**9)
    lone, state, faces = lax.optimization_barrier((lone, state, faces))
    edge = call(
        edge_kernel, shape((2, count - tokens, channels), bf16), [vmem] * 3, *faces, name="edges", flops=20 * 10**9
    )
    first_edge = lax.ppermute(edge, "tm", [(0, 1)])
    parts = [lone] + [flipped(lone, "tile", flip) for flip in range(1, tiles)]

    def rest(state, *flips, flops=0):
        return call(
            rest_kernel,
            [shape((step, channels), bf16)] * len(flips),
            [vmem] * 12,
            q,
            edge,
            first_tile,
            first_edge,
            *begun,
            *state,
            name="rest",
            geometry=geometry,
            heads=heads,
            flips=flips,
            flops=flops,
        )

    (for_side,) = rest(state, 3)
    got_side = flipped(for_side, "head", 2)
    state, for_side = lax.optimization_barrier((state, for_side))
    for_far, own_side = rest(state, 2, 1)
    got_far = [flipped_head(for_far, 2, 0)]
    parts, own_side = lax.optimization_barrier((parts, own_side))
    here = call(
        stack_kernel, shape((depth, broad), bf16), [vmem] * tiles, *parts, name="stack"
    )

    def project(part, mine, got, kind, flip, flops=0):
        return call(
            project_kernel,
            shape((step, broad), kind),
            [vmem] * (3 + len(got)),
            out_weight,
            part,
            mine,
            *got,
            name="project",
            flops=flops,
            flip=flip,
        )

    for_side = [project(here, own_side, [got_side], bf16, 0, 20 * 10**9)]
    from_side = [flipped(for_side[0], "head", 1)]
    state, here, for_far, for_side[0] = lax.optimization_barrier(
        (state, here, for_far, for_side[0])
    )
    got_far.append(flipped_head(for_far, 2, 1))
    there = flipped(here, "tm", 1)
    (own,) = rest(state, 0, flops=20 * 10**9)
    own_side, own = lax.optimization_barrier((own_side, own))
    for_side.append(project(there, own_side, [got_side], bf16, 1))
    from_side.append(flipped(for_side[1], "head", 1))
    own, for_side[1] = lax.optimization_barrier((own, for_side[1]))
    mine = [
        project(here, own, got_far, f32, 0),
        project(there, own, got_far, f32, 1, 20 * 10**9),
    ]
    pieces = 2
    mixed = []
    for flip in range(2):
        mixed = [
            pl.pallas_call(
                functools.partial(add_kernel, flip=flip),
                out_shape=shape((step, width), bf16),
                in_specs=[vmem] * 2 + [hbm] * flip,
                out_specs=hbm,
                input_output_aliases={2: 0} if flip else {},
                scratch_shapes=[
                    pltpu.VMEM((pieces, step // pieces, broad), bf16),
                    pltpu.SemaphoreType.DMA((pieces,)),
                ],
                compiler_params=pltpu.CompilerParams(vmem_limit_bytes=VMEM_LIMIT),
                name="add",
            )(mine[flip], from_side[flip], *mixed)
        ]
    (mixed,) = mixed
    return mixed.reshape(1, 1, step, width)


def solution(mesh):
    in_specs = (
        P("tm", "tile", None, None, None, "head"),
        P("tm", "tile", None, None, None, "head"),
        P("tm", "tile", None, None, None, "head"),
        P("head", None),
        P("head"),
        P("head", None, None),
    )
    out_specs = P("tm", "tile", "head", None)
    small = dict(mesh.shape) == {"tm": 2, "tile": 4, "head": 4}
    return jax.shard_map(
        two_by_two if small else any_grid,
        mesh=mesh,
        in_specs=in_specs,
        out_specs=out_specs,
        check_vma=False,
    )
```

```python
import functools
import math

import jax
import jax.numpy as jnp
from jax import lax
from jax.experimental import pallas as pl
from jax.experimental.pallas import tpu as pltpu
from jax.sharding import PartitionSpec as P

RMAX = 4
FAR = -1e30
LOG2E = 1.4426950408889634
VMEM_LIMIT = 24 * 1024 * 1024


def passed_along(value, axis, by):
    peers = lax.axis_size(axis)
    pairs = [(i, i + by) for i in range(peers) if 0 <= i + by < peers]
    return lax.ppermute(value, axis, pairs)


def widen(key_part, value_part, span, row_move, col_move):
    grid = math.isqrt(lax.axis_size("tile"))
    above = None
    below = None
    for offset in (grid, -grid):
        if offset > 0:
            face_key = key_part[:, :, key_part.shape[2] - span :]
            face_value = value_part[:, :, value_part.shape[2] - span :]
        else:
            face_key = key_part[:, :, :span]
            face_value = value_part[:, :, :span]
        got = row_move(face_key, face_value, offset)
        if offset > 0:
            above = got
        else:
            below = got
    key_rows = jnp.concatenate([above[0], key_part, below[0]], axis=2)
    value_rows = jnp.concatenate([above[1], value_part, below[1]], axis=2)
    left = None
    right = None
    for offset in (1, -1):
        if offset > 0:
            face_key = key_rows[:, :, :, key_rows.shape[3] - span :]
            face_value = value_rows[:, :, :, value_rows.shape[3] - span :]
        else:
            face_key = key_rows[:, :, :, :span]
            face_value = value_rows[:, :, :, :span]
        got = col_move(face_key, face_value, offset)
        if offset > 0:
            left = got
        else:
            right = got
    key_full = jnp.concatenate([left[0], key_rows, right[0]], axis=3)
    value_full = jnp.concatenate([left[1], value_rows, right[1]], axis=3)
    return (key_full, value_full)


def windows_of(block, half_high, half_wide, win_high, win_wide, heads_here, head_dim):
    parts = []
    for band in (0, 1):
        for strip in (0, 1):
            parts.append(
                block[
                    :,
                    band * half_high : band * half_high + win_high,
                    strip * half_wide : strip * half_wide + win_wide,
                ]
            )
    stacked = jnp.stack(parts)
    return stacked.reshape(4, -1, heads_here, head_dim)


def any_grid(query, keys, values, out_weight, radius, block_mask):
    span = RMAX
    grid = math.isqrt(lax.axis_size("tile"))
    tile_at = lax.axis_index("tile")
    row_at = tile_at // grid
    col_at = tile_at % grid
    stretch_at = lax.axis_index("tm")
    frames, high, wide, channels = query.shape[2:]
    heads_here = radius.shape[0]
    head_dim = channels // heads_here
    tokens_here = frames * high * wide
    half_high = high // 2
    half_wide = wide // 2
    win_high = half_high + 2 * span
    win_wide = half_wide + 2 * span
    quarter = frames * half_high * half_wide
    queries = query[0, 0].reshape(frames, 2, half_high, 2, half_wide, channels)
    queries = queries.transpose(1, 3, 0, 2, 4, 5).reshape(4, quarter, heads_here, head_dim)
    query_y = jnp.broadcast_to(
        jnp.arange(half_high, dtype=jnp.int32)[None, :, None], (frames, half_high, half_wide)
    ).reshape(-1)
    query_x = jnp.broadcast_to(
        jnp.arange(half_wide, dtype=jnp.int32)[None, None, :], (frames, half_high, half_wide)
    ).reshape(-1)
    key_y = jnp.broadcast_to(
        jnp.arange(win_high, dtype=jnp.int32)[None, :, None] - span, (frames, win_high, win_wide)
    ).reshape(-1)
    key_x = jnp.broadcast_to(
        jnp.arange(win_wide, dtype=jnp.int32)[None, None, :] - span, (frames, win_high, win_wide)
    ).reshape(-1)
    band_at = jnp.array([0, 0, 1, 1], dtype=jnp.int32)
    strip_at = jnp.array([0, 1, 0, 1], dtype=jnp.int32)
    global_y = row_at * high + band_at[:, None] * half_high + key_y[None, :]
    global_x = col_at * wide + strip_at[:, None] * half_wide + key_x[None, :]
    inside = (global_y >= 0) & (global_y < grid * high) & (global_x >= 0) & (global_x < grid * wide)
    distance = jnp.maximum(
        jnp.abs(query_y[:, None] - key_y[None, :]), jnp.abs(query_x[:, None] - key_x[None, :])
    )
    near = distance[None, :, :] <= radius[:, None, None]
    allowed = near[None, :, :, :] & inside[:, None, None, :]
    scale = 1.0 / math.sqrt(head_dim)
    initial = (
        jnp.full((4, heads_here, quarter), -1e30, jnp.float32),
        jnp.zeros((4, heads_here, quarter), jnp.float32),
        jnp.zeros((4, heads_here, quarter, head_dim), jnp.float32),
    )

    def tile_move(face_key, face_value, offset):
        return passed_along((face_key, face_value), "tile", offset)

    key_all, value_all = (
        lax.all_gather(keys[0], "tm", axis=0, tiled=True),
        lax.all_gather(values[0], "tm", axis=0, tiled=True),
    )
    key_full, value_full = widen(key_all, value_all, span, tile_move, tile_move)
    stretch_ids = jnp.arange(key_full.shape[0], dtype=jnp.int32)

    def one_stretch(state, item):
        key_block, value_block, stretch_id = item
        visible = (
            lax.dynamic_slice_in_dim(
                lax.dynamic_index_in_dim(block_mask, stretch_at, 1, False), stretch_id, 1, 1
            )[:, 0]
            > 0
        )
        best, total, acc = state
        key_win = windows_of(
            key_block, half_high, half_wide, win_high, win_wide, heads_here, head_dim
        )
        value_win = windows_of(
            value_block, half_high, half_wide, win_high, win_wide, heads_here, head_dim
        )
        usable = allowed & visible[None, :, None, None]
        scores = (
            jnp.einsum("nqhd,nkhd->nhqk", queries, key_win, preferred_element_type=jnp.float32)
            * scale
        )
        masked = jnp.where(usable, scores, jnp.float32(-1e30))
        fresh = jnp.maximum(best, jnp.max(masked, axis=3))
        probs = jnp.where(usable, jnp.exp(scores - fresh[..., None]), jnp.float32(0.0))
        shrink = jnp.exp(best - fresh)
        total = total * shrink + jnp.sum(probs, axis=3)
        acc = acc * shrink[..., None] + jnp.einsum(
            "nhqk,nkhd->nhqd",
            probs.astype(jnp.bfloat16),
            value_win,
            preferred_element_type=jnp.float32,
        )
        return ((fresh, total, acc), None)

    final, unused = lax.scan(one_stretch, initial, (key_full, value_full, stretch_ids))
    best, total, acc = final
    attn = (acc / total[..., None]).astype(jnp.bfloat16)
    attn = attn.transpose(0, 2, 1, 3).reshape(
        2, 2, frames, half_high, half_wide, heads_here * head_dim
    )
    attn = attn.transpose(2, 0, 3, 1, 4, 5).reshape(tokens_here, heads_here * head_dim)
    mixed = lax.psum_scatter(
        jnp.dot(attn, out_weight, preferred_element_type=jnp.float32).astype(jnp.bfloat16),
        "head",
        scatter_dimension=0,
        tiled=True,
    )
    return mixed.reshape(1, 1, -1, out_weight.shape[1])


def tile_place():
    tile_at = lax.axis_index("tile")
    return tile_at // 2, tile_at % 2


def part_kernel(w_ref, part_ref, sem):
    tall, broad = part_ref.shape
    top = pl.multiple_of(lax.axis_index("tile") * tall, 16)
    left = pl.multiple_of(lax.axis_index("tm") * broad, 128)
    copy = pltpu.make_async_copy(w_ref.at[pl.ds(top, tall), pl.ds(left, broad)], part_ref, sem)
    copy.start()
    copy.wait()


def face_kernel(k_ref, v_ref, part_ref, row_ref, col_ref, corner_ref, tile_ref, *, geometry):
    high, wide, span, frames = geometry[:4]
    cells = high * wide
    row_at, col_at = tile_place()
    y0 = jnp.where(row_at == 0, high - span, 0)
    x0 = jnp.where(col_at == 0, wide - span, 0)

    def picker(count, cell_of):
        row = lax.broadcasted_iota(jnp.int32, (count, cells), 0)
        col = lax.broadcasted_iota(jnp.int32, (count, cells), 1)
        return (col == cell_of(row)).astype(jnp.bfloat16)

    beside = picker(high * span, lambda i: (i // span) * wide + x0 + i % span)
    across = picker(span * span, lambda i: (y0 + i // span) * wide + x0 + i % span)
    for which, ref in enumerate((k_ref, v_ref)):
        tile_ref[which] = ref[...]
        for f in range(frames):
            start = pl.multiple_of(f * cells + y0 * wide, 16)
            row_ref[which, f] = ref[pl.ds(start, span * wide)]
            whole = ref[f * cells : (f + 1) * cells]
            col_ref[which, f] = jnp.dot(
                beside, whole, preferred_element_type=jnp.float32
            ).astype(jnp.bfloat16)
            corner_ref[which, f] = jnp.dot(
                across, whole, preferred_element_type=jnp.float32
            ).astype(jnp.bfloat16)


def edge_kernel(row_ref, col_ref, corner_ref, out_ref):
    for which in range(2):
        at = 0
        for part in (row_ref, col_ref, corner_ref):
            for f in range(part.shape[1]):
                size = part.shape[2]
                out_ref[which, at : at + size] = part[which, f]
                at += size


def distances(high, wide, span, frames):
    row_at, col_at = tile_place()
    cells = high * wide
    count = frames * (cells + span * (wide + high + span))
    j = lax.broadcasted_iota(jnp.int32, (1, count), 1)
    y_off = jnp.where(row_at == 0, high, -span)
    x_off = jnp.where(col_at == 0, wide, -span)
    c = j % cells
    ky, kx = c // wide, c % wide
    base = frames * cells
    c = (j - base) % (span * wide)
    ky = jnp.where(j >= base, y_off + c // wide, ky)
    kx = jnp.where(j >= base, c % wide, kx)
    base += frames * span * wide
    c = (j - base) % (span * high)
    ky = jnp.where(j >= base, c // span, ky)
    kx = jnp.where(j >= base, x_off + c % span, kx)
    base += frames * span * high
    c = (j - base) % (span * span)
    ky = jnp.where(j >= base, y_off + c // span, ky)
    kx = jnp.where(j >= base, x_off + c % span, kx)
    i = lax.broadcasted_iota(jnp.int32, (cells, 1), 0)
    return jnp.maximum(jnp.abs(i // wide - ky), jnp.abs(i % wide - kx))


def attend(units, factor):
    scores = [
        [
            jnp.where(
                dist <= reach,
                lax.dot_general(
                    q, k, (((1,), (1,)), ((), ())), preferred_element_type=jnp.float32
                )
                * factor,
                FAR,
            )
            for k, v, dist, reach in pieces
        ]
        for q, pieces, before in units
    ]
    tops = []
    for parts, (q, pieces, before) in zip(scores, units):
        found = [jnp.max(s, axis=1, keepdims=True) for s in parts]
        if before is not None:
            found.append(before)
        tops.append(functools.reduce(jnp.maximum, found))
    probs = [
        [jnp.exp2(s - m).astype(jnp.bfloat16) for s in parts] for parts, m in zip(scores, tops)
    ]
    sums = []
    for parts, (q, pieces, before) in zip(probs, units):
        total = None
        for p, (k, v, dist, reach) in zip(parts, pieces):
            both = jnp.concatenate([v, jnp.ones_like(v)], axis=1)
            got = jnp.dot(p, both, preferred_element_type=jnp.float32)
            total = got if total is None else total + got
        sums.append(total)
    return tops, sums


def attend_tile(q_ref, tile_ref, dist_ref, reach_of, heads, state, geometry):
    high, wide, span, frames, head_dim, factor, step = geometry
    cells = high * wide
    acc_ref, sum_ref, max_ref = state
    for at, head in enumerate(heads):
        cols = slice(head * head_dim, (head + 1) * head_dim)
        outs = slice(at * head_dim, (at + 1) * head_dim)
        starts = range(0, q_ref.shape[0], step)
        units = []
        for start in starts:
            near = dist_ref[start % cells : start % cells + step, : tile_ref.shape[1]]
            piece = (tile_ref[0, :, cols], tile_ref[1, :, cols], near, reach_of(head))
            units.append((q_ref[start : start + step, cols], [piece], None))
        for start, m, got in zip(starts, *attend(units, factor)):
            rows = slice(start, start + step)
            acc_ref[rows, outs] = got[:, :head_dim]
            sum_ref[rows, outs] = got[:, head_dim:]
            max_ref[rows, outs] = jnp.broadcast_to(m, (step, head_dim))


def begin_kernel(radius_ref, mask_ref, q_ref, tile_ref, *outs, geometry, heads):
    *state, dist_ref, reach_ref = outs
    high, wide, span, frames = geometry[:4]
    dist_ref[...] = distances(high, wide, span, frames)
    stretch_at = lax.axis_index("tm")
    line = (1, reach_ref.shape[1])
    for head in range(heads):
        radius = radius_ref[head]
        seen = mask_ref[stretch_at, 0, head] > 0
        reach_ref[head : head + 1] = jnp.full(line, radius, jnp.int32)
        reach_ref[heads + head : heads + head + 1] = jnp.full(
            line, jnp.where(seen, radius, -1), jnp.int32
        )
    attend_tile(q_ref, tile_ref, dist_ref, lambda h: radius_ref[h], (0,), state, geometry)


def tile_kernel(q_ref, tile_ref, dist_ref, reach_ref, *state, geometry, heads):
    attend_tile(
        q_ref,
        tile_ref,
        dist_ref,
        lambda h: reach_ref[h : h + 1, :1],
        range(1, heads),
        state,
        geometry,
    )


def pick_state(head_state, state, head, rows, head_dim):
    refs = head_state if head == 0 else state
    at = max(head - 1, 0) * head_dim
    return [ref[rows, at : at + head_dim] for ref in refs]


def rest_kernel(
    q_ref,
    edge_ref,
    first_tile_ref,
    first_edge_ref,
    *rest,
    geometry,
    heads,
    flips,
):
    head_state, dist_ref, reach_ref, state, outs = rest[:3], rest[3], rest[4], rest[5:8], rest[8:]
    high, wide, span, frames, head_dim, factor, step = geometry
    cells = high * wide
    base = frames * cells
    head_at = lax.axis_index("head")
    stretch_at = lax.axis_index("tm")

    def run(with_first):
        for flip, out_ref in zip(flips, outs):
            start = pl.multiple_of(jnp.bitwise_xor(head_at, flip) * step, step)
            rows = pl.ds(start, step)
            near = dist_ref[pl.ds(pl.multiple_of(lax.rem(start, cells), step), step)]
            beyond = near[:, base:]
            units = []
            olds = []
            for head in range(heads):
                cols = slice(head * head_dim, (head + 1) * head_dim)
                sources = [(edge_ref, beyond, head)]
                if with_first:
                    sources.append((first_tile_ref, near[:, :base], heads + head))
                    sources.append((first_edge_ref, beyond, heads + head))
                pieces = [
                    (ref[0, :, cols], ref[1, :, cols], dist, reach_ref[row : row + 1, :1])
                    for ref, dist, row in sources
                ]
                olds.append(pick_state(head_state, state, head, rows, head_dim))
                units.append((q_ref[rows, cols], pieces, olds[-1][2][:, :1]))
            for head, (m, got) in enumerate(zip(*attend(units, factor))):
                old_acc, old_total, old_max = olds[head]
                shrink = jnp.exp2(old_max - m)
                acc = old_acc * shrink + got[:, :head_dim]
                total = old_total * shrink + got[:, head_dim:]
                cols = slice(head * head_dim, (head + 1) * head_dim)
                out_ref[:, cols] = (acc / total).astype(jnp.bfloat16)

    @pl.when(stretch_at > 0)
    def _():
        run(True)

    @pl.when(stretch_at == 0)
    def _():
        run(False)


def copy_kernel(in_ref, out_ref):
    out_ref[...] = in_ref[...]


def stack_kernel(*refs):
    *parts, out_ref = refs
    tile_at = lax.axis_index("tile")
    for flip, part in enumerate(parts):
        tall = part.shape[0]
        top = pl.multiple_of(jnp.bitwise_xor(tile_at, flip) * tall, 16)
        out_ref[pl.ds(top, tall)] = part[...]


def project_kernel(w_ref, part_ref, own_ref, got_ref, out_ref, *, flip):
    broad = part_ref.shape[1]
    half = jnp.bitwise_xor(lax.axis_index("tm"), flip)
    cols = pl.ds(pl.multiple_of(half * broad, 128), broad)
    total = jnp.dot(own_ref[...], w_ref[:, cols], preferred_element_type=jnp.float32)
    total += jnp.dot(got_ref[...], part_ref[...], preferred_element_type=jnp.float32)
    out_ref[...] = total.astype(out_ref.dtype)


def add_kernel(mine_ref, got_ref, *rest, flip):
    out_ref, sum_ref, sems = rest[-3:]
    pieces, tall, broad = sum_ref.shape
    half = jnp.bitwise_xor(lax.axis_index("tm"), flip)
    cols = pl.ds(pl.multiple_of(half * broad, 128), broad)
    copies = []
    for i in range(pieces):
        rows = slice(i * tall, (i + 1) * tall)
        sum_ref[i] = (mine_ref[rows] + got_ref[rows].astype(jnp.float32)).astype(jnp.bfloat16)
        copies.append(pltpu.make_async_copy(sum_ref.at[i], out_ref.at[rows, cols], sems.at[i]))
        copies[-1].start()
    for copy in copies:
        copy.wait()


def two_by_two(query, keys, values, out_weight, radius, block_mask):
    span = RMAX
    frames, high, wide, channels = query.shape[2:]
    heads = radius.shape[0]
    head_dim = channels // heads
    cells = high * wide
    tokens = frames * cells
    groups = lax.axis_size("head")
    tiles = lax.axis_size("tile")
    depth, width = out_weight.shape
    step = tokens // groups
    geometry = (high, wide, span, frames, head_dim, LOG2E / math.sqrt(head_dim), step)
    count = frames * (cells + span * (wide + high + span))
    smem = pl.BlockSpec(memory_space=pltpu.SMEM)
    vmem = pl.BlockSpec(memory_space=pltpu.VMEM)
    hbm = pl.BlockSpec(memory_space=pltpu.HBM)
    bf16, f32 = jnp.bfloat16, jnp.float32
    shape = jax.ShapeDtypeStruct

    def call(kernel, out_shape, specs, *args, name, scratch=(), flops=0, **keys_of):
        return pl.pallas_call(
            functools.partial(kernel, **keys_of) if keys_of else kernel,
            out_shape=out_shape,
            in_specs=specs,
            out_specs=jax.tree.map(lambda _: vmem, out_shape),
            scratch_shapes=scratch,
            cost_estimate=pl.CostEstimate(flops=flops, bytes_accessed=0, transcendentals=0),
            compiler_params=pltpu.CompilerParams(vmem_limit_bytes=VMEM_LIMIT),
            name=name,
        )(*args)

    def flipped(value, axis, flip):
        return lax.ppermute(value, axis, [(i, i ^ flip) for i in range(lax.axis_size(axis))])

    q = query.reshape(tokens, channels)
    k = keys.reshape(tokens, channels)
    v = values.reshape(tokens, channels)

    tall, broad = depth // tiles, width // 2
    part_shape = shape((tall, broad), bf16)
    part = call(
        part_kernel,
        part_shape,
        [hbm],
        pltpu.with_memory_space_constraint(out_weight, pltpu.HBM),
        name="part",
        scratch=[pltpu.SemaphoreType.DMA],
    )
    *faces, tile = call(
        face_kernel,
        [
            shape((2, frames, span * wide, channels), bf16),
            shape((2, frames, span * high, channels), bf16),
            shape((2, frames, span * span, channels), bf16),
            shape((2, tokens, channels), bf16),
        ],
        [vmem] * 3,
        k,
        v,
        part,
        name="faces",
        geometry=geometry,
    )
    faces = [flipped(face, "tile", flip) for face, flip in zip(faces, (2, 1, 3))]
    lone = flipped(part, "head", 2)
    begun = call(
        begin_kernel,
        [shape((tokens, head_dim), f32)] * 3
        + [shape((cells, count), jnp.int32), shape((2 * heads, head_dim), jnp.int32)],
        [smem] * 2 + [vmem] * 2,
        radius,
        block_mask.transpose(1, 2, 0),
        q,
        tile,
        name="begin",
        geometry=geometry,
        heads=heads,
    )
    begun, tile = lax.optimization_barrier((begun, tile))
    first_tile = lax.ppermute(tile, "tm", [(0, 1)])
    state = call(
        tile_kernel,
        [shape((tokens, channels - head_dim), f32)] * 3,
        [vmem] * 4,
        q,
        tile,
        *begun[3:],
        name="tile",
        geometry=geometry,
        heads=heads,
    )
    lone, state = lax.optimization_barrier((lone, state))
    lone = call(copy_kernel, part_shape, [vmem], lone, name="lone", flops=2 * 10**9)
    lone, state, faces = lax.optimization_barrier((lone, state, faces))
    edge = call(
        edge_kernel, shape((2, count - tokens, channels), bf16), [vmem] * 3, *faces, name="edges", flops=20 * 10**9
    )
    first_edge = lax.ppermute(edge, "tm", [(0, 1)])
    parts = [lone] + [flipped(lone, "tile", flip) for flip in range(1, tiles)]

    def rest(state, *flips, flops=0):
        return call(
            rest_kernel,
            [shape((step, channels), bf16)] * len(flips),
            [vmem] * 12,
            q,
            edge,
            first_tile,
            first_edge,
            *begun,
            *state,
            name="rest",
            geometry=geometry,
            heads=heads,
            flips=flips,
            flops=flops,
        )

    (for_side,) = rest(state, 3)
    got_side = flipped(for_side, "head", 2)
    state, for_side = lax.optimization_barrier((state, for_side))
    (for_far,) = rest(state, 2)
    got_far = flipped(for_far, "head", 2)
    state, for_far = lax.optimization_barrier((state, for_far))
    (own_side,) = rest(state, 1)
    parts, own_side = lax.optimization_barrier((parts, own_side))
    here = call(
        stack_kernel, shape((depth, broad), bf16), [vmem] * tiles, *parts, name="stack"
    )

    there = flipped(here, "tm", 1)

    def project(part, mine, got, kind, flip, flops=0):
        return call(
            project_kernel,
            shape((step, broad), kind),
            [vmem] * 4,
            out_weight,
            part,
            mine,
            got,
            name="project",
            flops=flops,
            flip=flip,
        )

    for_side = [project(here, own_side, got_side, bf16, 0, 20 * 10**9)]
    from_side = [flipped(for_side[0], "head", 1)]
    for_side.append(project(there, own_side, got_side, bf16, 1))
    from_side.append(flipped(for_side[1], "head", 1))
    state, for_side[1] = lax.optimization_barrier((state, for_side[1]))
    (own,) = rest(state, 0, flops=20 * 10**9)
    mine = [
        project(here, own, got_far, f32, 0),
        project(there, own, got_far, f32, 1, 20 * 10**9),
    ]
    pieces = 2
    mixed = []
    for flip in range(2):
        mixed = [
            pl.pallas_call(
                functools.partial(add_kernel, flip=flip),
                out_shape=shape((step, width), bf16),
                in_specs=[vmem] * 2 + [hbm] * flip,
                out_specs=hbm,
                input_output_aliases={2: 0} if flip else {},
                scratch_shapes=[
                    pltpu.VMEM((pieces, step // pieces, broad), bf16),
                    pltpu.SemaphoreType.DMA((pieces,)),
                ],
                compiler_params=pltpu.CompilerParams(vmem_limit_bytes=VMEM_LIMIT),
                name="add",
            )(mine[flip], from_side[flip], *mixed)
        ]
    (mixed,) = mixed
    return mixed.reshape(1, 1, step, width)


def solution(mesh):
    in_specs = (
        P("tm", "tile", None, None, None, "head"),
        P("tm", "tile", None, None, None, "head"),
        P("tm", "tile", None, None, None, "head"),
        P("head", None),
        P("head"),
        P("head", None, None),
    )
    out_specs = P("tm", "tile", "head", None)
    small = dict(mesh.shape) == {"tm": 2, "tile": 4, "head": 4}
    return jax.shard_map(
        two_by_two if small else any_grid,
        mesh=mesh,
        in_specs=in_specs,
        out_specs=out_specs,
        check_vma=False,
    )
```

```python
import functools
import math

import jax
import jax.numpy as jnp
from jax import lax
from jax.experimental import pallas as pl
from jax.experimental.pallas import tpu as pltpu
from jax.sharding import PartitionSpec as P

RMAX = 4
FAR = -1e30
LOG2E = 1.4426950408889634
VMEM_LIMIT = 24 * 1024 * 1024


def passed_along(value, axis, by):
    peers = lax.axis_size(axis)
    pairs = [(i, i + by) for i in range(peers) if 0 <= i + by < peers]
    return lax.ppermute(value, axis, pairs)


def widen(key_part, value_part, span, row_move, col_move):
    grid = math.isqrt(lax.axis_size("tile"))
    above = None
    below = None
    for offset in (grid, -grid):
        if offset > 0:
            face_key = key_part[:, :, key_part.shape[2] - span :]
            face_value = value_part[:, :, value_part.shape[2] - span :]
        else:
            face_key = key_part[:, :, :span]
            face_value = value_part[:, :, :span]
        got = row_move(face_key, face_value, offset)
        if offset > 0:
            above = got
        else:
            below = got
    key_rows = jnp.concatenate([above[0], key_part, below[0]], axis=2)
    value_rows = jnp.concatenate([above[1], value_part, below[1]], axis=2)
    left = None
    right = None
    for offset in (1, -1):
        if offset > 0:
            face_key = key_rows[:, :, :, key_rows.shape[3] - span :]
            face_value = value_rows[:, :, :, value_rows.shape[3] - span :]
        else:
            face_key = key_rows[:, :, :, :span]
            face_value = value_rows[:, :, :, :span]
        got = col_move(face_key, face_value, offset)
        if offset > 0:
            left = got
        else:
            right = got
    key_full = jnp.concatenate([left[0], key_rows, right[0]], axis=3)
    value_full = jnp.concatenate([left[1], value_rows, right[1]], axis=3)
    return (key_full, value_full)


def windows_of(block, half_high, half_wide, win_high, win_wide, heads_here, head_dim):
    parts = []
    for band in (0, 1):
        for strip in (0, 1):
            parts.append(
                block[
                    :,
                    band * half_high : band * half_high + win_high,
                    strip * half_wide : strip * half_wide + win_wide,
                ]
            )
    stacked = jnp.stack(parts)
    return stacked.reshape(4, -1, heads_here, head_dim)


def any_grid(query, keys, values, out_weight, radius, block_mask):
    span = RMAX
    grid = math.isqrt(lax.axis_size("tile"))
    tile_at = lax.axis_index("tile")
    row_at = tile_at // grid
    col_at = tile_at % grid
    stretch_at = lax.axis_index("tm")
    frames, high, wide, channels = query.shape[2:]
    heads_here = radius.shape[0]
    head_dim = channels // heads_here
    tokens_here = frames * high * wide
    half_high = high // 2
    half_wide = wide // 2
    win_high = half_high + 2 * span
    win_wide = half_wide + 2 * span
    quarter = frames * half_high * half_wide
    queries = query[0, 0].reshape(frames, 2, half_high, 2, half_wide, channels)
    queries = queries.transpose(1, 3, 0, 2, 4, 5).reshape(4, quarter, heads_here, head_dim)
    query_y = jnp.broadcast_to(
        jnp.arange(half_high, dtype=jnp.int32)[None, :, None], (frames, half_high, half_wide)
    ).reshape(-1)
    query_x = jnp.broadcast_to(
        jnp.arange(half_wide, dtype=jnp.int32)[None, None, :], (frames, half_high, half_wide)
    ).reshape(-1)
    key_y = jnp.broadcast_to(
        jnp.arange(win_high, dtype=jnp.int32)[None, :, None] - span, (frames, win_high, win_wide)
    ).reshape(-1)
    key_x = jnp.broadcast_to(
        jnp.arange(win_wide, dtype=jnp.int32)[None, None, :] - span, (frames, win_high, win_wide)
    ).reshape(-1)
    band_at = jnp.array([0, 0, 1, 1], dtype=jnp.int32)
    strip_at = jnp.array([0, 1, 0, 1], dtype=jnp.int32)
    global_y = row_at * high + band_at[:, None] * half_high + key_y[None, :]
    global_x = col_at * wide + strip_at[:, None] * half_wide + key_x[None, :]
    inside = (global_y >= 0) & (global_y < grid * high) & (global_x >= 0) & (global_x < grid * wide)
    distance = jnp.maximum(
        jnp.abs(query_y[:, None] - key_y[None, :]), jnp.abs(query_x[:, None] - key_x[None, :])
    )
    near = distance[None, :, :] <= radius[:, None, None]
    allowed = near[None, :, :, :] & inside[:, None, None, :]
    scale = 1.0 / math.sqrt(head_dim)
    initial = (
        jnp.full((4, heads_here, quarter), -1e30, jnp.float32),
        jnp.zeros((4, heads_here, quarter), jnp.float32),
        jnp.zeros((4, heads_here, quarter, head_dim), jnp.float32),
    )

    def tile_move(face_key, face_value, offset):
        return passed_along((face_key, face_value), "tile", offset)

    key_all, value_all = (
        lax.all_gather(keys[0], "tm", axis=0, tiled=True),
        lax.all_gather(values[0], "tm", axis=0, tiled=True),
    )
    key_full, value_full = widen(key_all, value_all, span, tile_move, tile_move)
    stretch_ids = jnp.arange(key_full.shape[0], dtype=jnp.int32)

    def one_stretch(state, item):
        key_block, value_block, stretch_id = item
        visible = (
            lax.dynamic_slice_in_dim(
                lax.dynamic_index_in_dim(block_mask, stretch_at, 1, False), stretch_id, 1, 1
            )[:, 0]
            > 0
        )
        best, total, acc = state
        key_win = windows_of(
            key_block, half_high, half_wide, win_high, win_wide, heads_here, head_dim
        )
        value_win = windows_of(
            value_block, half_high, half_wide, win_high, win_wide, heads_here, head_dim
        )
        usable = allowed & visible[None, :, None, None]
        scores = (
            jnp.einsum("nqhd,nkhd->nhqk", queries, key_win, preferred_element_type=jnp.float32)
            * scale
        )
        masked = jnp.where(usable, scores, jnp.float32(-1e30))
        fresh = jnp.maximum(best, jnp.max(masked, axis=3))
        probs = jnp.where(usable, jnp.exp(scores - fresh[..., None]), jnp.float32(0.0))
        shrink = jnp.exp(best - fresh)
        total = total * shrink + jnp.sum(probs, axis=3)
        acc = acc * shrink[..., None] + jnp.einsum(
            "nhqk,nkhd->nhqd",
            probs.astype(jnp.bfloat16),
            value_win,
            preferred_element_type=jnp.float32,
        )
        return ((fresh, total, acc), None)

    final, unused = lax.scan(one_stretch, initial, (key_full, value_full, stretch_ids))
    best, total, acc = final
    attn = (acc / total[..., None]).astype(jnp.bfloat16)
    attn = attn.transpose(0, 2, 1, 3).reshape(
        2, 2, frames, half_high, half_wide, heads_here * head_dim
    )
    attn = attn.transpose(2, 0, 3, 1, 4, 5).reshape(tokens_here, heads_here * head_dim)
    mixed = lax.psum_scatter(
        jnp.dot(attn, out_weight, preferred_element_type=jnp.float32).astype(jnp.bfloat16),
        "head",
        scatter_dimension=0,
        tiled=True,
    )
    return mixed.reshape(1, 1, -1, out_weight.shape[1])


def tile_place():
    tile_at = lax.axis_index("tile")
    return tile_at // 2, tile_at % 2


def part_kernel(w_ref, part_ref, sem):
    tall, broad = part_ref.shape
    top = pl.multiple_of(lax.axis_index("tile") * tall, 16)
    left = pl.multiple_of(lax.axis_index("tm") * broad, 128)
    copy = pltpu.make_async_copy(w_ref.at[pl.ds(top, tall), pl.ds(left, broad)], part_ref, sem)
    copy.start()
    copy.wait()


def face_kernel(k_ref, v_ref, part_ref, row_ref, col_ref, corner_ref, tile_ref, *, geometry):
    high, wide, span, frames = geometry[:4]
    cells = high * wide
    row_at, col_at = tile_place()
    y0 = jnp.where(row_at == 0, high - span, 0)
    x0 = jnp.where(col_at == 0, wide - span, 0)

    def picker(count, cell_of):
        row = lax.broadcasted_iota(jnp.int32, (count, cells), 0)
        col = lax.broadcasted_iota(jnp.int32, (count, cells), 1)
        return (col == cell_of(row)).astype(jnp.bfloat16)

    beside = picker(high * span, lambda i: (i // span) * wide + x0 + i % span)
    across = picker(span * span, lambda i: (y0 + i // span) * wide + x0 + i % span)
    for which, ref in enumerate((k_ref, v_ref)):
        tile_ref[which] = ref[...]
        for f in range(frames):
            start = pl.multiple_of(f * cells + y0 * wide, 16)
            row_ref[which, f] = ref[pl.ds(start, span * wide)]
            whole = ref[f * cells : (f + 1) * cells]
            col_ref[which, f] = jnp.dot(
                beside, whole, preferred_element_type=jnp.float32
            ).astype(jnp.bfloat16)
            corner_ref[which, f] = jnp.dot(
                across, whole, preferred_element_type=jnp.float32
            ).astype(jnp.bfloat16)


def edge_kernel(row_ref, col_ref, corner_ref, out_ref):
    for which in range(2):
        at = 0
        for part in (row_ref, col_ref, corner_ref):
            for f in range(part.shape[1]):
                size = part.shape[2]
                out_ref[which, at : at + size] = part[which, f]
                at += size


def distances(high, wide, span, frames):
    row_at, col_at = tile_place()
    cells = high * wide
    count = frames * (cells + span * (wide + high + span))
    j = lax.broadcasted_iota(jnp.int32, (1, count), 1)
    y_off = jnp.where(row_at == 0, high, -span)
    x_off = jnp.where(col_at == 0, wide, -span)
    c = j % cells
    ky, kx = c // wide, c % wide
    base = frames * cells
    c = (j - base) % (span * wide)
    ky = jnp.where(j >= base, y_off + c // wide, ky)
    kx = jnp.where(j >= base, c % wide, kx)
    base += frames * span * wide
    c = (j - base) % (span * high)
    ky = jnp.where(j >= base, c // span, ky)
    kx = jnp.where(j >= base, x_off + c % span, kx)
    base += frames * span * high
    c = (j - base) % (span * span)
    ky = jnp.where(j >= base, y_off + c // span, ky)
    kx = jnp.where(j >= base, x_off + c % span, kx)
    i = lax.broadcasted_iota(jnp.int32, (cells, 1), 0)
    return jnp.maximum(jnp.abs(i // wide - ky), jnp.abs(i % wide - kx))


def attend(units, factor):
    scores = [
        [
            jnp.where(
                dist <= reach,
                lax.dot_general(
                    q, k, (((1,), (1,)), ((), ())), preferred_element_type=jnp.float32
                )
                * factor,
                FAR,
            )
            for k, v, dist, reach in pieces
        ]
        for q, pieces, before in units
    ]
    tops = []
    for parts, (q, pieces, before) in zip(scores, units):
        found = [jnp.max(s, axis=1, keepdims=True) for s in parts]
        if before is not None:
            found.append(before)
        tops.append(functools.reduce(jnp.maximum, found))
    probs = [
        [jnp.exp2(s - m).astype(jnp.bfloat16) for s in parts] for parts, m in zip(scores, tops)
    ]
    sums = []
    for parts, (q, pieces, before) in zip(probs, units):
        total = None
        for p, (k, v, dist, reach) in zip(parts, pieces):
            both = jnp.concatenate([v, jnp.ones_like(v)], axis=1)
            got = jnp.dot(p, both, preferred_element_type=jnp.float32)
            total = got if total is None else total + got
        sums.append(total)
    return tops, sums


def attend_tile(q_ref, tile_ref, dist_ref, reach_of, heads, state, geometry):
    high, wide, span, frames, head_dim, factor, step = geometry
    cells = high * wide
    acc_ref, sum_ref, max_ref = state
    for at, head in enumerate(heads):
        cols = slice(head * head_dim, (head + 1) * head_dim)
        outs = slice(at * head_dim, (at + 1) * head_dim)
        starts = range(0, q_ref.shape[0], step)
        units = []
        for start in starts:
            near = dist_ref[start % cells : start % cells + step, : tile_ref.shape[1]]
            piece = (tile_ref[0, :, cols], tile_ref[1, :, cols], near, reach_of(head))
            units.append((q_ref[start : start + step, cols], [piece], None))
        for start, m, got in zip(starts, *attend(units, factor)):
            rows = slice(start, start + step)
            acc_ref[rows, outs] = got[:, :head_dim]
            sum_ref[rows, outs] = got[:, head_dim:]
            max_ref[rows, outs] = jnp.broadcast_to(m, (step, head_dim))


def begin_kernel(radius_ref, mask_ref, q_ref, tile_ref, *outs, geometry, heads):
    *state, dist_ref, reach_ref = outs
    high, wide, span, frames = geometry[:4]
    dist_ref[...] = distances(high, wide, span, frames)
    stretch_at = lax.axis_index("tm")
    line = (1, reach_ref.shape[1])
    for head in range(heads):
        radius = radius_ref[head]
        seen = mask_ref[stretch_at, 0, head] > 0
        reach_ref[head : head + 1] = jnp.full(line, radius, jnp.int32)
        reach_ref[heads + head : heads + head + 1] = jnp.full(
            line, jnp.where(seen, radius, -1), jnp.int32
        )
    attend_tile(q_ref, tile_ref, dist_ref, lambda h: radius_ref[h], (0,), state, geometry)


def tile_kernel(q_ref, tile_ref, dist_ref, reach_ref, *state, geometry, heads):
    attend_tile(
        q_ref,
        tile_ref,
        dist_ref,
        lambda h: reach_ref[h : h + 1, :1],
        range(1, heads),
        state,
        geometry,
    )


def pick_state(head_state, state, head, rows, head_dim):
    refs = head_state if head == 0 else state
    at = max(head - 1, 0) * head_dim
    return [ref[rows, at : at + head_dim] for ref in refs]


def rest_kernel(
    q_ref,
    edge_ref,
    first_tile_ref,
    first_edge_ref,
    *rest,
    geometry,
    heads,
    flips,
):
    head_state, dist_ref, reach_ref, state, outs = rest[:3], rest[3], rest[4], rest[5:8], rest[8:]
    high, wide, span, frames, head_dim, factor, step = geometry
    cells = high * wide
    base = frames * cells
    head_at = lax.axis_index("head")
    stretch_at = lax.axis_index("tm")

    def run(with_first):
        for flip, out_ref in zip(flips, outs):
            start = pl.multiple_of(jnp.bitwise_xor(head_at, flip) * step, step)
            rows = pl.ds(start, step)
            near = dist_ref[pl.ds(pl.multiple_of(lax.rem(start, cells), step), step)]
            beyond = near[:, base:]
            units = []
            olds = []
            for head in range(heads):
                cols = slice(head * head_dim, (head + 1) * head_dim)
                sources = [(edge_ref, beyond, head)]
                if with_first:
                    sources.append((first_tile_ref, near[:, :base], heads + head))
                    sources.append((first_edge_ref, beyond, heads + head))
                pieces = [
                    (ref[0, :, cols], ref[1, :, cols], dist, reach_ref[row : row + 1, :1])
                    for ref, dist, row in sources
                ]
                olds.append(pick_state(head_state, state, head, rows, head_dim))
                units.append((q_ref[rows, cols], pieces, olds[-1][2][:, :1]))
            for head, (m, got) in enumerate(zip(*attend(units, factor))):
                old_acc, old_total, old_max = olds[head]
                shrink = jnp.exp2(old_max - m)
                acc = old_acc * shrink + got[:, :head_dim]
                total = old_total * shrink + got[:, head_dim:]
                cols = slice(head * head_dim, (head + 1) * head_dim)
                out_ref[:, cols] = (acc / total).astype(jnp.bfloat16)

    @pl.when(stretch_at > 0)
    def _():
        run(True)

    @pl.when(stretch_at == 0)
    def _():
        run(False)


def copy_kernel(in_ref, out_ref):
    out_ref[...] = in_ref[...]


def stack_kernel(*refs):
    *parts, out_ref = refs
    tile_at = lax.axis_index("tile")
    for flip, part in enumerate(parts):
        tall = part.shape[0]
        top = pl.multiple_of(jnp.bitwise_xor(tile_at, flip) * tall, 16)
        out_ref[pl.ds(top, tall)] = part[...]


def project_kernel(w_ref, part_ref, own_ref, got_ref, out_ref, *, flip):
    broad = part_ref.shape[1]
    half = jnp.bitwise_xor(lax.axis_index("tm"), flip)
    cols = pl.ds(pl.multiple_of(half * broad, 128), broad)
    total = jnp.dot(own_ref[...], w_ref[:, cols], preferred_element_type=jnp.float32)
    total += jnp.dot(got_ref[...], part_ref[...], preferred_element_type=jnp.float32)
    out_ref[...] = total.astype(out_ref.dtype)


def add_kernel(mine_ref, got_ref, *rest, flip):
    out_ref, sum_ref, sems = rest[-3:]
    pieces, tall, broad = sum_ref.shape
    half = jnp.bitwise_xor(lax.axis_index("tm"), flip)
    cols = pl.ds(pl.multiple_of(half * broad, 128), broad)
    copies = []
    for i in range(pieces):
        rows = slice(i * tall, (i + 1) * tall)
        sum_ref[i] = (mine_ref[rows] + got_ref[rows].astype(jnp.float32)).astype(jnp.bfloat16)
        copies.append(pltpu.make_async_copy(sum_ref.at[i], out_ref.at[rows, cols], sems.at[i]))
        copies[-1].start()
    for copy in copies:
        copy.wait()


def two_by_two(query, keys, values, out_weight, radius, block_mask):
    span = RMAX
    frames, high, wide, channels = query.shape[2:]
    heads = radius.shape[0]
    head_dim = channels // heads
    cells = high * wide
    tokens = frames * cells
    groups = lax.axis_size("head")
    tiles = lax.axis_size("tile")
    depth, width = out_weight.shape
    step = tokens // groups
    geometry = (high, wide, span, frames, head_dim, LOG2E / math.sqrt(head_dim), step)
    count = frames * (cells + span * (wide + high + span))
    smem = pl.BlockSpec(memory_space=pltpu.SMEM)
    vmem = pl.BlockSpec(memory_space=pltpu.VMEM)
    hbm = pl.BlockSpec(memory_space=pltpu.HBM)
    bf16, f32 = jnp.bfloat16, jnp.float32
    shape = jax.ShapeDtypeStruct

    def call(kernel, out_shape, specs, *args, name, scratch=(), flops=0, **keys_of):
        return pl.pallas_call(
            functools.partial(kernel, **keys_of) if keys_of else kernel,
            out_shape=out_shape,
            in_specs=specs,
            out_specs=jax.tree.map(lambda _: vmem, out_shape),
            scratch_shapes=scratch,
            cost_estimate=pl.CostEstimate(flops=flops, bytes_accessed=0, transcendentals=0),
            compiler_params=pltpu.CompilerParams(vmem_limit_bytes=VMEM_LIMIT),
            name=name,
        )(*args)

    def flipped(value, axis, flip):
        return lax.ppermute(value, axis, [(i, i ^ flip) for i in range(lax.axis_size(axis))])

    q = query.reshape(tokens, channels)
    k = keys.reshape(tokens, channels)
    v = values.reshape(tokens, channels)

    tall, broad = depth // tiles, width // 2
    part_shape = shape((tall, broad), bf16)
    part = call(
        part_kernel,
        part_shape,
        [hbm],
        pltpu.with_memory_space_constraint(out_weight, pltpu.HBM),
        name="part",
        scratch=[pltpu.SemaphoreType.DMA],
    )
    *faces, tile = call(
        face_kernel,
        [
            shape((2, frames, span * wide, channels), bf16),
            shape((2, frames, span * high, channels), bf16),
            shape((2, frames, span * span, channels), bf16),
            shape((2, tokens, channels), bf16),
        ],
        [vmem] * 3,
        k,
        v,
        part,
        name="faces",
        geometry=geometry,
    )
    faces = [flipped(face, "tile", flip) for face, flip in zip(faces, (2, 1, 3))]
    lone = flipped(part, "head", 2)
    begun = call(
        begin_kernel,
        [shape((tokens, head_dim), f32)] * 3
        + [shape((cells, count), jnp.int32), shape((2 * heads, head_dim), jnp.int32)],
        [smem] * 2 + [vmem] * 2,
        radius,
        block_mask.transpose(1, 2, 0),
        q,
        tile,
        name="begin",
        geometry=geometry,
        heads=heads,
    )
    begun, tile = lax.optimization_barrier((begun, tile))
    first_tile = lax.ppermute(tile, "tm", [(0, 1)])
    state = call(
        tile_kernel,
        [shape((tokens, channels - head_dim), f32)] * 3,
        [vmem] * 4,
        q,
        tile,
        *begun[3:],
        name="tile",
        geometry=geometry,
        heads=heads,
    )
    lone, state = lax.optimization_barrier((lone, state))
    lone = call(copy_kernel, part_shape, [vmem], lone, name="lone", flops=2 * 10**9)
    lone, state, faces = lax.optimization_barrier((lone, state, faces))
    edge = call(
        edge_kernel, shape((2, count - tokens, channels), bf16), [vmem] * 3, *faces, name="edges", flops=20 * 10**9
    )
    first_edge = lax.ppermute(edge, "tm", [(0, 1)])
    parts = [lone] + [flipped(lone, "tile", flip) for flip in range(1, tiles)]

    def rest(state, *flips, flops=0):
        return call(
            rest_kernel,
            [shape((step, channels), bf16)] * len(flips),
            [vmem] * 12,
            q,
            edge,
            first_tile,
            first_edge,
            *begun,
            *state,
            name="rest",
            geometry=geometry,
            heads=heads,
            flips=flips,
            flops=flops,
        )

    (for_side,) = rest(state, 3)
    got_side = flipped(for_side, "head", 2)
    state, for_side = lax.optimization_barrier((state, for_side))
    (for_far,) = rest(state, 2)
    got_far = flipped(for_far, "head", 2)
    state, for_far = lax.optimization_barrier((state, for_far))
    (own_side,) = rest(state, 1)
    parts, own_side = lax.optimization_barrier((parts, own_side))
    here = call(
        stack_kernel, shape((depth, broad), bf16), [vmem] * tiles, *parts, name="stack"
    )

    def project(part, mine, got, kind, flip, flops=0):
        return call(
            project_kernel,
            shape((step, broad), kind),
            [vmem] * 4,
            out_weight,
            part,
            mine,
            got,
            name="project",
            flops=flops,
            flip=flip,
        )

    for_side = [project(here, own_side, got_side, bf16, 0, 20 * 10**9)]
    from_side = [flipped(for_side[0], "head", 1)]
    state, here, for_side[0] = lax.optimization_barrier((state, here, for_side[0]))
    there = flipped(here, "tm", 1)
    (own,) = rest(state, 0, flops=20 * 10**9)
    own_side, own = lax.optimization_barrier((own_side, own))
    for_side.append(project(there, own_side, got_side, bf16, 1))
    from_side.append(flipped(for_side[1], "head", 1))
    own, for_side[1] = lax.optimization_barrier((own, for_side[1]))
    mine = [
        project(here, own, got_far, f32, 0),
        project(there, own, got_far, f32, 1, 20 * 10**9),
    ]
    pieces = 2
    mixed = []
    for flip in range(2):
        mixed = [
            pl.pallas_call(
                functools.partial(add_kernel, flip=flip),
                out_shape=shape((step, width), bf16),
                in_specs=[vmem] * 2 + [hbm] * flip,
                out_specs=hbm,
                input_output_aliases={2: 0} if flip else {},
                scratch_shapes=[
                    pltpu.VMEM((pieces, step // pieces, broad), bf16),
                    pltpu.SemaphoreType.DMA((pieces,)),
                ],
                compiler_params=pltpu.CompilerParams(vmem_limit_bytes=VMEM_LIMIT),
                name="add",
            )(mine[flip], from_side[flip], *mixed)
        ]
    (mixed,) = mixed
    return mixed.reshape(1, 1, step, width)


def solution(mesh):
    in_specs = (
        P("tm", "tile", None, None, None, "head"),
        P("tm", "tile", None, None, None, "head"),
        P("tm", "tile", None, None, None, "head"),
        P("head", None),
        P("head"),
        P("head", None, None),
    )
    out_specs = P("tm", "tile", "head", None)
    small = dict(mesh.shape) == {"tm": 2, "tile": 4, "head": 4}
    return jax.shard_map(
        two_by_two if small else any_grid,
        mesh=mesh,
        in_specs=in_specs,
        out_specs=out_specs,
        check_vma=False,
    )
```

```python
import functools
import math

import jax
import jax.numpy as jnp
from jax import lax
from jax.experimental import pallas as pl
from jax.experimental.pallas import tpu as pltpu
from jax.sharding import PartitionSpec as P

RMAX = 4
FAR = -1e30
LOG2E = 1.4426950408889634
VMEM_LIMIT = 24 * 1024 * 1024


def passed_along(value, axis, by):
    peers = lax.axis_size(axis)
    pairs = [(i, i + by) for i in range(peers) if 0 <= i + by < peers]
    return lax.ppermute(value, axis, pairs)


def widen(key_part, value_part, span, row_move, col_move):
    grid = math.isqrt(lax.axis_size("tile"))
    above = None
    below = None
    for offset in (grid, -grid):
        if offset > 0:
            face_key = key_part[:, :, key_part.shape[2] - span :]
            face_value = value_part[:, :, value_part.shape[2] - span :]
        else:
            face_key = key_part[:, :, :span]
            face_value = value_part[:, :, :span]
        got = row_move(face_key, face_value, offset)
        if offset > 0:
            above = got
        else:
            below = got
    key_rows = jnp.concatenate([above[0], key_part, below[0]], axis=2)
    value_rows = jnp.concatenate([above[1], value_part, below[1]], axis=2)
    left = None
    right = None
    for offset in (1, -1):
        if offset > 0:
            face_key = key_rows[:, :, :, key_rows.shape[3] - span :]
            face_value = value_rows[:, :, :, value_rows.shape[3] - span :]
        else:
            face_key = key_rows[:, :, :, :span]
            face_value = value_rows[:, :, :, :span]
        got = col_move(face_key, face_value, offset)
        if offset > 0:
            left = got
        else:
            right = got
    key_full = jnp.concatenate([left[0], key_rows, right[0]], axis=3)
    value_full = jnp.concatenate([left[1], value_rows, right[1]], axis=3)
    return (key_full, value_full)


def windows_of(block, half_high, half_wide, win_high, win_wide, heads_here, head_dim):
    parts = []
    for band in (0, 1):
        for strip in (0, 1):
            parts.append(
                block[
                    :,
                    band * half_high : band * half_high + win_high,
                    strip * half_wide : strip * half_wide + win_wide,
                ]
            )
    stacked = jnp.stack(parts)
    return stacked.reshape(4, -1, heads_here, head_dim)


def any_grid(query, keys, values, out_weight, radius, block_mask):
    span = RMAX
    grid = math.isqrt(lax.axis_size("tile"))
    tile_at = lax.axis_index("tile")
    row_at = tile_at // grid
    col_at = tile_at % grid
    stretch_at = lax.axis_index("tm")
    frames, high, wide, channels = query.shape[2:]
    heads_here = radius.shape[0]
    head_dim = channels // heads_here
    tokens_here = frames * high * wide
    half_high = high // 2
    half_wide = wide // 2
    win_high = half_high + 2 * span
    win_wide = half_wide + 2 * span
    quarter = frames * half_high * half_wide
    queries = query[0, 0].reshape(frames, 2, half_high, 2, half_wide, channels)
    queries = queries.transpose(1, 3, 0, 2, 4, 5).reshape(4, quarter, heads_here, head_dim)
    query_y = jnp.broadcast_to(
        jnp.arange(half_high, dtype=jnp.int32)[None, :, None], (frames, half_high, half_wide)
    ).reshape(-1)
    query_x = jnp.broadcast_to(
        jnp.arange(half_wide, dtype=jnp.int32)[None, None, :], (frames, half_high, half_wide)
    ).reshape(-1)
    key_y = jnp.broadcast_to(
        jnp.arange(win_high, dtype=jnp.int32)[None, :, None] - span, (frames, win_high, win_wide)
    ).reshape(-1)
    key_x = jnp.broadcast_to(
        jnp.arange(win_wide, dtype=jnp.int32)[None, None, :] - span, (frames, win_high, win_wide)
    ).reshape(-1)
    band_at = jnp.array([0, 0, 1, 1], dtype=jnp.int32)
    strip_at = jnp.array([0, 1, 0, 1], dtype=jnp.int32)
    global_y = row_at * high + band_at[:, None] * half_high + key_y[None, :]
    global_x = col_at * wide + strip_at[:, None] * half_wide + key_x[None, :]
    inside = (global_y >= 0) & (global_y < grid * high) & (global_x >= 0) & (global_x < grid * wide)
    distance = jnp.maximum(
        jnp.abs(query_y[:, None] - key_y[None, :]), jnp.abs(query_x[:, None] - key_x[None, :])
    )
    near = distance[None, :, :] <= radius[:, None, None]
    allowed = near[None, :, :, :] & inside[:, None, None, :]
    scale = 1.0 / math.sqrt(head_dim)
    initial = (
        jnp.full((4, heads_here, quarter), -1e30, jnp.float32),
        jnp.zeros((4, heads_here, quarter), jnp.float32),
        jnp.zeros((4, heads_here, quarter, head_dim), jnp.float32),
    )

    def tile_move(face_key, face_value, offset):
        return passed_along((face_key, face_value), "tile", offset)

    key_all, value_all = (
        lax.all_gather(keys[0], "tm", axis=0, tiled=True),
        lax.all_gather(values[0], "tm", axis=0, tiled=True),
    )
    key_full, value_full = widen(key_all, value_all, span, tile_move, tile_move)
    stretch_ids = jnp.arange(key_full.shape[0], dtype=jnp.int32)

    def one_stretch(state, item):
        key_block, value_block, stretch_id = item
        visible = (
            lax.dynamic_slice_in_dim(
                lax.dynamic_index_in_dim(block_mask, stretch_at, 1, False), stretch_id, 1, 1
            )[:, 0]
            > 0
        )
        best, total, acc = state
        key_win = windows_of(
            key_block, half_high, half_wide, win_high, win_wide, heads_here, head_dim
        )
        value_win = windows_of(
            value_block, half_high, half_wide, win_high, win_wide, heads_here, head_dim
        )
        usable = allowed & visible[None, :, None, None]
        scores = (
            jnp.einsum("nqhd,nkhd->nhqk", queries, key_win, preferred_element_type=jnp.float32)
            * scale
        )
        masked = jnp.where(usable, scores, jnp.float32(-1e30))
        fresh = jnp.maximum(best, jnp.max(masked, axis=3))
        probs = jnp.where(usable, jnp.exp(scores - fresh[..., None]), jnp.float32(0.0))
        shrink = jnp.exp(best - fresh)
        total = total * shrink + jnp.sum(probs, axis=3)
        acc = acc * shrink[..., None] + jnp.einsum(
            "nhqk,nkhd->nhqd",
            probs.astype(jnp.bfloat16),
            value_win,
            preferred_element_type=jnp.float32,
        )
        return ((fresh, total, acc), None)

    final, unused = lax.scan(one_stretch, initial, (key_full, value_full, stretch_ids))
    best, total, acc = final
    attn = (acc / total[..., None]).astype(jnp.bfloat16)
    attn = attn.transpose(0, 2, 1, 3).reshape(
        2, 2, frames, half_high, half_wide, heads_here * head_dim
    )
    attn = attn.transpose(2, 0, 3, 1, 4, 5).reshape(tokens_here, heads_here * head_dim)
    mixed = lax.psum_scatter(
        jnp.dot(attn, out_weight, preferred_element_type=jnp.float32).astype(jnp.bfloat16),
        "head",
        scatter_dimension=0,
        tiled=True,
    )
    return mixed.reshape(1, 1, -1, out_weight.shape[1])


def tile_place():
    tile_at = lax.axis_index("tile")
    return tile_at // 2, tile_at % 2


def part_kernel(w_ref, part_ref, sem):
    tall, broad = part_ref.shape
    top = pl.multiple_of(lax.axis_index("tile") * tall, 16)
    left = pl.multiple_of(lax.axis_index("tm") * broad, 128)
    copy = pltpu.make_async_copy(w_ref.at[pl.ds(top, tall), pl.ds(left, broad)], part_ref, sem)
    copy.start()
    copy.wait()


def face_kernel(k_ref, v_ref, part_ref, row_ref, col_ref, corner_ref, tile_ref, *, geometry):
    high, wide, span, frames = geometry[:4]
    cells = high * wide
    row_at, col_at = tile_place()
    y0 = jnp.where(row_at == 0, high - span, 0)
    x0 = jnp.where(col_at == 0, wide - span, 0)

    def picker(count, cell_of):
        row = lax.broadcasted_iota(jnp.int32, (count, cells), 0)
        col = lax.broadcasted_iota(jnp.int32, (count, cells), 1)
        return (col == cell_of(row)).astype(jnp.bfloat16)

    beside = picker(high * span, lambda i: (i // span) * wide + x0 + i % span)
    across = picker(span * span, lambda i: (y0 + i // span) * wide + x0 + i % span)
    for which, ref in enumerate((k_ref, v_ref)):
        tile_ref[which] = ref[...]
        for f in range(frames):
            start = pl.multiple_of(f * cells + y0 * wide, 16)
            row_ref[which, f] = ref[pl.ds(start, span * wide)]
            whole = ref[f * cells : (f + 1) * cells]
            col_ref[which, f] = jnp.dot(
                beside, whole, preferred_element_type=jnp.float32
            ).astype(jnp.bfloat16)
            corner_ref[which, f] = jnp.dot(
                across, whole, preferred_element_type=jnp.float32
            ).astype(jnp.bfloat16)


def edge_kernel(row_ref, col_ref, corner_ref, out_ref):
    for which in range(2):
        at = 0
        for part in (row_ref, col_ref, corner_ref):
            for f in range(part.shape[1]):
                size = part.shape[2]
                out_ref[which, at : at + size] = part[which, f]
                at += size


def distances(high, wide, span, frames):
    row_at, col_at = tile_place()
    cells = high * wide
    count = frames * (cells + span * (wide + high + span))
    j = lax.broadcasted_iota(jnp.int32, (1, count), 1)
    y_off = jnp.where(row_at == 0, high, -span)
    x_off = jnp.where(col_at == 0, wide, -span)
    c = j % cells
    ky, kx = c // wide, c % wide
    base = frames * cells
    c = (j - base) % (span * wide)
    ky = jnp.where(j >= base, y_off + c // wide, ky)
    kx = jnp.where(j >= base, c % wide, kx)
    base += frames * span * wide
    c = (j - base) % (span * high)
    ky = jnp.where(j >= base, c // span, ky)
    kx = jnp.where(j >= base, x_off + c % span, kx)
    base += frames * span * high
    c = (j - base) % (span * span)
    ky = jnp.where(j >= base, y_off + c // span, ky)
    kx = jnp.where(j >= base, x_off + c % span, kx)
    i = lax.broadcasted_iota(jnp.int32, (cells, 1), 0)
    return jnp.maximum(jnp.abs(i // wide - ky), jnp.abs(i % wide - kx))


def attend(units, factor):
    scores = [
        [
            jnp.where(
                dist <= reach,
                lax.dot_general(
                    q, k, (((1,), (1,)), ((), ())), preferred_element_type=jnp.float32
                )
                * factor,
                FAR,
            )
            for k, v, dist, reach in pieces
        ]
        for q, pieces, before in units
    ]
    tops = []
    for parts, (q, pieces, before) in zip(scores, units):
        found = [jnp.max(s, axis=1, keepdims=True) for s in parts]
        if before is not None:
            found.append(before)
        tops.append(functools.reduce(jnp.maximum, found))
    probs = [
        [jnp.exp2(s - m).astype(jnp.bfloat16) for s in parts] for parts, m in zip(scores, tops)
    ]
    sums = []
    for parts, (q, pieces, before) in zip(probs, units):
        total = None
        for p, (k, v, dist, reach) in zip(parts, pieces):
            both = jnp.concatenate([v, jnp.ones_like(v)], axis=1)
            got = jnp.dot(p, both, preferred_element_type=jnp.float32)
            total = got if total is None else total + got
        sums.append(total)
    return tops, sums


def attend_tile(q_ref, tile_ref, dist_ref, reach_of, heads, state, geometry):
    high, wide, span, frames, head_dim, factor, step = geometry
    cells = high * wide
    acc_ref, sum_ref, max_ref = state
    for at, head in enumerate(heads):
        cols = slice(head * head_dim, (head + 1) * head_dim)
        outs = slice(at * head_dim, (at + 1) * head_dim)
        starts = range(0, q_ref.shape[0], step)
        units = []
        for start in starts:
            near = dist_ref[start % cells : start % cells + step, : tile_ref.shape[1]]
            piece = (tile_ref[0, :, cols], tile_ref[1, :, cols], near, reach_of(head))
            units.append((q_ref[start : start + step, cols], [piece], None))
        for start, m, got in zip(starts, *attend(units, factor)):
            rows = slice(start, start + step)
            acc_ref[rows, outs] = got[:, :head_dim]
            sum_ref[rows, outs] = got[:, head_dim:]
            max_ref[rows, outs] = jnp.broadcast_to(m, (step, head_dim))


def begin_kernel(radius_ref, mask_ref, q_ref, tile_ref, *outs, geometry, heads):
    *state, dist_ref, reach_ref = outs
    high, wide, span, frames = geometry[:4]
    dist_ref[...] = distances(high, wide, span, frames)
    stretch_at = lax.axis_index("tm")
    line = (1, reach_ref.shape[1])
    for head in range(heads):
        radius = radius_ref[head]
        seen = mask_ref[stretch_at, 0, head] > 0
        reach_ref[head : head + 1] = jnp.full(line, radius, jnp.int32)
        reach_ref[heads + head : heads + head + 1] = jnp.full(
            line, jnp.where(seen, radius, -1), jnp.int32
        )
    attend_tile(q_ref, tile_ref, dist_ref, lambda h: radius_ref[h], (0,), state, geometry)


def tile_kernel(q_ref, tile_ref, dist_ref, reach_ref, *state, geometry, heads):
    attend_tile(
        q_ref,
        tile_ref,
        dist_ref,
        lambda h: reach_ref[h : h + 1, :1],
        range(1, heads),
        state,
        geometry,
    )


def pick_state(head_state, state, head, rows, head_dim):
    refs = head_state if head == 0 else state
    at = max(head - 1, 0) * head_dim
    return [ref[rows, at : at + head_dim] for ref in refs]


def rest_kernel(
    q_ref,
    edge_ref,
    first_tile_ref,
    first_edge_ref,
    *rest,
    geometry,
    heads,
    flips,
):
    head_state, dist_ref, reach_ref, state, outs = rest[:3], rest[3], rest[4], rest[5:8], rest[8:]
    high, wide, span, frames, head_dim, factor, step = geometry
    cells = high * wide
    base = frames * cells
    head_at = lax.axis_index("head")
    stretch_at = lax.axis_index("tm")

    def run(with_first):
        for flip, out_ref in zip(flips, outs):
            start = pl.multiple_of(jnp.bitwise_xor(head_at, flip) * step, step)
            rows = pl.ds(start, step)
            near = dist_ref[pl.ds(pl.multiple_of(lax.rem(start, cells), step), step)]
            beyond = near[:, base:]
            units = []
            olds = []
            for head in range(heads):
                cols = slice(head * head_dim, (head + 1) * head_dim)
                sources = [(edge_ref, beyond, head)]
                if with_first:
                    sources.append((first_tile_ref, near[:, :base], heads + head))
                    sources.append((first_edge_ref, beyond, heads + head))
                pieces = [
                    (ref[0, :, cols], ref[1, :, cols], dist, reach_ref[row : row + 1, :1])
                    for ref, dist, row in sources
                ]
                olds.append(pick_state(head_state, state, head, rows, head_dim))
                units.append((q_ref[rows, cols], pieces, olds[-1][2][:, :1]))
            for head, (m, got) in enumerate(zip(*attend(units, factor))):
                old_acc, old_total, old_max = olds[head]
                shrink = jnp.exp2(old_max - m)
                acc = old_acc * shrink + got[:, :head_dim]
                total = old_total * shrink + got[:, head_dim:]
                cols = slice(head * head_dim, (head + 1) * head_dim)
                out_ref[:, cols] = (acc / total).astype(jnp.bfloat16)

    @pl.when(stretch_at > 0)
    def _():
        run(True)

    @pl.when(stretch_at == 0)
    def _():
        run(False)


def copy_kernel(in_ref, out_ref):
    out_ref[...] = in_ref[...]


def stack_kernel(*refs):
    *parts, out_ref = refs
    tile_at = lax.axis_index("tile")
    for flip, part in enumerate(parts):
        tall = part.shape[0]
        top = pl.multiple_of(jnp.bitwise_xor(tile_at, flip) * tall, 16)
        out_ref[pl.ds(top, tall)] = part[...]


def project_kernel(w_ref, here_ref, there_ref, own_ref, got_ref, out_ref):
    broad = here_ref.shape[1]
    core = lax.axis_index("tm")
    for half, ref in ((core, here_ref), (1 - core, there_ref)):
        cols = pl.ds(pl.multiple_of(half * broad, 128), broad)
        total = jnp.dot(own_ref[...], w_ref[:, cols], preferred_element_type=jnp.float32)
        total += jnp.dot(got_ref[...], ref[...], preferred_element_type=jnp.float32)
        out_ref[:, cols] = total.astype(out_ref.dtype)


def add_kernel(mine_ref, got_ref, out_ref, sum_ref, sems):
    pieces, tall, width = sum_ref.shape
    copies = []
    for i in range(pieces):
        rows = slice(i * tall, (i + 1) * tall)
        sum_ref[i] = (mine_ref[rows] + got_ref[rows].astype(jnp.float32)).astype(jnp.bfloat16)
        copies.append(pltpu.make_async_copy(sum_ref.at[i], out_ref.at[rows], sems.at[i]))
        copies[-1].start()
    for copy in copies:
        copy.wait()


def two_by_two(query, keys, values, out_weight, radius, block_mask):
    span = RMAX
    frames, high, wide, channels = query.shape[2:]
    heads = radius.shape[0]
    head_dim = channels // heads
    cells = high * wide
    tokens = frames * cells
    groups = lax.axis_size("head")
    tiles = lax.axis_size("tile")
    depth, width = out_weight.shape
    step = tokens // groups
    geometry = (high, wide, span, frames, head_dim, LOG2E / math.sqrt(head_dim), step)
    count = frames * (cells + span * (wide + high + span))
    smem = pl.BlockSpec(memory_space=pltpu.SMEM)
    vmem = pl.BlockSpec(memory_space=pltpu.VMEM)
    hbm = pl.BlockSpec(memory_space=pltpu.HBM)
    bf16, f32 = jnp.bfloat16, jnp.float32
    shape = jax.ShapeDtypeStruct

    def call(kernel, out_shape, specs, *args, name, scratch=(), flops=0, **keys_of):
        return pl.pallas_call(
            functools.partial(kernel, **keys_of) if keys_of else kernel,
            out_shape=out_shape,
            in_specs=specs,
            out_specs=jax.tree.map(lambda _: vmem, out_shape),
            scratch_shapes=scratch,
            cost_estimate=pl.CostEstimate(flops=flops, bytes_accessed=0, transcendentals=0),
            compiler_params=pltpu.CompilerParams(vmem_limit_bytes=VMEM_LIMIT),
            name=name,
        )(*args)

    def flipped(value, axis, flip):
        return lax.ppermute(value, axis, [(i, i ^ flip) for i in range(lax.axis_size(axis))])

    q = query.reshape(tokens, channels)
    k = keys.reshape(tokens, channels)
    v = values.reshape(tokens, channels)

    tall, broad = depth // tiles, width // 2
    part_shape = shape((tall, broad), bf16)
    part = call(
        part_kernel,
        part_shape,
        [hbm],
        pltpu.with_memory_space_constraint(out_weight, pltpu.HBM),
        name="part",
        scratch=[pltpu.SemaphoreType.DMA],
    )
    *faces, tile = call(
        face_kernel,
        [
            shape((2, frames, span * wide, channels), bf16),
            shape((2, frames, span * high, channels), bf16),
            shape((2, frames, span * span, channels), bf16),
            shape((2, tokens, channels), bf16),
        ],
        [vmem] * 3,
        k,
        v,
        part,
        name="faces",
        geometry=geometry,
    )
    faces = [flipped(face, "tile", flip) for face, flip in zip(faces, (2, 1, 3))]
    lone = flipped(part, "head", 2)
    begun = call(
        begin_kernel,
        [shape((tokens, head_dim), f32)] * 3
        + [shape((cells, count), jnp.int32), shape((2 * heads, head_dim), jnp.int32)],
        [smem] * 2 + [vmem] * 2,
        radius,
        block_mask.transpose(1, 2, 0),
        q,
        tile,
        name="begin",
        geometry=geometry,
        heads=heads,
    )
    begun, tile = lax.optimization_barrier((begun, tile))
    first_tile = lax.ppermute(tile, "tm", [(0, 1)])
    state = call(
        tile_kernel,
        [shape((tokens, channels - head_dim), f32)] * 3,
        [vmem] * 4,
        q,
        tile,
        *begun[3:],
        name="tile",
        geometry=geometry,
        heads=heads,
    )
    lone, state = lax.optimization_barrier((lone, state))
    lone = call(copy_kernel, part_shape, [vmem], lone, name="lone", flops=2 * 10**9)
    lone, state, faces = lax.optimization_barrier((lone, state, faces))
    edge = call(
        edge_kernel, shape((2, count - tokens, channels), bf16), [vmem] * 3, *faces, name="edges", flops=20 * 10**9
    )
    first_edge = lax.ppermute(edge, "tm", [(0, 1)])
    parts = [lone] + [flipped(lone, "tile", flip) for flip in range(1, tiles)]

    def rest(state, *flips, flops=0):
        return call(
            rest_kernel,
            [shape((step, channels), bf16)] * len(flips),
            [vmem] * 12,
            q,
            edge,
            first_tile,
            first_edge,
            *begun,
            *state,
            name="rest",
            geometry=geometry,
            heads=heads,
            flips=flips,
            flops=flops,
        )

    (for_side,) = rest(state, 3)
    got_side = flipped(for_side, "head", 2)
    state, for_side = lax.optimization_barrier((state, for_side))
    for_far, own_side = rest(state, 2, 1)
    got_far = flipped(for_far, "head", 2)
    parts, own_side = lax.optimization_barrier((parts, own_side))
    here = call(
        stack_kernel, shape((depth, broad), bf16), [vmem] * tiles, *parts, name="stack"
    )

    there = flipped(here, "tm", 1)

    def project(mine, got, kind, flops=0):
        return call(
            project_kernel,
            shape((step, width), kind),
            [vmem] * 5,
            out_weight,
            here,
            there,
            mine,
            got,
            name="project",
            flops=flops,
        )

    got_side = call(
        copy_kernel, shape((step, channels), bf16), [vmem], got_side, name="got", flops=20 * 10**9
    )
    for_side = project(own_side, got_side, bf16)
    from_side = flipped(for_side, "head", 1)
    state, for_side = lax.optimization_barrier((state, for_side))
    (own,) = rest(state, 0, flops=20 * 10**9)
    mine = project(own, got_far, f32, flops=20 * 10**9)
    pieces = 4
    mixed = pl.pallas_call(
        add_kernel,
        out_shape=shape((step, width), bf16),
        in_specs=[vmem] * 2,
        out_specs=hbm,
        scratch_shapes=[
            pltpu.VMEM((pieces, step // pieces, width), bf16),
            pltpu.SemaphoreType.DMA((pieces,)),
        ],
        compiler_params=pltpu.CompilerParams(vmem_limit_bytes=VMEM_LIMIT),
        name="add",
    )(mine, from_side)
    return mixed.reshape(1, 1, step, width)


def solution(mesh):
    in_specs = (
        P("tm", "tile", None, None, None, "head"),
        P("tm", "tile", None, None, None, "head"),
        P("tm", "tile", None, None, None, "head"),
        P("head", None),
        P("head"),
        P("head", None, None),
    )
    out_specs = P("tm", "tile", "head", None)
    small = dict(mesh.shape) == {"tm": 2, "tile": 4, "head": 4}
    return jax.shard_map(
        two_by_two if small else any_grid,
        mesh=mesh,
        in_specs=in_specs,
        out_specs=out_specs,
        check_vma=False,
    )
```

```python
import functools
import math

import jax
import jax.numpy as jnp
from jax import lax
from jax.experimental import pallas as pl
from jax.experimental.pallas import tpu as pltpu
from jax.sharding import PartitionSpec as P

RMAX = 4
FAR = -1e30
LOG2E = 1.4426950408889634
VMEM_LIMIT = 24 * 1024 * 1024


def passed_along(value, axis, by):
    peers = lax.axis_size(axis)
    pairs = [(i, i + by) for i in range(peers) if 0 <= i + by < peers]
    return lax.ppermute(value, axis, pairs)


def widen(key_part, value_part, span, row_move, col_move):
    grid = math.isqrt(lax.axis_size("tile"))
    above = None
    below = None
    for offset in (grid, -grid):
        if offset > 0:
            face_key = key_part[:, :, key_part.shape[2] - span :]
            face_value = value_part[:, :, value_part.shape[2] - span :]
        else:
            face_key = key_part[:, :, :span]
            face_value = value_part[:, :, :span]
        got = row_move(face_key, face_value, offset)
        if offset > 0:
            above = got
        else:
            below = got
    key_rows = jnp.concatenate([above[0], key_part, below[0]], axis=2)
    value_rows = jnp.concatenate([above[1], value_part, below[1]], axis=2)
    left = None
    right = None
    for offset in (1, -1):
        if offset > 0:
            face_key = key_rows[:, :, :, key_rows.shape[3] - span :]
            face_value = value_rows[:, :, :, value_rows.shape[3] - span :]
        else:
            face_key = key_rows[:, :, :, :span]
            face_value = value_rows[:, :, :, :span]
        got = col_move(face_key, face_value, offset)
        if offset > 0:
            left = got
        else:
            right = got
    key_full = jnp.concatenate([left[0], key_rows, right[0]], axis=3)
    value_full = jnp.concatenate([left[1], value_rows, right[1]], axis=3)
    return (key_full, value_full)


def windows_of(block, half_high, half_wide, win_high, win_wide, heads_here, head_dim):
    parts = []
    for band in (0, 1):
        for strip in (0, 1):
            parts.append(
                block[
                    :,
                    band * half_high : band * half_high + win_high,
                    strip * half_wide : strip * half_wide + win_wide,
                ]
            )
    stacked = jnp.stack(parts)
    return stacked.reshape(4, -1, heads_here, head_dim)


def any_grid(query, keys, values, out_weight, radius, block_mask):
    span = RMAX
    grid = math.isqrt(lax.axis_size("tile"))
    tile_at = lax.axis_index("tile")
    row_at = tile_at // grid
    col_at = tile_at % grid
    stretch_at = lax.axis_index("tm")
    frames, high, wide, channels = query.shape[2:]
    heads_here = radius.shape[0]
    head_dim = channels // heads_here
    tokens_here = frames * high * wide
    half_high = high // 2
    half_wide = wide // 2
    win_high = half_high + 2 * span
    win_wide = half_wide + 2 * span
    quarter = frames * half_high * half_wide
    queries = query[0, 0].reshape(frames, 2, half_high, 2, half_wide, channels)
    queries = queries.transpose(1, 3, 0, 2, 4, 5).reshape(4, quarter, heads_here, head_dim)
    query_y = jnp.broadcast_to(
        jnp.arange(half_high, dtype=jnp.int32)[None, :, None], (frames, half_high, half_wide)
    ).reshape(-1)
    query_x = jnp.broadcast_to(
        jnp.arange(half_wide, dtype=jnp.int32)[None, None, :], (frames, half_high, half_wide)
    ).reshape(-1)
    key_y = jnp.broadcast_to(
        jnp.arange(win_high, dtype=jnp.int32)[None, :, None] - span, (frames, win_high, win_wide)
    ).reshape(-1)
    key_x = jnp.broadcast_to(
        jnp.arange(win_wide, dtype=jnp.int32)[None, None, :] - span, (frames, win_high, win_wide)
    ).reshape(-1)
    band_at = jnp.array([0, 0, 1, 1], dtype=jnp.int32)
    strip_at = jnp.array([0, 1, 0, 1], dtype=jnp.int32)
    global_y = row_at * high + band_at[:, None] * half_high + key_y[None, :]
    global_x = col_at * wide + strip_at[:, None] * half_wide + key_x[None, :]
    inside = (global_y >= 0) & (global_y < grid * high) & (global_x >= 0) & (global_x < grid * wide)
    distance = jnp.maximum(
        jnp.abs(query_y[:, None] - key_y[None, :]), jnp.abs(query_x[:, None] - key_x[None, :])
    )
    near = distance[None, :, :] <= radius[:, None, None]
    allowed = near[None, :, :, :] & inside[:, None, None, :]
    scale = 1.0 / math.sqrt(head_dim)
    initial = (
        jnp.full((4, heads_here, quarter), -1e30, jnp.float32),
        jnp.zeros((4, heads_here, quarter), jnp.float32),
        jnp.zeros((4, heads_here, quarter, head_dim), jnp.float32),
    )

    def tile_move(face_key, face_value, offset):
        return passed_along((face_key, face_value), "tile", offset)

    key_all, value_all = (
        lax.all_gather(keys[0], "tm", axis=0, tiled=True),
        lax.all_gather(values[0], "tm", axis=0, tiled=True),
    )
    key_full, value_full = widen(key_all, value_all, span, tile_move, tile_move)
    stretch_ids = jnp.arange(key_full.shape[0], dtype=jnp.int32)

    def one_stretch(state, item):
        key_block, value_block, stretch_id = item
        visible = (
            lax.dynamic_slice_in_dim(
                lax.dynamic_index_in_dim(block_mask, stretch_at, 1, False), stretch_id, 1, 1
            )[:, 0]
            > 0
        )
        best, total, acc = state
        key_win = windows_of(
            key_block, half_high, half_wide, win_high, win_wide, heads_here, head_dim
        )
        value_win = windows_of(
            value_block, half_high, half_wide, win_high, win_wide, heads_here, head_dim
        )
        usable = allowed & visible[None, :, None, None]
        scores = (
            jnp.einsum("nqhd,nkhd->nhqk", queries, key_win, preferred_element_type=jnp.float32)
            * scale
        )
        masked = jnp.where(usable, scores, jnp.float32(-1e30))
        fresh = jnp.maximum(best, jnp.max(masked, axis=3))
        probs = jnp.where(usable, jnp.exp(scores - fresh[..., None]), jnp.float32(0.0))
        shrink = jnp.exp(best - fresh)
        total = total * shrink + jnp.sum(probs, axis=3)
        acc = acc * shrink[..., None] + jnp.einsum(
            "nhqk,nkhd->nhqd",
            probs.astype(jnp.bfloat16),
            value_win,
            preferred_element_type=jnp.float32,
        )
        return ((fresh, total, acc), None)

    final, unused = lax.scan(one_stretch, initial, (key_full, value_full, stretch_ids))
    best, total, acc = final
    attn = (acc / total[..., None]).astype(jnp.bfloat16)
    attn = attn.transpose(0, 2, 1, 3).reshape(
        2, 2, frames, half_high, half_wide, heads_here * head_dim
    )
    attn = attn.transpose(2, 0, 3, 1, 4, 5).reshape(tokens_here, heads_here * head_dim)
    mixed = lax.psum_scatter(
        jnp.dot(attn, out_weight, preferred_element_type=jnp.float32).astype(jnp.bfloat16),
        "head",
        scatter_dimension=0,
        tiled=True,
    )
    return mixed.reshape(1, 1, -1, out_weight.shape[1])


def tile_place():
    tile_at = lax.axis_index("tile")
    return tile_at // 2, tile_at % 2


def part_kernel(w_ref, part_ref, sem):
    tall, broad = part_ref.shape
    top = pl.multiple_of(lax.axis_index("tile") * tall, 16)
    left = pl.multiple_of(lax.axis_index("tm") * broad, 128)
    copy = pltpu.make_async_copy(w_ref.at[pl.ds(top, tall), pl.ds(left, broad)], part_ref, sem)
    copy.start()
    copy.wait()


def face_kernel(k_ref, v_ref, part_ref, row_ref, col_ref, corner_ref, tile_ref, *, geometry):
    high, wide, span, frames = geometry[:4]
    cells = high * wide
    row_at, col_at = tile_place()
    y0 = jnp.where(row_at == 0, high - span, 0)
    x0 = jnp.where(col_at == 0, wide - span, 0)

    def picker(count, cell_of):
        row = lax.broadcasted_iota(jnp.int32, (count, cells), 0)
        col = lax.broadcasted_iota(jnp.int32, (count, cells), 1)
        return (col == cell_of(row)).astype(jnp.bfloat16)

    beside = picker(high * span, lambda i: (i // span) * wide + x0 + i % span)
    across = picker(span * span, lambda i: (y0 + i // span) * wide + x0 + i % span)
    for which, ref in enumerate((k_ref, v_ref)):
        tile_ref[which] = ref[...]
        for f in range(frames):
            start = pl.multiple_of(f * cells + y0 * wide, 16)
            row_ref[which, f] = ref[pl.ds(start, span * wide)]
            whole = ref[f * cells : (f + 1) * cells]
            col_ref[which, f] = jnp.dot(
                beside, whole, preferred_element_type=jnp.float32
            ).astype(jnp.bfloat16)
            corner_ref[which, f] = jnp.dot(
                across, whole, preferred_element_type=jnp.float32
            ).astype(jnp.bfloat16)


def edge_kernel(row_ref, col_ref, corner_ref, out_ref):
    for which in range(2):
        at = 0
        for part in (row_ref, col_ref, corner_ref):
            for f in range(part.shape[1]):
                size = part.shape[2]
                out_ref[which, at : at + size] = part[which, f]
                at += size


def distances(high, wide, span, frames):
    row_at, col_at = tile_place()
    cells = high * wide
    count = frames * (cells + span * (wide + high + span))
    j = lax.broadcasted_iota(jnp.int32, (1, count), 1)
    y_off = jnp.where(row_at == 0, high, -span)
    x_off = jnp.where(col_at == 0, wide, -span)
    c = j % cells
    ky, kx = c // wide, c % wide
    base = frames * cells
    c = (j - base) % (span * wide)
    ky = jnp.where(j >= base, y_off + c // wide, ky)
    kx = jnp.where(j >= base, c % wide, kx)
    base += frames * span * wide
    c = (j - base) % (span * high)
    ky = jnp.where(j >= base, c // span, ky)
    kx = jnp.where(j >= base, x_off + c % span, kx)
    base += frames * span * high
    c = (j - base) % (span * span)
    ky = jnp.where(j >= base, y_off + c // span, ky)
    kx = jnp.where(j >= base, x_off + c % span, kx)
    i = lax.broadcasted_iota(jnp.int32, (cells, 1), 0)
    return jnp.maximum(jnp.abs(i // wide - ky), jnp.abs(i % wide - kx))


def attend(units, factor):
    scores = [
        [
            jnp.where(
                dist <= reach,
                lax.dot_general(
                    q, k, (((1,), (1,)), ((), ())), preferred_element_type=jnp.float32
                )
                * factor,
                FAR,
            )
            for k, v, dist, reach in pieces
        ]
        for q, pieces, before in units
    ]
    tops = []
    for parts, (q, pieces, before) in zip(scores, units):
        found = [jnp.max(s, axis=1, keepdims=True) for s in parts]
        if before is not None:
            found.append(before)
        tops.append(functools.reduce(jnp.maximum, found))
    probs = [
        [jnp.exp2(s - m).astype(jnp.bfloat16) for s in parts] for parts, m in zip(scores, tops)
    ]
    sums = []
    for parts, (q, pieces, before) in zip(probs, units):
        total = None
        for p, (k, v, dist, reach) in zip(parts, pieces):
            both = jnp.concatenate([v, jnp.ones_like(v)], axis=1)
            got = jnp.dot(p, both, preferred_element_type=jnp.float32)
            total = got if total is None else total + got
        sums.append(total)
    return tops, sums


def attend_tile(q_ref, tile_ref, dist_ref, reach_of, heads, state, geometry):
    high, wide, span, frames, head_dim, factor, step = geometry
    cells = high * wide
    acc_ref, sum_ref, max_ref = state
    for at, head in enumerate(heads):
        cols = slice(head * head_dim, (head + 1) * head_dim)
        outs = slice(at * head_dim, (at + 1) * head_dim)
        starts = range(0, q_ref.shape[0], step)
        units = []
        for start in starts:
            near = dist_ref[start % cells : start % cells + step, : tile_ref.shape[1]]
            piece = (tile_ref[0, :, cols], tile_ref[1, :, cols], near, reach_of(head))
            units.append((q_ref[start : start + step, cols], [piece], None))
        for start, m, got in zip(starts, *attend(units, factor)):
            rows = slice(start, start + step)
            acc_ref[rows, outs] = got[:, :head_dim]
            sum_ref[rows, outs] = got[:, head_dim:]
            max_ref[rows, outs] = jnp.broadcast_to(m, (step, head_dim))


def begin_kernel(radius_ref, mask_ref, q_ref, tile_ref, *outs, geometry, heads):
    *state, dist_ref, reach_ref = outs
    high, wide, span, frames = geometry[:4]
    dist_ref[...] = distances(high, wide, span, frames)
    stretch_at = lax.axis_index("tm")
    line = (1, reach_ref.shape[1])
    for head in range(heads):
        radius = radius_ref[head]
        seen = mask_ref[stretch_at, 0, head] > 0
        reach_ref[head : head + 1] = jnp.full(line, radius, jnp.int32)
        reach_ref[heads + head : heads + head + 1] = jnp.full(
            line, jnp.where(seen, radius, -1), jnp.int32
        )
    attend_tile(q_ref, tile_ref, dist_ref, lambda h: radius_ref[h], (0,), state, geometry)


def tile_kernel(q_ref, tile_ref, dist_ref, reach_ref, *state, geometry, heads):
    attend_tile(
        q_ref,
        tile_ref,
        dist_ref,
        lambda h: reach_ref[h : h + 1, :1],
        range(1, heads),
        state,
        geometry,
    )


def pick_state(head_state, state, head, rows, head_dim):
    refs = head_state if head == 0 else state
    at = max(head - 1, 0) * head_dim
    return [ref[rows, at : at + head_dim] for ref in refs]


def rest_kernel(
    q_ref,
    edge_ref,
    first_tile_ref,
    first_edge_ref,
    *rest,
    geometry,
    heads,
    flips,
):
    head_state, dist_ref, reach_ref, state, outs = rest[:3], rest[3], rest[4], rest[5:8], rest[8:]
    high, wide, span, frames, head_dim, factor, step = geometry
    cells = high * wide
    base = frames * cells
    head_at = lax.axis_index("head")
    stretch_at = lax.axis_index("tm")

    def run(with_first):
        for flip, out_ref in zip(flips, outs):
            start = pl.multiple_of(jnp.bitwise_xor(head_at, flip) * step, step)
            rows = pl.ds(start, step)
            near = dist_ref[pl.ds(pl.multiple_of(lax.rem(start, cells), step), step)]
            beyond = near[:, base:]
            units = []
            olds = []
            for head in range(heads):
                cols = slice(head * head_dim, (head + 1) * head_dim)
                sources = [(edge_ref, beyond, head)]
                if with_first:
                    sources.append((first_tile_ref, near[:, :base], heads + head))
                    sources.append((first_edge_ref, beyond, heads + head))
                pieces = [
                    (ref[0, :, cols], ref[1, :, cols], dist, reach_ref[row : row + 1, :1])
                    for ref, dist, row in sources
                ]
                olds.append(pick_state(head_state, state, head, rows, head_dim))
                units.append((q_ref[rows, cols], pieces, olds[-1][2][:, :1]))
            for head, (m, got) in enumerate(zip(*attend(units, factor))):
                old_acc, old_total, old_max = olds[head]
                shrink = jnp.exp2(old_max - m)
                acc = old_acc * shrink + got[:, :head_dim]
                total = old_total * shrink + got[:, head_dim:]
                cols = slice(head * head_dim, (head + 1) * head_dim)
                out_ref[:, cols] = (acc / total).astype(jnp.bfloat16)

    @pl.when(stretch_at > 0)
    def _():
        run(True)

    @pl.when(stretch_at == 0)
    def _():
        run(False)


def copy_kernel(in_ref, out_ref):
    out_ref[...] = in_ref[...]


def stack_kernel(*refs):
    *parts, out_ref = refs
    tile_at = lax.axis_index("tile")
    for flip, part in enumerate(parts):
        tall = part.shape[0]
        top = pl.multiple_of(jnp.bitwise_xor(tile_at, flip) * tall, 16)
        out_ref[pl.ds(top, tall)] = part[...]


def project_kernel(w_ref, part_ref, own_ref, got_ref, out_ref, *, flip):
    broad = part_ref.shape[1]
    half = jnp.bitwise_xor(lax.axis_index("tm"), flip)
    cols = pl.ds(pl.multiple_of(half * broad, 128), broad)
    total = jnp.dot(own_ref[...], w_ref[:, cols], preferred_element_type=jnp.float32)
    total += jnp.dot(got_ref[...], part_ref[...], preferred_element_type=jnp.float32)
    out_ref[...] = total.astype(out_ref.dtype)


def add_kernel(mine_ref, got_ref, *rest, flip):
    out_ref, sum_ref, sems = rest[-3:]
    pieces, tall, broad = sum_ref.shape
    half = jnp.bitwise_xor(lax.axis_index("tm"), flip)
    cols = pl.ds(pl.multiple_of(half * broad, 128), broad)
    copies = []
    for i in range(pieces):
        rows = slice(i * tall, (i + 1) * tall)
        sum_ref[i] = (mine_ref[rows] + got_ref[rows].astype(jnp.float32)).astype(jnp.bfloat16)
        copies.append(pltpu.make_async_copy(sum_ref.at[i], out_ref.at[rows, cols], sems.at[i]))
        copies[-1].start()
    for copy in copies:
        copy.wait()


def two_by_two(query, keys, values, out_weight, radius, block_mask):
    span = RMAX
    frames, high, wide, channels = query.shape[2:]
    heads = radius.shape[0]
    head_dim = channels // heads
    cells = high * wide
    tokens = frames * cells
    groups = lax.axis_size("head")
    tiles = lax.axis_size("tile")
    depth, width = out_weight.shape
    step = tokens // groups
    geometry = (high, wide, span, frames, head_dim, LOG2E / math.sqrt(head_dim), step)
    count = frames * (cells + span * (wide + high + span))
    smem = pl.BlockSpec(memory_space=pltpu.SMEM)
    vmem = pl.BlockSpec(memory_space=pltpu.VMEM)
    hbm = pl.BlockSpec(memory_space=pltpu.HBM)
    bf16, f32 = jnp.bfloat16, jnp.float32
    shape = jax.ShapeDtypeStruct

    def call(kernel, out_shape, specs, *args, name, scratch=(), flops=0, **keys_of):
        return pl.pallas_call(
            functools.partial(kernel, **keys_of) if keys_of else kernel,
            out_shape=out_shape,
            in_specs=specs,
            out_specs=jax.tree.map(lambda _: vmem, out_shape),
            scratch_shapes=scratch,
            cost_estimate=pl.CostEstimate(flops=flops, bytes_accessed=0, transcendentals=0),
            compiler_params=pltpu.CompilerParams(vmem_limit_bytes=VMEM_LIMIT),
            name=name,
        )(*args)

    def flipped(value, axis, flip):
        return lax.ppermute(value, axis, [(i, i ^ flip) for i in range(lax.axis_size(axis))])

    q = query.reshape(tokens, channels)
    k = keys.reshape(tokens, channels)
    v = values.reshape(tokens, channels)

    tall, broad = depth // tiles, width // 2
    part_shape = shape((tall, broad), bf16)
    part = call(
        part_kernel,
        part_shape,
        [hbm],
        pltpu.with_memory_space_constraint(out_weight, pltpu.HBM),
        name="part",
        scratch=[pltpu.SemaphoreType.DMA],
    )
    *faces, tile = call(
        face_kernel,
        [
            shape((2, frames, span * wide, channels), bf16),
            shape((2, frames, span * high, channels), bf16),
            shape((2, frames, span * span, channels), bf16),
            shape((2, tokens, channels), bf16),
        ],
        [vmem] * 3,
        k,
        v,
        part,
        name="faces",
        geometry=geometry,
    )
    faces = [flipped(face, "tile", flip) for face, flip in zip(faces, (2, 1, 3))]
    lone = flipped(part, "head", 2)
    begun = call(
        begin_kernel,
        [shape((tokens, head_dim), f32)] * 3
        + [shape((cells, count), jnp.int32), shape((2 * heads, head_dim), jnp.int32)],
        [smem] * 2 + [vmem] * 2,
        radius,
        block_mask.transpose(1, 2, 0),
        q,
        tile,
        name="begin",
        geometry=geometry,
        heads=heads,
    )
    begun, tile = lax.optimization_barrier((begun, tile))
    first_tile = lax.ppermute(tile, "tm", [(0, 1)])
    state = call(
        tile_kernel,
        [shape((tokens, channels - head_dim), f32)] * 3,
        [vmem] * 4,
        q,
        tile,
        *begun[3:],
        name="tile",
        geometry=geometry,
        heads=heads,
    )
    lone, state = lax.optimization_barrier((lone, state))
    lone = call(copy_kernel, part_shape, [vmem], lone, name="lone", flops=2 * 10**9)
    lone, state, faces = lax.optimization_barrier((lone, state, faces))
    edge = call(
        edge_kernel, shape((2, count - tokens, channels), bf16), [vmem] * 3, *faces, name="edges", flops=20 * 10**9
    )
    first_edge = lax.ppermute(edge, "tm", [(0, 1)])
    parts = [lone] + [flipped(lone, "tile", flip) for flip in range(1, tiles)]

    def rest(state, *flips, flops=0):
        return call(
            rest_kernel,
            [shape((step, channels), bf16)] * len(flips),
            [vmem] * 12,
            q,
            edge,
            first_tile,
            first_edge,
            *begun,
            *state,
            name="rest",
            geometry=geometry,
            heads=heads,
            flips=flips,
            flops=flops,
        )

    (for_side,) = rest(state, 3)
    got_side = flipped(for_side, "head", 2)
    state, for_side = lax.optimization_barrier((state, for_side))
    for_far, own_side = rest(state, 2, 1)
    parts, own_side = lax.optimization_barrier((parts, own_side))
    here = call(
        stack_kernel, shape((depth, broad), bf16), [vmem] * tiles, *parts, name="stack"
    )

    there = flipped(here, "tm", 1)

    def project(part, mine, got, kind, flip, flops=0):
        return call(
            project_kernel,
            shape((step, broad), kind),
            [vmem] * 4,
            out_weight,
            part,
            mine,
            got,
            name="project",
            flops=flops,
            flip=flip,
        )

    got_side = call(
        copy_kernel, shape((step, channels), bf16), [vmem], got_side, name="got", flops=20 * 10**9
    )
    for_far, got_side = lax.optimization_barrier((for_far, got_side))
    got_far = flipped(for_far, "head", 2)
    for_side = [project(here, own_side, got_side, bf16, 0, 20 * 10**9)]
    from_side = [flipped(for_side[0], "head", 1)]
    for_side.append(project(there, own_side, got_side, bf16, 1))
    from_side.append(flipped(for_side[1], "head", 1))
    state, for_side[1] = lax.optimization_barrier((state, for_side[1]))
    (own,) = rest(state, 0, flops=20 * 10**9)
    mine = [
        project(here, own, got_far, f32, 0),
        project(there, own, got_far, f32, 1, 20 * 10**9),
    ]
    pieces = 2
    mixed = []
    for flip in range(2):
        mixed = [
            pl.pallas_call(
                functools.partial(add_kernel, flip=flip),
                out_shape=shape((step, width), bf16),
                in_specs=[vmem] * 2 + [hbm] * flip,
                out_specs=hbm,
                input_output_aliases={2: 0} if flip else {},
                scratch_shapes=[
                    pltpu.VMEM((pieces, step // pieces, broad), bf16),
                    pltpu.SemaphoreType.DMA((pieces,)),
                ],
                compiler_params=pltpu.CompilerParams(vmem_limit_bytes=VMEM_LIMIT),
                name="add",
            )(mine[flip], from_side[flip], *mixed)
        ]
    (mixed,) = mixed
    return mixed.reshape(1, 1, step, width)


def solution(mesh):
    in_specs = (
        P("tm", "tile", None, None, None, "head"),
        P("tm", "tile", None, None, None, "head"),
        P("tm", "tile", None, None, None, "head"),
        P("head", None),
        P("head"),
        P("head", None, None),
    )
    out_specs = P("tm", "tile", "head", None)
    small = dict(mesh.shape) == {"tm": 2, "tile": 4, "head": 4}
    return jax.shard_map(
        two_by_two if small else any_grid,
        mesh=mesh,
        in_specs=in_specs,
        out_specs=out_specs,
        check_vma=False,
    )
```

```python
import functools
import math

import jax
import jax.numpy as jnp
from jax import lax
from jax.experimental import pallas as pl
from jax.experimental.pallas import tpu as pltpu
from jax.sharding import PartitionSpec as P

RMAX = 4
FAR = -1e30
LOG2E = 1.4426950408889634
VMEM_LIMIT = 24 * 1024 * 1024


def passed_along(value, axis, by):
    peers = lax.axis_size(axis)
    pairs = [(i, i + by) for i in range(peers) if 0 <= i + by < peers]
    return lax.ppermute(value, axis, pairs)


def widen(key_part, value_part, span, row_move, col_move):
    grid = math.isqrt(lax.axis_size("tile"))
    above = None
    below = None
    for offset in (grid, -grid):
        if offset > 0:
            face_key = key_part[:, :, key_part.shape[2] - span :]
            face_value = value_part[:, :, value_part.shape[2] - span :]
        else:
            face_key = key_part[:, :, :span]
            face_value = value_part[:, :, :span]
        got = row_move(face_key, face_value, offset)
        if offset > 0:
            above = got
        else:
            below = got
    key_rows = jnp.concatenate([above[0], key_part, below[0]], axis=2)
    value_rows = jnp.concatenate([above[1], value_part, below[1]], axis=2)
    left = None
    right = None
    for offset in (1, -1):
        if offset > 0:
            face_key = key_rows[:, :, :, key_rows.shape[3] - span :]
            face_value = value_rows[:, :, :, value_rows.shape[3] - span :]
        else:
            face_key = key_rows[:, :, :, :span]
            face_value = value_rows[:, :, :, :span]
        got = col_move(face_key, face_value, offset)
        if offset > 0:
            left = got
        else:
            right = got
    key_full = jnp.concatenate([left[0], key_rows, right[0]], axis=3)
    value_full = jnp.concatenate([left[1], value_rows, right[1]], axis=3)
    return (key_full, value_full)


def windows_of(block, half_high, half_wide, win_high, win_wide, heads_here, head_dim):
    parts = []
    for band in (0, 1):
        for strip in (0, 1):
            parts.append(
                block[
                    :,
                    band * half_high : band * half_high + win_high,
                    strip * half_wide : strip * half_wide + win_wide,
                ]
            )
    stacked = jnp.stack(parts)
    return stacked.reshape(4, -1, heads_here, head_dim)


def any_grid(query, keys, values, out_weight, radius, block_mask):
    span = RMAX
    grid = math.isqrt(lax.axis_size("tile"))
    tile_at = lax.axis_index("tile")
    row_at = tile_at // grid
    col_at = tile_at % grid
    stretch_at = lax.axis_index("tm")
    frames, high, wide, channels = query.shape[2:]
    heads_here = radius.shape[0]
    head_dim = channels // heads_here
    tokens_here = frames * high * wide
    half_high = high // 2
    half_wide = wide // 2
    win_high = half_high + 2 * span
    win_wide = half_wide + 2 * span
    quarter = frames * half_high * half_wide
    queries = query[0, 0].reshape(frames, 2, half_high, 2, half_wide, channels)
    queries = queries.transpose(1, 3, 0, 2, 4, 5).reshape(4, quarter, heads_here, head_dim)
    query_y = jnp.broadcast_to(
        jnp.arange(half_high, dtype=jnp.int32)[None, :, None], (frames, half_high, half_wide)
    ).reshape(-1)
    query_x = jnp.broadcast_to(
        jnp.arange(half_wide, dtype=jnp.int32)[None, None, :], (frames, half_high, half_wide)
    ).reshape(-1)
    key_y = jnp.broadcast_to(
        jnp.arange(win_high, dtype=jnp.int32)[None, :, None] - span, (frames, win_high, win_wide)
    ).reshape(-1)
    key_x = jnp.broadcast_to(
        jnp.arange(win_wide, dtype=jnp.int32)[None, None, :] - span, (frames, win_high, win_wide)
    ).reshape(-1)
    band_at = jnp.array([0, 0, 1, 1], dtype=jnp.int32)
    strip_at = jnp.array([0, 1, 0, 1], dtype=jnp.int32)
    global_y = row_at * high + band_at[:, None] * half_high + key_y[None, :]
    global_x = col_at * wide + strip_at[:, None] * half_wide + key_x[None, :]
    inside = (global_y >= 0) & (global_y < grid * high) & (global_x >= 0) & (global_x < grid * wide)
    distance = jnp.maximum(
        jnp.abs(query_y[:, None] - key_y[None, :]), jnp.abs(query_x[:, None] - key_x[None, :])
    )
    near = distance[None, :, :] <= radius[:, None, None]
    allowed = near[None, :, :, :] & inside[:, None, None, :]
    scale = 1.0 / math.sqrt(head_dim)
    initial = (
        jnp.full((4, heads_here, quarter), -1e30, jnp.float32),
        jnp.zeros((4, heads_here, quarter), jnp.float32),
        jnp.zeros((4, heads_here, quarter, head_dim), jnp.float32),
    )

    def tile_move(face_key, face_value, offset):
        return passed_along((face_key, face_value), "tile", offset)

    key_all, value_all = (
        lax.all_gather(keys[0], "tm", axis=0, tiled=True),
        lax.all_gather(values[0], "tm", axis=0, tiled=True),
    )
    key_full, value_full = widen(key_all, value_all, span, tile_move, tile_move)
    stretch_ids = jnp.arange(key_full.shape[0], dtype=jnp.int32)

    def one_stretch(state, item):
        key_block, value_block, stretch_id = item
        visible = (
            lax.dynamic_slice_in_dim(
                lax.dynamic_index_in_dim(block_mask, stretch_at, 1, False), stretch_id, 1, 1
            )[:, 0]
            > 0
        )
        best, total, acc = state
        key_win = windows_of(
            key_block, half_high, half_wide, win_high, win_wide, heads_here, head_dim
        )
        value_win = windows_of(
            value_block, half_high, half_wide, win_high, win_wide, heads_here, head_dim
        )
        usable = allowed & visible[None, :, None, None]
        scores = (
            jnp.einsum("nqhd,nkhd->nhqk", queries, key_win, preferred_element_type=jnp.float32)
            * scale
        )
        masked = jnp.where(usable, scores, jnp.float32(-1e30))
        fresh = jnp.maximum(best, jnp.max(masked, axis=3))
        probs = jnp.where(usable, jnp.exp(scores - fresh[..., None]), jnp.float32(0.0))
        shrink = jnp.exp(best - fresh)
        total = total * shrink + jnp.sum(probs, axis=3)
        acc = acc * shrink[..., None] + jnp.einsum(
            "nhqk,nkhd->nhqd",
            probs.astype(jnp.bfloat16),
            value_win,
            preferred_element_type=jnp.float32,
        )
        return ((fresh, total, acc), None)

    final, unused = lax.scan(one_stretch, initial, (key_full, value_full, stretch_ids))
    best, total, acc = final
    attn = (acc / total[..., None]).astype(jnp.bfloat16)
    attn = attn.transpose(0, 2, 1, 3).reshape(
        2, 2, frames, half_high, half_wide, heads_here * head_dim
    )
    attn = attn.transpose(2, 0, 3, 1, 4, 5).reshape(tokens_here, heads_here * head_dim)
    mixed = lax.psum_scatter(
        jnp.dot(attn, out_weight, preferred_element_type=jnp.float32).astype(jnp.bfloat16),
        "head",
        scatter_dimension=0,
        tiled=True,
    )
    return mixed.reshape(1, 1, -1, out_weight.shape[1])


def tile_place():
    tile_at = lax.axis_index("tile")
    return tile_at // 2, tile_at % 2


def part_kernel(w_ref, part_ref, sem):
    tall, broad = part_ref.shape
    top = pl.multiple_of(lax.axis_index("tile") * tall, 16)
    left = pl.multiple_of(lax.axis_index("tm") * broad, 128)
    copy = pltpu.make_async_copy(w_ref.at[pl.ds(top, tall), pl.ds(left, broad)], part_ref, sem)
    copy.start()
    copy.wait()


def face_kernel(k_ref, v_ref, part_ref, row_ref, col_ref, corner_ref, tile_ref, *, geometry):
    high, wide, span, frames = geometry[:4]
    cells = high * wide
    row_at, col_at = tile_place()
    y0 = jnp.where(row_at == 0, high - span, 0)
    x0 = jnp.where(col_at == 0, wide - span, 0)

    def picker(count, cell_of):
        row = lax.broadcasted_iota(jnp.int32, (count, cells), 0)
        col = lax.broadcasted_iota(jnp.int32, (count, cells), 1)
        return (col == cell_of(row)).astype(jnp.bfloat16)

    beside = picker(high * span, lambda i: (i // span) * wide + x0 + i % span)
    across = picker(span * span, lambda i: (y0 + i // span) * wide + x0 + i % span)
    for which, ref in enumerate((k_ref, v_ref)):
        tile_ref[which] = ref[...]
        for f in range(frames):
            start = pl.multiple_of(f * cells + y0 * wide, 16)
            row_ref[which, f] = ref[pl.ds(start, span * wide)]
            whole = ref[f * cells : (f + 1) * cells]
            col_ref[which, f] = jnp.dot(
                beside, whole, preferred_element_type=jnp.float32
            ).astype(jnp.bfloat16)
            corner_ref[which, f] = jnp.dot(
                across, whole, preferred_element_type=jnp.float32
            ).astype(jnp.bfloat16)


def edge_kernel(row_ref, col_ref, corner_ref, out_ref):
    for which in range(2):
        at = 0
        for part in (row_ref, col_ref, corner_ref):
            for f in range(part.shape[1]):
                size = part.shape[2]
                out_ref[which, at : at + size] = part[which, f]
                at += size


def distances(high, wide, span, frames):
    row_at, col_at = tile_place()
    cells = high * wide
    count = frames * (cells + span * (wide + high + span))
    j = lax.broadcasted_iota(jnp.int32, (1, count), 1)
    y_off = jnp.where(row_at == 0, high, -span)
    x_off = jnp.where(col_at == 0, wide, -span)
    c = j % cells
    ky, kx = c // wide, c % wide
    base = frames * cells
    c = (j - base) % (span * wide)
    ky = jnp.where(j >= base, y_off + c // wide, ky)
    kx = jnp.where(j >= base, c % wide, kx)
    base += frames * span * wide
    c = (j - base) % (span * high)
    ky = jnp.where(j >= base, c // span, ky)
    kx = jnp.where(j >= base, x_off + c % span, kx)
    base += frames * span * high
    c = (j - base) % (span * span)
    ky = jnp.where(j >= base, y_off + c // span, ky)
    kx = jnp.where(j >= base, x_off + c % span, kx)
    i = lax.broadcasted_iota(jnp.int32, (cells, 1), 0)
    return jnp.maximum(jnp.abs(i // wide - ky), jnp.abs(i % wide - kx))


def attend(units, factor):
    scores = [
        [
            jnp.where(
                dist <= reach,
                lax.dot_general(
                    q, k, (((1,), (1,)), ((), ())), preferred_element_type=jnp.float32
                )
                * factor,
                FAR,
            )
            for k, v, dist, reach in pieces
        ]
        for q, pieces, before in units
    ]
    tops = []
    for parts, (q, pieces, before) in zip(scores, units):
        found = [jnp.max(s, axis=1, keepdims=True) for s in parts]
        if before is not None:
            found.append(before)
        tops.append(functools.reduce(jnp.maximum, found))
    probs = [
        [jnp.exp2(s - m).astype(jnp.bfloat16) for s in parts] for parts, m in zip(scores, tops)
    ]
    sums = []
    for parts, (q, pieces, before) in zip(probs, units):
        total = None
        for p, (k, v, dist, reach) in zip(parts, pieces):
            both = jnp.concatenate([v, jnp.ones_like(v)], axis=1)
            got = jnp.dot(p, both, preferred_element_type=jnp.float32)
            total = got if total is None else total + got
        sums.append(total)
    return tops, sums


def attend_tile(q_ref, tile_ref, dist_ref, reach_of, heads, state, geometry):
    high, wide, span, frames, head_dim, factor, step = geometry
    cells = high * wide
    acc_ref, sum_ref, max_ref = state
    for at, head in enumerate(heads):
        cols = slice(head * head_dim, (head + 1) * head_dim)
        outs = slice(at * head_dim, (at + 1) * head_dim)
        starts = range(0, q_ref.shape[0], step)
        units = []
        for start in starts:
            near = dist_ref[start % cells : start % cells + step, : tile_ref.shape[1]]
            piece = (tile_ref[0, :, cols], tile_ref[1, :, cols], near, reach_of(head))
            units.append((q_ref[start : start + step, cols], [piece], None))
        for start, m, got in zip(starts, *attend(units, factor)):
            rows = slice(start, start + step)
            acc_ref[rows, outs] = got[:, :head_dim]
            sum_ref[rows, outs] = got[:, head_dim:]
            max_ref[rows, outs] = jnp.broadcast_to(m, (step, head_dim))


def tile_kernel(radius_ref, mask_ref, q_ref, tile_ref, *outs, geometry, heads):
    *state, dist_ref, reach_ref = outs
    high, wide, span, frames = geometry[:4]
    dist_ref[...] = distances(high, wide, span, frames)
    stretch_at = lax.axis_index("tm")
    line = (1, reach_ref.shape[1])
    for head in range(heads):
        radius = radius_ref[head]
        seen = mask_ref[stretch_at, 0, head] > 0
        reach_ref[head : head + 1] = jnp.full(line, radius, jnp.int32)
        reach_ref[heads + head : heads + head + 1] = jnp.full(
            line, jnp.where(seen, radius, -1), jnp.int32
        )
    attend_tile(
        q_ref, tile_ref, dist_ref, lambda h: radius_ref[h], range(heads), state, geometry
    )


def first_kernel(
    q_ref, first_ref, acc_ref, sum_ref, max_ref, dist_ref, reach_ref, *outs, geometry, heads
):
    high, wide, span, frames, head_dim, factor, step = geometry
    cells = high * wide
    base = frames * cells
    olds = (acc_ref, sum_ref, max_ref)

    @pl.when(lax.axis_index("tm") > 0)
    def _():
        for head in range(heads):
            cols = slice(head * head_dim, (head + 1) * head_dim)
            units = []
            starts = range(0, q_ref.shape[0], step)
            for start in starts:
                rows = slice(start, start + step)
                near = dist_ref[start % cells : start % cells + step, :base]
                reach = reach_ref[heads + head : heads + head + 1, :1]
                piece = (first_ref[0, :, cols], first_ref[1, :, cols], near, reach)
                units.append((q_ref[rows, cols], [piece], max_ref[rows, cols][:, :1]))
            for start, m, got in zip(starts, *attend(units, factor)):
                rows = slice(start, start + step)
                acc, total, old = (ref[rows, cols] for ref in olds)
                shrink = jnp.exp2(old - m)
                outs[0][rows, cols] = acc * shrink + got[:, :head_dim]
                outs[1][rows, cols] = total * shrink + got[:, head_dim:]
                outs[2][rows, cols] = jnp.broadcast_to(m, old.shape)

    @pl.when(lax.axis_index("tm") == 0)
    def _():
        for ref, out_ref in zip(olds, outs):
            out_ref[...] = ref[...]


def rest_kernel(
    q_ref,
    edge_ref,
    first_ref,
    dist_ref,
    reach_ref,
    acc_ref,
    sum_ref,
    max_ref,
    *outs,
    geometry,
    heads,
    flips,
):
    high, wide, span, frames, head_dim, factor, step = geometry
    cells = high * wide
    base = frames * cells
    head_at = lax.axis_index("head")
    stretch_at = lax.axis_index("tm")

    def run(with_first):
        for flip, out_ref in zip(flips, outs):
            start = pl.multiple_of(jnp.bitwise_xor(head_at, flip) * step, step)
            rows = pl.ds(start, step)
            near = dist_ref[pl.ds(pl.multiple_of(lax.rem(start, cells), step), step), base:]
            units = []
            olds = []
            for head in range(heads):
                cols = slice(head * head_dim, (head + 1) * head_dim)
                sources = [(edge_ref, head)]
                if with_first:
                    sources.append((first_ref, heads + head))
                pieces = [
                    (ref[0, :, cols], ref[1, :, cols], near, reach_ref[row : row + 1, :1])
                    for ref, row in sources
                ]
                olds.append([ref[rows, cols] for ref in (acc_ref, sum_ref, max_ref)])
                units.append((q_ref[rows, cols], pieces, olds[-1][2][:, :1]))
            for head, (m, got) in enumerate(zip(*attend(units, factor))):
                old_acc, old_total, old_max = olds[head]
                shrink = jnp.exp2(old_max - m)
                acc = old_acc * shrink + got[:, :head_dim]
                total = old_total * shrink + got[:, head_dim:]
                cols = slice(head * head_dim, (head + 1) * head_dim)
                out_ref[:, cols] = (acc / total).astype(jnp.bfloat16)

    @pl.when(stretch_at > 0)
    def _():
        run(True)

    @pl.when(stretch_at == 0)
    def _():
        run(False)


def copy_kernel(in_ref, out_ref):
    out_ref[...] = in_ref[...]


def stack_kernel(*refs):
    *parts, out_ref = refs
    tile_at = lax.axis_index("tile")
    for flip, part in enumerate(parts):
        tall = part.shape[0]
        top = pl.multiple_of(jnp.bitwise_xor(tile_at, flip) * tall, 16)
        out_ref[pl.ds(top, tall)] = part[...]


def project_kernel(w_ref, part_ref, own_ref, got_ref, out_ref, *, flip):
    broad = part_ref.shape[1]
    half = jnp.bitwise_xor(lax.axis_index("tm"), flip)
    cols = pl.ds(pl.multiple_of(half * broad, 128), broad)
    total = jnp.dot(own_ref[...], w_ref[:, cols], preferred_element_type=jnp.float32)
    total += jnp.dot(got_ref[...], part_ref[...], preferred_element_type=jnp.float32)
    out_ref[...] = total.astype(out_ref.dtype)


def add_kernel(mine_ref, got_ref, *rest, flip):
    out_ref, sum_ref, sems = rest[-3:]
    pieces, tall, broad = sum_ref.shape
    half = jnp.bitwise_xor(lax.axis_index("tm"), flip)
    cols = pl.ds(pl.multiple_of(half * broad, 128), broad)
    copies = []
    for i in range(pieces):
        rows = slice(i * tall, (i + 1) * tall)
        sum_ref[i] = (mine_ref[rows] + got_ref[rows].astype(jnp.float32)).astype(jnp.bfloat16)
        copies.append(pltpu.make_async_copy(sum_ref.at[i], out_ref.at[rows, cols], sems.at[i]))
        copies[-1].start()
    for copy in copies:
        copy.wait()


def two_by_two(query, keys, values, out_weight, radius, block_mask):
    span = RMAX
    frames, high, wide, channels = query.shape[2:]
    heads = radius.shape[0]
    head_dim = channels // heads
    cells = high * wide
    tokens = frames * cells
    groups = lax.axis_size("head")
    tiles = lax.axis_size("tile")
    depth, width = out_weight.shape
    step = tokens // groups
    geometry = (high, wide, span, frames, head_dim, LOG2E / math.sqrt(head_dim), step)
    count = frames * (cells + span * (wide + high + span))
    smem = pl.BlockSpec(memory_space=pltpu.SMEM)
    vmem = pl.BlockSpec(memory_space=pltpu.VMEM)
    hbm = pl.BlockSpec(memory_space=pltpu.HBM)
    bf16, f32 = jnp.bfloat16, jnp.float32
    shape = jax.ShapeDtypeStruct

    def call(kernel, out_shape, specs, *args, name, scratch=(), flops=0, **keys_of):
        return pl.pallas_call(
            functools.partial(kernel, **keys_of) if keys_of else kernel,
            out_shape=out_shape,
            in_specs=specs,
            out_specs=jax.tree.map(lambda _: vmem, out_shape),
            scratch_shapes=scratch,
            cost_estimate=pl.CostEstimate(flops=flops, bytes_accessed=0, transcendentals=0),
            compiler_params=pltpu.CompilerParams(vmem_limit_bytes=VMEM_LIMIT),
            name=name,
        )(*args)

    def flipped(value, axis, flip):
        return lax.ppermute(value, axis, [(i, i ^ flip) for i in range(lax.axis_size(axis))])

    q = query.reshape(tokens, channels)
    k = keys.reshape(tokens, channels)
    v = values.reshape(tokens, channels)

    tall, broad = depth // tiles, width // 2
    part_shape = shape((tall, broad), bf16)
    part = call(
        part_kernel,
        part_shape,
        [hbm],
        pltpu.with_memory_space_constraint(out_weight, pltpu.HBM),
        name="part",
        scratch=[pltpu.SemaphoreType.DMA],
    )
    *faces, tile = call(
        face_kernel,
        [
            shape((2, frames, span * wide, channels), bf16),
            shape((2, frames, span * high, channels), bf16),
            shape((2, frames, span * span, channels), bf16),
            shape((2, tokens, channels), bf16),
        ],
        [vmem] * 3,
        k,
        v,
        part,
        name="faces",
        geometry=geometry,
    )
    faces = [flipped(face, "tile", flip) for face, flip in zip(faces, (2, 1, 3))]
    lone = flipped(part, "head", 2)
    first_tile = lax.ppermute(tile, "tm", [(0, 1)])
    *state, dist, reach = call(
        tile_kernel,
        [shape((tokens, channels), f32)] * 3
        + [shape((cells, count), jnp.int32), shape((2 * heads, head_dim), jnp.int32)],
        [smem] * 2 + [vmem] * 2,
        radius,
        block_mask.transpose(1, 2, 0),
        q,
        tile,
        name="tile",
        flops=20 * 10**9,
        geometry=geometry,
        heads=heads,
    )
    state = call(
        first_kernel,
        [shape((tokens, channels), f32)] * 3,
        [vmem] * 7,
        q,
        first_tile,
        *state,
        dist,
        reach,
        name="first",
        geometry=geometry,
        heads=heads,
    )
    lone, state = lax.optimization_barrier((lone, state))
    lone = call(copy_kernel, part_shape, [vmem], lone, name="lone", flops=2 * 10**9)
    lone, state, faces = lax.optimization_barrier((lone, state, faces))
    edge = call(
        edge_kernel, shape((2, count - tokens, channels), bf16), [vmem] * 3, *faces, name="edges", flops=20 * 10**9
    )
    first_edge = lax.ppermute(edge, "tm", [(0, 1)])
    parts = [lone] + [flipped(lone, "tile", flip) for flip in range(1, tiles)]

    def rest(state, *flips, flops=0):
        return call(
            rest_kernel,
            [shape((step, channels), bf16)] * len(flips),
            [vmem] * 8,
            q,
            edge,
            first_edge,
            dist,
            reach,
            *state,
            name="rest",
            geometry=geometry,
            heads=heads,
            flips=flips,
            flops=flops,
        )

    (for_side,) = rest(state, 3)
    got_side = flipped(for_side, "head", 2)
    state, for_side = lax.optimization_barrier((state, for_side))
    for_far, own_side = rest(state, 2, 1)
    got_far = flipped(for_far, "head", 2)
    parts, own_side = lax.optimization_barrier((parts, own_side))
    here = call(
        stack_kernel, shape((depth, broad), bf16), [vmem] * tiles, *parts, name="stack"
    )

    def project(part, mine, got, kind, flip, flops=0):
        return call(
            project_kernel,
            shape((step, broad), kind),
            [vmem] * 4,
            out_weight,
            part,
            mine,
            got,
            name="project",
            flops=flops,
            flip=flip,
        )

    for_side = [project(here, own_side, got_side, bf16, 0, 20 * 10**9)]
    from_side = [flipped(for_side[0], "head", 1)]
    state, here, for_side[0] = lax.optimization_barrier((state, here, for_side[0]))
    there = flipped(here, "tm", 1)
    (own,) = rest(state, 0, flops=20 * 10**9)
    own_side, own = lax.optimization_barrier((own_side, own))
    for_side.append(project(there, own_side, got_side, bf16, 1))
    from_side.append(flipped(for_side[1], "head", 1))
    own, for_side[1] = lax.optimization_barrier((own, for_side[1]))
    mine = [
        project(here, own, got_far, f32, 0),
        project(there, own, got_far, f32, 1, 20 * 10**9),
    ]
    pieces = 2
    mixed = []
    for flip in range(2):
        mixed = [
            pl.pallas_call(
                functools.partial(add_kernel, flip=flip),
                out_shape=shape((step, width), bf16),
                in_specs=[vmem] * 2 + [hbm] * flip,
                out_specs=hbm,
                input_output_aliases={2: 0} if flip else {},
                scratch_shapes=[
                    pltpu.VMEM((pieces, step // pieces, broad), bf16),
                    pltpu.SemaphoreType.DMA((pieces,)),
                ],
                compiler_params=pltpu.CompilerParams(vmem_limit_bytes=VMEM_LIMIT),
                name="add",
            )(mine[flip], from_side[flip], *mixed)
        ]
    (mixed,) = mixed
    return mixed.reshape(1, 1, step, width)


def solution(mesh):
    in_specs = (
        P("tm", "tile", None, None, None, "head"),
        P("tm", "tile", None, None, None, "head"),
        P("tm", "tile", None, None, None, "head"),
        P("head", None),
        P("head"),
        P("head", None, None),
    )
    out_specs = P("tm", "tile", "head", None)
    small = dict(mesh.shape) == {"tm": 2, "tile": 4, "head": 4}
    return jax.shard_map(
        two_by_two if small else any_grid,
        mesh=mesh,
        in_specs=in_specs,
        out_specs=out_specs,
        check_vma=False,
    )
```

```python
import functools
import math

import jax
import jax.numpy as jnp
from jax import lax
from jax.experimental import pallas as pl
from jax.experimental.pallas import tpu as pltpu
from jax.sharding import PartitionSpec as P

RMAX = 4
FAR = -1e30
LOG2E = 1.4426950408889634
VMEM_LIMIT = 24 * 1024 * 1024


def passed_along(value, axis, by):
    peers = lax.axis_size(axis)
    pairs = [(i, i + by) for i in range(peers) if 0 <= i + by < peers]
    return lax.ppermute(value, axis, pairs)


def widen(key_part, value_part, span, row_move, col_move):
    grid = math.isqrt(lax.axis_size("tile"))
    above = None
    below = None
    for offset in (grid, -grid):
        if offset > 0:
            face_key = key_part[:, :, key_part.shape[2] - span :]
            face_value = value_part[:, :, value_part.shape[2] - span :]
        else:
            face_key = key_part[:, :, :span]
            face_value = value_part[:, :, :span]
        got = row_move(face_key, face_value, offset)
        if offset > 0:
            above = got
        else:
            below = got
    key_rows = jnp.concatenate([above[0], key_part, below[0]], axis=2)
    value_rows = jnp.concatenate([above[1], value_part, below[1]], axis=2)
    left = None
    right = None
    for offset in (1, -1):
        if offset > 0:
            face_key = key_rows[:, :, :, key_rows.shape[3] - span :]
            face_value = value_rows[:, :, :, value_rows.shape[3] - span :]
        else:
            face_key = key_rows[:, :, :, :span]
            face_value = value_rows[:, :, :, :span]
        got = col_move(face_key, face_value, offset)
        if offset > 0:
            left = got
        else:
            right = got
    key_full = jnp.concatenate([left[0], key_rows, right[0]], axis=3)
    value_full = jnp.concatenate([left[1], value_rows, right[1]], axis=3)
    return (key_full, value_full)


def windows_of(block, half_high, half_wide, win_high, win_wide, heads_here, head_dim):
    parts = []
    for band in (0, 1):
        for strip in (0, 1):
            parts.append(
                block[
                    :,
                    band * half_high : band * half_high + win_high,
                    strip * half_wide : strip * half_wide + win_wide,
                ]
            )
    stacked = jnp.stack(parts)
    return stacked.reshape(4, -1, heads_here, head_dim)


def any_grid(query, keys, values, out_weight, radius, block_mask):
    span = RMAX
    grid = math.isqrt(lax.axis_size("tile"))
    tile_at = lax.axis_index("tile")
    row_at = tile_at // grid
    col_at = tile_at % grid
    stretch_at = lax.axis_index("tm")
    frames, high, wide, channels = query.shape[2:]
    heads_here = radius.shape[0]
    head_dim = channels // heads_here
    tokens_here = frames * high * wide
    half_high = high // 2
    half_wide = wide // 2
    win_high = half_high + 2 * span
    win_wide = half_wide + 2 * span
    quarter = frames * half_high * half_wide
    queries = query[0, 0].reshape(frames, 2, half_high, 2, half_wide, channels)
    queries = queries.transpose(1, 3, 0, 2, 4, 5).reshape(4, quarter, heads_here, head_dim)
    query_y = jnp.broadcast_to(
        jnp.arange(half_high, dtype=jnp.int32)[None, :, None], (frames, half_high, half_wide)
    ).reshape(-1)
    query_x = jnp.broadcast_to(
        jnp.arange(half_wide, dtype=jnp.int32)[None, None, :], (frames, half_high, half_wide)
    ).reshape(-1)
    key_y = jnp.broadcast_to(
        jnp.arange(win_high, dtype=jnp.int32)[None, :, None] - span, (frames, win_high, win_wide)
    ).reshape(-1)
    key_x = jnp.broadcast_to(
        jnp.arange(win_wide, dtype=jnp.int32)[None, None, :] - span, (frames, win_high, win_wide)
    ).reshape(-1)
    band_at = jnp.array([0, 0, 1, 1], dtype=jnp.int32)
    strip_at = jnp.array([0, 1, 0, 1], dtype=jnp.int32)
    global_y = row_at * high + band_at[:, None] * half_high + key_y[None, :]
    global_x = col_at * wide + strip_at[:, None] * half_wide + key_x[None, :]
    inside = (global_y >= 0) & (global_y < grid * high) & (global_x >= 0) & (global_x < grid * wide)
    distance = jnp.maximum(
        jnp.abs(query_y[:, None] - key_y[None, :]), jnp.abs(query_x[:, None] - key_x[None, :])
    )
    near = distance[None, :, :] <= radius[:, None, None]
    allowed = near[None, :, :, :] & inside[:, None, None, :]
    scale = 1.0 / math.sqrt(head_dim)
    initial = (
        jnp.full((4, heads_here, quarter), -1e30, jnp.float32),
        jnp.zeros((4, heads_here, quarter), jnp.float32),
        jnp.zeros((4, heads_here, quarter, head_dim), jnp.float32),
    )

    def tile_move(face_key, face_value, offset):
        return passed_along((face_key, face_value), "tile", offset)

    key_all, value_all = (
        lax.all_gather(keys[0], "tm", axis=0, tiled=True),
        lax.all_gather(values[0], "tm", axis=0, tiled=True),
    )
    key_full, value_full = widen(key_all, value_all, span, tile_move, tile_move)
    stretch_ids = jnp.arange(key_full.shape[0], dtype=jnp.int32)

    def one_stretch(state, item):
        key_block, value_block, stretch_id = item
        visible = (
            lax.dynamic_slice_in_dim(
                lax.dynamic_index_in_dim(block_mask, stretch_at, 1, False), stretch_id, 1, 1
            )[:, 0]
            > 0
        )
        best, total, acc = state
        key_win = windows_of(
            key_block, half_high, half_wide, win_high, win_wide, heads_here, head_dim
        )
        value_win = windows_of(
            value_block, half_high, half_wide, win_high, win_wide, heads_here, head_dim
        )
        usable = allowed & visible[None, :, None, None]
        scores = (
            jnp.einsum("nqhd,nkhd->nhqk", queries, key_win, preferred_element_type=jnp.float32)
            * scale
        )
        masked = jnp.where(usable, scores, jnp.float32(-1e30))
        fresh = jnp.maximum(best, jnp.max(masked, axis=3))
        probs = jnp.where(usable, jnp.exp(scores - fresh[..., None]), jnp.float32(0.0))
        shrink = jnp.exp(best - fresh)
        total = total * shrink + jnp.sum(probs, axis=3)
        acc = acc * shrink[..., None] + jnp.einsum(
            "nhqk,nkhd->nhqd",
            probs.astype(jnp.bfloat16),
            value_win,
            preferred_element_type=jnp.float32,
        )
        return ((fresh, total, acc), None)

    final, unused = lax.scan(one_stretch, initial, (key_full, value_full, stretch_ids))
    best, total, acc = final
    attn = (acc / total[..., None]).astype(jnp.bfloat16)
    attn = attn.transpose(0, 2, 1, 3).reshape(
        2, 2, frames, half_high, half_wide, heads_here * head_dim
    )
    attn = attn.transpose(2, 0, 3, 1, 4, 5).reshape(tokens_here, heads_here * head_dim)
    mixed = lax.psum_scatter(
        jnp.dot(attn, out_weight, preferred_element_type=jnp.float32).astype(jnp.bfloat16),
        "head",
        scatter_dimension=0,
        tiled=True,
    )
    return mixed.reshape(1, 1, -1, out_weight.shape[1])


def tile_place():
    tile_at = lax.axis_index("tile")
    return tile_at // 2, tile_at % 2


def part_kernel(w_ref, part_ref, sem):
    tall, broad = part_ref.shape
    top = pl.multiple_of(lax.axis_index("tile") * tall, 16)
    left = pl.multiple_of(lax.axis_index("tm") * broad, 128)
    copy = pltpu.make_async_copy(w_ref.at[pl.ds(top, tall), pl.ds(left, broad)], part_ref, sem)
    copy.start()
    copy.wait()


def face_kernel(k_ref, v_ref, part_ref, row_ref, col_ref, corner_ref, tile_ref, *, geometry):
    high, wide, span, frames = geometry[:4]
    cells = high * wide
    row_at, col_at = tile_place()
    y0 = jnp.where(row_at == 0, high - span, 0)
    x0 = jnp.where(col_at == 0, wide - span, 0)

    def picker(count, cell_of):
        row = lax.broadcasted_iota(jnp.int32, (count, cells), 0)
        col = lax.broadcasted_iota(jnp.int32, (count, cells), 1)
        return (col == cell_of(row)).astype(jnp.bfloat16)

    beside = picker(high * span, lambda i: (i // span) * wide + x0 + i % span)
    across = picker(span * span, lambda i: (y0 + i // span) * wide + x0 + i % span)
    for which, ref in enumerate((k_ref, v_ref)):
        tile_ref[which] = ref[...]
        for f in range(frames):
            start = pl.multiple_of(f * cells + y0 * wide, 16)
            row_ref[which, f] = ref[pl.ds(start, span * wide)]
            whole = ref[f * cells : (f + 1) * cells]
            col_ref[which, f] = jnp.dot(
                beside, whole, preferred_element_type=jnp.float32
            ).astype(jnp.bfloat16)
            corner_ref[which, f] = jnp.dot(
                across, whole, preferred_element_type=jnp.float32
            ).astype(jnp.bfloat16)


def edge_kernel(row_ref, col_ref, corner_ref, out_ref):
    for which in range(2):
        at = 0
        for part in (row_ref, col_ref, corner_ref):
            for f in range(part.shape[1]):
                size = part.shape[2]
                out_ref[which, at : at + size] = part[which, f]
                at += size


def distances(high, wide, span, frames):
    row_at, col_at = tile_place()
    cells = high * wide
    count = frames * (cells + span * (wide + high + span))
    j = lax.broadcasted_iota(jnp.int32, (1, count), 1)
    y_off = jnp.where(row_at == 0, high, -span)
    x_off = jnp.where(col_at == 0, wide, -span)
    c = j % cells
    ky, kx = c // wide, c % wide
    base = frames * cells
    c = (j - base) % (span * wide)
    ky = jnp.where(j >= base, y_off + c // wide, ky)
    kx = jnp.where(j >= base, c % wide, kx)
    base += frames * span * wide
    c = (j - base) % (span * high)
    ky = jnp.where(j >= base, c // span, ky)
    kx = jnp.where(j >= base, x_off + c % span, kx)
    base += frames * span * high
    c = (j - base) % (span * span)
    ky = jnp.where(j >= base, y_off + c // span, ky)
    kx = jnp.where(j >= base, x_off + c % span, kx)
    i = lax.broadcasted_iota(jnp.int32, (cells, 1), 0)
    return jnp.maximum(jnp.abs(i // wide - ky), jnp.abs(i % wide - kx))


def attend(units, factor):
    scores = [
        [
            jnp.where(
                dist <= reach,
                lax.dot_general(
                    q, k, (((1,), (1,)), ((), ())), preferred_element_type=jnp.float32
                )
                * factor,
                FAR,
            )
            for k, v, dist, reach in pieces
        ]
        for q, pieces, before in units
    ]
    tops = []
    for parts, (q, pieces, before) in zip(scores, units):
        found = [jnp.max(s, axis=1, keepdims=True) for s in parts]
        if before is not None:
            found.append(before)
        tops.append(functools.reduce(jnp.maximum, found))
    probs = [
        [jnp.exp2(s - m).astype(jnp.bfloat16) for s in parts] for parts, m in zip(scores, tops)
    ]
    sums = []
    for parts, (q, pieces, before) in zip(probs, units):
        total = None
        for p, (k, v, dist, reach) in zip(parts, pieces):
            both = jnp.concatenate([v, jnp.ones_like(v)], axis=1)
            got = jnp.dot(p, both, preferred_element_type=jnp.float32)
            total = got if total is None else total + got
        sums.append(total)
    return tops, sums


def attend_tile(q_ref, tile_ref, dist_ref, reach_of, heads, state, geometry):
    high, wide, span, frames, head_dim, factor, step = geometry
    cells = high * wide
    acc_ref, sum_ref, max_ref = state
    for at, head in enumerate(heads):
        cols = slice(head * head_dim, (head + 1) * head_dim)
        outs = slice(at * head_dim, (at + 1) * head_dim)
        starts = range(0, q_ref.shape[0], step)
        units = []
        for start in starts:
            near = dist_ref[start % cells : start % cells + step, : tile_ref.shape[1]]
            piece = (tile_ref[0, :, cols], tile_ref[1, :, cols], near, reach_of(head))
            units.append((q_ref[start : start + step, cols], [piece], None))
        for start, m, got in zip(starts, *attend(units, factor)):
            rows = slice(start, start + step)
            acc_ref[rows, outs] = got[:, :head_dim]
            sum_ref[rows, outs] = got[:, head_dim:]
            max_ref[rows, outs] = jnp.broadcast_to(m, (step, head_dim))


def begin_kernel(radius_ref, mask_ref, q_ref, tile_ref, *outs, geometry, heads):
    *state, dist_ref, reach_ref = outs
    high, wide, span, frames = geometry[:4]
    dist_ref[...] = distances(high, wide, span, frames)
    stretch_at = lax.axis_index("tm")
    line = (1, reach_ref.shape[1])
    for head in range(heads):
        radius = radius_ref[head]
        seen = mask_ref[stretch_at, 0, head] > 0
        reach_ref[head : head + 1] = jnp.full(line, radius, jnp.int32)
        reach_ref[heads + head : heads + head + 1] = jnp.full(
            line, jnp.where(seen, radius, -1), jnp.int32
        )
    attend_tile(q_ref, tile_ref, dist_ref, lambda h: radius_ref[h], (0,), state, geometry)


def tile_kernel(q_ref, tile_ref, dist_ref, reach_ref, *state, geometry, heads):
    attend_tile(
        q_ref,
        tile_ref,
        dist_ref,
        lambda h: reach_ref[h : h + 1, :1],
        range(1, heads),
        state,
        geometry,
    )


def pick_state(head_state, state, head, rows, head_dim):
    refs = head_state if head == 0 else state
    at = max(head - 1, 0) * head_dim
    return [ref[rows, at : at + head_dim] for ref in refs]


def rest_kernel(
    q_ref,
    edge_ref,
    first_tile_ref,
    first_edge_ref,
    *rest,
    geometry,
    heads,
    flips,
):
    head_state, dist_ref, reach_ref, state, outs = rest[:3], rest[3], rest[4], rest[5:8], rest[8:]
    high, wide, span, frames, head_dim, factor, step = geometry
    cells = high * wide
    base = frames * cells
    head_at = lax.axis_index("head")
    stretch_at = lax.axis_index("tm")

    def run(with_first):
        for flip, out_ref in zip(flips, outs):
            start = pl.multiple_of(jnp.bitwise_xor(head_at, flip) * step, step)
            rows = pl.ds(start, step)
            near = dist_ref[pl.ds(pl.multiple_of(lax.rem(start, cells), step), step)]
            beyond = near[:, base:]
            units = []
            olds = []
            for head in range(heads):
                cols = slice(head * head_dim, (head + 1) * head_dim)
                sources = [(edge_ref, beyond, head)]
                if with_first:
                    sources.append((first_tile_ref, near[:, :base], heads + head))
                    sources.append((first_edge_ref, beyond, heads + head))
                pieces = [
                    (ref[0, :, cols], ref[1, :, cols], dist, reach_ref[row : row + 1, :1])
                    for ref, dist, row in sources
                ]
                olds.append(pick_state(head_state, state, head, rows, head_dim))
                units.append((q_ref[rows, cols], pieces, olds[-1][2][:, :1]))
            for head, (m, got) in enumerate(zip(*attend(units, factor))):
                old_acc, old_total, old_max = olds[head]
                shrink = jnp.exp2(old_max - m)
                acc = old_acc * shrink + got[:, :head_dim]
                total = old_total * shrink + got[:, head_dim:]
                cols = slice(head * head_dim, (head + 1) * head_dim)
                out_ref[:, cols] = (acc / total).astype(jnp.bfloat16)

    @pl.when(stretch_at > 0)
    def _():
        run(True)

    @pl.when(stretch_at == 0)
    def _():
        run(False)


def copy_kernel(in_ref, out_ref):
    out_ref[...] = in_ref[...]


def stack_kernel(*refs):
    *parts, out_ref = refs
    tile_at = lax.axis_index("tile")
    for flip, part in enumerate(parts):
        tall = part.shape[0]
        top = pl.multiple_of(jnp.bitwise_xor(tile_at, flip) * tall, 16)
        out_ref[pl.ds(top, tall)] = part[...]


def project_kernel(w_ref, part_ref, own_ref, got_ref, out_ref, *, flip):
    broad = part_ref.shape[1]
    half = jnp.bitwise_xor(lax.axis_index("tm"), flip)
    cols = pl.ds(pl.multiple_of(half * broad, 128), broad)
    total = jnp.dot(own_ref[...], w_ref[:, cols], preferred_element_type=jnp.float32)
    total += jnp.dot(got_ref[...], part_ref[...], preferred_element_type=jnp.float32)
    out_ref[...] = total.astype(out_ref.dtype)


def add_kernel(mine_ref, got_ref, *rest, flip):
    out_ref, sum_ref, sems = rest[-3:]
    pieces, tall, broad = sum_ref.shape
    half = jnp.bitwise_xor(lax.axis_index("tm"), flip)
    cols = pl.ds(pl.multiple_of(half * broad, 128), broad)
    copies = []
    for i in range(pieces):
        rows = slice(i * tall, (i + 1) * tall)
        sum_ref[i] = (mine_ref[rows] + got_ref[rows].astype(jnp.float32)).astype(jnp.bfloat16)
        copies.append(pltpu.make_async_copy(sum_ref.at[i], out_ref.at[rows, cols], sems.at[i]))
        copies[-1].start()
    for copy in copies:
        copy.wait()


def two_by_two(query, keys, values, out_weight, radius, block_mask):
    span = RMAX
    frames, high, wide, channels = query.shape[2:]
    heads = radius.shape[0]
    head_dim = channels // heads
    cells = high * wide
    tokens = frames * cells
    groups = lax.axis_size("head")
    tiles = lax.axis_size("tile")
    depth, width = out_weight.shape
    step = tokens // groups
    geometry = (high, wide, span, frames, head_dim, LOG2E / math.sqrt(head_dim), step)
    count = frames * (cells + span * (wide + high + span))
    smem = pl.BlockSpec(memory_space=pltpu.SMEM)
    vmem = pl.BlockSpec(memory_space=pltpu.VMEM)
    hbm = pl.BlockSpec(memory_space=pltpu.HBM)
    bf16, f32 = jnp.bfloat16, jnp.float32
    shape = jax.ShapeDtypeStruct

    def call(kernel, out_shape, specs, *args, name, scratch=(), flops=0, **keys_of):
        return pl.pallas_call(
            functools.partial(kernel, **keys_of) if keys_of else kernel,
            out_shape=out_shape,
            in_specs=specs,
            out_specs=jax.tree.map(lambda _: vmem, out_shape),
            scratch_shapes=scratch,
            cost_estimate=pl.CostEstimate(flops=flops, bytes_accessed=0, transcendentals=0),
            compiler_params=pltpu.CompilerParams(vmem_limit_bytes=VMEM_LIMIT),
            name=name,
        )(*args)

    def flipped(value, axis, flip):
        return lax.ppermute(value, axis, [(i, i ^ flip) for i in range(lax.axis_size(axis))])

    q = query.reshape(tokens, channels)
    k = keys.reshape(tokens, channels)
    v = values.reshape(tokens, channels)

    tall, broad = depth // tiles, width // 2
    part_shape = shape((tall, broad), bf16)
    part = call(
        part_kernel,
        part_shape,
        [hbm],
        pltpu.with_memory_space_constraint(out_weight, pltpu.HBM),
        name="part",
        scratch=[pltpu.SemaphoreType.DMA],
    )
    *faces, tile = call(
        face_kernel,
        [
            shape((2, frames, span * wide, channels), bf16),
            shape((2, frames, span * high, channels), bf16),
            shape((2, frames, span * span, channels), bf16),
            shape((2, tokens, channels), bf16),
        ],
        [vmem] * 3,
        k,
        v,
        part,
        name="faces",
        geometry=geometry,
    )
    faces = [flipped(face, "tile", flip) for face, flip in zip(faces, (2, 1, 3))]
    lone = flipped(part, "head", 2)
    begun = call(
        begin_kernel,
        [shape((tokens, head_dim), f32)] * 3
        + [shape((cells, count), jnp.int32), shape((2 * heads, head_dim), jnp.int32)],
        [smem] * 2 + [vmem] * 2,
        radius,
        block_mask.transpose(1, 2, 0),
        q,
        tile,
        name="begin",
        geometry=geometry,
        heads=heads,
    )
    begun, tile = lax.optimization_barrier((begun, tile))
    first_tile = lax.ppermute(tile, "tm", [(0, 1)])
    state = call(
        tile_kernel,
        [shape((tokens, channels - head_dim), f32)] * 3,
        [vmem] * 4,
        q,
        tile,
        *begun[3:],
        name="tile",
        geometry=geometry,
        heads=heads,
    )
    lone, state = lax.optimization_barrier((lone, state))
    lone = call(copy_kernel, part_shape, [vmem], lone, name="lone", flops=20 * 10**9)
    lone, state, faces = lax.optimization_barrier((lone, state, faces))
    edge = call(
        edge_kernel, shape((2, count - tokens, channels), bf16), [vmem] * 3, *faces, name="edges"
    )
    first_edge = lax.ppermute(edge, "tm", [(0, 1)])
    parts = [lone] + [flipped(lone, "tile", flip) for flip in range(1, tiles)]

    def rest(state, *flips, flops=0):
        return call(
            rest_kernel,
            [shape((step, channels), bf16)] * len(flips),
            [vmem] * 12,
            q,
            edge,
            first_tile,
            first_edge,
            *begun,
            *state,
            name="rest",
            geometry=geometry,
            heads=heads,
            flips=flips,
            flops=flops,
        )

    (for_side,) = rest(state, 3)
    got_side = flipped(for_side, "head", 2)
    state, for_side = lax.optimization_barrier((state, for_side))
    for_far, own_side = rest(state, 2, 1)
    got_far = flipped(for_far, "head", 2)
    parts, own_side = lax.optimization_barrier((parts, own_side))
    here = call(
        stack_kernel, shape((depth, broad), bf16), [vmem] * tiles, *parts, name="stack"
    )

    def project(part, mine, got, kind, flip, flops=0):
        return call(
            project_kernel,
            shape((step, broad), kind),
            [vmem] * 4,
            out_weight,
            part,
            mine,
            got,
            name="project",
            flops=flops,
            flip=flip,
        )

    for_side = [project(here, own_side, got_side, bf16, 0, 20 * 10**9)]
    from_side = [flipped(for_side[0], "head", 1)]
    state, here, for_side[0] = lax.optimization_barrier((state, here, for_side[0]))
    there = flipped(here, "tm", 1)
    (own,) = rest(state, 0, flops=20 * 10**9)
    own_side, own = lax.optimization_barrier((own_side, own))
    for_side.append(project(there, own_side, got_side, bf16, 1))
    from_side.append(flipped(for_side[1], "head", 1))
    own, for_side[1] = lax.optimization_barrier((own, for_side[1]))
    mine = [
        project(here, own, got_far, f32, 0),
        project(there, own, got_far, f32, 1, 20 * 10**9),
    ]
    pieces = 2
    mixed = []
    for flip in range(2):
        mixed = [
            pl.pallas_call(
                functools.partial(add_kernel, flip=flip),
                out_shape=shape((step, width), bf16),
                in_specs=[vmem] * 2 + [hbm] * flip,
                out_specs=hbm,
                input_output_aliases={2: 0} if flip else {},
                scratch_shapes=[
                    pltpu.VMEM((pieces, step // pieces, broad), bf16),
                    pltpu.SemaphoreType.DMA((pieces,)),
                ],
                compiler_params=pltpu.CompilerParams(vmem_limit_bytes=VMEM_LIMIT),
                name="add",
            )(mine[flip], from_side[flip], *mixed)
        ]
    (mixed,) = mixed
    return mixed.reshape(1, 1, step, width)


def solution(mesh):
    in_specs = (
        P("tm", "tile", None, None, None, "head"),
        P("tm", "tile", None, None, None, "head"),
        P("tm", "tile", None, None, None, "head"),
        P("head", None),
        P("head"),
        P("head", None, None),
    )
    out_specs = P("tm", "tile", "head", None)
    small = dict(mesh.shape) == {"tm": 2, "tile": 4, "head": 4}
    return jax.shard_map(
        two_by_two if small else any_grid,
        mesh=mesh,
        in_specs=in_specs,
        out_specs=out_specs,
        check_vma=False,
    )
```

```python
import functools
import math

import jax
import jax.numpy as jnp
from jax import lax
from jax.experimental import pallas as pl
from jax.experimental.pallas import tpu as pltpu
from jax.sharding import PartitionSpec as P

RMAX = 4
FAR = -1e30
LOG2E = 1.4426950408889634
VMEM_LIMIT = 24 * 1024 * 1024


def passed_along(value, axis, by):
    peers = lax.axis_size(axis)
    pairs = [(i, i + by) for i in range(peers) if 0 <= i + by < peers]
    return lax.ppermute(value, axis, pairs)


def widen(key_part, value_part, span, row_move, col_move):
    grid = math.isqrt(lax.axis_size("tile"))
    above = None
    below = None
    for offset in (grid, -grid):
        if offset > 0:
            face_key = key_part[:, :, key_part.shape[2] - span :]
            face_value = value_part[:, :, value_part.shape[2] - span :]
        else:
            face_key = key_part[:, :, :span]
            face_value = value_part[:, :, :span]
        got = row_move(face_key, face_value, offset)
        if offset > 0:
            above = got
        else:
            below = got
    key_rows = jnp.concatenate([above[0], key_part, below[0]], axis=2)
    value_rows = jnp.concatenate([above[1], value_part, below[1]], axis=2)
    left = None
    right = None
    for offset in (1, -1):
        if offset > 0:
            face_key = key_rows[:, :, :, key_rows.shape[3] - span :]
            face_value = value_rows[:, :, :, value_rows.shape[3] - span :]
        else:
            face_key = key_rows[:, :, :, :span]
            face_value = value_rows[:, :, :, :span]
        got = col_move(face_key, face_value, offset)
        if offset > 0:
            left = got
        else:
            right = got
    key_full = jnp.concatenate([left[0], key_rows, right[0]], axis=3)
    value_full = jnp.concatenate([left[1], value_rows, right[1]], axis=3)
    return (key_full, value_full)


def windows_of(block, half_high, half_wide, win_high, win_wide, heads_here, head_dim):
    parts = []
    for band in (0, 1):
        for strip in (0, 1):
            parts.append(
                block[
                    :,
                    band * half_high : band * half_high + win_high,
                    strip * half_wide : strip * half_wide + win_wide,
                ]
            )
    stacked = jnp.stack(parts)
    return stacked.reshape(4, -1, heads_here, head_dim)


def any_grid(query, keys, values, out_weight, radius, block_mask):
    span = RMAX
    grid = math.isqrt(lax.axis_size("tile"))
    tile_at = lax.axis_index("tile")
    row_at = tile_at // grid
    col_at = tile_at % grid
    stretch_at = lax.axis_index("tm")
    frames, high, wide, channels = query.shape[2:]
    heads_here = radius.shape[0]
    head_dim = channels // heads_here
    tokens_here = frames * high * wide
    half_high = high // 2
    half_wide = wide // 2
    win_high = half_high + 2 * span
    win_wide = half_wide + 2 * span
    quarter = frames * half_high * half_wide
    queries = query[0, 0].reshape(frames, 2, half_high, 2, half_wide, channels)
    queries = queries.transpose(1, 3, 0, 2, 4, 5).reshape(4, quarter, heads_here, head_dim)
    query_y = jnp.broadcast_to(
        jnp.arange(half_high, dtype=jnp.int32)[None, :, None], (frames, half_high, half_wide)
    ).reshape(-1)
    query_x = jnp.broadcast_to(
        jnp.arange(half_wide, dtype=jnp.int32)[None, None, :], (frames, half_high, half_wide)
    ).reshape(-1)
    key_y = jnp.broadcast_to(
        jnp.arange(win_high, dtype=jnp.int32)[None, :, None] - span, (frames, win_high, win_wide)
    ).reshape(-1)
    key_x = jnp.broadcast_to(
        jnp.arange(win_wide, dtype=jnp.int32)[None, None, :] - span, (frames, win_high, win_wide)
    ).reshape(-1)
    band_at = jnp.array([0, 0, 1, 1], dtype=jnp.int32)
    strip_at = jnp.array([0, 1, 0, 1], dtype=jnp.int32)
    global_y = row_at * high + band_at[:, None] * half_high + key_y[None, :]
    global_x = col_at * wide + strip_at[:, None] * half_wide + key_x[None, :]
    inside = (global_y >= 0) & (global_y < grid * high) & (global_x >= 0) & (global_x < grid * wide)
    distance = jnp.maximum(
        jnp.abs(query_y[:, None] - key_y[None, :]), jnp.abs(query_x[:, None] - key_x[None, :])
    )
    near = distance[None, :, :] <= radius[:, None, None]
    allowed = near[None, :, :, :] & inside[:, None, None, :]
    scale = 1.0 / math.sqrt(head_dim)
    initial = (
        jnp.full((4, heads_here, quarter), -1e30, jnp.float32),
        jnp.zeros((4, heads_here, quarter), jnp.float32),
        jnp.zeros((4, heads_here, quarter, head_dim), jnp.float32),
    )

    def tile_move(face_key, face_value, offset):
        return passed_along((face_key, face_value), "tile", offset)

    key_all, value_all = (
        lax.all_gather(keys[0], "tm", axis=0, tiled=True),
        lax.all_gather(values[0], "tm", axis=0, tiled=True),
    )
    key_full, value_full = widen(key_all, value_all, span, tile_move, tile_move)
    stretch_ids = jnp.arange(key_full.shape[0], dtype=jnp.int32)

    def one_stretch(state, item):
        key_block, value_block, stretch_id = item
        visible = (
            lax.dynamic_slice_in_dim(
                lax.dynamic_index_in_dim(block_mask, stretch_at, 1, False), stretch_id, 1, 1
            )[:, 0]
            > 0
        )
        best, total, acc = state
        key_win = windows_of(
            key_block, half_high, half_wide, win_high, win_wide, heads_here, head_dim
        )
        value_win = windows_of(
            value_block, half_high, half_wide, win_high, win_wide, heads_here, head_dim
        )
        usable = allowed & visible[None, :, None, None]
        scores = (
            jnp.einsum("nqhd,nkhd->nhqk", queries, key_win, preferred_element_type=jnp.float32)
            * scale
        )
        masked = jnp.where(usable, scores, jnp.float32(-1e30))
        fresh = jnp.maximum(best, jnp.max(masked, axis=3))
        probs = jnp.where(usable, jnp.exp(scores - fresh[..., None]), jnp.float32(0.0))
        shrink = jnp.exp(best - fresh)
        total = total * shrink + jnp.sum(probs, axis=3)
        acc = acc * shrink[..., None] + jnp.einsum(
            "nhqk,nkhd->nhqd",
            probs.astype(jnp.bfloat16),
            value_win,
            preferred_element_type=jnp.float32,
        )
        return ((fresh, total, acc), None)

    final, unused = lax.scan(one_stretch, initial, (key_full, value_full, stretch_ids))
    best, total, acc = final
    attn = (acc / total[..., None]).astype(jnp.bfloat16)
    attn = attn.transpose(0, 2, 1, 3).reshape(
        2, 2, frames, half_high, half_wide, heads_here * head_dim
    )
    attn = attn.transpose(2, 0, 3, 1, 4, 5).reshape(tokens_here, heads_here * head_dim)
    mixed = lax.psum_scatter(
        jnp.dot(attn, out_weight, preferred_element_type=jnp.float32).astype(jnp.bfloat16),
        "head",
        scatter_dimension=0,
        tiled=True,
    )
    return mixed.reshape(1, 1, -1, out_weight.shape[1])


def tile_place():
    tile_at = lax.axis_index("tile")
    return tile_at // 2, tile_at % 2


def part_kernel(w_ref, part_ref, sem):
    tall, broad = part_ref.shape
    top = pl.multiple_of(lax.axis_index("tile") * tall, 16)
    left = pl.multiple_of(lax.axis_index("tm") * broad, 128)
    copy = pltpu.make_async_copy(w_ref.at[pl.ds(top, tall), pl.ds(left, broad)], part_ref, sem)
    copy.start()
    copy.wait()


def face_kernel(k_ref, v_ref, part_ref, row_ref, col_ref, corner_ref, tile_ref, *, geometry):
    high, wide, span, frames = geometry[:4]
    cells = high * wide
    row_at, col_at = tile_place()
    y0 = jnp.where(row_at == 0, high - span, 0)
    x0 = jnp.where(col_at == 0, wide - span, 0)

    def picker(count, cell_of):
        row = lax.broadcasted_iota(jnp.int32, (count, cells), 0)
        col = lax.broadcasted_iota(jnp.int32, (count, cells), 1)
        return (col == cell_of(row)).astype(jnp.bfloat16)

    beside = picker(high * span, lambda i: (i // span) * wide + x0 + i % span)
    across = picker(span * span, lambda i: (y0 + i // span) * wide + x0 + i % span)
    for which, ref in enumerate((k_ref, v_ref)):
        tile_ref[which] = ref[...]
        for f in range(frames):
            start = pl.multiple_of(f * cells + y0 * wide, 16)
            row_ref[which, f] = ref[pl.ds(start, span * wide)]
            whole = ref[f * cells : (f + 1) * cells]
            col_ref[which, f] = jnp.dot(
                beside, whole, preferred_element_type=jnp.float32
            ).astype(jnp.bfloat16)
            corner_ref[which, f] = jnp.dot(
                across, whole, preferred_element_type=jnp.float32
            ).astype(jnp.bfloat16)


def edge_kernel(row_ref, col_ref, corner_ref, out_ref):
    for which in range(2):
        at = 0
        for part in (row_ref, col_ref, corner_ref):
            for f in range(part.shape[1]):
                size = part.shape[2]
                out_ref[which, at : at + size] = part[which, f]
                at += size


def distances(high, wide, span, frames):
    row_at, col_at = tile_place()
    cells = high * wide
    count = frames * (cells + span * (wide + high + span))
    j = lax.broadcasted_iota(jnp.int32, (1, count), 1)
    y_off = jnp.where(row_at == 0, high, -span)
    x_off = jnp.where(col_at == 0, wide, -span)
    c = j % cells
    ky, kx = c // wide, c % wide
    base = frames * cells
    c = (j - base) % (span * wide)
    ky = jnp.where(j >= base, y_off + c // wide, ky)
    kx = jnp.where(j >= base, c % wide, kx)
    base += frames * span * wide
    c = (j - base) % (span * high)
    ky = jnp.where(j >= base, c // span, ky)
    kx = jnp.where(j >= base, x_off + c % span, kx)
    base += frames * span * high
    c = (j - base) % (span * span)
    ky = jnp.where(j >= base, y_off + c // span, ky)
    kx = jnp.where(j >= base, x_off + c % span, kx)
    i = lax.broadcasted_iota(jnp.int32, (cells, 1), 0)
    return jnp.maximum(jnp.abs(i // wide - ky), jnp.abs(i % wide - kx))


def attend(units, factor):
    scores = [
        [
            jnp.where(
                dist <= reach,
                lax.dot_general(
                    q, k, (((1,), (1,)), ((), ())), preferred_element_type=jnp.float32
                )
                * factor,
                FAR,
            )
            for k, v, dist, reach in pieces
        ]
        for q, pieces, before in units
    ]
    tops = []
    for parts, (q, pieces, before) in zip(scores, units):
        found = [jnp.max(s, axis=1, keepdims=True) for s in parts]
        if before is not None:
            found.append(before)
        tops.append(functools.reduce(jnp.maximum, found))
    probs = [
        [jnp.exp2(s - m).astype(jnp.bfloat16) for s in parts] for parts, m in zip(scores, tops)
    ]
    sums = []
    for parts, (q, pieces, before) in zip(probs, units):
        total = None
        for p, (k, v, dist, reach) in zip(parts, pieces):
            both = jnp.concatenate([v, jnp.ones_like(v)], axis=1)
            got = jnp.dot(p, both, preferred_element_type=jnp.float32)
            total = got if total is None else total + got
        sums.append(total)
    return tops, sums


def attend_tile(q_ref, tile_ref, dist_ref, reach_of, heads, state, geometry):
    high, wide, span, frames, head_dim, factor, step = geometry
    cells = high * wide
    acc_ref, sum_ref, max_ref = state
    for at, head in enumerate(heads):
        cols = slice(head * head_dim, (head + 1) * head_dim)
        outs = slice(at * head_dim, (at + 1) * head_dim)
        starts = range(0, q_ref.shape[0], step)
        units = []
        for start in starts:
            near = dist_ref[start % cells : start % cells + step, : tile_ref.shape[1]]
            piece = (tile_ref[0, :, cols], tile_ref[1, :, cols], near, reach_of(head))
            units.append((q_ref[start : start + step, cols], [piece], None))
        for start, m, got in zip(starts, *attend(units, factor)):
            rows = slice(start, start + step)
            acc_ref[rows, outs] = got[:, :head_dim]
            sum_ref[rows, outs] = got[:, head_dim:]
            max_ref[rows, outs] = jnp.broadcast_to(m, (step, head_dim))


def begin_kernel(radius_ref, mask_ref, q_ref, tile_ref, *outs, geometry, heads):
    *state, dist_ref, reach_ref = outs
    high, wide, span, frames = geometry[:4]
    dist_ref[...] = distances(high, wide, span, frames)
    stretch_at = lax.axis_index("tm")
    line = (1, reach_ref.shape[1])
    for head in range(heads):
        radius = radius_ref[head]
        seen = mask_ref[stretch_at, 0, head] > 0
        reach_ref[head : head + 1] = jnp.full(line, radius, jnp.int32)
        reach_ref[heads + head : heads + head + 1] = jnp.full(
            line, jnp.where(seen, radius, -1), jnp.int32
        )
    attend_tile(q_ref, tile_ref, dist_ref, lambda h: radius_ref[h], (0,), state, geometry)


def tile_kernel(q_ref, tile_ref, dist_ref, reach_ref, *state, geometry, heads):
    attend_tile(
        q_ref,
        tile_ref,
        dist_ref,
        lambda h: reach_ref[h : h + 1, :1],
        range(1, heads),
        state,
        geometry,
    )


def pick_state(head_state, state, head, rows, head_dim):
    refs = head_state if head == 0 else state
    at = max(head - 1, 0) * head_dim
    return [ref[rows, at : at + head_dim] for ref in refs]


def rest_kernel(
    q_ref,
    edge_ref,
    first_tile_ref,
    first_edge_ref,
    *rest,
    geometry,
    heads,
    flips,
):
    head_state, dist_ref, reach_ref, state, outs = rest[:3], rest[3], rest[4], rest[5:8], rest[8:]
    high, wide, span, frames, head_dim, factor, step = geometry
    cells = high * wide
    base = frames * cells
    head_at = lax.axis_index("head")
    stretch_at = lax.axis_index("tm")

    def run(with_first):
        for flip, out_ref in zip(flips, outs):
            start = pl.multiple_of(jnp.bitwise_xor(head_at, flip) * step, step)
            rows = pl.ds(start, step)
            near = dist_ref[pl.ds(pl.multiple_of(lax.rem(start, cells), step), step)]
            beyond = near[:, base:]
            units = []
            olds = []
            for head in range(heads):
                cols = slice(head * head_dim, (head + 1) * head_dim)
                sources = [(edge_ref, beyond, head)]
                if with_first:
                    sources.append((first_tile_ref, near[:, :base], heads + head))
                    sources.append((first_edge_ref, beyond, heads + head))
                pieces = [
                    (ref[0, :, cols], ref[1, :, cols], dist, reach_ref[row : row + 1, :1])
                    for ref, dist, row in sources
                ]
                olds.append(pick_state(head_state, state, head, rows, head_dim))
                units.append((q_ref[rows, cols], pieces, olds[-1][2][:, :1]))
            for head, (m, got) in enumerate(zip(*attend(units, factor))):
                old_acc, old_total, old_max = olds[head]
                shrink = jnp.exp2(old_max - m)
                acc = old_acc * shrink + got[:, :head_dim]
                total = old_total * shrink + got[:, head_dim:]
                cols = slice(head * head_dim, (head + 1) * head_dim)
                out_ref[:, cols] = (acc / total).astype(jnp.bfloat16)

    @pl.when(stretch_at > 0)
    def _():
        run(True)

    @pl.when(stretch_at == 0)
    def _():
        run(False)


def copy_kernel(in_ref, out_ref):
    out_ref[...] = in_ref[...]


def stack_kernel(*refs):
    *parts, out_ref = refs
    tile_at = lax.axis_index("tile")
    for flip, part in enumerate(parts):
        tall = part.shape[0]
        top = pl.multiple_of(jnp.bitwise_xor(tile_at, flip) * tall, 16)
        out_ref[pl.ds(top, tall)] = part[...]


def project_kernel(w_ref, part_ref, own_ref, got_ref, out_ref, *, flip):
    broad = part_ref.shape[1]
    half = jnp.bitwise_xor(lax.axis_index("tm"), flip)
    cols = pl.ds(pl.multiple_of(half * broad, 128), broad)
    total = jnp.dot(own_ref[...], w_ref[:, cols], preferred_element_type=jnp.float32)
    total += jnp.dot(got_ref[...], part_ref[...], preferred_element_type=jnp.float32)
    out_ref[...] = total.astype(out_ref.dtype)


def add_kernel(mine_ref, got_ref, *rest, flip):
    out_ref, sum_ref, sems = rest[-3:]
    pieces, tall, broad = sum_ref.shape
    half = jnp.bitwise_xor(lax.axis_index("tm"), flip)
    cols = pl.ds(pl.multiple_of(half * broad, 128), broad)
    copies = []
    for i in range(pieces):
        rows = slice(i * tall, (i + 1) * tall)
        sum_ref[i] = (mine_ref[rows] + got_ref[rows].astype(jnp.float32)).astype(jnp.bfloat16)
        copies.append(pltpu.make_async_copy(sum_ref.at[i], out_ref.at[rows, cols], sems.at[i]))
        copies[-1].start()
    for copy in copies:
        copy.wait()


def two_by_two(query, keys, values, out_weight, radius, block_mask):
    span = RMAX
    frames, high, wide, channels = query.shape[2:]
    heads = radius.shape[0]
    head_dim = channels // heads
    cells = high * wide
    tokens = frames * cells
    groups = lax.axis_size("head")
    tiles = lax.axis_size("tile")
    depth, width = out_weight.shape
    step = tokens // groups
    geometry = (high, wide, span, frames, head_dim, LOG2E / math.sqrt(head_dim), step)
    count = frames * (cells + span * (wide + high + span))
    smem = pl.BlockSpec(memory_space=pltpu.SMEM)
    vmem = pl.BlockSpec(memory_space=pltpu.VMEM)
    hbm = pl.BlockSpec(memory_space=pltpu.HBM)
    bf16, f32 = jnp.bfloat16, jnp.float32
    shape = jax.ShapeDtypeStruct

    def call(kernel, out_shape, specs, *args, name, scratch=(), flops=0, **keys_of):
        return pl.pallas_call(
            functools.partial(kernel, **keys_of) if keys_of else kernel,
            out_shape=out_shape,
            in_specs=specs,
            out_specs=jax.tree.map(lambda _: vmem, out_shape),
            scratch_shapes=scratch,
            cost_estimate=pl.CostEstimate(flops=flops, bytes_accessed=0, transcendentals=0),
            compiler_params=pltpu.CompilerParams(vmem_limit_bytes=VMEM_LIMIT),
            name=name,
        )(*args)

    def flipped(value, axis, flip):
        return lax.ppermute(value, axis, [(i, i ^ flip) for i in range(lax.axis_size(axis))])

    q = query.reshape(tokens, channels)
    k = keys.reshape(tokens, channels)
    v = values.reshape(tokens, channels)

    tall, broad = depth // tiles, width // 2
    part_shape = shape((tall, broad), bf16)
    part = call(
        part_kernel,
        part_shape,
        [hbm],
        pltpu.with_memory_space_constraint(out_weight, pltpu.HBM),
        name="part",
        scratch=[pltpu.SemaphoreType.DMA],
    )
    *faces, tile = call(
        face_kernel,
        [
            shape((2, frames, span * wide, channels), bf16),
            shape((2, frames, span * high, channels), bf16),
            shape((2, frames, span * span, channels), bf16),
            shape((2, tokens, channels), bf16),
        ],
        [vmem] * 3,
        k,
        v,
        part,
        name="faces",
        geometry=geometry,
    )
    faces = [flipped(face, "tile", flip) for face, flip in zip(faces, (2, 1, 3))]
    lone = flipped(part, "head", 2)
    begun = call(
        begin_kernel,
        [shape((tokens, head_dim), f32)] * 3
        + [shape((cells, count), jnp.int32), shape((2 * heads, head_dim), jnp.int32)],
        [smem] * 2 + [vmem] * 2,
        radius,
        block_mask.transpose(1, 2, 0),
        q,
        tile,
        name="begin",
        geometry=geometry,
        heads=heads,
    )
    begun, tile = lax.optimization_barrier((begun, tile))
    first_tile = lax.ppermute(tile, "tm", [(0, 1)])
    state = call(
        tile_kernel,
        [shape((tokens, channels - head_dim), f32)] * 3,
        [vmem] * 4,
        q,
        tile,
        *begun[3:],
        name="tile",
        geometry=geometry,
        heads=heads,
    )
    lone, state = lax.optimization_barrier((lone, state))
    lone = call(copy_kernel, part_shape, [vmem], lone, name="lone", flops=20 * 10**9)
    lone, state, faces = lax.optimization_barrier((lone, state, faces))
    edge = call(
        edge_kernel, shape((2, count - tokens, channels), bf16), [vmem] * 3, *faces, name="edges"
    )
    first_edge = lax.ppermute(edge, "tm", [(0, 1)])
    late = 1
    parts = [flipped(lone, "tile", flip) if flip != late else None for flip in range(1, tiles)]

    def rest(state, *flips, flops=0):
        return call(
            rest_kernel,
            [shape((step, channels), bf16)] * len(flips),
            [vmem] * 12,
            q,
            edge,
            first_tile,
            first_edge,
            *begun,
            *state,
            name="rest",
            geometry=geometry,
            heads=heads,
            flips=flips,
            flops=flops,
        )

    (for_side,) = rest(state, 3)
    got_side = flipped(for_side, "head", 2)
    state, lone, for_side = lax.optimization_barrier((state, lone, for_side))
    parts[late - 1] = flipped(lone, "tile", late)
    parts = [lone] + parts
    for_far, own_side = rest(state, 2, 1)
    got_far = flipped(for_far, "head", 2)
    parts, own_side = lax.optimization_barrier((parts, own_side))
    here = call(
        stack_kernel, shape((depth, broad), bf16), [vmem] * tiles, *parts, name="stack"
    )

    def project(part, mine, got, kind, flip, flops=0):
        return call(
            project_kernel,
            shape((step, broad), kind),
            [vmem] * 4,
            out_weight,
            part,
            mine,
            got,
            name="project",
            flops=flops,
            flip=flip,
        )

    for_side = [project(here, own_side, got_side, bf16, 0, 20 * 10**9)]
    from_side = [flipped(for_side[0], "head", 1)]
    state, here, for_side[0] = lax.optimization_barrier((state, here, for_side[0]))
    there = flipped(here, "tm", 1)
    (own,) = rest(state, 0, flops=20 * 10**9)
    own_side, own = lax.optimization_barrier((own_side, own))
    for_side.append(project(there, own_side, got_side, bf16, 1))
    from_side.append(flipped(for_side[1], "head", 1))
    own, for_side[1] = lax.optimization_barrier((own, for_side[1]))
    mine = [
        project(here, own, got_far, f32, 0),
        project(there, own, got_far, f32, 1, 20 * 10**9),
    ]
    pieces = 2
    mixed = []
    for flip in range(2):
        mixed = [
            pl.pallas_call(
                functools.partial(add_kernel, flip=flip),
                out_shape=shape((step, width), bf16),
                in_specs=[vmem] * 2 + [hbm] * flip,
                out_specs=hbm,
                input_output_aliases={2: 0} if flip else {},
                scratch_shapes=[
                    pltpu.VMEM((pieces, step // pieces, broad), bf16),
                    pltpu.SemaphoreType.DMA((pieces,)),
                ],
                compiler_params=pltpu.CompilerParams(vmem_limit_bytes=VMEM_LIMIT),
                name="add",
            )(mine[flip], from_side[flip], *mixed)
        ]
    (mixed,) = mixed
    return mixed.reshape(1, 1, step, width)


def solution(mesh):
    in_specs = (
        P("tm", "tile", None, None, None, "head"),
        P("tm", "tile", None, None, None, "head"),
        P("tm", "tile", None, None, None, "head"),
        P("head", None),
        P("head"),
        P("head", None, None),
    )
    out_specs = P("tm", "tile", "head", None)
    small = dict(mesh.shape) == {"tm": 2, "tile": 4, "head": 4}
    return jax.shard_map(
        two_by_two if small else any_grid,
        mesh=mesh,
        in_specs=in_specs,
        out_specs=out_specs,
        check_vma=False,
    )
```

```python
import functools
import math

import jax
import jax.numpy as jnp
from jax import lax
from jax.experimental import pallas as pl
from jax.experimental.pallas import tpu as pltpu
from jax.sharding import PartitionSpec as P

RMAX = 4
FAR = -1e30
LOG2E = 1.4426950408889634
VMEM_LIMIT = 24 * 1024 * 1024


def passed_along(value, axis, by):
    peers = lax.axis_size(axis)
    pairs = [(i, i + by) for i in range(peers) if 0 <= i + by < peers]
    return lax.ppermute(value, axis, pairs)


def widen(key_part, value_part, span, row_move, col_move):
    grid = math.isqrt(lax.axis_size("tile"))
    above = None
    below = None
    for offset in (grid, -grid):
        if offset > 0:
            face_key = key_part[:, :, key_part.shape[2] - span :]
            face_value = value_part[:, :, value_part.shape[2] - span :]
        else:
            face_key = key_part[:, :, :span]
            face_value = value_part[:, :, :span]
        got = row_move(face_key, face_value, offset)
        if offset > 0:
            above = got
        else:
            below = got
    key_rows = jnp.concatenate([above[0], key_part, below[0]], axis=2)
    value_rows = jnp.concatenate([above[1], value_part, below[1]], axis=2)
    left = None
    right = None
    for offset in (1, -1):
        if offset > 0:
            face_key = key_rows[:, :, :, key_rows.shape[3] - span :]
            face_value = value_rows[:, :, :, value_rows.shape[3] - span :]
        else:
            face_key = key_rows[:, :, :, :span]
            face_value = value_rows[:, :, :, :span]
        got = col_move(face_key, face_value, offset)
        if offset > 0:
            left = got
        else:
            right = got
    key_full = jnp.concatenate([left[0], key_rows, right[0]], axis=3)
    value_full = jnp.concatenate([left[1], value_rows, right[1]], axis=3)
    return (key_full, value_full)


def windows_of(block, half_high, half_wide, win_high, win_wide, heads_here, head_dim):
    parts = []
    for band in (0, 1):
        for strip in (0, 1):
            parts.append(
                block[
                    :,
                    band * half_high : band * half_high + win_high,
                    strip * half_wide : strip * half_wide + win_wide,
                ]
            )
    stacked = jnp.stack(parts)
    return stacked.reshape(4, -1, heads_here, head_dim)


def any_grid(query, keys, values, out_weight, radius, block_mask):
    span = RMAX
    grid = math.isqrt(lax.axis_size("tile"))
    tile_at = lax.axis_index("tile")
    row_at = tile_at // grid
    col_at = tile_at % grid
    stretch_at = lax.axis_index("tm")
    frames, high, wide, channels = query.shape[2:]
    heads_here = radius.shape[0]
    head_dim = channels // heads_here
    tokens_here = frames * high * wide
    half_high = high // 2
    half_wide = wide // 2
    win_high = half_high + 2 * span
    win_wide = half_wide + 2 * span
    quarter = frames * half_high * half_wide
    queries = query[0, 0].reshape(frames, 2, half_high, 2, half_wide, channels)
    queries = queries.transpose(1, 3, 0, 2, 4, 5).reshape(4, quarter, heads_here, head_dim)
    query_y = jnp.broadcast_to(
        jnp.arange(half_high, dtype=jnp.int32)[None, :, None], (frames, half_high, half_wide)
    ).reshape(-1)
    query_x = jnp.broadcast_to(
        jnp.arange(half_wide, dtype=jnp.int32)[None, None, :], (frames, half_high, half_wide)
    ).reshape(-1)
    key_y = jnp.broadcast_to(
        jnp.arange(win_high, dtype=jnp.int32)[None, :, None] - span, (frames, win_high, win_wide)
    ).reshape(-1)
    key_x = jnp.broadcast_to(
        jnp.arange(win_wide, dtype=jnp.int32)[None, None, :] - span, (frames, win_high, win_wide)
    ).reshape(-1)
    band_at = jnp.array([0, 0, 1, 1], dtype=jnp.int32)
    strip_at = jnp.array([0, 1, 0, 1], dtype=jnp.int32)
    global_y = row_at * high + band_at[:, None] * half_high + key_y[None, :]
    global_x = col_at * wide + strip_at[:, None] * half_wide + key_x[None, :]
    inside = (global_y >= 0) & (global_y < grid * high) & (global_x >= 0) & (global_x < grid * wide)
    distance = jnp.maximum(
        jnp.abs(query_y[:, None] - key_y[None, :]), jnp.abs(query_x[:, None] - key_x[None, :])
    )
    near = distance[None, :, :] <= radius[:, None, None]
    allowed = near[None, :, :, :] & inside[:, None, None, :]
    scale = 1.0 / math.sqrt(head_dim)
    initial = (
        jnp.full((4, heads_here, quarter), -1e30, jnp.float32),
        jnp.zeros((4, heads_here, quarter), jnp.float32),
        jnp.zeros((4, heads_here, quarter, head_dim), jnp.float32),
    )

    def tile_move(face_key, face_value, offset):
        return passed_along((face_key, face_value), "tile", offset)

    key_all, value_all = (
        lax.all_gather(keys[0], "tm", axis=0, tiled=True),
        lax.all_gather(values[0], "tm", axis=0, tiled=True),
    )
    key_full, value_full = widen(key_all, value_all, span, tile_move, tile_move)
    stretch_ids = jnp.arange(key_full.shape[0], dtype=jnp.int32)

    def one_stretch(state, item):
        key_block, value_block, stretch_id = item
        visible = (
            lax.dynamic_slice_in_dim(
                lax.dynamic_index_in_dim(block_mask, stretch_at, 1, False), stretch_id, 1, 1
            )[:, 0]
            > 0
        )
        best, total, acc = state
        key_win = windows_of(
            key_block, half_high, half_wide, win_high, win_wide, heads_here, head_dim
        )
        value_win = windows_of(
            value_block, half_high, half_wide, win_high, win_wide, heads_here, head_dim
        )
        usable = allowed & visible[None, :, None, None]
        scores = (
            jnp.einsum("nqhd,nkhd->nhqk", queries, key_win, preferred_element_type=jnp.float32)
            * scale
        )
        masked = jnp.where(usable, scores, jnp.float32(-1e30))
        fresh = jnp.maximum(best, jnp.max(masked, axis=3))
        probs = jnp.where(usable, jnp.exp(scores - fresh[..., None]), jnp.float32(0.0))
        shrink = jnp.exp(best - fresh)
        total = total * shrink + jnp.sum(probs, axis=3)
        acc = acc * shrink[..., None] + jnp.einsum(
            "nhqk,nkhd->nhqd",
            probs.astype(jnp.bfloat16),
            value_win,
            preferred_element_type=jnp.float32,
        )
        return ((fresh, total, acc), None)

    final, unused = lax.scan(one_stretch, initial, (key_full, value_full, stretch_ids))
    best, total, acc = final
    attn = (acc / total[..., None]).astype(jnp.bfloat16)
    attn = attn.transpose(0, 2, 1, 3).reshape(
        2, 2, frames, half_high, half_wide, heads_here * head_dim
    )
    attn = attn.transpose(2, 0, 3, 1, 4, 5).reshape(tokens_here, heads_here * head_dim)
    mixed = lax.psum_scatter(
        jnp.dot(attn, out_weight, preferred_element_type=jnp.float32).astype(jnp.bfloat16),
        "head",
        scatter_dimension=0,
        tiled=True,
    )
    return mixed.reshape(1, 1, -1, out_weight.shape[1])


def tile_place():
    tile_at = lax.axis_index("tile")
    return tile_at // 2, tile_at % 2


def part_kernel(w_ref, part_ref, sem):
    tall, broad = part_ref.shape
    top = pl.multiple_of(lax.axis_index("tile") * tall, 16)
    left = pl.multiple_of(lax.axis_index("tm") * broad, 128)
    copy = pltpu.make_async_copy(w_ref.at[pl.ds(top, tall), pl.ds(left, broad)], part_ref, sem)
    copy.start()
    copy.wait()


def face_kernel(k_ref, v_ref, part_ref, row_ref, col_ref, corner_ref, tile_ref, *, geometry):
    high, wide, span, frames = geometry[:4]
    cells = high * wide
    row_at, col_at = tile_place()
    y0 = jnp.where(row_at == 0, high - span, 0)
    x0 = jnp.where(col_at == 0, wide - span, 0)

    def picker(count, cell_of):
        row = lax.broadcasted_iota(jnp.int32, (count, cells), 0)
        col = lax.broadcasted_iota(jnp.int32, (count, cells), 1)
        return (col == cell_of(row)).astype(jnp.bfloat16)

    beside = picker(high * span, lambda i: (i // span) * wide + x0 + i % span)
    across = picker(span * span, lambda i: (y0 + i // span) * wide + x0 + i % span)
    for which, ref in enumerate((k_ref, v_ref)):
        tile_ref[which] = ref[...]
        for f in range(frames):
            start = pl.multiple_of(f * cells + y0 * wide, 16)
            row_ref[which, f] = ref[pl.ds(start, span * wide)]
            whole = ref[f * cells : (f + 1) * cells]
            col_ref[which, f] = jnp.dot(
                beside, whole, preferred_element_type=jnp.float32
            ).astype(jnp.bfloat16)
            corner_ref[which, f] = jnp.dot(
                across, whole, preferred_element_type=jnp.float32
            ).astype(jnp.bfloat16)


def edge_kernel(row_ref, col_ref, corner_ref, out_ref):
    for which in range(2):
        at = 0
        for part in (row_ref, col_ref, corner_ref):
            for f in range(part.shape[1]):
                size = part.shape[2]
                out_ref[which, at : at + size] = part[which, f]
                at += size


def distances(high, wide, span, frames):
    row_at, col_at = tile_place()
    cells = high * wide
    count = frames * (cells + span * (wide + high + span))
    j = lax.broadcasted_iota(jnp.int32, (1, count), 1)
    y_off = jnp.where(row_at == 0, high, -span)
    x_off = jnp.where(col_at == 0, wide, -span)
    c = j % cells
    ky, kx = c // wide, c % wide
    base = frames * cells
    c = (j - base) % (span * wide)
    ky = jnp.where(j >= base, y_off + c // wide, ky)
    kx = jnp.where(j >= base, c % wide, kx)
    base += frames * span * wide
    c = (j - base) % (span * high)
    ky = jnp.where(j >= base, c // span, ky)
    kx = jnp.where(j >= base, x_off + c % span, kx)
    base += frames * span * high
    c = (j - base) % (span * span)
    ky = jnp.where(j >= base, y_off + c // span, ky)
    kx = jnp.where(j >= base, x_off + c % span, kx)
    i = lax.broadcasted_iota(jnp.int32, (cells, 1), 0)
    return jnp.maximum(jnp.abs(i // wide - ky), jnp.abs(i % wide - kx))


def attend(units, factor):
    scores = [
        [
            jnp.where(
                dist <= reach,
                lax.dot_general(
                    q, k, (((1,), (1,)), ((), ())), preferred_element_type=jnp.float32
                )
                * factor,
                FAR,
            )
            for k, v, dist, reach in pieces
        ]
        for q, pieces, before in units
    ]
    tops = []
    for parts, (q, pieces, before) in zip(scores, units):
        found = [jnp.max(s, axis=1, keepdims=True) for s in parts]
        if before is not None:
            found.append(before)
        tops.append(functools.reduce(jnp.maximum, found))
    probs = [
        [jnp.exp2(s - m).astype(jnp.bfloat16) for s in parts] for parts, m in zip(scores, tops)
    ]
    sums = []
    for parts, (q, pieces, before) in zip(probs, units):
        total = None
        for p, (k, v, dist, reach) in zip(parts, pieces):
            both = jnp.concatenate([v, jnp.ones_like(v)], axis=1)
            got = jnp.dot(p, both, preferred_element_type=jnp.float32)
            total = got if total is None else total + got
        sums.append(total)
    return tops, sums


def attend_tile(q_ref, tile_ref, dist_ref, reach_of, heads, state, geometry):
    high, wide, span, frames, head_dim, factor, step = geometry
    cells = high * wide
    acc_ref, sum_ref, max_ref = state
    for at, head in enumerate(heads):
        cols = slice(head * head_dim, (head + 1) * head_dim)
        outs = slice(at * head_dim, (at + 1) * head_dim)
        starts = range(0, q_ref.shape[0], step)
        units = []
        for start in starts:
            near = dist_ref[start % cells : start % cells + step, : tile_ref.shape[1]]
            piece = (tile_ref[0, :, cols], tile_ref[1, :, cols], near, reach_of(head))
            units.append((q_ref[start : start + step, cols], [piece], None))
        for start, m, got in zip(starts, *attend(units, factor)):
            rows = slice(start, start + step)
            acc_ref[rows, outs] = got[:, :head_dim]
            sum_ref[rows, outs] = got[:, head_dim:]
            max_ref[rows, outs] = jnp.broadcast_to(m, (step, head_dim))


def begin_kernel(radius_ref, mask_ref, q_ref, tile_ref, *outs, geometry, heads):
    *state, dist_ref, reach_ref = outs
    high, wide, span, frames = geometry[:4]
    dist_ref[...] = distances(high, wide, span, frames)
    stretch_at = lax.axis_index("tm")
    line = (1, reach_ref.shape[1])
    for head in range(heads):
        radius = radius_ref[head]
        seen = mask_ref[stretch_at, 0, head] > 0
        reach_ref[head : head + 1] = jnp.full(line, radius, jnp.int32)
        reach_ref[heads + head : heads + head + 1] = jnp.full(
            line, jnp.where(seen, radius, -1), jnp.int32
        )
    attend_tile(q_ref, tile_ref, dist_ref, lambda h: radius_ref[h], (0,), state, geometry)


def tile_kernel(q_ref, tile_ref, dist_ref, reach_ref, *state, geometry, heads):
    attend_tile(
        q_ref,
        tile_ref,
        dist_ref,
        lambda h: reach_ref[h : h + 1, :1],
        range(1, heads),
        state,
        geometry,
    )


def pick_state(head_state, state, head, rows, head_dim):
    refs = head_state if head == 0 else state
    at = max(head - 1, 0) * head_dim
    return [ref[rows, at : at + head_dim] for ref in refs]


def rest_kernel(
    q_ref,
    edge_ref,
    first_tile_ref,
    first_edge_ref,
    *rest,
    geometry,
    heads,
    flips,
):
    head_state, dist_ref, reach_ref, state, outs = rest[:3], rest[3], rest[4], rest[5:8], rest[8:]
    high, wide, span, frames, head_dim, factor, step = geometry
    cells = high * wide
    base = frames * cells
    head_at = lax.axis_index("head")
    stretch_at = lax.axis_index("tm")

    def run(with_first):
        for flip, out_ref in zip(flips, outs):
            start = pl.multiple_of(jnp.bitwise_xor(head_at, flip) * step, step)
            rows = pl.ds(start, step)
            near = dist_ref[pl.ds(pl.multiple_of(lax.rem(start, cells), step), step)]
            beyond = near[:, base:]
            units = []
            olds = []
            for head in range(heads):
                cols = slice(head * head_dim, (head + 1) * head_dim)
                sources = [(edge_ref, beyond, head)]
                if with_first:
                    sources.append((first_tile_ref, near[:, :base], heads + head))
                    sources.append((first_edge_ref, beyond, heads + head))
                pieces = [
                    (ref[0, :, cols], ref[1, :, cols], dist, reach_ref[row : row + 1, :1])
                    for ref, dist, row in sources
                ]
                olds.append(pick_state(head_state, state, head, rows, head_dim))
                units.append((q_ref[rows, cols], pieces, olds[-1][2][:, :1]))
            for head, (m, got) in enumerate(zip(*attend(units, factor))):
                old_acc, old_total, old_max = olds[head]
                shrink = jnp.exp2(old_max - m)
                acc = old_acc * shrink + got[:, :head_dim]
                total = old_total * shrink + got[:, head_dim:]
                cols = slice(head * head_dim, (head + 1) * head_dim)
                out_ref[:, cols] = (acc / total).astype(jnp.bfloat16)

    @pl.when(stretch_at > 0)
    def _():
        run(True)

    @pl.when(stretch_at == 0)
    def _():
        run(False)


def copy_kernel(in_ref, out_ref):
    out_ref[...] = in_ref[...]


def stack_kernel(*refs):
    *parts, out_ref = refs
    tile_at = lax.axis_index("tile")
    for flip, part in enumerate(parts):
        tall = part.shape[0]
        top = pl.multiple_of(jnp.bitwise_xor(tile_at, flip) * tall, 16)
        out_ref[pl.ds(top, tall)] = part[...]


def project_kernel(w_ref, part_ref, own_ref, got_ref, out_ref, *, flip):
    broad = part_ref.shape[1]
    half = jnp.bitwise_xor(lax.axis_index("tm"), flip)
    cols = pl.ds(pl.multiple_of(half * broad, 128), broad)
    total = jnp.dot(own_ref[...], w_ref[:, cols], preferred_element_type=jnp.float32)
    total += jnp.dot(got_ref[...], part_ref[...], preferred_element_type=jnp.float32)
    out_ref[...] = total.astype(out_ref.dtype)


def add_kernel(mine_ref, got_ref, *rest, flip):
    out_ref, sum_ref, sems = rest[-3:]
    pieces, tall, broad = sum_ref.shape
    half = jnp.bitwise_xor(lax.axis_index("tm"), flip)
    cols = pl.ds(pl.multiple_of(half * broad, 128), broad)
    copies = []
    for i in range(pieces):
        rows = slice(i * tall, (i + 1) * tall)
        sum_ref[i] = (mine_ref[rows] + got_ref[rows].astype(jnp.float32)).astype(jnp.bfloat16)
        copies.append(pltpu.make_async_copy(sum_ref.at[i], out_ref.at[rows, cols], sems.at[i]))
        copies[-1].start()
    for copy in copies:
        copy.wait()


def two_by_two(query, keys, values, out_weight, radius, block_mask):
    span = RMAX
    frames, high, wide, channels = query.shape[2:]
    heads = radius.shape[0]
    head_dim = channels // heads
    cells = high * wide
    tokens = frames * cells
    groups = lax.axis_size("head")
    tiles = lax.axis_size("tile")
    depth, width = out_weight.shape
    step = tokens // groups
    geometry = (high, wide, span, frames, head_dim, LOG2E / math.sqrt(head_dim), step)
    count = frames * (cells + span * (wide + high + span))
    smem = pl.BlockSpec(memory_space=pltpu.SMEM)
    vmem = pl.BlockSpec(memory_space=pltpu.VMEM)
    hbm = pl.BlockSpec(memory_space=pltpu.HBM)
    bf16, f32 = jnp.bfloat16, jnp.float32
    shape = jax.ShapeDtypeStruct

    def call(kernel, out_shape, specs, *args, name, scratch=(), flops=0, **keys_of):
        return pl.pallas_call(
            functools.partial(kernel, **keys_of) if keys_of else kernel,
            out_shape=out_shape,
            in_specs=specs,
            out_specs=jax.tree.map(lambda _: vmem, out_shape),
            scratch_shapes=scratch,
            cost_estimate=pl.CostEstimate(flops=flops, bytes_accessed=0, transcendentals=0),
            compiler_params=pltpu.CompilerParams(vmem_limit_bytes=VMEM_LIMIT),
            name=name,
        )(*args)

    def flipped(value, axis, flip):
        return lax.ppermute(value, axis, [(i, i ^ flip) for i in range(lax.axis_size(axis))])

    q = query.reshape(tokens, channels)
    k = keys.reshape(tokens, channels)
    v = values.reshape(tokens, channels)

    tall, broad = depth // tiles, width // 2
    part_shape = shape((tall, broad), bf16)
    part = call(
        part_kernel,
        part_shape,
        [hbm],
        pltpu.with_memory_space_constraint(out_weight, pltpu.HBM),
        name="part",
        scratch=[pltpu.SemaphoreType.DMA],
    )
    *faces, tile = call(
        face_kernel,
        [
            shape((2, frames, span * wide, channels), bf16),
            shape((2, frames, span * high, channels), bf16),
            shape((2, frames, span * span, channels), bf16),
            shape((2, tokens, channels), bf16),
        ],
        [vmem] * 3,
        k,
        v,
        part,
        name="faces",
        geometry=geometry,
    )
    faces = [flipped(face, "tile", flip) for face, flip in zip(faces, (2, 1, 3))]
    lone = flipped(part, "head", 2)
    begun = call(
        begin_kernel,
        [shape((tokens, head_dim), f32)] * 3
        + [shape((cells, count), jnp.int32), shape((2 * heads, head_dim), jnp.int32)],
        [smem] * 2 + [vmem] * 2,
        radius,
        block_mask.transpose(1, 2, 0),
        q,
        tile,
        name="begin",
        geometry=geometry,
        heads=heads,
    )
    begun, tile = lax.optimization_barrier((begun, tile))
    first_tile = lax.ppermute(tile, "tm", [(0, 1)])
    state = call(
        tile_kernel,
        [shape((tokens, channels - head_dim), f32)] * 3,
        [vmem] * 4,
        q,
        tile,
        *begun[3:],
        name="tile",
        geometry=geometry,
        heads=heads,
    )
    lone, state = lax.optimization_barrier((lone, state))
    lone = call(copy_kernel, part_shape, [vmem], lone, name="lone", flops=20 * 10**9)
    lone, state, faces = lax.optimization_barrier((lone, state, faces))
    edge = call(
        edge_kernel, shape((2, count - tokens, channels), bf16), [vmem] * 3, *faces, name="edges"
    )
    first_edge = lax.ppermute(edge, "tm", [(0, 1)])
    parts = [lone] + [flipped(lone, "tile", flip) for flip in range(1, tiles)]

    def rest(state, *flips, flops=0):
        return call(
            rest_kernel,
            [shape((step, channels), bf16)] * len(flips),
            [vmem] * 12,
            q,
            edge,
            first_tile,
            first_edge,
            *begun,
            *state,
            name="rest",
            geometry=geometry,
            heads=heads,
            flips=flips,
            flops=flops,
        )

    (for_side,) = rest(state, 3)
    got_side = flipped(for_side, "head", 2)
    state, for_side = lax.optimization_barrier((state, for_side))
    for_far, own_side = rest(state, 2, 1)
    got_far = flipped(for_far, "head", 2)
    parts, own_side = lax.optimization_barrier((parts, own_side))
    here = call(
        stack_kernel, shape((depth, broad), bf16), [vmem] * tiles, *parts, name="stack"
    )

    there = flipped(here, "tm", 1)

    def project(part, mine, got, kind, flip, flops=0):
        return call(
            project_kernel,
            shape((step, broad), kind),
            [vmem] * 4,
            out_weight,
            part,
            mine,
            got,
            name="project",
            flops=flops,
            flip=flip,
        )

    for_side = [project(here, own_side, got_side, bf16, 0, 20 * 10**9)]
    from_side = [flipped(for_side[0], "head", 1)]
    state, for_side[0] = lax.optimization_barrier((state, for_side[0]))
    (own,) = rest(state, 0, flops=20 * 10**9)
    own_side, own = lax.optimization_barrier((own_side, own))
    for_side.append(project(there, own_side, got_side, bf16, 1))
    from_side.append(flipped(for_side[1], "head", 1))
    own, for_side[1] = lax.optimization_barrier((own, for_side[1]))
    mine = [
        project(here, own, got_far, f32, 0),
        project(there, own, got_far, f32, 1, 20 * 10**9),
    ]
    pieces = 2
    mixed = []
    for flip in range(2):
        mixed = [
            pl.pallas_call(
                functools.partial(add_kernel, flip=flip),
                out_shape=shape((step, width), bf16),
                in_specs=[vmem] * 2 + [hbm] * flip,
                out_specs=hbm,
                input_output_aliases={2: 0} if flip else {},
                scratch_shapes=[
                    pltpu.VMEM((pieces, step // pieces, broad), bf16),
                    pltpu.SemaphoreType.DMA((pieces,)),
                ],
                compiler_params=pltpu.CompilerParams(vmem_limit_bytes=VMEM_LIMIT),
                name="add",
            )(mine[flip], from_side[flip], *mixed)
        ]
    (mixed,) = mixed
    return mixed.reshape(1, 1, step, width)


def solution(mesh):
    in_specs = (
        P("tm", "tile", None, None, None, "head"),
        P("tm", "tile", None, None, None, "head"),
        P("tm", "tile", None, None, None, "head"),
        P("head", None),
        P("head"),
        P("head", None, None),
    )
    out_specs = P("tm", "tile", "head", None)
    small = dict(mesh.shape) == {"tm": 2, "tile": 4, "head": 4}
    return jax.shard_map(
        two_by_two if small else any_grid,
        mesh=mesh,
        in_specs=in_specs,
        out_specs=out_specs,
        check_vma=False,
    )
```

```python
import functools
import math

import jax
import jax.numpy as jnp
from jax import lax
from jax.experimental import pallas as pl
from jax.experimental.pallas import tpu as pltpu
from jax.sharding import PartitionSpec as P

RMAX = 4
FAR = -1e30
LOG2E = 1.4426950408889634
VMEM_LIMIT = 24 * 1024 * 1024


def passed_along(value, axis, by):
    peers = lax.axis_size(axis)
    pairs = [(i, i + by) for i in range(peers) if 0 <= i + by < peers]
    return lax.ppermute(value, axis, pairs)


def widen(key_part, value_part, span, row_move, col_move):
    grid = math.isqrt(lax.axis_size("tile"))
    above = None
    below = None
    for offset in (grid, -grid):
        if offset > 0:
            face_key = key_part[:, :, key_part.shape[2] - span :]
            face_value = value_part[:, :, value_part.shape[2] - span :]
        else:
            face_key = key_part[:, :, :span]
            face_value = value_part[:, :, :span]
        got = row_move(face_key, face_value, offset)
        if offset > 0:
            above = got
        else:
            below = got
    key_rows = jnp.concatenate([above[0], key_part, below[0]], axis=2)
    value_rows = jnp.concatenate([above[1], value_part, below[1]], axis=2)
    left = None
    right = None
    for offset in (1, -1):
        if offset > 0:
            face_key = key_rows[:, :, :, key_rows.shape[3] - span :]
            face_value = value_rows[:, :, :, value_rows.shape[3] - span :]
        else:
            face_key = key_rows[:, :, :, :span]
            face_value = value_rows[:, :, :, :span]
        got = col_move(face_key, face_value, offset)
        if offset > 0:
            left = got
        else:
            right = got
    key_full = jnp.concatenate([left[0], key_rows, right[0]], axis=3)
    value_full = jnp.concatenate([left[1], value_rows, right[1]], axis=3)
    return (key_full, value_full)


def windows_of(block, half_high, half_wide, win_high, win_wide, heads_here, head_dim):
    parts = []
    for band in (0, 1):
        for strip in (0, 1):
            parts.append(
                block[
                    :,
                    band * half_high : band * half_high + win_high,
                    strip * half_wide : strip * half_wide + win_wide,
                ]
            )
    stacked = jnp.stack(parts)
    return stacked.reshape(4, -1, heads_here, head_dim)


def any_grid(query, keys, values, out_weight, radius, block_mask):
    span = RMAX
    grid = math.isqrt(lax.axis_size("tile"))
    tile_at = lax.axis_index("tile")
    row_at = tile_at // grid
    col_at = tile_at % grid
    stretch_at = lax.axis_index("tm")
    frames, high, wide, channels = query.shape[2:]
    heads_here = radius.shape[0]
    head_dim = channels // heads_here
    tokens_here = frames * high * wide
    half_high = high // 2
    half_wide = wide // 2
    win_high = half_high + 2 * span
    win_wide = half_wide + 2 * span
    quarter = frames * half_high * half_wide
    queries = query[0, 0].reshape(frames, 2, half_high, 2, half_wide, channels)
    queries = queries.transpose(1, 3, 0, 2, 4, 5).reshape(4, quarter, heads_here, head_dim)
    query_y = jnp.broadcast_to(
        jnp.arange(half_high, dtype=jnp.int32)[None, :, None], (frames, half_high, half_wide)
    ).reshape(-1)
    query_x = jnp.broadcast_to(
        jnp.arange(half_wide, dtype=jnp.int32)[None, None, :], (frames, half_high, half_wide)
    ).reshape(-1)
    key_y = jnp.broadcast_to(
        jnp.arange(win_high, dtype=jnp.int32)[None, :, None] - span, (frames, win_high, win_wide)
    ).reshape(-1)
    key_x = jnp.broadcast_to(
        jnp.arange(win_wide, dtype=jnp.int32)[None, None, :] - span, (frames, win_high, win_wide)
    ).reshape(-1)
    band_at = jnp.array([0, 0, 1, 1], dtype=jnp.int32)
    strip_at = jnp.array([0, 1, 0, 1], dtype=jnp.int32)
    global_y = row_at * high + band_at[:, None] * half_high + key_y[None, :]
    global_x = col_at * wide + strip_at[:, None] * half_wide + key_x[None, :]
    inside = (global_y >= 0) & (global_y < grid * high) & (global_x >= 0) & (global_x < grid * wide)
    distance = jnp.maximum(
        jnp.abs(query_y[:, None] - key_y[None, :]), jnp.abs(query_x[:, None] - key_x[None, :])
    )
    near = distance[None, :, :] <= radius[:, None, None]
    allowed = near[None, :, :, :] & inside[:, None, None, :]
    scale = 1.0 / math.sqrt(head_dim)
    initial = (
        jnp.full((4, heads_here, quarter), -1e30, jnp.float32),
        jnp.zeros((4, heads_here, quarter), jnp.float32),
        jnp.zeros((4, heads_here, quarter, head_dim), jnp.float32),
    )

    def tile_move(face_key, face_value, offset):
        return passed_along((face_key, face_value), "tile", offset)

    key_all, value_all = (
        lax.all_gather(keys[0], "tm", axis=0, tiled=True),
        lax.all_gather(values[0], "tm", axis=0, tiled=True),
    )
    key_full, value_full = widen(key_all, value_all, span, tile_move, tile_move)
    stretch_ids = jnp.arange(key_full.shape[0], dtype=jnp.int32)

    def one_stretch(state, item):
        key_block, value_block, stretch_id = item
        visible = (
            lax.dynamic_slice_in_dim(
                lax.dynamic_index_in_dim(block_mask, stretch_at, 1, False), stretch_id, 1, 1
            )[:, 0]
            > 0
        )
        best, total, acc = state
        key_win = windows_of(
            key_block, half_high, half_wide, win_high, win_wide, heads_here, head_dim
        )
        value_win = windows_of(
            value_block, half_high, half_wide, win_high, win_wide, heads_here, head_dim
        )
        usable = allowed & visible[None, :, None, None]
        scores = (
            jnp.einsum("nqhd,nkhd->nhqk", queries, key_win, preferred_element_type=jnp.float32)
            * scale
        )
        masked = jnp.where(usable, scores, jnp.float32(-1e30))
        fresh = jnp.maximum(best, jnp.max(masked, axis=3))
        probs = jnp.where(usable, jnp.exp(scores - fresh[..., None]), jnp.float32(0.0))
        shrink = jnp.exp(best - fresh)
        total = total * shrink + jnp.sum(probs, axis=3)
        acc = acc * shrink[..., None] + jnp.einsum(
            "nhqk,nkhd->nhqd",
            probs.astype(jnp.bfloat16),
            value_win,
            preferred_element_type=jnp.float32,
        )
        return ((fresh, total, acc), None)

    final, unused = lax.scan(one_stretch, initial, (key_full, value_full, stretch_ids))
    best, total, acc = final
    attn = (acc / total[..., None]).astype(jnp.bfloat16)
    attn = attn.transpose(0, 2, 1, 3).reshape(
        2, 2, frames, half_high, half_wide, heads_here * head_dim
    )
    attn = attn.transpose(2, 0, 3, 1, 4, 5).reshape(tokens_here, heads_here * head_dim)
    mixed = lax.psum_scatter(
        jnp.dot(attn, out_weight, preferred_element_type=jnp.float32).astype(jnp.bfloat16),
        "head",
        scatter_dimension=0,
        tiled=True,
    )
    return mixed.reshape(1, 1, -1, out_weight.shape[1])


def tile_place():
    tile_at = lax.axis_index("tile")
    return tile_at // 2, tile_at % 2


def part_kernel(w_ref, part_ref, sem):
    tall, broad = part_ref.shape
    top = pl.multiple_of(lax.axis_index("tile") * tall, 16)
    left = pl.multiple_of(lax.axis_index("tm") * broad, 128)
    copy = pltpu.make_async_copy(w_ref.at[pl.ds(top, tall), pl.ds(left, broad)], part_ref, sem)
    copy.start()
    copy.wait()


def face_kernel(k_ref, v_ref, part_ref, row_ref, col_ref, corner_ref, tile_ref, *, geometry):
    high, wide, span, frames = geometry[:4]
    cells = high * wide
    row_at, col_at = tile_place()
    y0 = jnp.where(row_at == 0, high - span, 0)
    x0 = jnp.where(col_at == 0, wide - span, 0)

    def picker(count, cell_of):
        row = lax.broadcasted_iota(jnp.int32, (count, cells), 0)
        col = lax.broadcasted_iota(jnp.int32, (count, cells), 1)
        return (col == cell_of(row)).astype(jnp.bfloat16)

    beside = picker(high * span, lambda i: (i // span) * wide + x0 + i % span)
    across = picker(span * span, lambda i: (y0 + i // span) * wide + x0 + i % span)
    for which, ref in enumerate((k_ref, v_ref)):
        tile_ref[which] = ref[...]
        for f in range(frames):
            start = pl.multiple_of(f * cells + y0 * wide, 16)
            row_ref[which, f] = ref[pl.ds(start, span * wide)]
            whole = ref[f * cells : (f + 1) * cells]
            col_ref[which, f] = jnp.dot(
                beside, whole, preferred_element_type=jnp.float32
            ).astype(jnp.bfloat16)
            corner_ref[which, f] = jnp.dot(
                across, whole, preferred_element_type=jnp.float32
            ).astype(jnp.bfloat16)


def edge_kernel(row_ref, col_ref, corner_ref, out_ref):
    for which in range(2):
        at = 0
        for part in (row_ref, col_ref, corner_ref):
            for f in range(part.shape[1]):
                size = part.shape[2]
                out_ref[which, at : at + size] = part[which, f]
                at += size


def distances(high, wide, span, frames):
    row_at, col_at = tile_place()
    cells = high * wide
    count = frames * (cells + span * (wide + high + span))
    j = lax.broadcasted_iota(jnp.int32, (1, count), 1)
    y_off = jnp.where(row_at == 0, high, -span)
    x_off = jnp.where(col_at == 0, wide, -span)
    c = j % cells
    ky, kx = c // wide, c % wide
    base = frames * cells
    c = (j - base) % (span * wide)
    ky = jnp.where(j >= base, y_off + c // wide, ky)
    kx = jnp.where(j >= base, c % wide, kx)
    base += frames * span * wide
    c = (j - base) % (span * high)
    ky = jnp.where(j >= base, c // span, ky)
    kx = jnp.where(j >= base, x_off + c % span, kx)
    base += frames * span * high
    c = (j - base) % (span * span)
    ky = jnp.where(j >= base, y_off + c // span, ky)
    kx = jnp.where(j >= base, x_off + c % span, kx)
    i = lax.broadcasted_iota(jnp.int32, (cells, 1), 0)
    return jnp.maximum(jnp.abs(i // wide - ky), jnp.abs(i % wide - kx))


def attend(units, factor):
    scores = [
        [
            jnp.where(
                dist <= reach,
                lax.dot_general(
                    q, k, (((1,), (1,)), ((), ())), preferred_element_type=jnp.float32
                )
                * factor,
                FAR,
            )
            for k, v, dist, reach in pieces
        ]
        for q, pieces, before in units
    ]
    tops = []
    for parts, (q, pieces, before) in zip(scores, units):
        found = [jnp.max(s, axis=1, keepdims=True) for s in parts]
        if before is not None:
            found.append(before)
        tops.append(functools.reduce(jnp.maximum, found))
    probs = [
        [jnp.exp2(s - m).astype(jnp.bfloat16) for s in parts] for parts, m in zip(scores, tops)
    ]
    sums = []
    for parts, (q, pieces, before) in zip(probs, units):
        total = None
        for p, (k, v, dist, reach) in zip(parts, pieces):
            both = jnp.concatenate([v, jnp.ones_like(v)], axis=1)
            got = jnp.dot(p, both, preferred_element_type=jnp.float32)
            total = got if total is None else total + got
        sums.append(total)
    return tops, sums


def attend_tile(q_ref, tile_ref, dist_ref, reach_of, heads, state, geometry):
    high, wide, span, frames, head_dim, factor, step = geometry
    cells = high * wide
    acc_ref, sum_ref, max_ref = state
    for at, head in enumerate(heads):
        cols = slice(head * head_dim, (head + 1) * head_dim)
        outs = slice(at * head_dim, (at + 1) * head_dim)
        starts = range(0, q_ref.shape[0], step)
        units = []
        for start in starts:
            near = dist_ref[start % cells : start % cells + step, : tile_ref.shape[1]]
            piece = (tile_ref[0, :, cols], tile_ref[1, :, cols], near, reach_of(head))
            units.append((q_ref[start : start + step, cols], [piece], None))
        for start, m, got in zip(starts, *attend(units, factor)):
            rows = slice(start, start + step)
            acc_ref[rows, outs] = got[:, :head_dim]
            sum_ref[rows, outs] = got[:, head_dim:]
            max_ref[rows, outs] = jnp.broadcast_to(m, (step, head_dim))


def begin_kernel(radius_ref, mask_ref, q_ref, tile_ref, *outs, geometry, heads):
    *state, dist_ref, reach_ref = outs
    high, wide, span, frames = geometry[:4]
    dist_ref[...] = distances(high, wide, span, frames)
    stretch_at = lax.axis_index("tm")
    line = (1, reach_ref.shape[1])
    for head in range(heads):
        radius = radius_ref[head]
        seen = mask_ref[stretch_at, 0, head] > 0
        reach_ref[head : head + 1] = jnp.full(line, radius, jnp.int32)
        reach_ref[heads + head : heads + head + 1] = jnp.full(
            line, jnp.where(seen, radius, -1), jnp.int32
        )
    attend_tile(q_ref, tile_ref, dist_ref, lambda h: radius_ref[h], (0,), state, geometry)


def tile_kernel(q_ref, tile_ref, dist_ref, reach_ref, *state, geometry, heads):
    attend_tile(
        q_ref,
        tile_ref,
        dist_ref,
        lambda h: reach_ref[h : h + 1, :1],
        range(1, heads),
        state,
        geometry,
    )


def pick_state(head_state, state, head, rows, head_dim):
    refs = head_state if head == 0 else state
    at = max(head - 1, 0) * head_dim
    return [ref[rows, at : at + head_dim] for ref in refs]


def rest_kernel(
    q_ref,
    edge_ref,
    first_tile_ref,
    first_edge_ref,
    *rest,
    geometry,
    heads,
    flips,
):
    head_state, dist_ref, reach_ref, state, outs = rest[:3], rest[3], rest[4], rest[5:8], rest[8:]
    high, wide, span, frames, head_dim, factor, step = geometry
    cells = high * wide
    base = frames * cells
    head_at = lax.axis_index("head")
    stretch_at = lax.axis_index("tm")

    def run(with_first):
        for flip, out_ref in zip(flips, outs):
            start = pl.multiple_of(jnp.bitwise_xor(head_at, flip) * step, step)
            rows = pl.ds(start, step)
            near = dist_ref[pl.ds(pl.multiple_of(lax.rem(start, cells), step), step)]
            beyond = near[:, base:]
            units = []
            olds = []
            for head in range(heads):
                cols = slice(head * head_dim, (head + 1) * head_dim)
                sources = [(edge_ref, beyond, head)]
                if with_first:
                    sources.append((first_tile_ref, near[:, :base], heads + head))
                    sources.append((first_edge_ref, beyond, heads + head))
                pieces = [
                    (ref[0, :, cols], ref[1, :, cols], dist, reach_ref[row : row + 1, :1])
                    for ref, dist, row in sources
                ]
                olds.append(pick_state(head_state, state, head, rows, head_dim))
                units.append((q_ref[rows, cols], pieces, olds[-1][2][:, :1]))
            for head, (m, got) in enumerate(zip(*attend(units, factor))):
                old_acc, old_total, old_max = olds[head]
                shrink = jnp.exp2(old_max - m)
                acc = old_acc * shrink + got[:, :head_dim]
                total = old_total * shrink + got[:, head_dim:]
                cols = slice(head * head_dim, (head + 1) * head_dim)
                out_ref[:, cols] = (acc / total).astype(jnp.bfloat16)

    @pl.when(stretch_at > 0)
    def _():
        run(True)

    @pl.when(stretch_at == 0)
    def _():
        run(False)


def copy_kernel(in_ref, out_ref):
    out_ref[...] = in_ref[...]


def stack_kernel(*refs):
    *parts, out_ref = refs
    tile_at = lax.axis_index("tile")
    for flip, part in enumerate(parts):
        tall = part.shape[0]
        top = pl.multiple_of(jnp.bitwise_xor(tile_at, flip) * tall, 16)
        out_ref[pl.ds(top, tall)] = part[...]


def project_kernel(w_ref, part_ref, own_ref, got_ref, out_ref, *, flip):
    broad = part_ref.shape[1]
    half = jnp.bitwise_xor(lax.axis_index("tm"), flip)
    cols = pl.ds(pl.multiple_of(half * broad, 128), broad)
    total = jnp.dot(own_ref[...], w_ref[:, cols], preferred_element_type=jnp.float32)
    total += jnp.dot(got_ref[...], part_ref[...], preferred_element_type=jnp.float32)
    out_ref[...] = total.astype(out_ref.dtype)


def add_kernel(mine_ref, got_ref, *rest, flip):
    out_ref, sum_ref, sems = rest[-3:]
    pieces, tall, broad = sum_ref.shape
    half = jnp.bitwise_xor(lax.axis_index("tm"), flip)
    cols = pl.ds(pl.multiple_of(half * broad, 128), broad)
    copies = []
    for i in range(pieces):
        rows = slice(i * tall, (i + 1) * tall)
        sum_ref[i] = (mine_ref[rows] + got_ref[rows].astype(jnp.float32)).astype(jnp.bfloat16)
        copies.append(pltpu.make_async_copy(sum_ref.at[i], out_ref.at[rows, cols], sems.at[i]))
        copies[-1].start()
    for copy in copies:
        copy.wait()


def two_by_two(query, keys, values, out_weight, radius, block_mask):
    span = RMAX
    frames, high, wide, channels = query.shape[2:]
    heads = radius.shape[0]
    head_dim = channels // heads
    cells = high * wide
    tokens = frames * cells
    groups = lax.axis_size("head")
    tiles = lax.axis_size("tile")
    depth, width = out_weight.shape
    step = tokens // groups
    geometry = (high, wide, span, frames, head_dim, LOG2E / math.sqrt(head_dim), step)
    count = frames * (cells + span * (wide + high + span))
    smem = pl.BlockSpec(memory_space=pltpu.SMEM)
    vmem = pl.BlockSpec(memory_space=pltpu.VMEM)
    hbm = pl.BlockSpec(memory_space=pltpu.HBM)
    bf16, f32 = jnp.bfloat16, jnp.float32
    shape = jax.ShapeDtypeStruct

    def call(kernel, out_shape, specs, *args, name, scratch=(), flops=0, **keys_of):
        return pl.pallas_call(
            functools.partial(kernel, **keys_of) if keys_of else kernel,
            out_shape=out_shape,
            in_specs=specs,
            out_specs=jax.tree.map(lambda _: vmem, out_shape),
            scratch_shapes=scratch,
            cost_estimate=pl.CostEstimate(flops=flops, bytes_accessed=0, transcendentals=0),
            compiler_params=pltpu.CompilerParams(vmem_limit_bytes=VMEM_LIMIT),
            name=name,
        )(*args)

    def flipped(value, axis, flip):
        return lax.ppermute(value, axis, [(i, i ^ flip) for i in range(lax.axis_size(axis))])

    q = query.reshape(tokens, channels)
    k = keys.reshape(tokens, channels)
    v = values.reshape(tokens, channels)

    tall, broad = depth // tiles, width // 2
    part_shape = shape((tall, broad), bf16)
    part = call(
        part_kernel,
        part_shape,
        [hbm],
        pltpu.with_memory_space_constraint(out_weight, pltpu.HBM),
        name="part",
        scratch=[pltpu.SemaphoreType.DMA],
    )
    *faces, tile = call(
        face_kernel,
        [
            shape((2, frames, span * wide, channels), bf16),
            shape((2, frames, span * high, channels), bf16),
            shape((2, frames, span * span, channels), bf16),
            shape((2, tokens, channels), bf16),
        ],
        [vmem] * 3,
        k,
        v,
        part,
        name="faces",
        geometry=geometry,
    )
    faces = [flipped(face, "tile", flip) for face, flip in zip(faces, (2, 1, 3))]
    lone = flipped(part, "head", 2)
    begun = call(
        begin_kernel,
        [shape((tokens, head_dim), f32)] * 3
        + [shape((cells, count), jnp.int32), shape((2 * heads, head_dim), jnp.int32)],
        [smem] * 2 + [vmem] * 2,
        radius,
        block_mask.transpose(1, 2, 0),
        q,
        tile,
        name="begin",
        geometry=geometry,
        heads=heads,
    )
    begun, tile = lax.optimization_barrier((begun, tile))
    first_tile = lax.ppermute(tile, "tm", [(0, 1)])
    state = call(
        tile_kernel,
        [shape((tokens, channels - head_dim), f32)] * 3,
        [vmem] * 4,
        q,
        tile,
        *begun[3:],
        name="tile",
        geometry=geometry,
        heads=heads,
    )
    lone, state = lax.optimization_barrier((lone, state))
    lone = call(copy_kernel, part_shape, [vmem], lone, name="lone", flops=20 * 10**9)
    lone, state, faces = lax.optimization_barrier((lone, state, faces))
    edge = call(
        edge_kernel, shape((2, count - tokens, channels), bf16), [vmem] * 3, *faces, name="edges"
    )
    first_edge = lax.ppermute(edge, "tm", [(0, 1)])
    parts = [lone] + [flipped(lone, "tile", flip) for flip in range(1, tiles)]

    def rest(state, *flips, flops=0):
        return call(
            rest_kernel,
            [shape((step, channels), bf16)] * len(flips),
            [vmem] * 12,
            q,
            edge,
            first_tile,
            first_edge,
            *begun,
            *state,
            name="rest",
            geometry=geometry,
            heads=heads,
            flips=flips,
            flops=flops,
        )

    (for_side,) = rest(state, 3)
    got_side = flipped(for_side, "head", 2)
    state, for_side = lax.optimization_barrier((state, for_side))
    for_far, own_side = rest(state, 2, 1)
    got_far = flipped(for_far, "head", 2)
    parts, own_side = lax.optimization_barrier((parts[::-1], own_side))
    parts = parts[::-1]
    here = call(
        stack_kernel, shape((depth, broad), bf16), [vmem] * tiles, *parts, name="stack"
    )

    def project(part, mine, got, kind, flip, flops=0):
        return call(
            project_kernel,
            shape((step, broad), kind),
            [vmem] * 4,
            out_weight,
            part,
            mine,
            got,
            name="project",
            flops=flops,
            flip=flip,
        )

    for_side = [project(here, own_side, got_side, bf16, 0, 20 * 10**9)]
    from_side = [flipped(for_side[0], "head", 1)]
    state, here, for_side[0] = lax.optimization_barrier((state, here, for_side[0]))
    there = flipped(here, "tm", 1)
    (own,) = rest(state, 0, flops=20 * 10**9)
    own_side, own = lax.optimization_barrier((own_side, own))
    for_side.append(project(there, own_side, got_side, bf16, 1))
    from_side.append(flipped(for_side[1], "head", 1))
    own, for_side[1] = lax.optimization_barrier((own, for_side[1]))
    mine = [
        project(here, own, got_far, f32, 0),
        project(there, own, got_far, f32, 1, 20 * 10**9),
    ]
    pieces = 2
    mixed = []
    for flip in range(2):
        mixed = [
            pl.pallas_call(
                functools.partial(add_kernel, flip=flip),
                out_shape=shape((step, width), bf16),
                in_specs=[vmem] * 2 + [hbm] * flip,
                out_specs=hbm,
                input_output_aliases={2: 0} if flip else {},
                scratch_shapes=[
                    pltpu.VMEM((pieces, step // pieces, broad), bf16),
                    pltpu.SemaphoreType.DMA((pieces,)),
                ],
                compiler_params=pltpu.CompilerParams(vmem_limit_bytes=VMEM_LIMIT),
                name="add",
            )(mine[flip], from_side[flip], *mixed)
        ]
    (mixed,) = mixed
    return mixed.reshape(1, 1, step, width)


def solution(mesh):
    in_specs = (
        P("tm", "tile", None, None, None, "head"),
        P("tm", "tile", None, None, None, "head"),
        P("tm", "tile", None, None, None, "head"),
        P("head", None),
        P("head"),
        P("head", None, None),
    )
    out_specs = P("tm", "tile", "head", None)
    small = dict(mesh.shape) == {"tm": 2, "tile": 4, "head": 4}
    return jax.shard_map(
        two_by_two if small else any_grid,
        mesh=mesh,
        in_specs=in_specs,
        out_specs=out_specs,
        check_vma=False,
    )
```

```python
import functools
import math

import jax
import jax.numpy as jnp
from jax import lax
from jax.experimental import pallas as pl
from jax.experimental.pallas import tpu as pltpu
from jax.sharding import PartitionSpec as P

RMAX = 4
FAR = -1e30
LOG2E = 1.4426950408889634
VMEM_LIMIT = 24 * 1024 * 1024


def passed_along(value, axis, by):
    peers = lax.axis_size(axis)
    pairs = [(i, i + by) for i in range(peers) if 0 <= i + by < peers]
    return lax.ppermute(value, axis, pairs)


def widen(key_part, value_part, span, row_move, col_move):
    grid = math.isqrt(lax.axis_size("tile"))
    above = None
    below = None
    for offset in (grid, -grid):
        if offset > 0:
            face_key = key_part[:, :, key_part.shape[2] - span :]
            face_value = value_part[:, :, value_part.shape[2] - span :]
        else:
            face_key = key_part[:, :, :span]
            face_value = value_part[:, :, :span]
        got = row_move(face_key, face_value, offset)
        if offset > 0:
            above = got
        else:
            below = got
    key_rows = jnp.concatenate([above[0], key_part, below[0]], axis=2)
    value_rows = jnp.concatenate([above[1], value_part, below[1]], axis=2)
    left = None
    right = None
    for offset in (1, -1):
        if offset > 0:
            face_key = key_rows[:, :, :, key_rows.shape[3] - span :]
            face_value = value_rows[:, :, :, value_rows.shape[3] - span :]
        else:
            face_key = key_rows[:, :, :, :span]
            face_value = value_rows[:, :, :, :span]
        got = col_move(face_key, face_value, offset)
        if offset > 0:
            left = got
        else:
            right = got
    key_full = jnp.concatenate([left[0], key_rows, right[0]], axis=3)
    value_full = jnp.concatenate([left[1], value_rows, right[1]], axis=3)
    return (key_full, value_full)


def windows_of(block, half_high, half_wide, win_high, win_wide, heads_here, head_dim):
    parts = []
    for band in (0, 1):
        for strip in (0, 1):
            parts.append(
                block[
                    :,
                    band * half_high : band * half_high + win_high,
                    strip * half_wide : strip * half_wide + win_wide,
                ]
            )
    stacked = jnp.stack(parts)
    return stacked.reshape(4, -1, heads_here, head_dim)


def any_grid(query, keys, values, out_weight, radius, block_mask):
    span = RMAX
    grid = math.isqrt(lax.axis_size("tile"))
    tile_at = lax.axis_index("tile")
    row_at = tile_at // grid
    col_at = tile_at % grid
    stretch_at = lax.axis_index("tm")
    frames, high, wide, channels = query.shape[2:]
    heads_here = radius.shape[0]
    head_dim = channels // heads_here
    tokens_here = frames * high * wide
    half_high = high // 2
    half_wide = wide // 2
    win_high = half_high + 2 * span
    win_wide = half_wide + 2 * span
    quarter = frames * half_high * half_wide
    queries = query[0, 0].reshape(frames, 2, half_high, 2, half_wide, channels)
    queries = queries.transpose(1, 3, 0, 2, 4, 5).reshape(4, quarter, heads_here, head_dim)
    query_y = jnp.broadcast_to(
        jnp.arange(half_high, dtype=jnp.int32)[None, :, None], (frames, half_high, half_wide)
    ).reshape(-1)
    query_x = jnp.broadcast_to(
        jnp.arange(half_wide, dtype=jnp.int32)[None, None, :], (frames, half_high, half_wide)
    ).reshape(-1)
    key_y = jnp.broadcast_to(
        jnp.arange(win_high, dtype=jnp.int32)[None, :, None] - span, (frames, win_high, win_wide)
    ).reshape(-1)
    key_x = jnp.broadcast_to(
        jnp.arange(win_wide, dtype=jnp.int32)[None, None, :] - span, (frames, win_high, win_wide)
    ).reshape(-1)
    band_at = jnp.array([0, 0, 1, 1], dtype=jnp.int32)
    strip_at = jnp.array([0, 1, 0, 1], dtype=jnp.int32)
    global_y = row_at * high + band_at[:, None] * half_high + key_y[None, :]
    global_x = col_at * wide + strip_at[:, None] * half_wide + key_x[None, :]
    inside = (global_y >= 0) & (global_y < grid * high) & (global_x >= 0) & (global_x < grid * wide)
    distance = jnp.maximum(
        jnp.abs(query_y[:, None] - key_y[None, :]), jnp.abs(query_x[:, None] - key_x[None, :])
    )
    near = distance[None, :, :] <= radius[:, None, None]
    allowed = near[None, :, :, :] & inside[:, None, None, :]
    scale = 1.0 / math.sqrt(head_dim)
    initial = (
        jnp.full((4, heads_here, quarter), -1e30, jnp.float32),
        jnp.zeros((4, heads_here, quarter), jnp.float32),
        jnp.zeros((4, heads_here, quarter, head_dim), jnp.float32),
    )

    def tile_move(face_key, face_value, offset):
        return passed_along((face_key, face_value), "tile", offset)

    key_all, value_all = (
        lax.all_gather(keys[0], "tm", axis=0, tiled=True),
        lax.all_gather(values[0], "tm", axis=0, tiled=True),
    )
    key_full, value_full = widen(key_all, value_all, span, tile_move, tile_move)
    stretch_ids = jnp.arange(key_full.shape[0], dtype=jnp.int32)

    def one_stretch(state, item):
        key_block, value_block, stretch_id = item
        visible = (
            lax.dynamic_slice_in_dim(
                lax.dynamic_index_in_dim(block_mask, stretch_at, 1, False), stretch_id, 1, 1
            )[:, 0]
            > 0
        )
        best, total, acc = state
        key_win = windows_of(
            key_block, half_high, half_wide, win_high, win_wide, heads_here, head_dim
        )
        value_win = windows_of(
            value_block, half_high, half_wide, win_high, win_wide, heads_here, head_dim
        )
        usable = allowed & visible[None, :, None, None]
        scores = (
            jnp.einsum("nqhd,nkhd->nhqk", queries, key_win, preferred_element_type=jnp.float32)
            * scale
        )
        masked = jnp.where(usable, scores, jnp.float32(-1e30))
        fresh = jnp.maximum(best, jnp.max(masked, axis=3))
        probs = jnp.where(usable, jnp.exp(scores - fresh[..., None]), jnp.float32(0.0))
        shrink = jnp.exp(best - fresh)
        total = total * shrink + jnp.sum(probs, axis=3)
        acc = acc * shrink[..., None] + jnp.einsum(
            "nhqk,nkhd->nhqd",
            probs.astype(jnp.bfloat16),
            value_win,
            preferred_element_type=jnp.float32,
        )
        return ((fresh, total, acc), None)

    final, unused = lax.scan(one_stretch, initial, (key_full, value_full, stretch_ids))
    best, total, acc = final
    attn = (acc / total[..., None]).astype(jnp.bfloat16)
    attn = attn.transpose(0, 2, 1, 3).reshape(
        2, 2, frames, half_high, half_wide, heads_here * head_dim
    )
    attn = attn.transpose(2, 0, 3, 1, 4, 5).reshape(tokens_here, heads_here * head_dim)
    mixed = lax.psum_scatter(
        jnp.dot(attn, out_weight, preferred_element_type=jnp.float32).astype(jnp.bfloat16),
        "head",
        scatter_dimension=0,
        tiled=True,
    )
    return mixed.reshape(1, 1, -1, out_weight.shape[1])


def tile_place():
    tile_at = lax.axis_index("tile")
    return tile_at // 2, tile_at % 2


def part_kernel(w_ref, part_ref, sem):
    tall, broad = part_ref.shape
    top = pl.multiple_of(lax.axis_index("tile") * tall, 16)
    left = pl.multiple_of(lax.axis_index("tm") * broad, 128)
    copy = pltpu.make_async_copy(w_ref.at[pl.ds(top, tall), pl.ds(left, broad)], part_ref, sem)
    copy.start()
    copy.wait()


def face_kernel(k_ref, v_ref, part_ref, row_ref, col_ref, corner_ref, tile_ref, *, geometry):
    high, wide, span, frames = geometry[:4]
    cells = high * wide
    row_at, col_at = tile_place()
    y0 = jnp.where(row_at == 0, high - span, 0)
    x0 = jnp.where(col_at == 0, wide - span, 0)

    def picker(count, cell_of):
        row = lax.broadcasted_iota(jnp.int32, (count, cells), 0)
        col = lax.broadcasted_iota(jnp.int32, (count, cells), 1)
        return (col == cell_of(row)).astype(jnp.bfloat16)

    beside = picker(high * span, lambda i: (i // span) * wide + x0 + i % span)
    across = picker(span * span, lambda i: (y0 + i // span) * wide + x0 + i % span)
    for which, ref in enumerate((k_ref, v_ref)):
        tile_ref[which] = ref[...]
        for f in range(frames):
            start = pl.multiple_of(f * cells + y0 * wide, 16)
            row_ref[which, f] = ref[pl.ds(start, span * wide)]
            whole = ref[f * cells : (f + 1) * cells]
            col_ref[which, f] = jnp.dot(
                beside, whole, preferred_element_type=jnp.float32
            ).astype(jnp.bfloat16)
            corner_ref[which, f] = jnp.dot(
                across, whole, preferred_element_type=jnp.float32
            ).astype(jnp.bfloat16)


def edge_kernel(row_ref, col_ref, corner_ref, out_ref):
    for which in range(2):
        at = 0
        for part in (row_ref, col_ref, corner_ref):
            for f in range(part.shape[1]):
                size = part.shape[2]
                out_ref[which, at : at + size] = part[which, f]
                at += size


def distances(high, wide, span, frames):
    row_at, col_at = tile_place()
    cells = high * wide
    count = frames * (cells + span * (wide + high + span))
    j = lax.broadcasted_iota(jnp.int32, (1, count), 1)
    y_off = jnp.where(row_at == 0, high, -span)
    x_off = jnp.where(col_at == 0, wide, -span)
    c = j % cells
    ky, kx = c // wide, c % wide
    base = frames * cells
    c = (j - base) % (span * wide)
    ky = jnp.where(j >= base, y_off + c // wide, ky)
    kx = jnp.where(j >= base, c % wide, kx)
    base += frames * span * wide
    c = (j - base) % (span * high)
    ky = jnp.where(j >= base, c // span, ky)
    kx = jnp.where(j >= base, x_off + c % span, kx)
    base += frames * span * high
    c = (j - base) % (span * span)
    ky = jnp.where(j >= base, y_off + c // span, ky)
    kx = jnp.where(j >= base, x_off + c % span, kx)
    i = lax.broadcasted_iota(jnp.int32, (cells, 1), 0)
    return jnp.maximum(jnp.abs(i // wide - ky), jnp.abs(i % wide - kx))


def attend(units, factor):
    scores = [
        [
            jnp.where(
                dist <= reach,
                lax.dot_general(
                    q, k, (((1,), (1,)), ((), ())), preferred_element_type=jnp.float32
                )
                * factor,
                FAR,
            )
            for k, v, dist, reach in pieces
        ]
        for q, pieces, before in units
    ]
    tops = []
    for parts, (q, pieces, before) in zip(scores, units):
        found = [jnp.max(s, axis=1, keepdims=True) for s in parts]
        if before is not None:
            found.append(before)
        tops.append(functools.reduce(jnp.maximum, found))
    probs = [
        [jnp.exp2(s - m).astype(jnp.bfloat16) for s in parts] for parts, m in zip(scores, tops)
    ]
    sums = []
    for parts, (q, pieces, before) in zip(probs, units):
        total = None
        for p, (k, v, dist, reach) in zip(parts, pieces):
            both = jnp.concatenate([v, jnp.ones_like(v)], axis=1)
            got = jnp.dot(p, both, preferred_element_type=jnp.float32)
            total = got if total is None else total + got
        sums.append(total)
    return tops, sums


def attend_tile(q_ref, tile_ref, dist_ref, reach_of, heads, state, geometry):
    high, wide, span, frames, head_dim, factor, step = geometry
    cells = high * wide
    acc_ref, sum_ref, max_ref = state
    for at, head in enumerate(heads):
        cols = slice(head * head_dim, (head + 1) * head_dim)
        outs = slice(at * head_dim, (at + 1) * head_dim)
        starts = range(0, q_ref.shape[0], step)
        units = []
        for start in starts:
            near = dist_ref[start % cells : start % cells + step, : tile_ref.shape[1]]
            piece = (tile_ref[0, :, cols], tile_ref[1, :, cols], near, reach_of(head))
            units.append((q_ref[start : start + step, cols], [piece], None))
        for start, m, got in zip(starts, *attend(units, factor)):
            rows = slice(start, start + step)
            acc_ref[rows, outs] = got[:, :head_dim]
            sum_ref[rows, outs] = got[:, head_dim:]
            max_ref[rows, outs] = jnp.broadcast_to(m, (step, head_dim))


def begin_kernel(radius_ref, mask_ref, q_ref, tile_ref, *outs, geometry, heads):
    *state, dist_ref, reach_ref = outs
    high, wide, span, frames = geometry[:4]
    dist_ref[...] = distances(high, wide, span, frames)
    stretch_at = lax.axis_index("tm")
    line = (1, reach_ref.shape[1])
    for head in range(heads):
        radius = radius_ref[head]
        seen = mask_ref[stretch_at, 0, head] > 0
        reach_ref[head : head + 1] = jnp.full(line, radius, jnp.int32)
        reach_ref[heads + head : heads + head + 1] = jnp.full(
            line, jnp.where(seen, radius, -1), jnp.int32
        )
    attend_tile(q_ref, tile_ref, dist_ref, lambda h: radius_ref[h], (0,), state, geometry)


def tile_kernel(q_ref, tile_ref, dist_ref, reach_ref, *state, geometry, heads):
    attend_tile(
        q_ref,
        tile_ref,
        dist_ref,
        lambda h: reach_ref[h : h + 1, :1],
        range(1, heads),
        state,
        geometry,
    )


def pick_state(head_state, state, head, rows, head_dim):
    refs = head_state if head == 0 else state
    at = max(head - 1, 0) * head_dim
    return [ref[rows, at : at + head_dim] for ref in refs]


def rest_kernel(
    q_ref,
    edge_ref,
    first_tile_ref,
    first_edge_ref,
    *rest,
    geometry,
    heads,
    flips,
):
    head_state, dist_ref, reach_ref, state, outs = rest[:3], rest[3], rest[4], rest[5:8], rest[8:]
    high, wide, span, frames, head_dim, factor, step = geometry
    cells = high * wide
    base = frames * cells
    head_at = lax.axis_index("head")
    stretch_at = lax.axis_index("tm")

    def run(with_first):
        for flip, out_ref in zip(flips, outs):
            start = pl.multiple_of(jnp.bitwise_xor(head_at, flip) * step, step)
            rows = pl.ds(start, step)
            near = dist_ref[pl.ds(pl.multiple_of(lax.rem(start, cells), step), step)]
            beyond = near[:, base:]
            units = []
            olds = []
            for head in range(heads):
                cols = slice(head * head_dim, (head + 1) * head_dim)
                sources = [(edge_ref, beyond, head)]
                if with_first:
                    sources.append((first_tile_ref, near[:, :base], heads + head))
                    sources.append((first_edge_ref, beyond, heads + head))
                pieces = [
                    (ref[0, :, cols], ref[1, :, cols], dist, reach_ref[row : row + 1, :1])
                    for ref, dist, row in sources
                ]
                olds.append(pick_state(head_state, state, head, rows, head_dim))
                units.append((q_ref[rows, cols], pieces, olds[-1][2][:, :1]))
            for head, (m, got) in enumerate(zip(*attend(units, factor))):
                old_acc, old_total, old_max = olds[head]
                shrink = jnp.exp2(old_max - m)
                acc = old_acc * shrink + got[:, :head_dim]
                total = old_total * shrink + got[:, head_dim:]
                cols = slice(head * head_dim, (head + 1) * head_dim)
                out_ref[:, cols] = (acc / total).astype(jnp.bfloat16)

    @pl.when(stretch_at > 0)
    def _():
        run(True)

    @pl.when(stretch_at == 0)
    def _():
        run(False)


def copy_kernel(in_ref, out_ref):
    out_ref[...] = in_ref[...]


def stack_kernel(*refs):
    *parts, out_ref = refs
    tile_at = lax.axis_index("tile")
    for flip, part in enumerate(parts):
        tall = part.shape[0]
        top = pl.multiple_of(jnp.bitwise_xor(tile_at, flip) * tall, 16)
        out_ref[pl.ds(top, tall)] = part[...]


def project_kernel(w_ref, part_ref, own_ref, got_ref, out_ref, *, flip):
    broad = part_ref.shape[1]
    half = jnp.bitwise_xor(lax.axis_index("tm"), flip)
    cols = pl.ds(pl.multiple_of(half * broad, 128), broad)
    total = jnp.dot(own_ref[...], w_ref[:, cols], preferred_element_type=jnp.float32)
    total += jnp.dot(got_ref[...], part_ref[...], preferred_element_type=jnp.float32)
    out_ref[...] = total.astype(out_ref.dtype)


def add_kernel(mine_ref, got_ref, *rest, flip):
    out_ref, sum_ref, sems = rest[-3:]
    pieces, tall, broad = sum_ref.shape
    half = jnp.bitwise_xor(lax.axis_index("tm"), flip)
    cols = pl.ds(pl.multiple_of(half * broad, 128), broad)
    copies = []
    for i in range(pieces):
        rows = slice(i * tall, (i + 1) * tall)
        sum_ref[i] = (mine_ref[rows] + got_ref[rows].astype(jnp.float32)).astype(jnp.bfloat16)
        copies.append(pltpu.make_async_copy(sum_ref.at[i], out_ref.at[rows, cols], sems.at[i]))
        copies[-1].start()
    for copy in copies:
        copy.wait()


def two_by_two(query, keys, values, out_weight, radius, block_mask):
    span = RMAX
    frames, high, wide, channels = query.shape[2:]
    heads = radius.shape[0]
    head_dim = channels // heads
    cells = high * wide
    tokens = frames * cells
    groups = lax.axis_size("head")
    tiles = lax.axis_size("tile")
    depth, width = out_weight.shape
    step = tokens // groups
    geometry = (high, wide, span, frames, head_dim, LOG2E / math.sqrt(head_dim), step)
    count = frames * (cells + span * (wide + high + span))
    smem = pl.BlockSpec(memory_space=pltpu.SMEM)
    vmem = pl.BlockSpec(memory_space=pltpu.VMEM)
    hbm = pl.BlockSpec(memory_space=pltpu.HBM)
    bf16, f32 = jnp.bfloat16, jnp.float32
    shape = jax.ShapeDtypeStruct

    def call(kernel, out_shape, specs, *args, name, scratch=(), flops=0, **keys_of):
        return pl.pallas_call(
            functools.partial(kernel, **keys_of) if keys_of else kernel,
            out_shape=out_shape,
            in_specs=specs,
            out_specs=jax.tree.map(lambda _: vmem, out_shape),
            scratch_shapes=scratch,
            cost_estimate=pl.CostEstimate(flops=flops, bytes_accessed=0, transcendentals=0),
            compiler_params=pltpu.CompilerParams(vmem_limit_bytes=VMEM_LIMIT),
            name=name,
        )(*args)

    def flipped(value, axis, flip):
        return lax.ppermute(value, axis, [(i, i ^ flip) for i in range(lax.axis_size(axis))])

    q = query.reshape(tokens, channels)
    k = keys.reshape(tokens, channels)
    v = values.reshape(tokens, channels)

    tall, broad = depth // tiles, width // 2
    part_shape = shape((tall, broad), bf16)
    part = call(
        part_kernel,
        part_shape,
        [hbm],
        pltpu.with_memory_space_constraint(out_weight, pltpu.HBM),
        name="part",
        scratch=[pltpu.SemaphoreType.DMA],
    )
    *faces, tile = call(
        face_kernel,
        [
            shape((2, frames, span * wide, channels), bf16),
            shape((2, frames, span * high, channels), bf16),
            shape((2, frames, span * span, channels), bf16),
            shape((2, tokens, channels), bf16),
        ],
        [vmem] * 3,
        k,
        v,
        part,
        name="faces",
        geometry=geometry,
    )
    faces = [flipped(face, "tile", flip) for face, flip in zip(faces, (2, 1, 3))]
    lone = flipped(part, "head", 2)
    begun = call(
        begin_kernel,
        [shape((tokens, head_dim), f32)] * 3
        + [shape((cells, count), jnp.int32), shape((2 * heads, head_dim), jnp.int32)],
        [smem] * 2 + [vmem] * 2,
        radius,
        block_mask.transpose(1, 2, 0),
        q,
        tile,
        name="begin",
        geometry=geometry,
        heads=heads,
    )
    begun, tile = lax.optimization_barrier((begun, tile))
    first_tile = lax.ppermute(tile, "tm", [(0, 1)])
    state = call(
        tile_kernel,
        [shape((tokens, channels - head_dim), f32)] * 3,
        [vmem] * 4,
        q,
        tile,
        *begun[3:],
        name="tile",
        geometry=geometry,
        heads=heads,
    )
    lone, state = lax.optimization_barrier((lone, state))
    lone = call(copy_kernel, part_shape, [vmem], lone, name="lone", flops=20 * 10**9)
    lone, state, faces = lax.optimization_barrier((lone, state, faces))
    edge = call(
        edge_kernel, shape((2, count - tokens, channels), bf16), [vmem] * 3, *faces, name="edges"
    )
    first_edge = lax.ppermute(edge, "tm", [(0, 1)])
    parts = [lone] + [flipped(lone, "tile", flip) for flip in range(1, tiles)]

    def rest(state, *flips, flops=0):
        return call(
            rest_kernel,
            [shape((step, channels), bf16)] * len(flips),
            [vmem] * 12,
            q,
            edge,
            first_tile,
            first_edge,
            *begun,
            *state,
            name="rest",
            geometry=geometry,
            heads=heads,
            flips=flips,
            flops=flops,
        )

    (for_side,) = rest(state, 3)
    got_side = flipped(for_side, "head", 2)
    state, for_side = lax.optimization_barrier((state, for_side))
    for_far, own_side = rest(state, 2, 1)
    got_far = flipped(for_far, "head", 2)
    order = [0, 2, 1, 3]
    parts, own_side = lax.optimization_barrier(([parts[i] for i in order], own_side))
    parts = [parts[i] for i in order]
    here = call(
        stack_kernel, shape((depth, broad), bf16), [vmem] * tiles, *parts, name="stack"
    )

    def project(part, mine, got, kind, flip, flops=0):
        return call(
            project_kernel,
            shape((step, broad), kind),
            [vmem] * 4,
            out_weight,
            part,
            mine,
            got,
            name="project",
            flops=flops,
            flip=flip,
        )

    for_side = [project(here, own_side, got_side, bf16, 0, 20 * 10**9)]
    from_side = [flipped(for_side[0], "head", 1)]
    state, here, for_side[0] = lax.optimization_barrier((state, here, for_side[0]))
    there = flipped(here, "tm", 1)
    (own,) = rest(state, 0, flops=20 * 10**9)
    own_side, own = lax.optimization_barrier((own_side, own))
    for_side.append(project(there, own_side, got_side, bf16, 1))
    from_side.append(flipped(for_side[1], "head", 1))
    own, for_side[1] = lax.optimization_barrier((own, for_side[1]))
    mine = [
        project(here, own, got_far, f32, 0),
        project(there, own, got_far, f32, 1, 20 * 10**9),
    ]
    pieces = 2
    mixed = []
    for flip in range(2):
        mixed = [
            pl.pallas_call(
                functools.partial(add_kernel, flip=flip),
                out_shape=shape((step, width), bf16),
                in_specs=[vmem] * 2 + [hbm] * flip,
                out_specs=hbm,
                input_output_aliases={2: 0} if flip else {},
                scratch_shapes=[
                    pltpu.VMEM((pieces, step // pieces, broad), bf16),
                    pltpu.SemaphoreType.DMA((pieces,)),
                ],
                compiler_params=pltpu.CompilerParams(vmem_limit_bytes=VMEM_LIMIT),
                name="add",
            )(mine[flip], from_side[flip], *mixed)
        ]
    (mixed,) = mixed
    return mixed.reshape(1, 1, step, width)


def solution(mesh):
    in_specs = (
        P("tm", "tile", None, None, None, "head"),
        P("tm", "tile", None, None, None, "head"),
        P("tm", "tile", None, None, None, "head"),
        P("head", None),
        P("head"),
        P("head", None, None),
    )
    out_specs = P("tm", "tile", "head", None)
    small = dict(mesh.shape) == {"tm": 2, "tile": 4, "head": 4}
    return jax.shard_map(
        two_by_two if small else any_grid,
        mesh=mesh,
        in_specs=in_specs,
        out_specs=out_specs,
        check_vma=False,
    )
```

```python
import functools
import math

import jax
import jax.numpy as jnp
from jax import lax
from jax.experimental import pallas as pl
from jax.experimental.pallas import tpu as pltpu
from jax.sharding import PartitionSpec as P

RMAX = 4
FAR = -1e30
LOG2E = 1.4426950408889634
VMEM_LIMIT = 24 * 1024 * 1024


def passed_along(value, axis, by):
    peers = lax.axis_size(axis)
    pairs = [(i, i + by) for i in range(peers) if 0 <= i + by < peers]
    return lax.ppermute(value, axis, pairs)


def widen(key_part, value_part, span, row_move, col_move):
    grid = math.isqrt(lax.axis_size("tile"))
    above = None
    below = None
    for offset in (grid, -grid):
        if offset > 0:
            face_key = key_part[:, :, key_part.shape[2] - span :]
            face_value = value_part[:, :, value_part.shape[2] - span :]
        else:
            face_key = key_part[:, :, :span]
            face_value = value_part[:, :, :span]
        got = row_move(face_key, face_value, offset)
        if offset > 0:
            above = got
        else:
            below = got
    key_rows = jnp.concatenate([above[0], key_part, below[0]], axis=2)
    value_rows = jnp.concatenate([above[1], value_part, below[1]], axis=2)
    left = None
    right = None
    for offset in (1, -1):
        if offset > 0:
            face_key = key_rows[:, :, :, key_rows.shape[3] - span :]
            face_value = value_rows[:, :, :, value_rows.shape[3] - span :]
        else:
            face_key = key_rows[:, :, :, :span]
            face_value = value_rows[:, :, :, :span]
        got = col_move(face_key, face_value, offset)
        if offset > 0:
            left = got
        else:
            right = got
    key_full = jnp.concatenate([left[0], key_rows, right[0]], axis=3)
    value_full = jnp.concatenate([left[1], value_rows, right[1]], axis=3)
    return (key_full, value_full)


def windows_of(block, half_high, half_wide, win_high, win_wide, heads_here, head_dim):
    parts = []
    for band in (0, 1):
        for strip in (0, 1):
            parts.append(
                block[
                    :,
                    band * half_high : band * half_high + win_high,
                    strip * half_wide : strip * half_wide + win_wide,
                ]
            )
    stacked = jnp.stack(parts)
    return stacked.reshape(4, -1, heads_here, head_dim)


def any_grid(query, keys, values, out_weight, radius, block_mask):
    span = RMAX
    grid = math.isqrt(lax.axis_size("tile"))
    tile_at = lax.axis_index("tile")
    row_at = tile_at // grid
    col_at = tile_at % grid
    stretch_at = lax.axis_index("tm")
    frames, high, wide, channels = query.shape[2:]
    heads_here = radius.shape[0]
    head_dim = channels // heads_here
    tokens_here = frames * high * wide
    half_high = high // 2
    half_wide = wide // 2
    win_high = half_high + 2 * span
    win_wide = half_wide + 2 * span
    quarter = frames * half_high * half_wide
    queries = query[0, 0].reshape(frames, 2, half_high, 2, half_wide, channels)
    queries = queries.transpose(1, 3, 0, 2, 4, 5).reshape(4, quarter, heads_here, head_dim)
    query_y = jnp.broadcast_to(
        jnp.arange(half_high, dtype=jnp.int32)[None, :, None], (frames, half_high, half_wide)
    ).reshape(-1)
    query_x = jnp.broadcast_to(
        jnp.arange(half_wide, dtype=jnp.int32)[None, None, :], (frames, half_high, half_wide)
    ).reshape(-1)
    key_y = jnp.broadcast_to(
        jnp.arange(win_high, dtype=jnp.int32)[None, :, None] - span, (frames, win_high, win_wide)
    ).reshape(-1)
    key_x = jnp.broadcast_to(
        jnp.arange(win_wide, dtype=jnp.int32)[None, None, :] - span, (frames, win_high, win_wide)
    ).reshape(-1)
    band_at = jnp.array([0, 0, 1, 1], dtype=jnp.int32)
    strip_at = jnp.array([0, 1, 0, 1], dtype=jnp.int32)
    global_y = row_at * high + band_at[:, None] * half_high + key_y[None, :]
    global_x = col_at * wide + strip_at[:, None] * half_wide + key_x[None, :]
    inside = (global_y >= 0) & (global_y < grid * high) & (global_x >= 0) & (global_x < grid * wide)
    distance = jnp.maximum(
        jnp.abs(query_y[:, None] - key_y[None, :]), jnp.abs(query_x[:, None] - key_x[None, :])
    )
    near = distance[None, :, :] <= radius[:, None, None]
    allowed = near[None, :, :, :] & inside[:, None, None, :]
    scale = 1.0 / math.sqrt(head_dim)
    initial = (
        jnp.full((4, heads_here, quarter), -1e30, jnp.float32),
        jnp.zeros((4, heads_here, quarter), jnp.float32),
        jnp.zeros((4, heads_here, quarter, head_dim), jnp.float32),
    )

    def tile_move(face_key, face_value, offset):
        return passed_along((face_key, face_value), "tile", offset)

    key_all, value_all = (
        lax.all_gather(keys[0], "tm", axis=0, tiled=True),
        lax.all_gather(values[0], "tm", axis=0, tiled=True),
    )
    key_full, value_full = widen(key_all, value_all, span, tile_move, tile_move)
    stretch_ids = jnp.arange(key_full.shape[0], dtype=jnp.int32)

    def one_stretch(state, item):
        key_block, value_block, stretch_id = item
        visible = (
            lax.dynamic_slice_in_dim(
                lax.dynamic_index_in_dim(block_mask, stretch_at, 1, False), stretch_id, 1, 1
            )[:, 0]
            > 0
        )
        best, total, acc = state
        key_win = windows_of(
            key_block, half_high, half_wide, win_high, win_wide, heads_here, head_dim
        )
        value_win = windows_of(
            value_block, half_high, half_wide, win_high, win_wide, heads_here, head_dim
        )
        usable = allowed & visible[None, :, None, None]
        scores = (
            jnp.einsum("nqhd,nkhd->nhqk", queries, key_win, preferred_element_type=jnp.float32)
            * scale
        )
        masked = jnp.where(usable, scores, jnp.float32(-1e30))
        fresh = jnp.maximum(best, jnp.max(masked, axis=3))
        probs = jnp.where(usable, jnp.exp(scores - fresh[..., None]), jnp.float32(0.0))
        shrink = jnp.exp(best - fresh)
        total = total * shrink + jnp.sum(probs, axis=3)
        acc = acc * shrink[..., None] + jnp.einsum(
            "nhqk,nkhd->nhqd",
            probs.astype(jnp.bfloat16),
            value_win,
            preferred_element_type=jnp.float32,
        )
        return ((fresh, total, acc), None)

    final, unused = lax.scan(one_stretch, initial, (key_full, value_full, stretch_ids))
    best, total, acc = final
    attn = (acc / total[..., None]).astype(jnp.bfloat16)
    attn = attn.transpose(0, 2, 1, 3).reshape(
        2, 2, frames, half_high, half_wide, heads_here * head_dim
    )
    attn = attn.transpose(2, 0, 3, 1, 4, 5).reshape(tokens_here, heads_here * head_dim)
    mixed = lax.psum_scatter(
        jnp.dot(attn, out_weight, preferred_element_type=jnp.float32).astype(jnp.bfloat16),
        "head",
        scatter_dimension=0,
        tiled=True,
    )
    return mixed.reshape(1, 1, -1, out_weight.shape[1])


def tile_place():
    tile_at = lax.axis_index("tile")
    return tile_at // 2, tile_at % 2


def part_kernel(w_ref, part_ref, sem):
    tall, broad = part_ref.shape
    top = pl.multiple_of(lax.axis_index("tile") * tall, 16)
    left = pl.multiple_of(lax.axis_index("tm") * broad, 128)
    copy = pltpu.make_async_copy(w_ref.at[pl.ds(top, tall), pl.ds(left, broad)], part_ref, sem)
    copy.start()
    copy.wait()


def face_kernel(k_ref, v_ref, part_ref, row_ref, col_ref, corner_ref, tile_ref, *, geometry):
    high, wide, span, frames = geometry[:4]
    cells = high * wide
    row_at, col_at = tile_place()
    y0 = jnp.where(row_at == 0, high - span, 0)
    x0 = jnp.where(col_at == 0, wide - span, 0)

    def picker(count, cell_of):
        row = lax.broadcasted_iota(jnp.int32, (count, cells), 0)
        col = lax.broadcasted_iota(jnp.int32, (count, cells), 1)
        return (col == cell_of(row)).astype(jnp.bfloat16)

    beside = picker(high * span, lambda i: (i // span) * wide + x0 + i % span)
    across = picker(span * span, lambda i: (y0 + i // span) * wide + x0 + i % span)
    for which, ref in enumerate((k_ref, v_ref)):
        tile_ref[which] = ref[...]
        for f in range(frames):
            start = pl.multiple_of(f * cells + y0 * wide, 16)
            row_ref[which, f] = ref[pl.ds(start, span * wide)]
            whole = ref[f * cells : (f + 1) * cells]
            col_ref[which, f] = jnp.dot(
                beside, whole, preferred_element_type=jnp.float32
            ).astype(jnp.bfloat16)
            corner_ref[which, f] = jnp.dot(
                across, whole, preferred_element_type=jnp.float32
            ).astype(jnp.bfloat16)


def edge_kernel(row_ref, col_ref, corner_ref, out_ref):
    for which in range(2):
        at = 0
        for part in (row_ref, col_ref, corner_ref):
            for f in range(part.shape[1]):
                size = part.shape[2]
                out_ref[which, at : at + size] = part[which, f]
                at += size


def distances(high, wide, span, frames):
    row_at, col_at = tile_place()
    cells = high * wide
    count = frames * (cells + span * (wide + high + span))
    j = lax.broadcasted_iota(jnp.int32, (1, count), 1)
    y_off = jnp.where(row_at == 0, high, -span)
    x_off = jnp.where(col_at == 0, wide, -span)
    c = j % cells
    ky, kx = c // wide, c % wide
    base = frames * cells
    c = (j - base) % (span * wide)
    ky = jnp.where(j >= base, y_off + c // wide, ky)
    kx = jnp.where(j >= base, c % wide, kx)
    base += frames * span * wide
    c = (j - base) % (span * high)
    ky = jnp.where(j >= base, c // span, ky)
    kx = jnp.where(j >= base, x_off + c % span, kx)
    base += frames * span * high
    c = (j - base) % (span * span)
    ky = jnp.where(j >= base, y_off + c // span, ky)
    kx = jnp.where(j >= base, x_off + c % span, kx)
    i = lax.broadcasted_iota(jnp.int32, (cells, 1), 0)
    return jnp.maximum(jnp.abs(i // wide - ky), jnp.abs(i % wide - kx))


def attend(units, factor):
    scores = [
        [
            jnp.where(
                dist <= reach,
                lax.dot_general(
                    q, k, (((1,), (1,)), ((), ())), preferred_element_type=jnp.float32
                )
                * factor,
                FAR,
            )
            for k, v, dist, reach in pieces
        ]
        for q, pieces, before in units
    ]
    tops = []
    for parts, (q, pieces, before) in zip(scores, units):
        found = [jnp.max(s, axis=1, keepdims=True) for s in parts]
        if before is not None:
            found.append(before)
        tops.append(functools.reduce(jnp.maximum, found))
    probs = [
        [jnp.exp2(s - m).astype(jnp.bfloat16) for s in parts] for parts, m in zip(scores, tops)
    ]
    sums = []
    for parts, (q, pieces, before) in zip(probs, units):
        total = None
        for p, (k, v, dist, reach) in zip(parts, pieces):
            both = jnp.concatenate([v, jnp.ones_like(v)], axis=1)
            got = jnp.dot(p, both, preferred_element_type=jnp.float32)
            total = got if total is None else total + got
        sums.append(total)
    return tops, sums


def attend_tile(q_ref, tile_ref, dist_ref, reach_of, heads, state, geometry):
    high, wide, span, frames, head_dim, factor, step = geometry
    cells = high * wide
    acc_ref, sum_ref, max_ref = state
    for at, head in enumerate(heads):
        cols = slice(head * head_dim, (head + 1) * head_dim)
        outs = slice(at * head_dim, (at + 1) * head_dim)
        starts = range(0, q_ref.shape[0], step)
        units = []
        for start in starts:
            near = dist_ref[start % cells : start % cells + step, : tile_ref.shape[1]]
            piece = (tile_ref[0, :, cols], tile_ref[1, :, cols], near, reach_of(head))
            units.append((q_ref[start : start + step, cols], [piece], None))
        for start, m, got in zip(starts, *attend(units, factor)):
            rows = slice(start, start + step)
            acc_ref[rows, outs] = got[:, :head_dim]
            sum_ref[rows, outs] = got[:, head_dim:]
            max_ref[rows, outs] = jnp.broadcast_to(m, (step, head_dim))


def begin_kernel(radius_ref, mask_ref, q_ref, tile_ref, *outs, geometry, heads):
    *state, dist_ref, reach_ref = outs
    high, wide, span, frames = geometry[:4]
    dist_ref[...] = distances(high, wide, span, frames)
    stretch_at = lax.axis_index("tm")
    line = (1, reach_ref.shape[1])
    for head in range(heads):
        radius = radius_ref[head]
        seen = mask_ref[stretch_at, 0, head] > 0
        reach_ref[head : head + 1] = jnp.full(line, radius, jnp.int32)
        reach_ref[heads + head : heads + head + 1] = jnp.full(
            line, jnp.where(seen, radius, -1), jnp.int32
        )
    attend_tile(q_ref, tile_ref, dist_ref, lambda h: radius_ref[h], (0,), state, geometry)


def tile_kernel(q_ref, tile_ref, dist_ref, reach_ref, *state, geometry, heads):
    attend_tile(
        q_ref,
        tile_ref,
        dist_ref,
        lambda h: reach_ref[h : h + 1, :1],
        range(1, heads),
        state,
        geometry,
    )


def pick_state(head_state, state, head, rows, head_dim):
    refs = head_state if head == 0 else state
    at = max(head - 1, 0) * head_dim
    return [ref[rows, at : at + head_dim] for ref in refs]


def rest_kernel(
    q_ref,
    edge_ref,
    first_tile_ref,
    first_edge_ref,
    *rest,
    geometry,
    heads,
    flips,
):
    head_state, dist_ref, reach_ref, state, outs = rest[:3], rest[3], rest[4], rest[5:8], rest[8:]
    high, wide, span, frames, head_dim, factor, step = geometry
    cells = high * wide
    base = frames * cells
    head_at = lax.axis_index("head")
    stretch_at = lax.axis_index("tm")

    def run(with_first):
        for flip, out_ref in zip(flips, outs):
            start = pl.multiple_of(jnp.bitwise_xor(head_at, flip) * step, step)
            rows = pl.ds(start, step)
            near = dist_ref[pl.ds(pl.multiple_of(lax.rem(start, cells), step), step)]
            beyond = near[:, base:]
            units = []
            olds = []
            for head in range(heads):
                cols = slice(head * head_dim, (head + 1) * head_dim)
                sources = [(edge_ref, beyond, head)]
                if with_first:
                    sources.append((first_tile_ref, near[:, :base], heads + head))
                    sources.append((first_edge_ref, beyond, heads + head))
                pieces = [
                    (ref[0, :, cols], ref[1, :, cols], dist, reach_ref[row : row + 1, :1])
                    for ref, dist, row in sources
                ]
                olds.append(pick_state(head_state, state, head, rows, head_dim))
                units.append((q_ref[rows, cols], pieces, olds[-1][2][:, :1]))
            for head, (m, got) in enumerate(zip(*attend(units, factor))):
                old_acc, old_total, old_max = olds[head]
                shrink = jnp.exp2(old_max - m)
                acc = old_acc * shrink + got[:, :head_dim]
                total = old_total * shrink + got[:, head_dim:]
                cols = slice(head * head_dim, (head + 1) * head_dim)
                out_ref[:, cols] = (acc / total).astype(jnp.bfloat16)

    @pl.when(stretch_at > 0)
    def _():
        run(True)

    @pl.when(stretch_at == 0)
    def _():
        run(False)


def copy_kernel(in_ref, out_ref):
    out_ref[...] = in_ref[...]


def stack_kernel(*refs):
    *parts, out_ref = refs
    tile_at = lax.axis_index("tile")
    for flip, part in enumerate(parts):
        tall = part.shape[0]
        top = pl.multiple_of(jnp.bitwise_xor(tile_at, flip) * tall, 16)
        out_ref[pl.ds(top, tall)] = part[...]


def project_kernel(w_ref, part_ref, own_ref, got_ref, out_ref, *, flip):
    broad = part_ref.shape[1]
    half = jnp.bitwise_xor(lax.axis_index("tm"), flip)
    cols = pl.ds(pl.multiple_of(half * broad, 128), broad)
    total = jnp.dot(own_ref[...], w_ref[:, cols], preferred_element_type=jnp.float32)
    total += jnp.dot(got_ref[...], part_ref[...], preferred_element_type=jnp.float32)
    out_ref[...] = total.astype(out_ref.dtype)


def add_kernel(mine_ref, got_ref, *rest, flip):
    out_ref, sum_ref, sems = rest[-3:]
    pieces, tall, broad = sum_ref.shape
    half = jnp.bitwise_xor(lax.axis_index("tm"), flip)
    cols = pl.ds(pl.multiple_of(half * broad, 128), broad)
    copies = []
    for i in range(pieces):
        rows = slice(i * tall, (i + 1) * tall)
        sum_ref[i] = (mine_ref[rows] + got_ref[rows].astype(jnp.float32)).astype(jnp.bfloat16)
        copies.append(pltpu.make_async_copy(sum_ref.at[i], out_ref.at[rows, cols], sems.at[i]))
        copies[-1].start()
    for copy in copies:
        copy.wait()


def two_by_two(query, keys, values, out_weight, radius, block_mask):
    span = RMAX
    frames, high, wide, channels = query.shape[2:]
    heads = radius.shape[0]
    head_dim = channels // heads
    cells = high * wide
    tokens = frames * cells
    groups = lax.axis_size("head")
    tiles = lax.axis_size("tile")
    depth, width = out_weight.shape
    step = tokens // groups
    geometry = (high, wide, span, frames, head_dim, LOG2E / math.sqrt(head_dim), step)
    count = frames * (cells + span * (wide + high + span))
    smem = pl.BlockSpec(memory_space=pltpu.SMEM)
    vmem = pl.BlockSpec(memory_space=pltpu.VMEM)
    hbm = pl.BlockSpec(memory_space=pltpu.HBM)
    bf16, f32 = jnp.bfloat16, jnp.float32
    shape = jax.ShapeDtypeStruct

    def call(kernel, out_shape, specs, *args, name, scratch=(), flops=0, **keys_of):
        return pl.pallas_call(
            functools.partial(kernel, **keys_of) if keys_of else kernel,
            out_shape=out_shape,
            in_specs=specs,
            out_specs=jax.tree.map(lambda _: vmem, out_shape),
            scratch_shapes=scratch,
            cost_estimate=pl.CostEstimate(flops=flops, bytes_accessed=0, transcendentals=0),
            compiler_params=pltpu.CompilerParams(vmem_limit_bytes=VMEM_LIMIT),
            name=name,
        )(*args)

    def flipped(value, axis, flip):
        return lax.ppermute(value, axis, [(i, i ^ flip) for i in range(lax.axis_size(axis))])

    q = query.reshape(tokens, channels)
    k = keys.reshape(tokens, channels)
    v = values.reshape(tokens, channels)

    tall, broad = depth // tiles, width // 2
    part_shape = shape((tall, broad), bf16)
    part = call(
        part_kernel,
        part_shape,
        [hbm],
        pltpu.with_memory_space_constraint(out_weight, pltpu.HBM),
        name="part",
        scratch=[pltpu.SemaphoreType.DMA],
    )
    *faces, tile = call(
        face_kernel,
        [
            shape((2, frames, span * wide, channels), bf16),
            shape((2, frames, span * high, channels), bf16),
            shape((2, frames, span * span, channels), bf16),
            shape((2, tokens, channels), bf16),
        ],
        [vmem] * 3,
        k,
        v,
        part,
        name="faces",
        geometry=geometry,
    )
    faces = [flipped(face, "tile", flip) for face, flip in zip(faces, (2, 1, 3))]
    lone = flipped(part, "head", 2)
    begun = call(
        begin_kernel,
        [shape((tokens, head_dim), f32)] * 3
        + [shape((cells, count), jnp.int32), shape((2 * heads, head_dim), jnp.int32)],
        [smem] * 2 + [vmem] * 2,
        radius,
        block_mask.transpose(1, 2, 0),
        q,
        tile,
        name="begin",
        geometry=geometry,
        heads=heads,
    )
    begun, tile = lax.optimization_barrier((begun, tile))
    first_tile = lax.ppermute(tile, "tm", [(0, 1)])
    state = call(
        tile_kernel,
        [shape((tokens, channels - head_dim), f32)] * 3,
        [vmem] * 4,
        q,
        tile,
        *begun[3:],
        name="tile",
        geometry=geometry,
        heads=heads,
    )
    lone, state = lax.optimization_barrier((lone, state))
    lone = call(copy_kernel, part_shape, [vmem], lone, name="lone", flops=20 * 10**9)
    lone, state, faces = lax.optimization_barrier((lone, state, faces))
    edge = call(
        edge_kernel, shape((2, count - tokens, channels), bf16), [vmem] * 3, *faces, name="edges"
    )
    first_edge = lax.ppermute(edge, "tm", [(0, 1)])
    parts = [lone] + [flipped(lone, "tile", flip) for flip in range(1, tiles)]

    def rest(state, *flips, flops=0):
        return call(
            rest_kernel,
            [shape((step, channels), bf16)] * len(flips),
            [vmem] * 12,
            q,
            edge,
            first_tile,
            first_edge,
            *begun,
            *state,
            name="rest",
            geometry=geometry,
            heads=heads,
            flips=flips,
            flops=flops,
        )

    (for_side,) = rest(state, 3)
    got_side = flipped(for_side, "head", 2)
    state, for_side = lax.optimization_barrier((state, for_side))
    for_far, own_side = rest(state, 2, 1)
    got_far = flipped(for_far, "head", 2)
    parts, own_side = lax.optimization_barrier((parts, own_side))
    here = call(
        stack_kernel, shape((depth, broad), bf16), [vmem] * tiles, *parts, name="stack"
    )

    def project(part, mine, got, kind, flip, flops=0):
        return call(
            project_kernel,
            shape((step, broad), kind),
            [vmem] * 4,
            out_weight,
            part,
            mine,
            got,
            name="project",
            flops=flops,
            flip=flip,
        )

    for_side = [project(here, own_side, got_side, bf16, 0, 20 * 10**9)]
    from_side = [flipped(for_side[0], "head", 1)]
    state, here, for_side[0] = lax.optimization_barrier((state, here, for_side[0]))
    there = flipped(here, "tm", 1)
    (own,) = rest(state, 0, flops=20 * 10**9)
    own_side, own = lax.optimization_barrier((own_side, own))
    for_side.append(project(there, own_side, got_side, bf16, 1))
    from_side.append(flipped(for_side[1], "head", 1))
    own, for_side[1] = lax.optimization_barrier((own, for_side[1]))
    mine = [
        project(here, own, got_far, f32, 0),
        project(there, own, got_far, f32, 1, 20 * 10**9),
    ]
    pieces = 1
    mixed = []
    for flip in range(2):
        mixed = [
            pl.pallas_call(
                functools.partial(add_kernel, flip=flip),
                out_shape=shape((step, width), bf16),
                in_specs=[vmem] * 2 + [hbm] * flip,
                out_specs=hbm,
                input_output_aliases={2: 0} if flip else {},
                scratch_shapes=[
                    pltpu.VMEM((pieces, step // pieces, broad), bf16),
                    pltpu.SemaphoreType.DMA((pieces,)),
                ],
                compiler_params=pltpu.CompilerParams(vmem_limit_bytes=VMEM_LIMIT),
                name="add",
            )(mine[flip], from_side[flip], *mixed)
        ]
    (mixed,) = mixed
    return mixed.reshape(1, 1, step, width)


def solution(mesh):
    in_specs = (
        P("tm", "tile", None, None, None, "head"),
        P("tm", "tile", None, None, None, "head"),
        P("tm", "tile", None, None, None, "head"),
        P("head", None),
        P("head"),
        P("head", None, None),
    )
    out_specs = P("tm", "tile", "head", None)
    small = dict(mesh.shape) == {"tm": 2, "tile": 4, "head": 4}
    return jax.shard_map(
        two_by_two if small else any_grid,
        mesh=mesh,
        in_specs=in_specs,
        out_specs=out_specs,
        check_vma=False,
    )
```
